32 devices in a mesh: store: 4 (over x, core), sku: 8 (over z, y).
Axes of the slice: x: 2, y: 2, z: 4, core: 2. Of those that a mesh axis runs over, the one named last changes fastest.
Arguments:
- base_bottom: float32 [32, 13, 4096], P(('store', 'sku')), may hold values from -6 to 6
- weight_bottom: float32 [32, 13, 4096], P(('store', 'sku')), may hold values from 0.5 to 4
- base_category: float32 [32, 13, 1024], P(('store', 'sku')), may hold values from -24 to 24
- weight_category: float32 [32, 13, 1024], P(('store', 'sku')), may hold values from 0.02 to 0.2
- base_region: float32 [32, 13, 4096], P(None, None, ('store', 'sku')), may hold values from -24 to 24
- weight_region: float32 [32, 13, 4096], P(None, None, ('store', 'sku')), may hold values from 0.02 to 0.2
- category_map: int32 [4096], replicated, may hold values from 0 to 1023
- region_map: int32 [32], replicated, may hold values from 0 to 31
Outputs:
- reconciled: float32 [32, 13, 4096], P(('store', 'sku'))
- residual: float32 [32, 13, 4096], P(('store', 'sku'))
The draws below stay inside these ranges and needn't reach their ends.
All inputs are finite; a program needn't handle non-finite values.
Results may differ from the reference program's by a relative error of at most 0.0003.
Values sent between devices are 32-bit elements; how exact they have to be, the bound alone decides.
No kernel may reach another device: no remote copies, remote signals or barrier semaphores. Data moves between devices by JAX's collectives and lax.ppermute only.
A program may use at most 128 MiB of HBM per device.

```python
import math
import jax
import jax.numpy as jnp

H = 13
NCAT = 1024
REGIONS = 32
ITERS = 3
STORE = 32
SKU = 4096


def set_ends(entries, stream_key, low, top_value):
    place = [jax.random.randint(jax.random.fold_in(stream_key, axis), (), 0, length) for axis, length in enumerate(entries.shape)]
    widest = entries.shape.index(max(entries.shape))
    neighbour = place[:widest] + [(place[widest] + 1) % entries.shape[widest]] + place[widest + 1:]
    return entries.at[tuple(place)].set(low).at[tuple(neighbour)].set(top_value)


def block_scale(rng, dims, pieces, least, top_value):
    loudness, own = 1.0, jax.random.fold_in(rng, 6)
    for dim, shards_of in pieces:
        heights = jnp.exp(jax.random.uniform(jax.random.fold_in(own, dim), (shards_of,), jnp.float32, least / len(pieces), top_value / len(pieces)))
        loudness = loudness * jnp.repeat(heights, dims[dim] // shards_of).reshape([-1 if axis == dim else 1 for axis in range(len(dims))])
    return loudness


def normal_values(own_key, shape, scale, limit, shards=(), kind=jnp.bfloat16):
    loudness = block_scale(own_key, shape, shards, -0.22, 0.18) if shards else 1.0
    result = jax.random.normal(own_key, shape, jnp.float32) * scale * loudness
    return jnp.minimum(jnp.maximum(result, -limit), limit).astype(kind)


def setup_inputs(seed: int = 0) -> dict:
    keys = jax.random.split(jax.random.key(seed), 9)
    base_bottom = normal_values(keys[0], (STORE, H, SKU), 1.0, 6.0, ((0, 32),), jnp.float32)
    weight_bottom = jnp.clip(jnp.exp(math.log(4.0) - 2.0794415 * jax.random.uniform(keys[1], (STORE, H, SKU), jnp.float32) ** block_scale(keys[1], (STORE, H, SKU), ((0, 32),), -0.2, 0.2)), 0.5, 4.0)
    base_category = normal_values(keys[2], (STORE, H, NCAT), 4.0, 24.0, ((0, 32),), jnp.float32)
    weight_category = jnp.clip(jnp.exp(math.log(0.2) - 2.3025851 * jax.random.uniform(keys[3], (STORE, H, NCAT), jnp.float32) ** block_scale(keys[3], (STORE, H, NCAT), ((0, 32),), -0.2, 0.2)), 0.02, 0.2)
    base_region = normal_values(keys[4], (REGIONS, H, SKU), 4.0, 24.0, ((2, 32),), jnp.float32)
    weight_region = jnp.clip(jnp.exp(math.log(0.2) - 2.3025851 * jax.random.uniform(keys[5], (REGIONS, H, SKU), jnp.float32) ** block_scale(keys[5], (REGIONS, H, SKU), ((2, 32),), -0.2, 0.2)), 0.02, 0.2)
    category_map = set_ends(jax.random.randint(keys[6], (SKU,), 0, NCAT), jax.random.fold_in(keys[6], 1), 0, NCAT - 1).astype(jnp.int32)
    region_map = set_ends(jax.random.randint(keys[7], (STORE,), 0, REGIONS), jax.random.fold_in(keys[7], 1), 0, REGIONS - 1).astype(jnp.int32)
    return {"base_bottom": base_bottom, "weight_bottom": weight_bottom, "base_category": base_category, "weight_category": weight_category, "base_region": base_region, "weight_region": weight_region, "category_map": category_map, "region_map": region_map}


def category_sums(field, category_map):
    moved = jnp.transpose(field, (2, 0, 1))
    summed = jax.ops.segment_sum(moved, category_map, num_segments=NCAT)
    return jnp.transpose(summed, (1, 2, 0))


def category_spread(values, category_map):
    return jnp.take(values, category_map, axis=2)


def region_sums(field, region_map):
    return jax.ops.segment_sum(field, region_map, num_segments=REGIONS)


def region_spread(values, region_map):
    return jnp.take(values, region_map, axis=0)


def reference(base_bottom, weight_bottom, base_category, weight_category, base_region, weight_region, category_map, region_map):
    def operate(field):
        first = category_spread(weight_category * category_sums(field, category_map), category_map)
        second = region_spread(weight_region * region_sums(field, region_map), region_map)
        return weight_bottom * field + first + second

    reconciled = base_bottom
    residual = category_spread(weight_category * (base_category - category_sums(base_bottom, category_map)), category_map)
    residual = residual + region_spread(weight_region * (base_region - region_sums(base_bottom, region_map)), region_map)
    direction = residual
    norm_now = jnp.sum(residual * residual)
    for repeat in range(ITERS):
        image = operate(direction)
        step_size = norm_now / jnp.sum(direction * image)
        reconciled = reconciled + step_size * direction
        residual = residual - step_size * image
        norm_next = jnp.sum(residual * residual)
        direction = residual + (norm_next / norm_now) * direction
        norm_now = norm_next
    return reconciled, residual
```

```python
import jax
import jax.numpy as jnp
from jax import lax
from jax.experimental import pallas as pl
from jax.experimental.pallas import tpu as pltpu
from jax.sharding import PartitionSpec as P

LANES = 128
PAD = 16
VMEM = pl.BlockSpec(memory_space=pltpu.VMEM)
SMEM = pl.BlockSpec(memory_space=pltpu.SMEM)


def exchange(blocks):
    return lax.all_to_all(blocks, ("store", "sku"), split_axis=0, concat_axis=0, tiled=True)


def call(body, outs, scratch, args, specs):
    return pl.pallas_call(
        body,
        out_shape=tuple(jax.ShapeDtypeStruct(shape, jnp.float32) for shape in outs),
        in_specs=specs,
        out_specs=tuple(VMEM for _ in outs),
        scratch_shapes=scratch,
        compiler_params=pltpu.CompilerParams(vmem_limit_bytes=40 << 20),
    )(*args)


def valid_rows(horizon):
    return lax.broadcasted_iota(jnp.int32, (PAD, LANES), 0) < horizon


def to_block(rows):
    horizon, lanes = rows.shape
    return jnp.concatenate([rows, jnp.zeros((PAD - horizon, lanes), rows.dtype)], axis=0)


def block_of(natural, j, horizon):
    return natural[0, :, pl.ds(pl.multiple_of(j * LANES, LANES), LANES)]


def category_sums(load, cat_ref, n_blocks, groups):
    width = 4 if n_blocks % 4 == 0 else 1
    lanes = width * LANES
    rows = groups * PAD

    def step(c, total):
        field = jnp.concatenate([load(c * width + i) for i in range(width)], axis=1)
        high = field.astype(jnp.bfloat16)
        low = (field - high.astype(jnp.float32)).astype(jnp.bfloat16)
        members = cat_ref[0:1, pl.ds(pl.multiple_of(c * lanes, LANES), lanes)]
        group = members // LANES
        labels = lax.broadcasted_iota(jnp.int32, (LANES, lanes), 0)
        table = jnp.where(labels == members % LANES, 1.0, 0.0).astype(jnp.bfloat16)
        group = jnp.broadcast_to(group, (PAD, lanes))
        masks = [jnp.where(group == g, 1.0, 0.0).astype(jnp.bfloat16) for g in range(groups)]
        spread = jnp.concatenate([high * m for m in masks] + [low * m for m in masks], axis=0)
        return total + lax.dot_general(
            spread, table, (((1,), (1,)), ((), ())), preferred_element_type=jnp.float32
        )

    total = lax.fori_loop(
        0, n_blocks // width, step, jnp.zeros((2 * rows, LANES), jnp.float32), unroll=2
    )
    return (total[:rows] + total[rows:]).reshape(groups, PAD, LANES)


def category_block(values, cat_ref, j, groups):
    members = cat_ref[0:1, pl.ds(pl.multiple_of(j * LANES, LANES), LANES)]
    members = jnp.broadcast_to(members, (PAD, LANES))
    place = members % LANES
    group = members // LANES
    result = jnp.zeros((PAD, LANES), jnp.float32)
    for g in range(groups):
        found = jnp.take_along_axis(values[g], place, axis=1)
        result = jnp.where(group == g, found, result)
    return result


def region_sums(load, map_ref, sums, n_blocks):
    sums[...] = jnp.zeros_like(sums)

    def step(s, carry):
        g = map_ref[s]
        sums[g] = sums[g] + load(s)
        return carry

    lax.fori_loop(0, n_blocks, step, 0, unroll=4)


def pack_body(base_ref, out_ref):
    n_blocks = out_ref.shape[0]
    horizon = base_ref.shape[1]

    def step(j, carry):
        out_ref[j] = to_block(block_of(base_ref, j, horizon))
        return carry

    lax.fori_loop(0, n_blocks, step, 0, unroll=4)


def category_start_body(
    base_ref, weight_ref, base_cat_ref, weight_cat_ref, cat_ref, spread_ref, diag_ref, wcat_ref
):
    n_blocks = spread_ref.shape[0]
    groups = wcat_ref.shape[0]
    horizon = weight_ref.shape[1]
    sums = category_sums(
        lambda j: to_block(block_of(base_ref, j, horizon)), cat_ref, n_blocks, groups
    )
    values = []
    for g in range(groups):
        lanes = slice(g * LANES, (g + 1) * LANES)
        weight = to_block(weight_cat_ref[0, :, lanes])
        wcat_ref[g] = weight
        values.append(weight * (to_block(base_cat_ref[0, :, lanes]) - sums[g]))

    def step(j, carry):
        diag_ref[j] = to_block(block_of(weight_ref, j, horizon))
        spread_ref[j] = category_block(values, cat_ref, j, groups)
        return carry

    lax.fori_loop(0, n_blocks, step, 0, unroll=2)


def region_start_body(moved_ref, base_ref, weight_ref, cat_part_ref, map_ref, send_ref, sums):
    n_blocks = moved_ref.shape[0]
    n_regions, horizon, _ = weight_ref.shape
    region_sums(lambda s: moved_ref[s], map_ref, sums, n_blocks)

    def scale(g, carry):
        weight = to_block(weight_ref[g])
        sums[g] = weight * (to_block(base_ref[g]) - sums[g])
        return carry

    lax.fori_loop(0, n_regions, scale, 0, unroll=4)

    def place(s, carry):
        send_ref[s, 0:PAD] = cat_part_ref[s]
        send_ref[s, PAD : 2 * PAD] = sums[map_ref[s]]
        return carry

    lax.fori_loop(0, n_blocks, place, 0, unroll=4)


def operate(r_ref, rs_ref, eps, diag_ref, wcat_ref, wreg_ref, cat_ref, map_ref, a_ref, q_ref, sums, merged):
    n_blocks = r_ref.shape[0]
    groups = wcat_ref.shape[0]
    n_regions, horizon, _ = wreg_ref.shape
    region_sums(lambda s: rs_ref[s], map_ref, sums, n_blocks)

    def scale(g, total):
        value = sums[g]
        scaled = to_block(wreg_ref[g]) * value
        sums[g] = scaled
        return total + scaled * value

    delta = lax.fori_loop(0, n_regions, scale, jnp.zeros((PAD, LANES), jnp.float32), unroll=4)

    cats = category_sums(lambda j: r_ref[j], cat_ref, n_blocks, groups)
    values = []
    for g in range(groups):
        scaled = wcat_ref[g] * cats[g]
        values.append(scaled)
        delta = delta + scaled * cats[g]

    def dots(j, carry):
        gamma, delta = carry
        r = r_ref[j]
        square = r * r
        return gamma + square, delta + diag_ref[j] * square

    gamma, delta = lax.fori_loop(
        0, n_blocks, dots, (jnp.zeros((PAD, LANES), jnp.float32), delta), unroll=4
    )
    line = lax.broadcasted_iota(jnp.int32, (PAD, LANES), 0)
    extra = jnp.zeros((PAD, LANES), jnp.float32)
    for i, part in enumerate((gamma, delta, eps)):
        extra = jnp.where(line == horizon + i, jnp.sum(part, axis=0, keepdims=True), extra)

    def place(j, carry):
        a = category_block(values, cat_ref, j, groups) + diag_ref[j] * r_ref[j]
        reg = sums[map_ref[j]]
        if merged:
            q_ref[j, 0:PAD] = a + extra
            q_ref[j, PAD : 2 * PAD] = reg
        else:
            a_ref[j] = a
            q_ref[j] = reg + extra
        return carry

    lax.fori_loop(0, n_blocks, place, 0, unroll=2)


def total_rows(load, n_blocks, horizon):
    total = lax.fori_loop(
        0,
        n_blocks,
        lambda j, total: total + load(j),
        jnp.zeros((PAD, LANES), jnp.float32),
        unroll=4,
    )
    sums = jnp.broadcast_to(jnp.sum(total, axis=1, keepdims=True), (PAD, LANES))
    return [
        jnp.broadcast_to(sums[horizon + i : horizon + i + 1], (PAD, LANES)) for i in range(3)
    ]


def first_body(
    sent_ref, got_ref, diag_ref, wcat_ref, wreg_ref, cat_ref, map_ref, r_ref, rs_ref, send_ref, sums
):
    n_blocks = r_ref.shape[0]

    def step(j, carry):
        r_ref[j] = sent_ref[j, 0:PAD] + got_ref[j, PAD : 2 * PAD]
        rs_ref[j] = got_ref[j, 0:PAD] + sent_ref[j, PAD : 2 * PAD]
        return carry

    lax.fori_loop(0, n_blocks, step, 0, unroll=4)
    operate(
        r_ref, rs_ref, jnp.zeros((PAD, LANES), jnp.float32), diag_ref, wcat_ref, wreg_ref,
        cat_ref, map_ref, None, send_ref, sums, True,
    )


def second_body(
    sent_ref, got_ref, x_ref, r_ref, rs_ref, diag_ref, wcat_ref, wreg_ref, cat_ref, map_ref,
    x_out, r_out, rs_out, s_out, ss_out, scal_ref, send_ref, sums,
):
    n_blocks = r_ref.shape[0]
    horizon = wreg_ref.shape[1]
    gamma, delta, _ = total_rows(lambda j: got_ref[j, 0:PAD], n_blocks, horizon)
    alpha = gamma / delta
    scal_ref[0] = gamma
    scal_ref[1] = delta
    valid = valid_rows(horizon)

    def step(j, eps):
        w = jnp.where(valid, sent_ref[j, 0:PAD] + got_ref[j, PAD : 2 * PAD], 0.0)
        ws = jnp.where(valid, got_ref[j, 0:PAD] + sent_ref[j, PAD : 2 * PAD], 0.0)
        r = r_ref[j]
        x_out[j] = x_ref[j] + alpha * r
        r = r - alpha * w
        r_out[j] = r
        s_out[j] = w
        rs_out[j] = rs_ref[j] - alpha * ws
        ss_out[j] = ws
        return eps + r * w

    eps = lax.fori_loop(0, n_blocks, step, jnp.zeros((PAD, LANES), jnp.float32), unroll=2)
    operate(
        r_out, rs_out, eps, diag_ref, wcat_ref, wreg_ref, cat_ref, map_ref, None, send_ref,
        sums, True,
    )


def third_body(
    sent_ref, got_ref, x_ref, r_ref, rs_ref, p_ref, s_ref, ss_ref, scal_ref,
    diag_ref, wcat_ref, wreg_ref, cat_ref, map_ref,
    x_out, r_out, p_out, s_out, scal_out, a_out, send_ref, sums, rs_out,
):
    n_blocks = r_ref.shape[0]
    horizon = wreg_ref.shape[1]
    gamma, delta, eps = total_rows(lambda j: got_ref[j, 0:PAD], n_blocks, horizon)
    beta = gamma / scal_ref[0]
    curve = delta + 2.0 * beta * eps + beta * beta * scal_ref[1]
    alpha = gamma / curve
    scal_out[0] = gamma
    scal_out[1] = curve
    valid = valid_rows(horizon)

    def step(j, eps):
        w = jnp.where(valid, sent_ref[j, 0:PAD] + got_ref[j, PAD : 2 * PAD], 0.0)
        ws = jnp.where(valid, got_ref[j, 0:PAD] + sent_ref[j, PAD : 2 * PAD], 0.0)
        s = w + beta * s_ref[j]
        r = r_ref[j]
        p = r + beta * p_ref[j]
        x_out[j] = x_ref[j] + alpha * p
        r = r - alpha * s
        r_out[j] = r
        p_out[j] = p
        s_out[j] = s
        rs_out[j] = rs_ref[j] - alpha * (ws + beta * ss_ref[j])
        return eps + r * s

    eps = lax.fori_loop(0, n_blocks, step, jnp.zeros((PAD, LANES), jnp.float32), unroll=2)
    operate(
        r_out, rs_out, eps, diag_ref, wcat_ref, wreg_ref, cat_ref, map_ref, a_out, send_ref,
        sums, False,
    )


def last_body(a_ref, got_ref, x_ref, r_ref, p_ref, s_ref, scal_ref, x_out, r_out):
    n_blocks = r_ref.shape[0]
    horizon = x_out.shape[1]
    gamma, delta, eps = total_rows(lambda j: got_ref[j], n_blocks, horizon)
    beta = gamma / scal_ref[0]
    alpha = gamma / (delta + 2.0 * beta * eps + beta * beta * scal_ref[1])

    def step(j, carry):
        r = r_ref[j]
        s = a_ref[j] + got_ref[j] + beta * s_ref[j]
        p = r + beta * p_ref[j]
        lanes = pl.ds(pl.multiple_of(j * LANES, LANES), LANES)
        x_out[0, :, lanes] = (x_ref[j] + alpha * p)[:horizon]
        r_out[0, :, lanes] = (r - alpha * s)[:horizon]
        return carry

    lax.fori_loop(0, n_blocks, step, 0, unroll=2)


def on_device(
    base_bottom,
    weight_bottom,
    base_category,
    weight_category,
    base_region,
    weight_region,
    category_map,
    region_map,
):
    n_cat = weight_category.shape[2]
    n_regions = weight_region.shape[0]
    n_blocks = region_map.shape[0]
    groups = n_cat // LANES
    cats = category_map.reshape(1, -1)
    blocks = (n_blocks, PAD, LANES)
    double = (n_blocks, 2 * PAD, LANES)
    sums = pltpu.VMEM((n_regions, PAD, LANES), jnp.float32)
    scal = (2, PAD, LANES)

    (x,) = call(pack_body, [blocks], [], (base_bottom,), [VMEM])
    moved = exchange(x)
    cat_part, diag, wcat = call(
        category_start_body,
        [blocks, blocks, (groups, PAD, LANES)],
        [],
        (base_bottom, weight_bottom, base_category, weight_category, cats),
        [VMEM] * 5,
    )
    (sent,) = call(
        region_start_body,
        [double],
        [sums],
        (moved, base_region, weight_region, cat_part, region_map),
        [VMEM] * 4 + [SMEM],
    )
    got = exchange(sent)
    fixed = (diag, wcat, weight_region, cats, region_map)
    fixed_specs = [VMEM] * 4 + [SMEM]
    r, rs, sent = call(
        first_body, [blocks, blocks, double], [sums], (sent, got) + fixed, [VMEM] * 2 + fixed_specs
    )
    got = exchange(sent)
    p = r
    x, r, rs, s, ss, scalars, sent = call(
        second_body,
        [blocks] * 5 + [scal, double],
        [sums],
        (sent, got, x, r, rs) + fixed,
        [VMEM] * 5 + fixed_specs,
    )
    got = exchange(sent)
    x, r, p, s, scalars, a, sent = call(
        third_body,
        [blocks] * 4 + [scal, blocks, blocks],
        [sums, pltpu.VMEM(blocks, jnp.float32)],
        (sent, got, x, r, rs, p, s, ss, scalars) + fixed,
        [VMEM] * 9 + fixed_specs,
    )
    got = exchange(sent)
    return call(
        last_body,
        [base_bottom.shape, base_bottom.shape],
        [],
        (a, got, x, r, p, s, scalars),
        [VMEM] * 7,
    )


def solution(mesh):
    in_specs = (
        P(("store", "sku"), None, None),
        P(("store", "sku"), None, None),
        P(("store", "sku"), None, None),
        P(("store", "sku"), None, None),
        P(None, None, ("store", "sku")),
        P(None, None, ("store", "sku")),
        P(),
        P(),
    )
    out_specs = (P(("store", "sku"), None, None), P(("store", "sku"), None, None))
    return jax.shard_map(
        on_device, mesh=mesh, in_specs=in_specs, out_specs=out_specs, check_vma=False
    )
```

```python
import jax
import jax.numpy as jnp
from jax import lax
from jax.experimental import pallas as pl
from jax.experimental.pallas import tpu as pltpu
from jax.sharding import PartitionSpec as P

LANES = 128
PAD = 16
VMEM = pl.BlockSpec(memory_space=pltpu.VMEM)


def exchange(blocks, n):
    moved = lax.all_to_all(
        blocks.reshape(n, 1, -1), ("store", "sku"), split_axis=0, concat_axis=0, tiled=True
    )
    return moved.reshape(blocks.shape)


def call(body, outs, scratch, args):
    return pl.pallas_call(
        body,
        out_shape=tuple(
            out if isinstance(out, jax.ShapeDtypeStruct) else jax.ShapeDtypeStruct(out, jnp.float32)
            for out in outs
        ),
        in_specs=[VMEM] * len(args),
        out_specs=tuple(VMEM for _ in outs),
        scratch_shapes=scratch,
        compiler_params=pltpu.CompilerParams(vmem_limit_bytes=40 << 20),
    )(*args)


def split(value):
    high = value.astype(jnp.bfloat16)
    return high, (value - high.astype(jnp.float32)).astype(jnp.bfloat16)


def product(left, right, contract):
    return lax.dot_general(left, right, (contract, ((), ())), preferred_element_type=jnp.float32)


def rows_of(ref, n, h):
    return ref[pl.ds(h, n, stride=ref.shape[0] // n), :]


def put_rows(ref, n, h, value):
    ref[pl.ds(h, n, stride=ref.shape[0] // n), :] = value


def category_sums(field, cat_ref, n, groups):
    width = 4 if n % 4 == 0 else 1
    lanes = width * LANES
    rows = groups * PAD

    def step(c, total):
        pieces = [field[pl.ds(c * width + i, PAD, stride=n), :] for i in range(width)]
        high, low = split(jnp.concatenate(pieces, axis=1))
        members = cat_ref[0:1, pl.ds(pl.multiple_of(c * lanes, LANES), lanes)]
        labels = lax.broadcasted_iota(jnp.int32, (LANES, lanes), 0)
        table = jnp.where(labels == members % LANES, 1.0, 0.0).astype(jnp.bfloat16)
        group = jnp.broadcast_to(members // LANES, (PAD, lanes))
        masks = [jnp.where(group == g, 1.0, 0.0).astype(jnp.bfloat16) for g in range(groups)]
        spread = jnp.concatenate([high * m for m in masks] + [low * m for m in masks], axis=0)
        return total + product(spread, table, ((1,), (1,)))

    steps = n // width
    total = lax.fori_loop(
        0, steps, step, jnp.zeros((2 * rows, LANES), jnp.float32), unroll=min(steps, 8)
    )
    return total[:rows] + total[rows:]


def category_spread(values, cats, h, groups):
    shape = cats.shape
    place = cats % LANES
    group = cats // LANES
    result = jnp.zeros(shape, jnp.float32)
    for g in range(groups):
        row = jnp.broadcast_to(values[g * PAD + h : g * PAD + h + 1, :], shape)
        result = jnp.where(group == g, jnp.take_along_axis(row, place, axis=1), result)
    return result


def region_sums(load, same, n, horizon):
    high, low = split(jnp.concatenate([load(h) for h in range(horizon)], axis=1))
    total = product(same, high, ((1,), (0,))) + product(same, low, ((1,), (0,)))
    return [total[:, h * LANES : (h + 1) * LANES] for h in range(horizon)]


def pack_body(base_ref, out_ref):
    n = base_ref.shape[1]
    for h in range(base_ref.shape[0]):
        put_rows(out_ref, n, h, base_ref[h])


def prepare_body(
    base_ref, base_cat_ref, weight_cat_ref, base_reg_ref, weight_reg_ref, cat_ref, cats_ref, map_ref,
    spread_out, wcat_out, wstore_out, bstore_out, same_out, field, values,
):
    horizon, n, _ = base_ref.shape
    groups = wcat_out.shape[0] // PAD
    n_regions = weight_reg_ref.shape[1]
    field[...] = jnp.zeros_like(field)
    for h in range(horizon):
        field[h * n : (h + 1) * n, :] = base_ref[h]
    sums = category_sums(field, cat_ref, n, groups)
    wcat_out[...] = jnp.zeros_like(wcat_out)
    values[...] = jnp.zeros_like(values)
    for g in range(groups):
        weight = weight_cat_ref[:, g, :]
        wcat_out[g * PAD : g * PAD + horizon, :] = weight
        values[g * PAD : g * PAD + horizon, :] = weight * (
            base_cat_ref[:, g, :] - sums[g * PAD : g * PAD + horizon]
        )
    cats = cats_ref[...]
    for h in range(horizon):
        spread_out[h] = category_spread(values, cats, h, groups)

    labels = lax.broadcasted_iota(jnp.int32, (n_regions, n), 0)
    table = jnp.where(labels == map_ref[...], 1.0, 0.0).astype(jnp.bfloat16)
    same_out[...] = product(table, table, ((0,), (0,))).astype(jnp.bfloat16)
    for source, target in ((weight_reg_ref, wstore_out), (base_reg_ref, bstore_out)):
        for h in range(horizon):
            high, low = split(source[h])
            rest = source[h] - high.astype(jnp.float32) - low.astype(jnp.float32)
            target[h] = (
                product(table, high, ((0,), (0,)))
                + product(table, low, ((0,), (0,)))
                + product(table, rest.astype(jnp.bfloat16), ((0,), (0,)))
            )


def region_start_body(got_ref, spread_ref, wstore_ref, bstore_ref, same_ref, send_ref):
    horizon, n, _ = spread_ref.shape
    sums = region_sums(lambda h: rows_of(got_ref, n, h), same_ref[...], n, horizon)
    for h in range(horizon):
        put_rows(send_ref, n, h, spread_ref[h])
        put_rows(send_ref, n, horizon + h, wstore_ref[h] * (bstore_ref[h] - sums[h]))


def operate(r_ref, rs, eps, diag_ref, wcat_ref, wstore_ref, cat_ref, cats_ref, same_ref, a_put, reg_put, sum_put, values):
    horizon, n, _ = diag_ref.shape
    groups = wcat_ref.shape[0] // PAD
    gamma = jnp.zeros((n, LANES), jnp.float32)
    delta = jnp.zeros((n, LANES), jnp.float32)
    sums = region_sums(lambda h: rs[h], same_ref[...], n, horizon)
    for h in range(horizon):
        reg = wstore_ref[h] * sums[h]
        delta = delta + reg * rs[h]
        reg_put(h, reg)

    sums = category_sums(r_ref, cat_ref, n, groups)
    scaled = wcat_ref[...] * sums
    values[...] = scaled
    cats = cats_ref[...]
    for h in range(horizon):
        r = r_ref[h * n : (h + 1) * n, :]
        scaled_r = diag_ref[h] * r
        gamma = gamma + r * r
        delta = delta + scaled_r * r
        a_put(h, scaled_r + category_spread(values, cats, h, groups))

    delta = jnp.sum(delta, axis=0, keepdims=True) + jnp.sum(scaled * sums, axis=0, keepdims=True)
    lane = lax.broadcasted_iota(jnp.int32, (1, LANES), 1)
    line = jnp.zeros((1, LANES), jnp.float32)
    for i, part in enumerate((gamma, delta, eps)):
        if part is not None:
            whole = jnp.sum(jnp.sum(part, axis=0, keepdims=True), axis=1, keepdims=True)
            line = jnp.where(lane == i, whole, line)
    sum_put(jnp.broadcast_to(line, (n, LANES)))


def totals(got_ref, n, row):
    total = jnp.sum(rows_of(got_ref, n, row), axis=0, keepdims=True)
    lane = lax.broadcasted_iota(jnp.int32, (1, LANES), 1)
    return [
        jnp.broadcast_to(
            jnp.sum(jnp.where(lane == i, total, 0.0), axis=1, keepdims=True), (1, LANES)
        )
        for i in range(3)
    ]


def sender(ref, n, first):
    return lambda h, value: put_rows(ref, n, first + h, value)


def clear_tail(r_ref, horizon, n):
    r_ref[horizon * n :, :] = jnp.zeros((r_ref.shape[0] - horizon * n, LANES), jnp.float32)


def first_body(
    sent_ref, got_ref, diag_ref, wcat_ref, wstore_ref, cat_ref, cats_ref, same_ref,
    r_ref, rs_ref, send_ref, values,
):
    horizon, n, _ = diag_ref.shape
    clear_tail(r_ref, horizon, n)
    for h in range(horizon):
        r_ref[h * n : (h + 1) * n, :] = rows_of(sent_ref, n, h) + rows_of(got_ref, n, horizon + h)
        rs_ref[h] = rows_of(got_ref, n, h) + rows_of(sent_ref, n, horizon + h)
    operate(
        r_ref, rs_ref, None, diag_ref, wcat_ref, wstore_ref, cat_ref, cats_ref, same_ref,
        sender(send_ref, n, 0), sender(send_ref, n, horizon),
        lambda line: put_rows(send_ref, n, 2 * horizon, line), values,
    )


def second_body(
    sent_ref, got_ref, x_ref, r_ref, rs_ref, diag_ref, wcat_ref, wstore_ref, cat_ref, cats_ref, same_ref,
    x_out, r_out, rs_out, s_out, ss_out, scal_ref, send_ref, values,
):
    horizon, n, _ = diag_ref.shape
    gamma, delta, _ = totals(got_ref, n, 2 * horizon)
    alpha = gamma / delta
    scal_ref[0:1, :] = gamma
    scal_ref[1:2, :] = delta
    clear_tail(r_out, horizon, n)
    eps = jnp.zeros((n, LANES), jnp.float32)
    for h in range(horizon):
        ws = rows_of(got_ref, n, h) + rows_of(sent_ref, n, horizon + h)
        ss_out[h] = ws
        rs_out[h] = rs_ref[h] - alpha * ws
        w = rows_of(sent_ref, n, h) + rows_of(got_ref, n, horizon + h)
        s_out[h] = w
        r = r_ref[h * n : (h + 1) * n, :]
        x_out[h] = x_ref[h] + alpha * r
        r = r - alpha * w
        r_out[h * n : (h + 1) * n, :] = r
        eps = eps + r * w
    operate(
        r_out, rs_out, eps, diag_ref, wcat_ref, wstore_ref, cat_ref, cats_ref, same_ref,
        sender(send_ref, n, 0), sender(send_ref, n, horizon),
        lambda line: put_rows(send_ref, n, 2 * horizon, line), values,
    )


def third_body(
    sent_ref, got_ref, x_ref, r_ref, rs_ref, p_ref, s_ref, ss_ref, scal_ref,
    diag_ref, wcat_ref, wstore_ref, cat_ref, cats_ref, same_ref,
    x_out, r_out, p_out, s_out, scal_out, a_out, send_ref, values, rs_out,
):
    horizon, n, _ = diag_ref.shape
    gamma, delta, eps = totals(got_ref, n, 2 * horizon)
    beta = gamma / scal_ref[0:1, :]
    curve = delta + 2.0 * beta * eps + beta * beta * scal_ref[1:2, :]
    alpha = gamma / curve
    scal_out[0:1, :] = gamma
    scal_out[1:2, :] = curve
    clear_tail(r_out, horizon, n)
    eps = jnp.zeros((n, LANES), jnp.float32)
    for h in range(horizon):
        ws = rows_of(got_ref, n, h) + rows_of(sent_ref, n, horizon + h)
        rs_out[h] = rs_ref[h] - alpha * (ws + beta * ss_ref[h])
        w = rows_of(sent_ref, n, h) + rows_of(got_ref, n, horizon + h)
        s = w + beta * s_ref[h]
        s_out[h] = s
        r = r_ref[h * n : (h + 1) * n, :]
        p = r + beta * p_ref[h * n : (h + 1) * n, :]
        p_out[h] = p
        x_out[h] = x_ref[h] + alpha * p
        r = r - alpha * s
        r_out[h * n : (h + 1) * n, :] = r
        eps = eps + r * s

    def keep(h, value):
        a_out[h] = value

    operate(
        r_out, rs_out, eps, diag_ref, wcat_ref, wstore_ref, cat_ref, cats_ref, same_ref,
        keep, sender(send_ref, n, 0), lambda line: put_rows(send_ref, n, horizon, line), values,
    )


def last_body(a_ref, got_ref, x_ref, r_ref, p_ref, s_ref, scal_ref, x_out, r_out):
    horizon, n, _ = a_ref.shape
    gamma, delta, eps = totals(got_ref, n, horizon)
    beta = gamma / scal_ref[0:1, :]
    alpha = gamma / (delta + 2.0 * beta * eps + beta * beta * scal_ref[1:2, :])
    for h in range(horizon):
        r = r_ref[h * n : (h + 1) * n, :]
        s = a_ref[h] + rows_of(got_ref, n, h) + beta * s_ref[h]
        x_out[h] = x_ref[h] + alpha * (r + beta * p_ref[h])
        r_out[h] = r - alpha * s


def on_device(
    base_bottom,
    weight_bottom,
    base_category,
    weight_category,
    base_region,
    weight_region,
    category_map,
    region_map,
):
    stores, horizon, skus = base_bottom.shape
    n = region_map.shape[0]
    groups = weight_category.shape[2] // LANES
    cat = category_map.reshape(1, skus)
    cats = category_map.reshape(n, LANES)
    field = (horizon, n, LANES)
    padded = (PAD * n, LANES)
    by_category = (horizon, groups, LANES)
    scal = (2, LANES)
    values = pltpu.VMEM((groups * PAD, LANES), jnp.float32)

    x = base_bottom.reshape(field)
    diag = weight_bottom.reshape(field)
    (sent,) = call(pack_body, [(n * horizon, LANES)], [], (x,))
    got = exchange(sent, n)
    spread, wcat, wstore, bstore, same = call(
        prepare_body,
        [field, (groups * PAD, LANES), field, field, jax.ShapeDtypeStruct((n, n), jnp.bfloat16)],
        [pltpu.VMEM(padded, jnp.float32), values],
        (
            x,
            base_category.reshape(by_category),
            weight_category.reshape(by_category),
            jnp.transpose(base_region, (1, 0, 2)),
            jnp.transpose(weight_region, (1, 0, 2)),
            cat,
            cats,
            region_map.reshape(1, n),
        ),
    )
    (sent,) = call(
        region_start_body, [(n * 2 * horizon, LANES)], [], (got, spread, wstore, bstore, same)
    )
    got = exchange(sent, n)
    fixed = (diag, wcat, wstore, cat, cats, same)
    both = (n * (2 * horizon + 1), LANES)
    r, rs, sent = call(first_body, [padded, field, both], [values], (sent, got) + fixed)
    got = exchange(sent, n)
    p = r
    x, r, rs, s, ss, scalars, sent = call(
        second_body,
        [field, padded, field, field, field, scal, both],
        [values],
        (sent, got, x, r, rs) + fixed,
    )
    got = exchange(sent, n)
    x, r, p, s, scalars, a, sent = call(
        third_body,
        [field, padded, field, field, scal, field, (n * (horizon + 1), LANES)],
        [values, pltpu.VMEM(field, jnp.float32)],
        (sent, got, x, r, rs, p, s, ss, scalars) + fixed,
    )
    got = exchange(sent, n)
    x, r = call(last_body, [field, field], [], (a, got, x, r, p, s, scalars))
    return x.reshape(base_bottom.shape), r.reshape(base_bottom.shape)


def solution(mesh):
    in_specs = (
        P(("store", "sku"), None, None),
        P(("store", "sku"), None, None),
        P(("store", "sku"), None, None),
        P(("store", "sku"), None, None),
        P(None, None, ("store", "sku")),
        P(None, None, ("store", "sku")),
        P(),
        P(),
    )
    out_specs = (P(("store", "sku"), None, None), P(("store", "sku"), None, None))
    return jax.shard_map(
        on_device, mesh=mesh, in_specs=in_specs, out_specs=out_specs, check_vma=False
    )
```

```python
import jax
import jax.numpy as jnp
from jax import lax
from jax.experimental import pallas as pl
from jax.experimental.pallas import tpu as pltpu
from jax.sharding import PartitionSpec as P

LANES = 128
PAD = 16
VMEM = pl.BlockSpec(memory_space=pltpu.VMEM)


def exchange(blocks, n):
    moved = lax.all_to_all(
        blocks.reshape(n, 1, -1), ("store", "sku"), split_axis=0, concat_axis=0, tiled=True
    )
    return moved.reshape(blocks.shape)


def call(body, outs, scratch, args):
    return pl.pallas_call(
        body,
        out_shape=tuple(
            out if isinstance(out, jax.ShapeDtypeStruct) else jax.ShapeDtypeStruct(out, jnp.float32)
            for out in outs
        ),
        in_specs=[VMEM] * len(args),
        out_specs=tuple(VMEM for _ in outs),
        scratch_shapes=scratch,
        compiler_params=pltpu.CompilerParams(vmem_limit_bytes=40 << 20),
    )(*args)


def split(value):
    high = value.astype(jnp.bfloat16)
    return high, (value - high.astype(jnp.float32)).astype(jnp.bfloat16)


def product(left, right, contract):
    return lax.dot_general(left, right, (contract, ((), ())), preferred_element_type=jnp.float32)


def rows_of(ref, n, h):
    return ref[pl.ds(h, n, stride=ref.shape[0] // n), :]


def put_rows(ref, n, h, value):
    ref[pl.ds(h, n, stride=ref.shape[0] // n), :] = value


def category_sums(field, cat_ref, n, groups):
    width = 4 if n % 4 == 0 else 1
    lanes = width * LANES
    rows = groups * PAD

    def step(c, total):
        pieces = [field[pl.ds(c * width + i, PAD, stride=n), :] for i in range(width)]
        high, low = split(jnp.concatenate(pieces, axis=1))
        members = cat_ref[0:1, pl.ds(pl.multiple_of(c * lanes, LANES), lanes)]
        labels = lax.broadcasted_iota(jnp.int32, (LANES, lanes), 0)
        table = jnp.where(labels == members % LANES, 1.0, 0.0).astype(jnp.bfloat16)
        group = jnp.broadcast_to(members // LANES, (PAD, lanes))
        masks = [jnp.where(group == g, 1.0, 0.0).astype(jnp.bfloat16) for g in range(groups)]
        spread = jnp.concatenate([high * m for m in masks] + [low * m for m in masks], axis=0)
        return total + product(spread, table, ((1,), (1,)))

    steps = n // width
    total = lax.fori_loop(
        0, steps, step, jnp.zeros((2 * rows, LANES), jnp.float32), unroll=min(steps, 8)
    )
    return total[:rows] + total[rows:]


def category_spread(values, cats, h, groups):
    shape = cats.shape
    place = cats % LANES
    group = cats // LANES
    result = jnp.zeros(shape, jnp.float32)
    for g in range(groups):
        row = jnp.broadcast_to(values[g * PAD + h : g * PAD + h + 1, :], shape)
        result = jnp.where(group == g, jnp.take_along_axis(row, place, axis=1), result)
    return result


def region_sums(load, same, n, horizon):
    high, low = split(jnp.concatenate([load(h) for h in range(horizon)], axis=1))
    total = product(same, high, ((1,), (0,))) + product(same, low, ((1,), (0,)))
    return [total[:, h * LANES : (h + 1) * LANES] for h in range(horizon)]


def pack_body(base_ref, out_ref):
    n = base_ref.shape[1]
    for h in range(base_ref.shape[0]):
        put_rows(out_ref, n, h, base_ref[h])


def prepare_body(
    base_ref, base_cat_ref, weight_cat_ref, base_reg_ref, weight_reg_ref, cat_ref, cats_ref, map_ref,
    spread_out, wcat_out, wstore_out, bstore_out, same_out, field, values,
):
    horizon, n, _ = base_ref.shape
    groups = wcat_out.shape[0] // PAD
    n_regions = weight_reg_ref.shape[1]
    field[...] = jnp.zeros_like(field)
    for h in range(horizon):
        field[h * n : (h + 1) * n, :] = base_ref[h]
    sums = category_sums(field, cat_ref, n, groups)
    wcat_out[...] = jnp.zeros_like(wcat_out)
    values[...] = jnp.zeros_like(values)
    for g in range(groups):
        weight = weight_cat_ref[:, g, :]
        wcat_out[g * PAD : g * PAD + horizon, :] = weight
        values[g * PAD : g * PAD + horizon, :] = weight * (
            base_cat_ref[:, g, :] - sums[g * PAD : g * PAD + horizon]
        )
    cats = cats_ref[...]
    for h in range(horizon):
        put_rows(spread_out, n, h, category_spread(values, cats, h, groups))

    labels = lax.broadcasted_iota(jnp.int32, (n_regions, n), 0)
    table = jnp.where(labels == map_ref[...], 1.0, 0.0).astype(jnp.bfloat16)
    same_out[...] = product(table, table, ((0,), (0,))).astype(jnp.bfloat16)
    for source, target in ((weight_reg_ref, wstore_out), (base_reg_ref, bstore_out)):
        for h in range(horizon):
            high, low = split(source[h])
            rest = source[h] - high.astype(jnp.float32) - low.astype(jnp.float32)
            target[h] = (
                product(table, high, ((0,), (0,)))
                + product(table, low, ((0,), (0,)))
                + product(table, rest.astype(jnp.bfloat16), ((0,), (0,)))
            )


def region_part(load, wstore_ref, same_ref, n, horizon, send_ref, share_ref):
    sums = region_sums(load, same_ref[...], n, horizon)
    share = jnp.zeros((n, LANES), jnp.float32)
    for h in range(horizon):
        part = wstore_ref[h] * sums[h]
        share = share + part * load(h)
        put_rows(send_ref, n, h, part)
    share_ref[...] = jnp.sum(share, axis=0, keepdims=True)


def store_part(
    r_ref, eps, share_ref, diag_ref, wcat_ref, cat_ref, cats_ref, put, put_line, values
):
    horizon, n, _ = diag_ref.shape
    groups = wcat_ref.shape[0] // PAD
    gamma = jnp.zeros((n, LANES), jnp.float32)
    delta = jnp.zeros((n, LANES), jnp.float32)
    sums = category_sums(r_ref, cat_ref, n, groups)
    scaled = wcat_ref[...] * sums
    values[...] = scaled
    cats = cats_ref[...]
    for h in range(horizon):
        r = r_ref[h * n : (h + 1) * n, :]
        scaled_r = diag_ref[h] * r
        gamma = gamma + r * r
        delta = delta + scaled_r * r
        put(h, scaled_r + category_spread(values, cats, h, groups))

    delta = jnp.sum(delta, axis=0, keepdims=True) + jnp.sum(scaled * sums, axis=0, keepdims=True)
    delta = delta + share_ref[...]
    lane = lax.broadcasted_iota(jnp.int32, (1, LANES), 1)
    line = jnp.zeros((1, LANES), jnp.float32)
    for i, part in enumerate((gamma, delta, eps)):
        if part is not None:
            whole = jnp.sum(jnp.sum(part, axis=0, keepdims=True), axis=1, keepdims=True)
            line = jnp.where(lane == i, whole, line)
    put_line(jnp.broadcast_to(line, (n, LANES)))


def totals(got_ref, n, row):
    total = jnp.sum(rows_of(got_ref, n, row), axis=0, keepdims=True)
    lane = lax.broadcasted_iota(jnp.int32, (1, LANES), 1)
    return [
        jnp.broadcast_to(
            jnp.sum(jnp.where(lane == i, total, 0.0), axis=1, keepdims=True), (1, LANES)
        )
        for i in range(3)
    ]


def step_sizes(sums, before):
    gamma, delta, eps = sums
    beta = gamma / before[0:1, :]
    curve = delta + 2.0 * beta * eps + beta * beta * before[1:2, :]
    return gamma / curve, beta, gamma, curve


def clear_tail(r_ref, horizon, n):
    r_ref[horizon * n :, :] = jnp.zeros((r_ref.shape[0] - horizon * n, LANES), jnp.float32)


def region_start_body(got_ref, wstore_ref, bstore_ref, same_ref, send_ref):
    horizon, n, _ = wstore_ref.shape
    sums = region_sums(lambda h: rows_of(got_ref, n, h), same_ref[...], n, horizon)
    for h in range(horizon):
        put_rows(send_ref, n, h, wstore_ref[h] * (bstore_ref[h] - sums[h]))


def region_first_body(got_ref, own_ref, wstore_ref, same_ref, rs_ref, send_ref, share_ref):
    horizon, n, _ = wstore_ref.shape
    for h in range(horizon):
        rs_ref[h] = rows_of(got_ref, n, h) + rows_of(own_ref, n, h)
    region_part(lambda h: rs_ref[h], wstore_ref, same_ref, n, horizon, send_ref, share_ref)


def store_first_body(
    own_ref, got_ref, share_ref, diag_ref, wcat_ref, cat_ref, cats_ref, r_ref, send_ref, values
):
    horizon, n, _ = diag_ref.shape
    clear_tail(r_ref, horizon, n)
    for h in range(horizon):
        r_ref[h * n : (h + 1) * n, :] = rows_of(own_ref, n, h) + rows_of(got_ref, n, h)
    store_part(
        r_ref, None, share_ref, diag_ref, wcat_ref, cat_ref, cats_ref,
        lambda h, value: put_rows(send_ref, n, h, value),
        lambda line: put_rows(send_ref, n, horizon, line), values,
    )


def region_second_body(
    got_ref, own_ref, rs_ref, wstore_ref, same_ref, rs_out, ss_out, scal_ref, send_ref, share_ref
):
    horizon, n, _ = wstore_ref.shape
    gamma, delta, _ = totals(got_ref, n, horizon)
    alpha = gamma / delta
    scal_ref[0:1, :] = gamma
    scal_ref[1:2, :] = delta
    scal_ref[2:3, :] = alpha
    for h in range(horizon):
        ws = rows_of(got_ref, n, h) + rows_of(own_ref, n, h)
        ss_out[h] = ws
        rs_out[h] = rs_ref[h] - alpha * ws
    region_part(lambda h: rs_out[h], wstore_ref, same_ref, n, horizon, send_ref, share_ref)


def store_second_body(
    own_ref, got_ref, x_ref, r_ref, scal_ref, share_ref, diag_ref, wcat_ref, cat_ref, cats_ref,
    x_out, r_out, s_out, send_ref, values,
):
    horizon, n, _ = diag_ref.shape
    alpha = scal_ref[2:3, :]
    clear_tail(r_out, horizon, n)
    eps = jnp.zeros((n, LANES), jnp.float32)
    for h in range(horizon):
        w = rows_of(own_ref, n, h) + rows_of(got_ref, n, h)
        s_out[h] = w
        r = r_ref[h * n : (h + 1) * n, :]
        x_out[h] = x_ref[h] + alpha * r
        r = r - alpha * w
        r_out[h * n : (h + 1) * n, :] = r
        eps = eps + r * w
    store_part(
        r_out, eps, share_ref, diag_ref, wcat_ref, cat_ref, cats_ref,
        lambda h, value: put_rows(send_ref, n, h, value),
        lambda line: put_rows(send_ref, n, horizon, line), values,
    )


def region_third_body(
    got_ref, own_ref, rs_ref, ss_ref, before_ref, wstore_ref, same_ref,
    scal_ref, send_ref, share_ref, rs_out,
):
    horizon, n, _ = wstore_ref.shape
    alpha, beta, gamma, curve = step_sizes(totals(got_ref, n, horizon), before_ref)
    for i, value in enumerate((gamma, curve, alpha, beta)):
        scal_ref[i : i + 1, :] = value
    for h in range(horizon):
        ws = rows_of(got_ref, n, h) + rows_of(own_ref, n, h)
        rs_out[h] = rs_ref[h] - alpha * (ws + beta * ss_ref[h])
    region_part(lambda h: rs_out[h], wstore_ref, same_ref, n, horizon, send_ref, share_ref)


def store_third_body(
    own_ref, got_ref, x_ref, r_ref, p_ref, s_ref, scal_ref, share_ref, diag_ref, wcat_ref, cat_ref, cats_ref,
    x_out, r_out, p_out, s_out, a_out, send_ref, values,
):
    horizon, n, _ = diag_ref.shape
    alpha = scal_ref[2:3, :]
    beta = scal_ref[3:4, :]
    clear_tail(r_out, horizon, n)
    eps = jnp.zeros((n, LANES), jnp.float32)
    for h in range(horizon):
        s = rows_of(own_ref, n, h) + rows_of(got_ref, n, h) + beta * s_ref[h]
        s_out[h] = s
        r = r_ref[h * n : (h + 1) * n, :]
        p = r + beta * p_ref[h * n : (h + 1) * n, :]
        p_out[h] = p
        x_out[h] = x_ref[h] + alpha * p
        r = r - alpha * s
        r_out[h * n : (h + 1) * n, :] = r
        eps = eps + r * s

    def keep(h, value):
        a_out[h] = value

    def put_line(line):
        send_ref[...] = line

    store_part(
        r_out, eps, share_ref, diag_ref, wcat_ref, cat_ref, cats_ref, keep, put_line, values
    )


def last_body(a_ref, got_ref, sums_ref, x_ref, r_ref, p_ref, s_ref, before_ref, x_out, r_out):
    horizon, n, _ = a_ref.shape
    alpha, beta, _, _ = step_sizes(totals(sums_ref, n, 0), before_ref)
    for h in range(horizon):
        r = r_ref[h * n : (h + 1) * n, :]
        s = a_ref[h] + rows_of(got_ref, n, h) + beta * s_ref[h]
        x_out[h] = x_ref[h] + alpha * (r + beta * p_ref[h])
        r_out[h] = r - alpha * s


def on_device(
    base_bottom,
    weight_bottom,
    base_category,
    weight_category,
    base_region,
    weight_region,
    category_map,
    region_map,
):
    stores, horizon, skus = base_bottom.shape
    n = region_map.shape[0]
    groups = weight_category.shape[2] // LANES
    cat = category_map.reshape(1, skus)
    cats = category_map.reshape(n, LANES)
    field = (horizon, n, LANES)
    padded = (PAD * n, LANES)
    blocks = (n * horizon, LANES)
    blocks_sums = (n * (horizon + 1), LANES)
    by_category = (horizon, groups, LANES)
    line = (1, LANES)
    scal = (8, LANES)
    values = pltpu.VMEM((groups * PAD, LANES), jnp.float32)

    x = base_bottom.reshape(field)
    diag = weight_bottom.reshape(field)
    (sent,) = call(pack_body, [blocks], [], (x,))
    got = exchange(sent, n)
    cat_start, wcat, wstore, bstore, same = call(
        prepare_body,
        [blocks, (groups * PAD, LANES), field, field, jax.ShapeDtypeStruct((n, n), jnp.bfloat16)],
        [pltpu.VMEM(padded, jnp.float32), values],
        (
            x,
            base_category.reshape(by_category),
            weight_category.reshape(by_category),
            jnp.transpose(base_region, (1, 0, 2)),
            jnp.transpose(weight_region, (1, 0, 2)),
            cat,
            cats,
            region_map.reshape(1, n),
        ),
    )
    got_cat = exchange(cat_start, n)
    reg_fixed = (wstore, same)
    store_fixed = (diag, wcat, cat, cats)

    (reg_start,) = call(region_start_body, [blocks], [], (got, wstore, bstore, same))
    got_reg = exchange(reg_start, n)
    rs, reg, share = call(
        region_first_body, [field, blocks, line], [], (got_cat, reg_start) + reg_fixed
    )
    got_next = exchange(reg, n)
    r, a = call(
        store_first_body, [padded, blocks_sums], [values], (cat_start, got_reg, share) + store_fixed
    )
    got_a = exchange(a, n)

    got_reg = got_next
    rs, ss, scalars, next_reg, share = call(
        region_second_body, [field, field, scal, blocks, line], [], (got_a, reg, rs) + reg_fixed
    )
    got_next = exchange(next_reg, n)
    p = r
    x, r, s, next_a = call(
        store_second_body,
        [field, padded, field, blocks_sums],
        [values],
        (a, got_reg, x, r, scalars, share) + store_fixed,
    )
    got_a = exchange(next_a, n)

    a, reg, got_reg = next_a, next_reg, got_next
    scalars, next_reg, share = call(
        region_third_body,
        [scal, blocks, line],
        [pltpu.VMEM(field, jnp.float32)],
        (got_a, reg, rs, ss, scalars) + reg_fixed,
    )
    got_next = exchange(next_reg, n)
    x, r, p, s, a, sums = call(
        store_third_body,
        [field, padded, field, field, field, (n, LANES)],
        [values],
        (a, got_reg, x, r, p, s, scalars, share) + store_fixed,
    )
    got_sums = exchange(sums, n)
    x, r = call(
        last_body, [field, field], [], (a, got_next, got_sums, x, r, p, s, scalars)
    )
    return x.reshape(base_bottom.shape), r.reshape(base_bottom.shape)


def solution(mesh):
    in_specs = (
        P(("store", "sku"), None, None),
        P(("store", "sku"), None, None),
        P(("store", "sku"), None, None),
        P(("store", "sku"), None, None),
        P(None, None, ("store", "sku")),
        P(None, None, ("store", "sku")),
        P(),
        P(),
    )
    out_specs = (P(("store", "sku"), None, None), P(("store", "sku"), None, None))
    return jax.shard_map(
        on_device, mesh=mesh, in_specs=in_specs, out_specs=out_specs, check_vma=False
    )
```

```python
import jax
import jax.numpy as jnp
from jax import lax
from jax.experimental import pallas as pl
from jax.experimental.pallas import tpu as pltpu
from jax.sharding import PartitionSpec as P

LANES = 128
PAD = 16
VMEM = pl.BlockSpec(memory_space=pltpu.VMEM)


def exchange(blocks):
    n = len(blocks)
    return [
        block if k == 0 else lax.ppermute(block, ("store", "sku"), [(i, i ^ k) for i in range(n)])
        for k, block in enumerate(blocks)
    ]


def call(body, outs, scratch, args, me, n, got=(), got_at=0, send=False):
    outs = [
        out if isinstance(out, jax.ShapeDtypeStruct) else jax.ShapeDtypeStruct(out, jnp.float32)
        for out in outs
    ]
    n_args, n_got, n_outs = len(args), len(got), len(outs)
    scratch = list(scratch)
    if got:
        rows = got[0].shape[0]
        scratch.append(pltpu.VMEM((n * rows, LANES), jnp.float32))
    if send:
        block = outs[-1].shape[0] // n
        outs += [jax.ShapeDtypeStruct((block, LANES), jnp.float32)] * n

    def kernel(me_ref, *refs):
        refs = list(refs)
        arg_refs, refs = refs[:n_args], refs[n_args:]
        got_refs, refs = refs[:n_got], refs[n_got:]
        out_refs, refs = refs[:n_outs], refs[n_outs:]
        send_refs, refs = (refs[:n], refs[n:]) if send else ([], refs)
        own = me_ref[0]
        if got:
            stage = refs.pop()
            for k in range(n):
                stage[pl.ds(pl.multiple_of((own ^ k) * rows, 8), rows), :] = got_refs[k][...]
            arg_refs.insert(got_at, stage)
        body(*arg_refs, *out_refs, *refs)
        for k, target in enumerate(send_refs):
            target[...] = out_refs[-1][pl.ds(pl.multiple_of((own ^ k) * block, 8), block), :]

    results = pl.pallas_call(
        kernel,
        out_shape=tuple(outs),
        in_specs=[pl.BlockSpec(memory_space=pltpu.SMEM)] + [VMEM] * (n_args + n_got),
        out_specs=tuple(VMEM for _ in outs),
        scratch_shapes=scratch,
        compiler_params=pltpu.CompilerParams(vmem_limit_bytes=40 << 20),
    )(me, *args, *got)
    if send:
        return results[:n_outs], results[n_outs:]
    return results


def split(value):
    high = value.astype(jnp.bfloat16)
    return high, (value - high.astype(jnp.float32)).astype(jnp.bfloat16)


def product(left, right, contract):
    return lax.dot_general(left, right, (contract, ((), ())), preferred_element_type=jnp.float32)


def rows_of(ref, n, h):
    return ref[pl.ds(h, n, stride=ref.shape[0] // n), :]


def put_rows(ref, n, h, value):
    ref[pl.ds(h, n, stride=ref.shape[0] // n), :] = value


def category_sums(field, cat_ref, n, groups):
    width = 4 if n % 4 == 0 else 1
    lanes = width * LANES
    rows = groups * PAD

    def step(c, total):
        pieces = [field[pl.ds(c * width + i, PAD, stride=n), :] for i in range(width)]
        high, low = split(jnp.concatenate(pieces, axis=1))
        members = cat_ref[0:1, pl.ds(pl.multiple_of(c * lanes, LANES), lanes)]
        labels = lax.broadcasted_iota(jnp.int32, (LANES, lanes), 0)
        table = jnp.where(labels == members % LANES, 1.0, 0.0).astype(jnp.bfloat16)
        group = jnp.broadcast_to(members // LANES, (PAD, lanes))
        masks = [jnp.where(group == g, 1.0, 0.0).astype(jnp.bfloat16) for g in range(groups)]
        spread = jnp.concatenate([high * m for m in masks] + [low * m for m in masks], axis=0)
        return total + product(spread, table, ((1,), (1,)))

    steps = n // width
    total = lax.fori_loop(
        0, steps, step, jnp.zeros((2 * rows, LANES), jnp.float32), unroll=min(steps, 8)
    )
    return total[:rows] + total[rows:]


def category_spread(values, cats, h, groups):
    shape = cats.shape
    place = cats % LANES
    group = cats // LANES
    result = jnp.zeros(shape, jnp.float32)
    for g in range(groups):
        row = jnp.broadcast_to(values[g * PAD + h : g * PAD + h + 1, :], shape)
        result = jnp.where(group == g, jnp.take_along_axis(row, place, axis=1), result)
    return result


def region_sums(load, same, n, horizon):
    high, low = split(jnp.concatenate([load(h) for h in range(horizon)], axis=1))
    total = product(same, high, ((1,), (0,))) + product(same, low, ((1,), (0,)))
    return [total[:, h * LANES : (h + 1) * LANES] for h in range(horizon)]


def pack_body(base_ref, out_ref):
    n = base_ref.shape[1]
    for h in range(base_ref.shape[0]):
        put_rows(out_ref, n, h, base_ref[h])


def prepare_body(
    base_ref, base_cat_ref, weight_cat_ref, base_reg_ref, weight_reg_ref, cat_ref, cats_ref, map_ref,
    spread_out, wcat_out, wstore_out, bstore_out, same_out, field, values,
):
    horizon, n, _ = base_ref.shape
    groups = wcat_out.shape[0] // PAD
    n_regions = weight_reg_ref.shape[1]
    field[...] = jnp.zeros_like(field)
    for h in range(horizon):
        field[h * n : (h + 1) * n, :] = base_ref[h]
    sums = category_sums(field, cat_ref, n, groups)
    wcat_out[...] = jnp.zeros_like(wcat_out)
    values[...] = jnp.zeros_like(values)
    for g in range(groups):
        weight = weight_cat_ref[:, g, :]
        wcat_out[g * PAD : g * PAD + horizon, :] = weight
        values[g * PAD : g * PAD + horizon, :] = weight * (
            base_cat_ref[:, g, :] - sums[g * PAD : g * PAD + horizon]
        )
    cats = cats_ref[...]
    for h in range(horizon):
        spread_out[h] = category_spread(values, cats, h, groups)

    labels = lax.broadcasted_iota(jnp.int32, (n_regions, n), 0)
    table = jnp.where(labels == map_ref[...], 1.0, 0.0).astype(jnp.bfloat16)
    same_out[...] = product(table, table, ((0,), (0,))).astype(jnp.bfloat16)
    for source, target in ((weight_reg_ref, wstore_out), (base_reg_ref, bstore_out)):
        for h in range(horizon):
            high, low = split(source[h])
            rest = source[h] - high.astype(jnp.float32) - low.astype(jnp.float32)
            target[h] = (
                product(table, high, ((0,), (0,)))
                + product(table, low, ((0,), (0,)))
                + product(table, rest.astype(jnp.bfloat16), ((0,), (0,)))
            )


def region_start_body(got_ref, spread_ref, wstore_ref, bstore_ref, same_ref, send_ref):
    horizon, n, _ = spread_ref.shape
    sums = region_sums(lambda h: rows_of(got_ref, n, h), same_ref[...], n, horizon)
    for h in range(horizon):
        put_rows(send_ref, n, h, spread_ref[h])
        put_rows(send_ref, n, horizon + h, wstore_ref[h] * (bstore_ref[h] - sums[h]))


def operate(r_ref, rs, eps, diag_ref, wcat_ref, wstore_ref, cat_ref, cats_ref, same_ref, a_put, reg_put, sum_put, values):
    horizon, n, _ = diag_ref.shape
    groups = wcat_ref.shape[0] // PAD
    gamma = jnp.zeros((n, LANES), jnp.float32)
    delta = jnp.zeros((n, LANES), jnp.float32)
    sums = region_sums(lambda h: rs[h], same_ref[...], n, horizon)
    for h in range(horizon):
        reg = wstore_ref[h] * sums[h]
        delta = delta + reg * rs[h]
        reg_put(h, reg)

    sums = category_sums(r_ref, cat_ref, n, groups)
    scaled = wcat_ref[...] * sums
    values[...] = scaled
    cats = cats_ref[...]
    for h in range(horizon):
        r = r_ref[h * n : (h + 1) * n, :]
        scaled_r = diag_ref[h] * r
        gamma = gamma + r * r
        delta = delta + scaled_r * r
        a_put(h, scaled_r + category_spread(values, cats, h, groups))

    delta = jnp.sum(delta, axis=0, keepdims=True) + jnp.sum(scaled * sums, axis=0, keepdims=True)
    lane = lax.broadcasted_iota(jnp.int32, (1, LANES), 1)
    line = jnp.zeros((1, LANES), jnp.float32)
    for i, part in enumerate((gamma, delta, eps)):
        if part is not None:
            whole = jnp.sum(jnp.sum(part, axis=0, keepdims=True), axis=1, keepdims=True)
            line = jnp.where(lane == i, whole, line)
    sum_put(jnp.broadcast_to(line, (n, LANES)))


def totals(got_ref, n, row):
    total = jnp.sum(rows_of(got_ref, n, row), axis=0, keepdims=True)
    lane = lax.broadcasted_iota(jnp.int32, (1, LANES), 1)
    return [
        jnp.broadcast_to(
            jnp.sum(jnp.where(lane == i, total, 0.0), axis=1, keepdims=True), (1, LANES)
        )
        for i in range(3)
    ]


def sender(ref, n, first):
    return lambda h, value: put_rows(ref, n, first + h, value)


def clear_tail(r_ref, horizon, n):
    r_ref[horizon * n :, :] = jnp.zeros((r_ref.shape[0] - horizon * n, LANES), jnp.float32)


def first_body(
    sent_ref, got_ref, diag_ref, wcat_ref, wstore_ref, cat_ref, cats_ref, same_ref,
    r_ref, rs_ref, send_ref, values,
):
    horizon, n, _ = diag_ref.shape
    clear_tail(r_ref, horizon, n)
    for h in range(horizon):
        r_ref[h * n : (h + 1) * n, :] = rows_of(sent_ref, n, h) + rows_of(got_ref, n, horizon + h)
        rs_ref[h] = rows_of(got_ref, n, h) + rows_of(sent_ref, n, horizon + h)
    operate(
        r_ref, rs_ref, None, diag_ref, wcat_ref, wstore_ref, cat_ref, cats_ref, same_ref,
        sender(send_ref, n, 0), sender(send_ref, n, horizon),
        lambda line: put_rows(send_ref, n, 2 * horizon, line), values,
    )


def second_body(
    sent_ref, got_ref, x_ref, r_ref, rs_ref, diag_ref, wcat_ref, wstore_ref, cat_ref, cats_ref, same_ref,
    x_out, r_out, rs_out, s_out, ss_out, scal_ref, send_ref, values,
):
    horizon, n, _ = diag_ref.shape
    gamma, delta, _ = totals(got_ref, n, 2 * horizon)
    alpha = gamma / delta
    scal_ref[0:1, :] = gamma
    scal_ref[1:2, :] = delta
    clear_tail(r_out, horizon, n)
    eps = jnp.zeros((n, LANES), jnp.float32)
    for h in range(horizon):
        ws = rows_of(got_ref, n, h) + rows_of(sent_ref, n, horizon + h)
        ss_out[h] = ws
        rs_out[h] = rs_ref[h] - alpha * ws
        w = rows_of(sent_ref, n, h) + rows_of(got_ref, n, horizon + h)
        s_out[h] = w
        r = r_ref[h * n : (h + 1) * n, :]
        x_out[h] = x_ref[h] + alpha * r
        r = r - alpha * w
        r_out[h * n : (h + 1) * n, :] = r
        eps = eps + r * w
    operate(
        r_out, rs_out, eps, diag_ref, wcat_ref, wstore_ref, cat_ref, cats_ref, same_ref,
        sender(send_ref, n, 0), sender(send_ref, n, horizon),
        lambda line: put_rows(send_ref, n, 2 * horizon, line), values,
    )


def third_body(
    sent_ref, got_ref, x_ref, r_ref, rs_ref, p_ref, s_ref, ss_ref, scal_ref,
    diag_ref, wcat_ref, wstore_ref, cat_ref, cats_ref, same_ref,
    x_out, r_out, p_out, s_out, scal_out, a_out, send_ref, values, rs_out,
):
    horizon, n, _ = diag_ref.shape
    gamma, delta, eps = totals(got_ref, n, 2 * horizon)
    beta = gamma / scal_ref[0:1, :]
    curve = delta + 2.0 * beta * eps + beta * beta * scal_ref[1:2, :]
    alpha = gamma / curve
    scal_out[0:1, :] = gamma
    scal_out[1:2, :] = curve
    clear_tail(r_out, horizon, n)
    eps = jnp.zeros((n, LANES), jnp.float32)
    for h in range(horizon):
        ws = rows_of(got_ref, n, h) + rows_of(sent_ref, n, horizon + h)
        rs_out[h] = rs_ref[h] - alpha * (ws + beta * ss_ref[h])
        w = rows_of(sent_ref, n, h) + rows_of(got_ref, n, horizon + h)
        s = w + beta * s_ref[h]
        s_out[h] = s
        r = r_ref[h * n : (h + 1) * n, :]
        p = r + beta * p_ref[h * n : (h + 1) * n, :]
        p_out[h] = p
        x_out[h] = x_ref[h] + alpha * p
        r = r - alpha * s
        r_out[h * n : (h + 1) * n, :] = r
        eps = eps + r * s

    def keep(h, value):
        a_out[h] = value

    operate(
        r_out, rs_out, eps, diag_ref, wcat_ref, wstore_ref, cat_ref, cats_ref, same_ref,
        keep, sender(send_ref, n, 0), lambda line: put_rows(send_ref, n, horizon, line), values,
    )


def last_body(a_ref, got_ref, x_ref, r_ref, p_ref, s_ref, scal_ref, x_out, r_out):
    horizon, n, _ = a_ref.shape
    gamma, delta, eps = totals(got_ref, n, horizon)
    beta = gamma / scal_ref[0:1, :]
    alpha = gamma / (delta + 2.0 * beta * eps + beta * beta * scal_ref[1:2, :])
    for h in range(horizon):
        r = r_ref[h * n : (h + 1) * n, :]
        s = a_ref[h] + rows_of(got_ref, n, h) + beta * s_ref[h]
        x_out[h] = x_ref[h] + alpha * (r + beta * p_ref[h])
        r_out[h] = r - alpha * s


def on_device(
    base_bottom,
    weight_bottom,
    base_category,
    weight_category,
    base_region,
    weight_region,
    category_map,
    region_map,
):
    stores, horizon, skus = base_bottom.shape
    n = region_map.shape[0]
    groups = weight_category.shape[2] // LANES
    cat = category_map.reshape(1, skus)
    cats = category_map.reshape(n, LANES)
    field = (horizon, n, LANES)
    padded = (PAD * n, LANES)
    by_category = (horizon, groups, LANES)
    scal = (2, LANES)
    values = pltpu.VMEM((groups * PAD, LANES), jnp.float32)

    one = (n * PAD, LANES)
    two = (n * 2 * PAD, LANES)
    me = (lax.axis_index("store") * lax.axis_size("sku") + lax.axis_index("sku")).reshape(1)

    x = base_bottom.reshape(field)
    diag = weight_bottom.reshape(field)
    _, blocks = call(pack_body, [one], [], (x,), me, n, send=True)
    got = exchange(blocks)
    spread, wcat, wstore, bstore, same = call(
        prepare_body,
        [field, (groups * PAD, LANES), field, field, jax.ShapeDtypeStruct((n, n), jnp.bfloat16)],
        [pltpu.VMEM(padded, jnp.float32), values],
        (
            x,
            base_category.reshape(by_category),
            weight_category.reshape(by_category),
            jnp.transpose(base_region, (1, 0, 2)),
            jnp.transpose(weight_region, (1, 0, 2)),
            cat,
            cats,
            region_map.reshape(1, n),
        ),
        me,
        n,
    )
    (sent,), blocks = call(
        region_start_body, [two], [], (spread, wstore, bstore, same), me, n, got, 0, True
    )
    got = exchange(blocks)
    fixed = (diag, wcat, wstore, cat, cats, same)
    (r, rs, sent), blocks = call(
        first_body, [padded, field, two], [values], (sent,) + fixed, me, n, got, 1, True
    )
    got = exchange(blocks)
    p = r
    (x, r, rs, s, ss, scalars, sent), blocks = call(
        second_body,
        [field, padded, field, field, field, scal, two],
        [values],
        (sent, x, r, rs) + fixed,
        me, n, got, 1, True,
    )
    got = exchange(blocks)
    (x, r, p, s, scalars, a, sent), blocks = call(
        third_body,
        [field, padded, field, field, scal, field, one],
        [values, pltpu.VMEM(field, jnp.float32)],
        (sent, x, r, rs, p, s, ss, scalars) + fixed,
        me, n, got, 1, True,
    )
    got = exchange(blocks)
    x, r = call(last_body, [field, field], [], (a, x, r, p, s, scalars), me, n, got, 1)
    return x.reshape(base_bottom.shape), r.reshape(base_bottom.shape)


def solution(mesh):
    in_specs = (
        P(("store", "sku"), None, None),
        P(("store", "sku"), None, None),
        P(("store", "sku"), None, None),
        P(("store", "sku"), None, None),
        P(None, None, ("store", "sku")),
        P(None, None, ("store", "sku")),
        P(),
        P(),
    )
    out_specs = (P(("store", "sku"), None, None), P(("store", "sku"), None, None))
    return jax.shard_map(
        on_device, mesh=mesh, in_specs=in_specs, out_specs=out_specs, check_vma=False
    )
```

```python
import jax
import jax.numpy as jnp
from jax import lax
from jax.experimental import pallas as pl
from jax.experimental.pallas import tpu as pltpu
from jax.sharding import PartitionSpec as P

LANES = 128
PAD = 16
WIDE = 256
VMEM = pl.BlockSpec(memory_space=pltpu.VMEM)


def exchange(blocks, n):
    moved = lax.all_to_all(
        blocks.reshape(n, 1, -1), ("store", "sku"), split_axis=0, concat_axis=0, tiled=True
    )
    return moved.reshape(blocks.shape)


def call(body, outs, scratch, args):
    return pl.pallas_call(
        body,
        out_shape=tuple(
            out if isinstance(out, jax.ShapeDtypeStruct) else jax.ShapeDtypeStruct(out, jnp.float32)
            for out in outs
        ),
        in_specs=[VMEM] * len(args),
        out_specs=tuple(VMEM for _ in outs),
        scratch_shapes=scratch,
        compiler_params=pltpu.CompilerParams(vmem_limit_bytes=40 << 20),
    )(*args)


def split(value):
    high = value.astype(jnp.bfloat16)
    return high, (value - high.astype(jnp.float32)).astype(jnp.bfloat16)


def product(left, right, contract):
    return lax.dot_general(left, right, (contract, ((), ())), preferred_element_type=jnp.float32)


def rows_of(ref, n, h):
    return ref[pl.ds(h, n, stride=ref.shape[0] // n), :]


def put_rows(ref, n, h, value):
    ref[pl.ds(h, n, stride=ref.shape[0] // n), :] = value


def category_sums(field, table_ref, mask_ref, n):
    width = 4 if n % 4 == 0 else 1
    lanes = width * LANES
    rows = mask_ref.shape[0]

    def step(c, total):
        pieces = [field[pl.ds(c * width + i, PAD, stride=n), :] for i in range(width)]
        parts = split(jnp.concatenate(pieces, axis=1))
        start = pl.multiple_of(c * lanes, lanes)
        masks = mask_ref[:, pl.ds(start, lanes)]
        spread = jnp.concatenate(
            [part * masks[g : g + PAD] for part in parts for g in range(0, rows, PAD)], axis=0
        )
        return total + product(spread, table_ref[pl.ds(start, lanes), :], ((1,), (0,)))

    steps = n // width
    total = lax.fori_loop(
        0, steps, step, jnp.zeros((2 * rows, WIDE), jnp.float32), unroll=min(steps, 8)
    )
    return total[:rows] + total[rows:]


def category_spread(values, cats, h):
    place = cats % LANES
    group = cats // LANES
    found = []
    for g in range(0, values.shape[0], PAD):
        for lane in range(0, WIDE, LANES):
            row = jnp.broadcast_to(values[g + h : g + h + 1, lane : lane + LANES], cats.shape)
            found.append(jnp.take_along_axis(row, place, axis=1))
    bit = 1
    while len(found) > 1:
        odd = (group & bit) != 0
        pairs = [found[i : i + 2] for i in range(0, len(found), 2)]
        found = [jnp.where(odd, pair[1], pair[0]) if len(pair) == 2 else pair[0] for pair in pairs]
        bit *= 2
    return found[0]


def region_sums(load, same, n, horizon):
    high, low = split(jnp.concatenate([load(h) for h in range(horizon)], axis=1))
    total = product(same, high, ((1,), (0,))) + product(same, low, ((1,), (0,)))
    return [total[:, h * LANES : (h + 1) * LANES] for h in range(horizon)]


def pack_body(base_ref, out_ref):
    n = base_ref.shape[1]
    for h in range(base_ref.shape[0]):
        put_rows(out_ref, n, h, base_ref[h])


def prepare_body(
    base_ref, base_cat_ref, weight_cat_ref, base_reg_ref, weight_reg_ref, cats_ref, map_ref,
    spread_out, wcat_out, wstore_out, bstore_out, same_out, table_out, mask_out, field, values,
):
    horizon, n, _ = base_ref.shape
    n_regions = weight_reg_ref.shape[1]
    square = jnp.concatenate([cats_ref[...].astype(jnp.float32)] * (LANES // min(n, LANES)), axis=0)
    labels = lax.broadcasted_iota(jnp.int32, (LANES, WIDE), 1)
    columns = [
        jnp.transpose(square[i : i + LANES]).astype(jnp.int32) % WIDE
        for i in range(0, square.shape[0], LANES)
    ]
    for j in range(n):
        column = jnp.broadcast_to(columns[j // LANES][:, j % LANES : j % LANES + 1], (LANES, WIDE))
        table_out[j * LANES : (j + 1) * LANES, :] = jnp.where(
            column == labels, 1.0, 0.0
        ).astype(jnp.bfloat16)
        group = jnp.broadcast_to(cats_ref[j : j + 1, :] // WIDE, (PAD, LANES))
        for g in range(0, mask_out.shape[0], PAD):
            mask_out[g : g + PAD, j * LANES : (j + 1) * LANES] = jnp.where(
                group == g // PAD, 1.0, 0.0
            ).astype(jnp.bfloat16)

    field[...] = jnp.zeros_like(field)
    for h in range(horizon):
        field[h * n : (h + 1) * n, :] = base_ref[h]
    sums = category_sums(field, table_out, mask_out, n)
    wcat_out[...] = jnp.zeros_like(wcat_out)
    values[...] = jnp.zeros_like(values)
    for g in range(0, wcat_out.shape[0], PAD):
        for lane in range(0, WIDE, LANES):
            tile = (g // PAD * WIDE + lane) // LANES
            lanes = slice(lane, lane + LANES)
            weight = weight_cat_ref[:, tile, :]
            wcat_out[g : g + horizon, lanes] = weight
            values[g : g + horizon, lanes] = weight * (
                base_cat_ref[:, tile, :] - sums[g : g + horizon, lanes]
            )
    cats = cats_ref[...]
    for h in range(horizon):
        spread_out[h] = category_spread(values, cats, h)

    labels = lax.broadcasted_iota(jnp.int32, (n_regions, n), 0)
    table = jnp.where(labels == map_ref[...], 1.0, 0.0).astype(jnp.bfloat16)
    same_out[...] = product(table, table, ((0,), (0,))).astype(jnp.bfloat16)
    for source, target in ((weight_reg_ref, wstore_out), (base_reg_ref, bstore_out)):
        for h in range(horizon):
            high, low = split(source[h])
            rest = source[h] - high.astype(jnp.float32) - low.astype(jnp.float32)
            target[h] = (
                product(table, high, ((0,), (0,)))
                + product(table, low, ((0,), (0,)))
                + product(table, rest.astype(jnp.bfloat16), ((0,), (0,)))
            )


def region_start_body(got_ref, spread_ref, wstore_ref, bstore_ref, same_ref, send_ref):
    horizon, n, _ = spread_ref.shape
    sums = region_sums(lambda h: rows_of(got_ref, n, h), same_ref[...], n, horizon)
    for h in range(horizon):
        put_rows(send_ref, n, h, spread_ref[h])
        put_rows(send_ref, n, horizon + h, wstore_ref[h] * (bstore_ref[h] - sums[h]))


def operate(r_ref, rs, eps, diag_ref, wcat_ref, wstore_ref, table_ref, mask_ref, cats_ref, same_ref, a_put, reg_put, sum_put, values):
    horizon, n, _ = diag_ref.shape
    gamma = jnp.zeros((n, LANES), jnp.float32)
    delta = jnp.zeros((n, LANES), jnp.float32)
    sums = region_sums(lambda h: rs[h], same_ref[...], n, horizon)
    for h in range(horizon):
        reg = wstore_ref[h] * sums[h]
        delta = delta + reg * rs[h]
        reg_put(h, reg)

    sums = category_sums(r_ref, table_ref, mask_ref, n)
    scaled = wcat_ref[...] * sums
    values[...] = scaled
    cats = cats_ref[...]
    for h in range(horizon):
        r = r_ref[h * n : (h + 1) * n, :]
        scaled_r = diag_ref[h] * r
        gamma = gamma + r * r
        delta = delta + scaled_r * r
        a_put(h, scaled_r + category_spread(values, cats, h))

    square = scaled * sums
    delta = jnp.sum(delta, axis=0, keepdims=True)
    for lane in range(0, WIDE, LANES):
        delta = delta + jnp.sum(square[:, lane : lane + LANES], axis=0, keepdims=True)
    lane = lax.broadcasted_iota(jnp.int32, (1, LANES), 1)
    line = jnp.zeros((1, LANES), jnp.float32)
    for i, part in enumerate((gamma, delta, eps)):
        if part is not None:
            whole = jnp.sum(jnp.sum(part, axis=0, keepdims=True), axis=1, keepdims=True)
            line = jnp.where(lane == i, whole, line)
    sum_put(jnp.broadcast_to(line, (n, LANES)))


def totals(got_ref, n, row):
    total = jnp.sum(rows_of(got_ref, n, row), axis=0, keepdims=True)
    total = jnp.broadcast_to(total, (8, LANES))
    return [
        jnp.take_along_axis(total, jnp.full((8, LANES), i, jnp.int32), axis=1)[0:1] for i in range(3)
    ]


def sender(ref, n, first):
    return lambda h, value: put_rows(ref, n, first + h, value)


def clear_tail(r_ref, horizon, n):
    r_ref[horizon * n :, :] = jnp.zeros((r_ref.shape[0] - horizon * n, LANES), jnp.float32)


def first_body(
    sent_ref, got_ref, diag_ref, wcat_ref, wstore_ref, table_ref, mask_ref, cats_ref, same_ref,
    r_ref, rs_ref, send_ref, values,
):
    horizon, n, _ = diag_ref.shape
    clear_tail(r_ref, horizon, n)
    for h in range(horizon):
        r_ref[h * n : (h + 1) * n, :] = rows_of(sent_ref, n, h) + rows_of(got_ref, n, horizon + h)
        rs_ref[h] = rows_of(got_ref, n, h) + rows_of(sent_ref, n, horizon + h)
    operate(
        r_ref, rs_ref, None, diag_ref, wcat_ref, wstore_ref, table_ref, mask_ref, cats_ref, same_ref,
        sender(send_ref, n, 0), sender(send_ref, n, horizon),
        lambda line: put_rows(send_ref, n, 2 * horizon, line), values,
    )


def second_body(
    sent_ref, got_ref, x_ref, r_ref, rs_ref, diag_ref, wcat_ref, wstore_ref, table_ref, mask_ref, cats_ref, same_ref,
    x_out, r_out, rs_out, s_out, ss_out, scal_ref, send_ref, values,
):
    horizon, n, _ = diag_ref.shape
    gamma, delta, _ = totals(got_ref, n, 2 * horizon)
    alpha = gamma / delta
    scal_ref[0:1, :] = gamma
    scal_ref[1:2, :] = delta
    clear_tail(r_out, horizon, n)
    eps = jnp.zeros((n, LANES), jnp.float32)
    for h in range(horizon):
        ws = rows_of(got_ref, n, h) + rows_of(sent_ref, n, horizon + h)
        ss_out[h] = ws
        rs_out[h] = rs_ref[h] - alpha * ws
        w = rows_of(sent_ref, n, h) + rows_of(got_ref, n, horizon + h)
        s_out[h] = w
        r = r_ref[h * n : (h + 1) * n, :]
        x_out[h] = x_ref[h] + alpha * r
        r = r - alpha * w
        r_out[h * n : (h + 1) * n, :] = r
        eps = eps + r * w
    operate(
        r_out, rs_out, eps, diag_ref, wcat_ref, wstore_ref, table_ref, mask_ref, cats_ref, same_ref,
        sender(send_ref, n, 0), sender(send_ref, n, horizon),
        lambda line: put_rows(send_ref, n, 2 * horizon, line), values,
    )


def third_body(
    sent_ref, got_ref, x_ref, r_ref, rs_ref, p_ref, s_ref, ss_ref, scal_ref,
    diag_ref, wcat_ref, wstore_ref, table_ref, mask_ref, cats_ref, same_ref,
    x_out, r_out, p_out, s_out, scal_out, a_out, send_ref, values, rs_out,
):
    horizon, n, _ = diag_ref.shape
    gamma, delta, eps = totals(got_ref, n, 2 * horizon)
    beta = gamma / scal_ref[0:1, :]
    curve = delta + 2.0 * beta * eps + beta * beta * scal_ref[1:2, :]
    alpha = gamma / curve
    scal_out[0:1, :] = gamma
    scal_out[1:2, :] = curve
    clear_tail(r_out, horizon, n)
    eps = jnp.zeros((n, LANES), jnp.float32)
    for h in range(horizon):
        ws = rows_of(got_ref, n, h) + rows_of(sent_ref, n, horizon + h)
        rs_out[h] = rs_ref[h] - alpha * (ws + beta * ss_ref[h])
        w = rows_of(sent_ref, n, h) + rows_of(got_ref, n, horizon + h)
        s = w + beta * s_ref[h]
        s_out[h] = s
        r = r_ref[h * n : (h + 1) * n, :]
        p = r + beta * p_ref[h * n : (h + 1) * n, :]
        p_out[h] = p
        x_out[h] = x_ref[h] + alpha * p
        r = r - alpha * s
        r_out[h * n : (h + 1) * n, :] = r
        eps = eps + r * s

    def keep(h, value):
        a_out[h] = value

    operate(
        r_out, rs_out, eps, diag_ref, wcat_ref, wstore_ref, table_ref, mask_ref, cats_ref, same_ref,
        keep, sender(send_ref, n, 0), lambda line: put_rows(send_ref, n, horizon, line), values,
    )


def last_body(a_ref, got_ref, x_ref, r_ref, p_ref, s_ref, scal_ref, x_out, r_out):
    horizon, n, _ = a_ref.shape
    gamma, delta, eps = totals(got_ref, n, horizon)
    beta = gamma / scal_ref[0:1, :]
    alpha = gamma / (delta + 2.0 * beta * eps + beta * beta * scal_ref[1:2, :])
    for h in range(horizon):
        r = r_ref[h * n : (h + 1) * n, :]
        s = a_ref[h] + rows_of(got_ref, n, h) + beta * s_ref[h]
        x_out[h] = x_ref[h] + alpha * (r + beta * p_ref[h])
        r_out[h] = r - alpha * s


def on_device(
    base_bottom,
    weight_bottom,
    base_category,
    weight_category,
    base_region,
    weight_region,
    category_map,
    region_map,
):
    stores, horizon, skus = base_bottom.shape
    n = region_map.shape[0]
    groups = weight_category.shape[2] // WIDE
    tiles = weight_category.shape[2] // LANES
    cats = category_map.reshape(n, LANES)
    field = (horizon, n, LANES)
    padded = (PAD * n, LANES)
    by_category = (horizon, tiles, LANES)
    scal = (2, LANES)
    values = pltpu.VMEM((groups * PAD, WIDE), jnp.float32)

    x = base_bottom.reshape(field)
    diag = weight_bottom.reshape(field)
    (sent,) = call(pack_body, [(n * horizon, LANES)], [], (x,))
    got = exchange(sent, n)
    spread, wcat, wstore, bstore, same, table, mask = call(
        prepare_body,
        [
            field,
            (groups * PAD, WIDE),
            field,
            field,
            jax.ShapeDtypeStruct((n, n), jnp.bfloat16),
            jax.ShapeDtypeStruct((skus, WIDE), jnp.bfloat16),
            jax.ShapeDtypeStruct((groups * PAD, skus), jnp.bfloat16),
        ],
        [pltpu.VMEM(padded, jnp.float32), values],
        (
            x,
            base_category.reshape(by_category),
            weight_category.reshape(by_category),
            jnp.transpose(base_region, (1, 0, 2)),
            jnp.transpose(weight_region, (1, 0, 2)),
            cats,
            region_map.reshape(1, n),
        ),
    )
    (sent,) = call(
        region_start_body, [(n * 2 * horizon, LANES)], [], (got, spread, wstore, bstore, same)
    )
    got = exchange(sent, n)
    fixed = (diag, wcat, wstore, table, mask, cats, same)
    both = (n * (2 * horizon + 1), LANES)
    r, rs, sent = call(first_body, [padded, field, both], [values], (sent, got) + fixed)
    got = exchange(sent, n)
    p = r
    x, r, rs, s, ss, scalars, sent = call(
        second_body,
        [field, padded, field, field, field, scal, both],
        [values],
        (sent, got, x, r, rs) + fixed,
    )
    got = exchange(sent, n)
    x, r, p, s, scalars, a, sent = call(
        third_body,
        [field, padded, field, field, scal, field, (n * (horizon + 1), LANES)],
        [values, pltpu.VMEM(field, jnp.float32)],
        (sent, got, x, r, rs, p, s, ss, scalars) + fixed,
    )
    got = exchange(sent, n)
    x, r = call(last_body, [field, field], [], (a, got, x, r, p, s, scalars))
    return x.reshape(base_bottom.shape), r.reshape(base_bottom.shape)


def solution(mesh):
    in_specs = (
        P(("store", "sku"), None, None),
        P(("store", "sku"), None, None),
        P(("store", "sku"), None, None),
        P(("store", "sku"), None, None),
        P(None, None, ("store", "sku")),
        P(None, None, ("store", "sku")),
        P(),
        P(),
    )
    out_specs = (P(("store", "sku"), None, None), P(("store", "sku"), None, None))
    return jax.shard_map(
        on_device, mesh=mesh, in_specs=in_specs, out_specs=out_specs, check_vma=False
    )
```

```python
import jax
import jax.numpy as jnp
from jax import lax
from jax.experimental import pallas as pl
from jax.experimental.pallas import tpu as pltpu
from jax.sharding import PartitionSpec as P

LANES = 128
PAD = 16
WIDE = 256
VMEM = pl.BlockSpec(memory_space=pltpu.VMEM)
HBM = pl.BlockSpec(memory_space=pltpu.HBM)


def exchange(blocks, n):
    moved = lax.all_to_all(
        blocks.reshape(n, 1, -1), ("store", "sku"), split_axis=0, concat_axis=0, tiled=True
    )
    return moved.reshape(blocks.shape)


def call(body, outs, scratch, args, specs=None, out_specs=None):
    if specs:
        args = [
            pltpu.with_memory_space_constraint(arg, pltpu.HBM) if spec is HBM else arg
            for arg, spec in zip(args, specs)
        ]
    return pl.pallas_call(
        body,
        out_shape=tuple(
            out if isinstance(out, jax.ShapeDtypeStruct) else jax.ShapeDtypeStruct(out, jnp.float32)
            for out in outs
        ),
        in_specs=specs or [VMEM] * len(args),
        out_specs=tuple(out_specs or [VMEM] * len(outs)),
        scratch_shapes=scratch,
        compiler_params=pltpu.CompilerParams(vmem_limit_bytes=40 << 20),
    )(*args)


def split(value):
    high = value.astype(jnp.bfloat16)
    return high, (value - high.astype(jnp.float32)).astype(jnp.bfloat16)


def product(left, right, contract):
    return lax.dot_general(left, right, (contract, ((), ())), preferred_element_type=jnp.float32)


def rows_of(ref, n, h):
    return ref[pl.ds(h, n, stride=ref.shape[0] // n), :]


def put_rows(ref, n, h, value):
    ref[pl.ds(h, n, stride=ref.shape[0] // n), :] = value


def category_sums(field, table_ref, mask_ref, n):
    width = 4 if n % 4 == 0 else 1
    lanes = width * LANES
    rows = mask_ref.shape[0]

    def step(c, total):
        pieces = [field[pl.ds(c * width + i, PAD, stride=n), :] for i in range(width)]
        parts = split(jnp.concatenate(pieces, axis=1))
        start = pl.multiple_of(c * lanes, lanes)
        masks = mask_ref[:, pl.ds(start, lanes)]
        spread = jnp.concatenate(
            [part * masks[g : g + PAD] for part in parts for g in range(0, rows, PAD)], axis=0
        )
        return total + product(spread, table_ref[pl.ds(start, lanes), :], ((1,), (0,)))

    steps = n // width
    total = lax.fori_loop(
        0, steps, step, jnp.zeros((2 * rows, WIDE), jnp.float32), unroll=min(steps, 8)
    )
    return total[:rows] + total[rows:]


def category_spread(values, cats, h):
    place = cats % LANES
    group = cats // LANES
    found = []
    for g in range(0, values.shape[0], PAD):
        for lane in range(0, WIDE, LANES):
            row = jnp.broadcast_to(values[g + h : g + h + 1, lane : lane + LANES], cats.shape)
            found.append(jnp.take_along_axis(row, place, axis=1))
    bit = 1
    while len(found) > 1:
        odd = (group & bit) != 0
        pairs = [found[i : i + 2] for i in range(0, len(found), 2)]
        found = [jnp.where(odd, pair[1], pair[0]) if len(pair) == 2 else pair[0] for pair in pairs]
        bit *= 2
    return found[0]


def region_sums(load, same, n, horizon):
    high, low = split(jnp.concatenate([load(h) for h in range(horizon)], axis=1))
    total = product(same, high, ((1,), (0,))) + product(same, low, ((1,), (0,)))
    return [total[:, h * LANES : (h + 1) * LANES] for h in range(horizon)]


def pack_body(base_ref, out_ref, sems):
    copies = [
        pltpu.make_async_copy(base_ref.at[h], out_ref.at[:, h], sems.at[h])
        for h in range(base_ref.shape[0])
    ]
    for copy in copies:
        copy.start()
    for copy in copies:
        copy.wait()


def prepare_body(
    base_hbm, diag_hbm, base_cat_hbm, weight_cat_hbm, base_reg_hbm, weight_reg_hbm, cats_hbm, map_hbm,
    spread_out, wcat_out, wstore_out, bstore_out, same_out, table_out, mask_out,
    base_ref, diag_out, cats_ref,
    field, values, base_cat_ref, weight_cat_ref, base_reg_ref, weight_reg_ref, map_ref, sems,
):
    copies = [
        pltpu.make_async_copy(source, target, sems.at[i])
        for i, (source, target) in enumerate(
            (
                (cats_hbm, cats_ref),
                (base_hbm, base_ref),
                (weight_cat_hbm, weight_cat_ref),
                (base_cat_hbm, base_cat_ref),
                (map_hbm, map_ref),
                (weight_reg_hbm, weight_reg_ref),
                (base_reg_hbm, base_reg_ref),
                (diag_hbm, diag_out),
            )
        )
    ]
    for copy in copies:
        copy.start()
    for copy in copies:
        copy.wait()
    horizon, n, _ = base_ref.shape
    n_regions = weight_reg_ref.shape[1]
    square = jnp.concatenate([cats_ref[...].astype(jnp.float32)] * (LANES // min(n, LANES)), axis=0)
    labels = lax.broadcasted_iota(jnp.int32, (LANES, WIDE), 1)
    columns = [
        jnp.transpose(square[i : i + LANES]).astype(jnp.int32) % WIDE
        for i in range(0, square.shape[0], LANES)
    ]
    for j in range(n):
        column = jnp.broadcast_to(columns[j // LANES][:, j % LANES : j % LANES + 1], (LANES, WIDE))
        table_out[j * LANES : (j + 1) * LANES, :] = jnp.where(
            column == labels, 1.0, 0.0
        ).astype(jnp.bfloat16)
        group = jnp.broadcast_to(cats_ref[j : j + 1, :] // WIDE, (PAD, LANES))
        for g in range(0, mask_out.shape[0], PAD):
            mask_out[g : g + PAD, j * LANES : (j + 1) * LANES] = jnp.where(
                group == g // PAD, 1.0, 0.0
            ).astype(jnp.bfloat16)

    field[...] = jnp.zeros_like(field)
    for h in range(horizon):
        field[h * n : (h + 1) * n, :] = base_ref[h]
    sums = category_sums(field, table_out, mask_out, n)
    wcat_out[...] = jnp.zeros_like(wcat_out)
    values[...] = jnp.zeros_like(values)
    for g in range(0, wcat_out.shape[0], PAD):
        for lane in range(0, WIDE, LANES):
            tile = (g // PAD * WIDE + lane) // LANES
            lanes = slice(lane, lane + LANES)
            weight = weight_cat_ref[:, tile, :]
            wcat_out[g : g + horizon, lanes] = weight
            values[g : g + horizon, lanes] = weight * (
                base_cat_ref[:, tile, :] - sums[g : g + horizon, lanes]
            )
    cats = cats_ref[...]
    for h in range(horizon):
        spread_out[h] = category_spread(values, cats, h)

    labels = lax.broadcasted_iota(jnp.int32, (n_regions, n), 0)
    table = jnp.where(labels == map_ref[...], 1.0, 0.0).astype(jnp.bfloat16)
    same_out[...] = product(table, table, ((0,), (0,))).astype(jnp.bfloat16)
    for source, target in ((weight_reg_ref, wstore_out), (base_reg_ref, bstore_out)):
        for h in range(horizon):
            high, low = split(source[h])
            rest = source[h] - high.astype(jnp.float32) - low.astype(jnp.float32)
            target[h] = (
                product(table, high, ((0,), (0,)))
                + product(table, low, ((0,), (0,)))
                + product(table, rest.astype(jnp.bfloat16), ((0,), (0,)))
            )


def region_start_body(got_ref, spread_ref, wstore_ref, bstore_ref, same_ref, send_ref):
    horizon, n, _ = spread_ref.shape
    sums = region_sums(lambda h: rows_of(got_ref, n, h), same_ref[...], n, horizon)
    for h in range(horizon):
        put_rows(send_ref, n, h, spread_ref[h])
        put_rows(send_ref, n, horizon + h, wstore_ref[h] * (bstore_ref[h] - sums[h]))


def operate(r_ref, rs, eps, diag_ref, wcat_ref, wstore_ref, table_ref, mask_ref, cats_ref, same_ref, a_put, reg_put, sum_put, values):
    horizon, n, _ = diag_ref.shape
    gamma = jnp.zeros((n, LANES), jnp.float32)
    delta = jnp.zeros((n, LANES), jnp.float32)
    sums = region_sums(lambda h: rs[h], same_ref[...], n, horizon)
    for h in range(horizon):
        reg = wstore_ref[h] * sums[h]
        delta = delta + reg * rs[h]
        reg_put(h, reg)

    sums = category_sums(r_ref, table_ref, mask_ref, n)
    scaled = wcat_ref[...] * sums
    values[...] = scaled
    cats = cats_ref[...]
    for h in range(horizon):
        r = r_ref[h * n : (h + 1) * n, :]
        scaled_r = diag_ref[h] * r
        gamma = gamma + r * r
        delta = delta + scaled_r * r
        a_put(h, scaled_r + category_spread(values, cats, h))

    square = scaled * sums
    delta = jnp.sum(delta, axis=0, keepdims=True)
    for lane in range(0, WIDE, LANES):
        delta = delta + jnp.sum(square[:, lane : lane + LANES], axis=0, keepdims=True)
    lane = lax.broadcasted_iota(jnp.int32, (1, LANES), 1)
    line = jnp.zeros((1, LANES), jnp.float32)
    for i, part in enumerate((gamma, delta, eps)):
        if part is not None:
            whole = jnp.sum(jnp.sum(part, axis=0, keepdims=True), axis=1, keepdims=True)
            line = jnp.where(lane == i, whole, line)
    sum_put(jnp.broadcast_to(line, (n, LANES)))


def totals(got_ref, n, row):
    total = jnp.sum(rows_of(got_ref, n, row), axis=0, keepdims=True)
    total = jnp.broadcast_to(total, (8, LANES))
    return [
        jnp.take_along_axis(total, jnp.full((8, LANES), i, jnp.int32), axis=1)[0:1] for i in range(3)
    ]


def sender(ref, n, first):
    return lambda h, value: put_rows(ref, n, first + h, value)


def clear_tail(r_ref, horizon, n):
    r_ref[horizon * n :, :] = jnp.zeros((r_ref.shape[0] - horizon * n, LANES), jnp.float32)


def first_body(
    sent_ref, got_ref, diag_ref, wcat_ref, wstore_ref, table_ref, mask_ref, cats_ref, same_ref,
    r_ref, rs_ref, send_ref, values,
):
    horizon, n, _ = diag_ref.shape
    clear_tail(r_ref, horizon, n)
    for h in range(horizon):
        r_ref[h * n : (h + 1) * n, :] = rows_of(sent_ref, n, h) + rows_of(got_ref, n, horizon + h)
        rs_ref[h] = rows_of(got_ref, n, h) + rows_of(sent_ref, n, horizon + h)
    operate(
        r_ref, rs_ref, None, diag_ref, wcat_ref, wstore_ref, table_ref, mask_ref, cats_ref, same_ref,
        sender(send_ref, n, 0), sender(send_ref, n, horizon),
        lambda line: put_rows(send_ref, n, 2 * horizon, line), values,
    )


def second_body(
    sent_ref, got_ref, x_ref, r_ref, rs_ref, diag_ref, wcat_ref, wstore_ref, table_ref, mask_ref, cats_ref, same_ref,
    x_out, r_out, rs_out, s_out, ss_out, scal_ref, send_ref, values,
):
    horizon, n, _ = diag_ref.shape
    gamma, delta, _ = totals(got_ref, n, 2 * horizon)
    alpha = gamma / delta
    scal_ref[0:1, :] = gamma
    scal_ref[1:2, :] = delta
    clear_tail(r_out, horizon, n)
    eps = jnp.zeros((n, LANES), jnp.float32)
    for h in range(horizon):
        ws = rows_of(got_ref, n, h) + rows_of(sent_ref, n, horizon + h)
        ss_out[h] = ws
        rs_out[h] = rs_ref[h] - alpha * ws
        w = rows_of(sent_ref, n, h) + rows_of(got_ref, n, horizon + h)
        s_out[h] = w
        r = r_ref[h * n : (h + 1) * n, :]
        x_out[h] = x_ref[h] + alpha * r
        r = r - alpha * w
        r_out[h * n : (h + 1) * n, :] = r
        eps = eps + r * w
    operate(
        r_out, rs_out, eps, diag_ref, wcat_ref, wstore_ref, table_ref, mask_ref, cats_ref, same_ref,
        sender(send_ref, n, 0), sender(send_ref, n, horizon),
        lambda line: put_rows(send_ref, n, 2 * horizon, line), values,
    )


def third_body(
    sent_ref, got_ref, x_ref, r_ref, rs_ref, p_ref, s_ref, ss_ref, scal_ref,
    diag_ref, wcat_ref, wstore_ref, table_ref, mask_ref, cats_ref, same_ref,
    x_out, r_out, p_out, s_out, scal_out, a_out, send_ref, values, rs_out,
):
    horizon, n, _ = diag_ref.shape
    gamma, delta, eps = totals(got_ref, n, 2 * horizon)
    beta = gamma / scal_ref[0:1, :]
    curve = delta + 2.0 * beta * eps + beta * beta * scal_ref[1:2, :]
    alpha = gamma / curve
    scal_out[0:1, :] = gamma
    scal_out[1:2, :] = curve
    clear_tail(r_out, horizon, n)
    eps = jnp.zeros((n, LANES), jnp.float32)
    for h in range(horizon):
        ws = rows_of(got_ref, n, h) + rows_of(sent_ref, n, horizon + h)
        rs_out[h] = rs_ref[h] - alpha * (ws + beta * ss_ref[h])
        w = rows_of(sent_ref, n, h) + rows_of(got_ref, n, horizon + h)
        s = w + beta * s_ref[h]
        s_out[h] = s
        r = r_ref[h * n : (h + 1) * n, :]
        p = r + beta * p_ref[h * n : (h + 1) * n, :]
        p_out[h] = p
        x_out[h] = x_ref[h] + alpha * p
        r = r - alpha * s
        r_out[h * n : (h + 1) * n, :] = r
        eps = eps + r * s

    def keep(h, value):
        a_out[h] = value

    operate(
        r_out, rs_out, eps, diag_ref, wcat_ref, wstore_ref, table_ref, mask_ref, cats_ref, same_ref,
        keep, sender(send_ref, n, 0), lambda line: put_rows(send_ref, n, horizon, line), values,
    )


def last_body(a_ref, got_ref, x_ref, r_ref, p_ref, s_ref, scal_ref, x_out, r_out):
    horizon, n, _ = a_ref.shape
    gamma, delta, eps = totals(got_ref, n, horizon)
    beta = gamma / scal_ref[0:1, :]
    alpha = gamma / (delta + 2.0 * beta * eps + beta * beta * scal_ref[1:2, :])
    for h in range(horizon):
        r = r_ref[h * n : (h + 1) * n, :]
        s = a_ref[h] + rows_of(got_ref, n, h) + beta * s_ref[h]
        x_out[h] = x_ref[h] + alpha * (r + beta * p_ref[h])
        r_out[h] = r - alpha * s


def on_device(
    base_bottom,
    weight_bottom,
    base_category,
    weight_category,
    base_region,
    weight_region,
    category_map,
    region_map,
):
    stores, horizon, skus = base_bottom.shape
    n = region_map.shape[0]
    groups = weight_category.shape[2] // WIDE
    tiles = weight_category.shape[2] // LANES
    field = (horizon, n, LANES)
    padded = (PAD * n, LANES)
    by_category = (horizon, tiles, LANES)
    scal = (2, LANES)
    values = pltpu.VMEM((groups * PAD, WIDE), jnp.float32)

    lines = (horizon, n, 1, LANES)
    (sent,) = call(
        pack_body,
        [(n, horizon, 1, LANES)],
        [pltpu.SemaphoreType.DMA((horizon,))],
        (base_bottom.reshape(lines),),
        [HBM],
        [HBM],
    )
    got = exchange(sent.reshape(n * horizon, LANES), n)
    arguments = (
        base_bottom.reshape(field),
        weight_bottom.reshape(field),
        base_category.reshape(by_category),
        weight_category.reshape(by_category),
        jnp.transpose(base_region, (1, 0, 2)),
        jnp.transpose(weight_region, (1, 0, 2)),
        category_map.reshape(n, LANES),
        region_map.reshape(1, n),
    )
    held = [pltpu.VMEM(arguments[i].shape, arguments[i].dtype) for i in (2, 3, 4, 5, 7)]
    spread, wcat, wstore, bstore, same, table, mask, x, diag, cats = call(
        prepare_body,
        [
            field,
            (groups * PAD, WIDE),
            field,
            field,
            jax.ShapeDtypeStruct((n, n), jnp.bfloat16),
            jax.ShapeDtypeStruct((skus, WIDE), jnp.bfloat16),
            jax.ShapeDtypeStruct((groups * PAD, skus), jnp.bfloat16),
            field,
            field,
            jax.ShapeDtypeStruct((n, LANES), jnp.int32),
        ],
        [
            pltpu.VMEM(padded, jnp.float32),
            values,
            *held,
            pltpu.SemaphoreType.DMA((len(arguments),)),
        ],
        arguments,
        [HBM] * len(arguments),
    )
    (sent,) = call(
        region_start_body, [(n * 2 * horizon, LANES)], [], (got, spread, wstore, bstore, same)
    )
    got = exchange(sent, n)
    fixed = (diag, wcat, wstore, table, mask, cats, same)
    both = (n * (2 * horizon + 1), LANES)
    r, rs, sent = call(first_body, [padded, field, both], [values], (sent, got) + fixed)
    got = exchange(sent, n)
    p = r
    x, r, rs, s, ss, scalars, sent = call(
        second_body,
        [field, padded, field, field, field, scal, both],
        [values],
        (sent, got, x, r, rs) + fixed,
    )
    got = exchange(sent, n)
    x, r, p, s, scalars, a, sent = call(
        third_body,
        [field, padded, field, field, scal, field, (n * (horizon + 1), LANES)],
        [values, pltpu.VMEM(field, jnp.float32)],
        (sent, got, x, r, rs, p, s, ss, scalars) + fixed,
    )
    got = exchange(sent, n)
    x, r = call(last_body, [field, field], [], (a, got, x, r, p, s, scalars))
    return x.reshape(base_bottom.shape), r.reshape(base_bottom.shape)


def solution(mesh):
    in_specs = (
        P(("store", "sku"), None, None),
        P(("store", "sku"), None, None),
        P(("store", "sku"), None, None),
        P(("store", "sku"), None, None),
        P(None, None, ("store", "sku")),
        P(None, None, ("store", "sku")),
        P(),
        P(),
    )
    out_specs = (P(("store", "sku"), None, None), P(("store", "sku"), None, None))
    return jax.shard_map(
        on_device, mesh=mesh, in_specs=in_specs, out_specs=out_specs, check_vma=False
    )
```

```python
import jax
import jax.numpy as jnp
from jax import lax
from jax.experimental import pallas as pl
from jax.experimental.pallas import tpu as pltpu
from jax.sharding import PartitionSpec as P

LANES = 128
PAD = 16
WIDE = 256
VMEM = pl.BlockSpec(memory_space=pltpu.VMEM)
HBM = pl.BlockSpec(memory_space=pltpu.HBM)


def exchange(blocks, n):
    moved = lax.all_to_all(
        blocks.reshape(n, 1, -1), ("store", "sku"), split_axis=0, concat_axis=0, tiled=True
    )
    return moved.reshape(blocks.shape)


def call(body, outs, scratch, args, specs=None, held=False):
    outs = [
        out if isinstance(out, jax.ShapeDtypeStruct) else jax.ShapeDtypeStruct(out, jnp.float32)
        for out in outs
    ]
    if specs:
        args = [pltpu.with_memory_space_constraint(arg, spec.memory_space) for arg, spec in zip(args, specs)]
    return pl.pallas_call(
        body,
        out_shape=tuple(pltpu.VMEM(out.shape, out.dtype) if held else out for out in outs),
        in_specs=specs or [VMEM] * len(args),
        out_specs=tuple(VMEM for _ in outs),
        scratch_shapes=scratch,
        compiler_params=pltpu.CompilerParams(vmem_limit_bytes=40 << 20),
    )(*args)


def split(value):
    high = value.astype(jnp.bfloat16)
    return high, (value - high.astype(jnp.float32)).astype(jnp.bfloat16)


def product(left, right, contract):
    return lax.dot_general(left, right, (contract, ((), ())), preferred_element_type=jnp.float32)


def rows_of(ref, n, h):
    return ref[pl.ds(h, n, stride=ref.shape[0] // n), :]


def put_rows(ref, n, h, value):
    ref[pl.ds(h, n, stride=ref.shape[0] // n), :] = value


def category_sums(field, table_ref, mask_ref, n):
    width = 4 if n % 4 == 0 else 1
    lanes = width * LANES
    rows = mask_ref.shape[0]

    def step(c, total):
        pieces = [field[pl.ds(c * width + i, PAD, stride=n), :] for i in range(width)]
        parts = split(jnp.concatenate(pieces, axis=1))
        start = pl.multiple_of(c * lanes, lanes)
        masks = mask_ref[:, pl.ds(start, lanes)]
        spread = jnp.concatenate(
            [part * masks[g : g + PAD] for part in parts for g in range(0, rows, PAD)], axis=0
        )
        return total + product(spread, table_ref[pl.ds(start, lanes), :], ((1,), (0,)))

    steps = n // width
    total = lax.fori_loop(
        0, steps, step, jnp.zeros((2 * rows, WIDE), jnp.float32), unroll=min(steps, 8)
    )
    return total[:rows] + total[rows:]


def category_spread(values, cats, h):
    place = cats % LANES
    group = cats // LANES
    found = []
    for g in range(0, values.shape[0], PAD):
        for lane in range(0, WIDE, LANES):
            row = jnp.broadcast_to(values[g + h : g + h + 1, lane : lane + LANES], cats.shape)
            found.append(jnp.take_along_axis(row, place, axis=1))
    bit = 1
    while len(found) > 1:
        odd = (group & bit) != 0
        pairs = [found[i : i + 2] for i in range(0, len(found), 2)]
        found = [jnp.where(odd, pair[1], pair[0]) if len(pair) == 2 else pair[0] for pair in pairs]
        bit *= 2
    return found[0]


def region_sums(load, same, n, horizon):
    high, low = split(jnp.concatenate([load(h) for h in range(horizon)], axis=1))
    total = product(same, high, ((1,), (0,))) + product(same, low, ((1,), (0,)))
    return [total[:, h * LANES : (h + 1) * LANES] for h in range(horizon)]


def pack_body(base_hbm, out_ref, base_ref, sem):
    copy = pltpu.make_async_copy(base_hbm, base_ref, sem)
    copy.start()
    copy.wait()
    n = base_ref.shape[1]
    for h in range(base_ref.shape[0]):
        put_rows(out_ref, n, h, base_ref[h])


def prepare_body(
    base_hbm, diag_hbm, base_cat_hbm, weight_cat_hbm, base_reg_hbm, weight_reg_hbm, cats_hbm, map_hbm,
    spread_out, wcat_out, wstore_out, bstore_out, same_out, table_out, mask_out,
    base_ref, diag_out, cats_ref,
    field, values, base_cat_ref, weight_cat_ref, base_reg_ref, weight_reg_ref, map_ref, sems,
):
    copies = [
        pltpu.make_async_copy(source, target, sems.at[i])
        for i, (source, target) in enumerate(
            (
                (cats_hbm, cats_ref),
                (base_hbm, base_ref),
                (weight_cat_hbm, weight_cat_ref),
                (base_cat_hbm, base_cat_ref),
                (map_hbm, map_ref),
                (weight_reg_hbm, weight_reg_ref),
                (base_reg_hbm, base_reg_ref),
                (diag_hbm, diag_out),
            )
        )
    ]
    for copy in copies:
        copy.start()
    for copy in copies:
        copy.wait()
    horizon, n, _ = base_ref.shape
    n_regions = weight_reg_ref.shape[1]
    square = jnp.concatenate([cats_ref[...].astype(jnp.float32)] * (LANES // min(n, LANES)), axis=0)
    labels = lax.broadcasted_iota(jnp.int32, (LANES, WIDE), 1)
    columns = [
        jnp.transpose(square[i : i + LANES]).astype(jnp.int32) % WIDE
        for i in range(0, square.shape[0], LANES)
    ]
    for j in range(n):
        column = jnp.broadcast_to(columns[j // LANES][:, j % LANES : j % LANES + 1], (LANES, WIDE))
        table_out[j * LANES : (j + 1) * LANES, :] = jnp.where(
            column == labels, 1.0, 0.0
        ).astype(jnp.bfloat16)
        group = jnp.broadcast_to(cats_ref[j : j + 1, :] // WIDE, (PAD, LANES))
        for g in range(0, mask_out.shape[0], PAD):
            mask_out[g : g + PAD, j * LANES : (j + 1) * LANES] = jnp.where(
                group == g // PAD, 1.0, 0.0
            ).astype(jnp.bfloat16)

    field[...] = jnp.zeros_like(field)
    for h in range(horizon):
        field[h * n : (h + 1) * n, :] = base_ref[h]
    sums = category_sums(field, table_out, mask_out, n)
    wcat_out[...] = jnp.zeros_like(wcat_out)
    values[...] = jnp.zeros_like(values)
    for g in range(0, wcat_out.shape[0], PAD):
        for lane in range(0, WIDE, LANES):
            tile = (g // PAD * WIDE + lane) // LANES
            lanes = slice(lane, lane + LANES)
            weight = weight_cat_ref[:, tile, :]
            wcat_out[g : g + horizon, lanes] = weight
            values[g : g + horizon, lanes] = weight * (
                base_cat_ref[:, tile, :] - sums[g : g + horizon, lanes]
            )
    cats = cats_ref[...]
    for h in range(horizon):
        spread_out[h] = category_spread(values, cats, h)

    labels = lax.broadcasted_iota(jnp.int32, (n_regions, n), 0)
    table = jnp.where(labels == map_ref[...], 1.0, 0.0).astype(jnp.bfloat16)
    same_out[...] = product(table, table, ((0,), (0,))).astype(jnp.bfloat16)
    for source, target in ((weight_reg_ref, wstore_out), (base_reg_ref, bstore_out)):
        for h in range(horizon):
            high, low = split(source[h])
            rest = source[h] - high.astype(jnp.float32) - low.astype(jnp.float32)
            target[h] = (
                product(table, high, ((0,), (0,)))
                + product(table, low, ((0,), (0,)))
                + product(table, rest.astype(jnp.bfloat16), ((0,), (0,)))
            )


def region_start_body(got_ref, spread_ref, wstore_ref, bstore_ref, same_ref, send_ref):
    horizon, n, _ = spread_ref.shape
    sums = region_sums(lambda h: rows_of(got_ref, n, h), same_ref[...], n, horizon)
    for h in range(horizon):
        put_rows(send_ref, n, h, spread_ref[h])
        put_rows(send_ref, n, horizon + h, wstore_ref[h] * (bstore_ref[h] - sums[h]))


def operate(r_ref, rs, eps, diag_ref, wcat_ref, wstore_ref, table_ref, mask_ref, cats_ref, same_ref, a_put, reg_put, sum_put, values):
    horizon, n, _ = diag_ref.shape
    gamma = jnp.zeros((n, LANES), jnp.float32)
    delta = jnp.zeros((n, LANES), jnp.float32)
    sums = region_sums(lambda h: rs[h], same_ref[...], n, horizon)
    for h in range(horizon):
        reg = wstore_ref[h] * sums[h]
        delta = delta + reg * rs[h]
        reg_put(h, reg)

    sums = category_sums(r_ref, table_ref, mask_ref, n)
    scaled = wcat_ref[...] * sums
    values[...] = scaled
    cats = cats_ref[...]
    for h in range(horizon):
        r = r_ref[h * n : (h + 1) * n, :]
        scaled_r = diag_ref[h] * r
        gamma = gamma + r * r
        delta = delta + scaled_r * r
        a_put(h, scaled_r + category_spread(values, cats, h))

    square = scaled * sums
    delta = jnp.sum(delta, axis=0, keepdims=True)
    for lane in range(0, WIDE, LANES):
        delta = delta + jnp.sum(square[:, lane : lane + LANES], axis=0, keepdims=True)
    lane = lax.broadcasted_iota(jnp.int32, (1, LANES), 1)
    line = jnp.zeros((1, LANES), jnp.float32)
    for i, part in enumerate((gamma, delta, eps)):
        if part is not None:
            whole = jnp.sum(jnp.sum(part, axis=0, keepdims=True), axis=1, keepdims=True)
            line = jnp.where(lane == i, whole, line)
    sum_put(jnp.broadcast_to(line, (n, LANES)))


def totals(got_ref, n, row):
    total = jnp.sum(rows_of(got_ref, n, row), axis=0, keepdims=True)
    total = jnp.broadcast_to(total, (8, LANES))
    return [
        jnp.take_along_axis(total, jnp.full((8, LANES), i, jnp.int32), axis=1)[0:1] for i in range(3)
    ]


def sender(ref, n, first):
    return lambda h, value: put_rows(ref, n, first + h, value)


def clear_tail(r_ref, horizon, n):
    r_ref[horizon * n :, :] = jnp.zeros((r_ref.shape[0] - horizon * n, LANES), jnp.float32)


def first_body(
    sent_ref, got_ref, diag_ref, wcat_ref, wstore_ref, table_ref, mask_ref, cats_ref, same_ref,
    r_ref, rs_ref, send_ref, values,
):
    horizon, n, _ = diag_ref.shape
    clear_tail(r_ref, horizon, n)
    for h in range(horizon):
        r_ref[h * n : (h + 1) * n, :] = rows_of(sent_ref, n, h) + rows_of(got_ref, n, horizon + h)
        rs_ref[h] = rows_of(got_ref, n, h) + rows_of(sent_ref, n, horizon + h)
    operate(
        r_ref, rs_ref, None, diag_ref, wcat_ref, wstore_ref, table_ref, mask_ref, cats_ref, same_ref,
        sender(send_ref, n, 0), sender(send_ref, n, horizon),
        lambda line: put_rows(send_ref, n, 2 * horizon, line), values,
    )


def second_body(
    sent_ref, got_ref, x_ref, r_ref, rs_ref, diag_ref, wcat_ref, wstore_ref, table_ref, mask_ref, cats_ref, same_ref,
    x_out, r_out, rs_out, s_out, ss_out, scal_ref, send_ref, values,
):
    horizon, n, _ = diag_ref.shape
    gamma, delta, _ = totals(got_ref, n, 2 * horizon)
    alpha = gamma / delta
    scal_ref[0:1, :] = gamma
    scal_ref[1:2, :] = delta
    clear_tail(r_out, horizon, n)
    eps = jnp.zeros((n, LANES), jnp.float32)
    for h in range(horizon):
        ws = rows_of(got_ref, n, h) + rows_of(sent_ref, n, horizon + h)
        ss_out[h] = ws
        rs_out[h] = rs_ref[h] - alpha * ws
        w = rows_of(sent_ref, n, h) + rows_of(got_ref, n, horizon + h)
        s_out[h] = w
        r = r_ref[h * n : (h + 1) * n, :]
        x_out[h] = x_ref[h] + alpha * r
        r = r - alpha * w
        r_out[h * n : (h + 1) * n, :] = r
        eps = eps + r * w
    operate(
        r_out, rs_out, eps, diag_ref, wcat_ref, wstore_ref, table_ref, mask_ref, cats_ref, same_ref,
        sender(send_ref, n, 0), sender(send_ref, n, horizon),
        lambda line: put_rows(send_ref, n, 2 * horizon, line), values,
    )


def third_body(
    sent_ref, got_ref, x_ref, r_ref, rs_ref, p_ref, s_ref, ss_ref, scal_ref,
    diag_ref, wcat_ref, wstore_ref, table_ref, mask_ref, cats_ref, same_ref,
    x_out, r_out, p_out, s_out, scal_out, a_out, send_ref, values, rs_out,
):
    horizon, n, _ = diag_ref.shape
    gamma, delta, eps = totals(got_ref, n, 2 * horizon)
    beta = gamma / scal_ref[0:1, :]
    curve = delta + 2.0 * beta * eps + beta * beta * scal_ref[1:2, :]
    alpha = gamma / curve
    scal_out[0:1, :] = gamma
    scal_out[1:2, :] = curve
    clear_tail(r_out, horizon, n)
    eps = jnp.zeros((n, LANES), jnp.float32)
    for h in range(horizon):
        ws = rows_of(got_ref, n, h) + rows_of(sent_ref, n, horizon + h)
        rs_out[h] = rs_ref[h] - alpha * (ws + beta * ss_ref[h])
        w = rows_of(sent_ref, n, h) + rows_of(got_ref, n, horizon + h)
        s = w + beta * s_ref[h]
        s_out[h] = s
        r = r_ref[h * n : (h + 1) * n, :]
        p = r + beta * p_ref[h * n : (h + 1) * n, :]
        p_out[h] = p
        x_out[h] = x_ref[h] + alpha * p
        r = r - alpha * s
        r_out[h * n : (h + 1) * n, :] = r
        eps = eps + r * s

    def keep(h, value):
        a_out[h] = value

    operate(
        r_out, rs_out, eps, diag_ref, wcat_ref, wstore_ref, table_ref, mask_ref, cats_ref, same_ref,
        keep, sender(send_ref, n, 0), lambda line: put_rows(send_ref, n, horizon, line), values,
    )


def last_body(a_ref, got_ref, x_ref, r_ref, p_ref, s_ref, scal_ref, x_out, r_out):
    horizon, n, _ = a_ref.shape
    gamma, delta, eps = totals(got_ref, n, horizon)
    beta = gamma / scal_ref[0:1, :]
    alpha = gamma / (delta + 2.0 * beta * eps + beta * beta * scal_ref[1:2, :])
    for h in range(horizon):
        r = r_ref[h * n : (h + 1) * n, :]
        s = a_ref[h] + rows_of(got_ref, n, h) + beta * s_ref[h]
        x_out[h] = x_ref[h] + alpha * (r + beta * p_ref[h])
        r_out[h] = r - alpha * s


def on_device(
    base_bottom,
    weight_bottom,
    base_category,
    weight_category,
    base_region,
    weight_region,
    category_map,
    region_map,
):
    stores, horizon, skus = base_bottom.shape
    n = region_map.shape[0]
    groups = weight_category.shape[2] // WIDE
    tiles = weight_category.shape[2] // LANES
    field = (horizon, n, LANES)
    padded = (PAD * n, LANES)
    by_category = (horizon, tiles, LANES)
    scal = (2, LANES)
    values = pltpu.VMEM((groups * PAD, WIDE), jnp.float32)

    (sent,) = call(
        pack_body,
        [(n * horizon, LANES)],
        [pltpu.VMEM(field, jnp.float32), pltpu.SemaphoreType.DMA],
        (base_bottom.reshape(field),),
        [HBM],
    )
    got = exchange(sent, n)
    arguments = (
        base_bottom.reshape(field),
        weight_bottom.reshape(field),
        base_category.reshape(by_category),
        weight_category.reshape(by_category),
        jnp.transpose(base_region, (1, 0, 2)),
        jnp.transpose(weight_region, (1, 0, 2)),
        category_map.reshape(n, LANES),
        region_map.reshape(1, n),
    )
    held = [pltpu.VMEM(arguments[i].shape, arguments[i].dtype) for i in (2, 3, 4, 5, 7)]
    spread, wcat, wstore, bstore, same, table, mask, x, diag, cats = call(
        prepare_body,
        [
            field,
            (groups * PAD, WIDE),
            field,
            field,
            jax.ShapeDtypeStruct((n, n), jnp.bfloat16),
            jax.ShapeDtypeStruct((skus, WIDE), jnp.bfloat16),
            jax.ShapeDtypeStruct((groups * PAD, skus), jnp.bfloat16),
            field,
            field,
            jax.ShapeDtypeStruct((n, LANES), jnp.int32),
        ],
        [
            pltpu.VMEM(padded, jnp.float32),
            values,
            *held,
            pltpu.SemaphoreType.DMA((len(arguments),)),
        ],
        arguments,
        [HBM] * len(arguments),
        True,
    )
    (sent,) = call(
        region_start_body,
        [(n * 2 * horizon, LANES)],
        [],
        (got, spread, wstore, bstore, same),
    )
    got = exchange(sent, n)
    fixed = (diag, wcat, wstore, table, mask, cats, same)
    both = (n * (2 * horizon + 1), LANES)
    r, rs, sent = call(first_body, [padded, field, both], [values], (sent, got) + fixed)
    got = exchange(sent, n)
    p = r
    x, r, rs, s, ss, scalars, sent = call(
        second_body,
        [field, padded, field, field, field, scal, both],
        [values],
        (sent, got, x, r, rs) + fixed,
    )
    got = exchange(sent, n)
    x, r, p, s, scalars, a, sent = call(
        third_body,
        [field, padded, field, field, scal, field, (n * (horizon + 1), LANES)],
        [values, pltpu.VMEM(field, jnp.float32)],
        (sent, got, x, r, rs, p, s, ss, scalars) + fixed,
    )
    got = exchange(sent, n)
    x, r = call(last_body, [field, field], [], (a, got, x, r, p, s, scalars))
    return x.reshape(base_bottom.shape), r.reshape(base_bottom.shape)


def solution(mesh):
    in_specs = (
        P(("store", "sku"), None, None),
        P(("store", "sku"), None, None),
        P(("store", "sku"), None, None),
        P(("store", "sku"), None, None),
        P(None, None, ("store", "sku")),
        P(None, None, ("store", "sku")),
        P(),
        P(),
    )
    out_specs = (P(("store", "sku"), None, None), P(("store", "sku"), None, None))
    return jax.shard_map(
        on_device, mesh=mesh, in_specs=in_specs, out_specs=out_specs, check_vma=False
    )
```

```python
import jax
import jax.numpy as jnp
from jax import lax
from jax.experimental import pallas as pl
from jax.experimental.pallas import tpu as pltpu
from jax.sharding import PartitionSpec as P

LANES = 128
PAD = 16
WIDE = 256
VMEM = pl.BlockSpec(memory_space=pltpu.VMEM)
HBM = pl.BlockSpec(memory_space=pltpu.HBM)


def exchange(blocks, n):
    moved = lax.all_to_all(
        blocks.reshape(n, 1, -1), ("store", "sku"), split_axis=0, concat_axis=0, tiled=True
    )
    return moved.reshape(blocks.shape)


def call(body, outs, scratch, args, specs=None):
    outs = [
        out if isinstance(out, jax.ShapeDtypeStruct) else jax.ShapeDtypeStruct(out, jnp.float32)
        for out in outs
    ]
    specs = specs or [VMEM] * len(args)
    args = [
        pltpu.with_memory_space_constraint(arg, spec.memory_space) for arg, spec in zip(args, specs)
    ]
    return pl.pallas_call(
        body,
        out_shape=tuple(outs),
        in_specs=specs,
        out_specs=tuple(VMEM for _ in outs),
        scratch_shapes=scratch,
        compiler_params=pltpu.CompilerParams(vmem_limit_bytes=24 << 20),
    )(*args)


def split(value):
    high = value.astype(jnp.bfloat16)
    return high, (value - high.astype(jnp.float32)).astype(jnp.bfloat16)


def product(left, right, contract):
    return lax.dot_general(left, right, (contract, ((), ())), preferred_element_type=jnp.float32)


def rows_of(ref, n, h):
    return ref[pl.ds(h, n, stride=ref.shape[0] // n), :]


def put_rows(ref, n, h, value):
    ref[pl.ds(h, n, stride=ref.shape[0] // n), :] = value


def category_sums(field, table_ref, mask_ref, n):
    width = 4 if n % 4 == 0 else 1
    lanes = width * LANES
    rows = mask_ref.shape[0]

    def step(c, total):
        pieces = [field[pl.ds(c * width + i, PAD, stride=n), :] for i in range(width)]
        parts = split(jnp.concatenate(pieces, axis=1))
        start = pl.multiple_of(c * lanes, lanes)
        masks = mask_ref[:, pl.ds(start, lanes)]
        spread = jnp.concatenate(
            [part * masks[g : g + PAD] for part in parts for g in range(0, rows, PAD)], axis=0
        )
        return total + product(spread, table_ref[pl.ds(start, lanes), :], ((1,), (0,)))

    steps = n // width
    total = lax.fori_loop(
        0, steps, step, jnp.zeros((2 * rows, WIDE), jnp.float32), unroll=min(steps, 8)
    )
    return total[:rows] + total[rows:]


def category_spread(values, cats, h):
    place = cats % LANES
    group = cats // LANES
    found = []
    for g in range(0, values.shape[0], PAD):
        for lane in range(0, WIDE, LANES):
            row = jnp.broadcast_to(values[g + h : g + h + 1, lane : lane + LANES], cats.shape)
            found.append(jnp.take_along_axis(row, place, axis=1))
    bit = 1
    while len(found) > 1:
        odd = (group & bit) != 0
        pairs = [found[i : i + 2] for i in range(0, len(found), 2)]
        found = [jnp.where(odd, pair[1], pair[0]) if len(pair) == 2 else pair[0] for pair in pairs]
        bit *= 2
    return found[0]


def region_sums(load, same, n, horizon):
    high, low = split(jnp.concatenate([load(h) for h in range(horizon)], axis=1))
    total = product(same, high, ((1,), (0,))) + product(same, low, ((1,), (0,)))
    return [total[:, h * LANES : (h + 1) * LANES] for h in range(horizon)]


def pack_body(base_hbm, out_ref, base_ref, sem):
    copy = pltpu.make_async_copy(base_hbm, base_ref, sem)
    copy.start()
    copy.wait()
    n = base_ref.shape[1]
    for h in range(base_ref.shape[0]):
        put_rows(out_ref, n, h, base_ref[h])


def prepare_body(
    base_hbm, diag_hbm, base_cat_hbm, weight_cat_hbm, base_reg_hbm, weight_reg_hbm, cats_hbm, map_hbm,
    spread_out, wcat_out, wstore_out, bstore_out, same_out, table_out, mask_out,
    base_ref, diag_out, cats_ref,
    field, values, base_cat_ref, weight_cat_ref, base_reg_ref, weight_reg_ref, map_ref, sems,
):
    copies = [
        pltpu.make_async_copy(source, target, sems.at[i])
        for i, (source, target) in enumerate(
            (
                (cats_hbm, cats_ref),
                (base_hbm, base_ref),
                (weight_cat_hbm, weight_cat_ref),
                (base_cat_hbm, base_cat_ref),
                (map_hbm, map_ref),
                (weight_reg_hbm, weight_reg_ref),
                (base_reg_hbm, base_reg_ref),
                (diag_hbm, diag_out),
            )
        )
    ]
    for copy in copies:
        copy.start()
    for copy in copies:
        copy.wait()
    horizon, n, _ = base_ref.shape
    n_regions = weight_reg_ref.shape[1]
    square = jnp.concatenate([cats_ref[...].astype(jnp.float32)] * (LANES // min(n, LANES)), axis=0)
    labels = lax.broadcasted_iota(jnp.int32, (LANES, WIDE), 1)
    columns = [
        jnp.transpose(square[i : i + LANES]).astype(jnp.int32) % WIDE
        for i in range(0, square.shape[0], LANES)
    ]
    for j in range(n):
        column = jnp.broadcast_to(columns[j // LANES][:, j % LANES : j % LANES + 1], (LANES, WIDE))
        table_out[j * LANES : (j + 1) * LANES, :] = jnp.where(
            column == labels, 1.0, 0.0
        ).astype(jnp.bfloat16)
        group = jnp.broadcast_to(cats_ref[j : j + 1, :] // WIDE, (PAD, LANES))
        for g in range(0, mask_out.shape[0], PAD):
            mask_out[g : g + PAD, j * LANES : (j + 1) * LANES] = jnp.where(
                group == g // PAD, 1.0, 0.0
            ).astype(jnp.bfloat16)

    field[...] = jnp.zeros_like(field)
    for h in range(horizon):
        field[h * n : (h + 1) * n, :] = base_ref[h]
    sums = category_sums(field, table_out, mask_out, n)
    wcat_out[...] = jnp.zeros_like(wcat_out)
    values[...] = jnp.zeros_like(values)
    for g in range(0, wcat_out.shape[0], PAD):
        for lane in range(0, WIDE, LANES):
            tile = (g // PAD * WIDE + lane) // LANES
            lanes = slice(lane, lane + LANES)
            weight = weight_cat_ref[:, tile, :]
            wcat_out[g : g + horizon, lanes] = weight
            values[g : g + horizon, lanes] = weight * (
                base_cat_ref[:, tile, :] - sums[g : g + horizon, lanes]
            )
    cats = cats_ref[...]
    for h in range(horizon):
        spread_out[h] = category_spread(values, cats, h)

    labels = lax.broadcasted_iota(jnp.int32, (n_regions, n), 0)
    table = jnp.where(labels == map_ref[...], 1.0, 0.0).astype(jnp.bfloat16)
    same_out[...] = product(table, table, ((0,), (0,))).astype(jnp.bfloat16)
    for source, target in ((weight_reg_ref, wstore_out), (base_reg_ref, bstore_out)):
        for h in range(horizon):
            high, low = split(source[h])
            rest = source[h] - high.astype(jnp.float32) - low.astype(jnp.float32)
            target[h] = (
                product(table, high, ((0,), (0,)))
                + product(table, low, ((0,), (0,)))
                + product(table, rest.astype(jnp.bfloat16), ((0,), (0,)))
            )


def region_start_body(got_ref, spread_ref, wstore_ref, bstore_ref, same_ref, send_ref):
    horizon, n, _ = spread_ref.shape
    sums = region_sums(lambda h: rows_of(got_ref, n, h), same_ref[...], n, horizon)
    for h in range(horizon):
        put_rows(send_ref, n, h, spread_ref[h])
        put_rows(send_ref, n, horizon + h, wstore_ref[h] * (bstore_ref[h] - sums[h]))


def operate(r_ref, rs, eps, diag_ref, wcat_ref, wstore_ref, table_ref, mask_ref, cats_ref, same_ref, a_put, reg_put, sum_put, values):
    horizon, n, _ = diag_ref.shape
    gamma = jnp.zeros((n, LANES), jnp.float32)
    delta = jnp.zeros((n, LANES), jnp.float32)
    sums = region_sums(lambda h: rs[h], same_ref[...], n, horizon)
    for h in range(horizon):
        reg = wstore_ref[h] * sums[h]
        delta = delta + reg * rs[h]
        reg_put(h, reg)

    sums = category_sums(r_ref, table_ref, mask_ref, n)
    scaled = wcat_ref[...] * sums
    values[...] = scaled
    cats = cats_ref[...]
    for h in range(horizon):
        r = r_ref[h * n : (h + 1) * n, :]
        scaled_r = diag_ref[h] * r
        gamma = gamma + r * r
        delta = delta + scaled_r * r
        a_put(h, scaled_r + category_spread(values, cats, h))

    square = scaled * sums
    delta = jnp.sum(delta, axis=0, keepdims=True)
    for lane in range(0, WIDE, LANES):
        delta = delta + jnp.sum(square[:, lane : lane + LANES], axis=0, keepdims=True)
    lane = lax.broadcasted_iota(jnp.int32, (1, LANES), 1)
    line = jnp.zeros((1, LANES), jnp.float32)
    for i, part in enumerate((gamma, delta, eps)):
        if part is not None:
            whole = jnp.sum(jnp.sum(part, axis=0, keepdims=True), axis=1, keepdims=True)
            line = jnp.where(lane == i, whole, line)
    sum_put(jnp.broadcast_to(line, (n, LANES)))


def totals(got_ref, n, row):
    total = jnp.sum(rows_of(got_ref, n, row), axis=0, keepdims=True)
    total = jnp.broadcast_to(total, (8, LANES))
    return [
        jnp.take_along_axis(total, jnp.full((8, LANES), i, jnp.int32), axis=1)[0:1] for i in range(3)
    ]


def sender(ref, n, first):
    return lambda h, value: put_rows(ref, n, first + h, value)


def clear_tail(r_ref, horizon, n):
    r_ref[horizon * n :, :] = jnp.zeros((r_ref.shape[0] - horizon * n, LANES), jnp.float32)


def first_body(
    sent_ref, got_ref, diag_ref, wcat_ref, wstore_ref, table_ref, mask_ref, cats_ref, same_ref,
    r_ref, rs_ref, send_ref, values,
):
    horizon, n, _ = diag_ref.shape
    clear_tail(r_ref, horizon, n)
    for h in range(horizon):
        r_ref[h * n : (h + 1) * n, :] = rows_of(sent_ref, n, h) + rows_of(got_ref, n, horizon + h)
        rs_ref[h] = rows_of(got_ref, n, h) + rows_of(sent_ref, n, horizon + h)
    operate(
        r_ref, rs_ref, None, diag_ref, wcat_ref, wstore_ref, table_ref, mask_ref, cats_ref, same_ref,
        sender(send_ref, n, 0), sender(send_ref, n, horizon),
        lambda line: put_rows(send_ref, n, 2 * horizon, line), values,
    )


def second_body(
    sent_ref, got_ref, x_ref, r_ref, rs_ref, diag_ref, wcat_ref, wstore_ref, table_ref, mask_ref, cats_ref, same_ref,
    x_out, r_out, rs_out, s_out, ss_out, scal_ref, send_ref, values,
):
    horizon, n, _ = diag_ref.shape
    gamma, delta, _ = totals(got_ref, n, 2 * horizon)
    alpha = gamma / delta
    scal_ref[0:1, :] = gamma
    scal_ref[1:2, :] = delta
    clear_tail(r_out, horizon, n)
    eps = jnp.zeros((n, LANES), jnp.float32)
    for h in range(horizon):
        ws = rows_of(got_ref, n, h) + rows_of(sent_ref, n, horizon + h)
        ss_out[h] = ws
        rs_out[h] = rs_ref[h] - alpha * ws
        w = rows_of(sent_ref, n, h) + rows_of(got_ref, n, horizon + h)
        s_out[h] = w
        r = r_ref[h * n : (h + 1) * n, :]
        x_out[h] = x_ref[h] + alpha * r
        r = r - alpha * w
        r_out[h * n : (h + 1) * n, :] = r
        eps = eps + r * w
    operate(
        r_out, rs_out, eps, diag_ref, wcat_ref, wstore_ref, table_ref, mask_ref, cats_ref, same_ref,
        sender(send_ref, n, 0), sender(send_ref, n, horizon),
        lambda line: put_rows(send_ref, n, 2 * horizon, line), values,
    )


def third_body(
    sent_ref, got_ref, x_ref, r_ref, rs_ref, p_ref, s_ref, ss_ref, scal_ref,
    diag_ref, wcat_ref, wstore_ref, table_ref, mask_ref, cats_ref, same_ref,
    x_out, r_out, p_out, s_out, scal_out, a_out, send_ref, values, rs_out,
):
    horizon, n, _ = diag_ref.shape
    gamma, delta, eps = totals(got_ref, n, 2 * horizon)
    beta = gamma / scal_ref[0:1, :]
    curve = delta + 2.0 * beta * eps + beta * beta * scal_ref[1:2, :]
    alpha = gamma / curve
    scal_out[0:1, :] = gamma
    scal_out[1:2, :] = curve
    clear_tail(r_out, horizon, n)
    eps = jnp.zeros((n, LANES), jnp.float32)
    for h in range(horizon):
        ws = rows_of(got_ref, n, h) + rows_of(sent_ref, n, horizon + h)
        rs_out[h] = rs_ref[h] - alpha * (ws + beta * ss_ref[h])
        w = rows_of(sent_ref, n, h) + rows_of(got_ref, n, horizon + h)
        s = w + beta * s_ref[h]
        s_out[h] = s
        r = r_ref[h * n : (h + 1) * n, :]
        p = r + beta * p_ref[h * n : (h + 1) * n, :]
        p_out[h] = p
        x_out[h] = x_ref[h] + alpha * p
        r = r - alpha * s
        r_out[h * n : (h + 1) * n, :] = r
        eps = eps + r * s

    def keep(h, value):
        a_out[h] = value

    operate(
        r_out, rs_out, eps, diag_ref, wcat_ref, wstore_ref, table_ref, mask_ref, cats_ref, same_ref,
        keep, sender(send_ref, n, 0), lambda line: put_rows(send_ref, n, horizon, line), values,
    )


def last_body(a_ref, got_ref, x_ref, r_ref, p_ref, s_ref, scal_ref, x_out, r_out):
    horizon, n, _ = a_ref.shape
    gamma, delta, eps = totals(got_ref, n, horizon)
    beta = gamma / scal_ref[0:1, :]
    alpha = gamma / (delta + 2.0 * beta * eps + beta * beta * scal_ref[1:2, :])
    for h in range(horizon):
        r = r_ref[h * n : (h + 1) * n, :]
        s = a_ref[h] + rows_of(got_ref, n, h) + beta * s_ref[h]
        x_out[h] = x_ref[h] + alpha * (r + beta * p_ref[h])
        r_out[h] = r - alpha * s


def on_device(
    base_bottom,
    weight_bottom,
    base_category,
    weight_category,
    base_region,
    weight_region,
    category_map,
    region_map,
):
    stores, horizon, skus = base_bottom.shape
    n = region_map.shape[0]
    groups = weight_category.shape[2] // WIDE
    tiles = weight_category.shape[2] // LANES
    field = (horizon, n, LANES)
    padded = (PAD * n, LANES)
    by_category = (horizon, tiles, LANES)
    scal = (2, LANES)
    values = pltpu.VMEM((groups * PAD, WIDE), jnp.float32)

    (sent,) = call(
        pack_body,
        [(n * horizon, LANES)],
        [pltpu.VMEM(field, jnp.float32), pltpu.SemaphoreType.DMA],
        (base_bottom.reshape(field),),
        [HBM],
    )
    got = exchange(sent, n)
    arguments = (
        base_bottom.reshape(field),
        weight_bottom.reshape(field),
        base_category.reshape(by_category),
        weight_category.reshape(by_category),
        jnp.transpose(base_region, (1, 0, 2)),
        jnp.transpose(weight_region, (1, 0, 2)),
        category_map.reshape(n, LANES),
        region_map.reshape(1, n),
    )
    held = [pltpu.VMEM(arguments[i].shape, arguments[i].dtype) for i in (2, 3, 4, 5, 7)]
    spread, wcat, wstore, bstore, same, table, mask, x, diag, cats = call(
        prepare_body,
        [
            field,
            (groups * PAD, WIDE),
            field,
            field,
            jax.ShapeDtypeStruct((n, n), jnp.bfloat16),
            jax.ShapeDtypeStruct((skus, WIDE), jnp.bfloat16),
            jax.ShapeDtypeStruct((groups * PAD, skus), jnp.bfloat16),
            field,
            field,
            jax.ShapeDtypeStruct((n, LANES), jnp.int32),
        ],
        [
            pltpu.VMEM(padded, jnp.float32),
            values,
            *held,
            pltpu.SemaphoreType.DMA((len(arguments),)),
        ],
        arguments,
        [HBM] * len(arguments),
    )
    (sent,) = call(
        region_start_body,
        [(n * 2 * horizon, LANES)],
        [],
        (got, spread, wstore, bstore, same),
    )
    got = exchange(sent, n)
    fixed = (diag, wcat, wstore, table, mask, cats, same)
    both = (n * (2 * horizon + 1), LANES)
    r, rs, sent = call(first_body, [padded, field, both], [values], (sent, got) + fixed)
    got = exchange(sent, n)
    p = r
    x, r, rs, s, ss, scalars, sent = call(
        second_body,
        [field, padded, field, field, field, scal, both],
        [values],
        (sent, got, x, r, rs) + fixed,
    )
    got = exchange(sent, n)
    x, r, p, s, scalars, a, sent = call(
        third_body,
        [field, padded, field, field, scal, field, (n * (horizon + 1), LANES)],
        [values, pltpu.VMEM(field, jnp.float32)],
        (sent, got, x, r, rs, p, s, ss, scalars) + fixed,
    )
    got = exchange(sent, n)
    x, r = call(last_body, [field, field], [], (a, got, x, r, p, s, scalars))
    return x.reshape(base_bottom.shape), r.reshape(base_bottom.shape)


def solution(mesh):
    in_specs = (
        P(("store", "sku"), None, None),
        P(("store", "sku"), None, None),
        P(("store", "sku"), None, None),
        P(("store", "sku"), None, None),
        P(None, None, ("store", "sku")),
        P(None, None, ("store", "sku")),
        P(),
        P(),
    )
    out_specs = (P(("store", "sku"), None, None), P(("store", "sku"), None, None))
    return jax.shard_map(
        on_device, mesh=mesh, in_specs=in_specs, out_specs=out_specs, check_vma=False
    )
```

```python
import jax
import jax.numpy as jnp
from jax import lax
from jax.experimental import pallas as pl
from jax.experimental.pallas import tpu as pltpu
from jax.sharding import PartitionSpec as P

LANES = 128
PAD = 16
WIDE = 256
VMEM = pl.BlockSpec(memory_space=pltpu.VMEM)
HBM = pl.BlockSpec(memory_space=pltpu.HBM)


def exchange(blocks, n):
    moved = lax.all_to_all(
        blocks.reshape(n, 1, -1), ("store", "sku"), split_axis=0, concat_axis=0, tiled=True
    )
    return moved.reshape(blocks.shape)


def call(body, outs, scratch, args, specs=None):
    outs = [
        out if isinstance(out, jax.ShapeDtypeStruct) else jax.ShapeDtypeStruct(out, jnp.float32)
        for out in outs
    ]
    specs = specs or [VMEM] * len(args)
    args = [
        pltpu.with_memory_space_constraint(arg, spec.memory_space) for arg, spec in zip(args, specs)
    ]
    return pl.pallas_call(
        body,
        out_shape=tuple(outs),
        in_specs=specs,
        out_specs=tuple(VMEM for _ in outs),
        scratch_shapes=scratch,
        compiler_params=pltpu.CompilerParams(vmem_limit_bytes=24 << 20),
    )(*args)


def split(value):
    high = value.astype(jnp.bfloat16)
    return high, (value - high.astype(jnp.float32)).astype(jnp.bfloat16)


def product(left, right, contract):
    return lax.dot_general(left, right, (contract, ((), ())), preferred_element_type=jnp.float32)


def rows_of(ref, n, h):
    return ref[pl.ds(h, n, stride=ref.shape[0] // n), :]


def put_rows(ref, n, h, value):
    ref[pl.ds(h, n, stride=ref.shape[0] // n), :] = value


def category_sums(field, table_ref, mask_ref, n):
    width = 4 if n % 4 == 0 else 1
    lanes = width * LANES
    rows = mask_ref.shape[0]

    def step(c, total):
        pieces = [field[pl.ds(c * width + i, PAD, stride=n), :] for i in range(width)]
        parts = split(jnp.concatenate(pieces, axis=1))
        start = pl.multiple_of(c * lanes, lanes)
        masks = mask_ref[:, pl.ds(start, lanes)]
        spread = jnp.concatenate(
            [part * masks[g : g + PAD] for part in parts for g in range(0, rows, PAD)], axis=0
        )
        return total + product(spread, table_ref[pl.ds(start, lanes), :], ((1,), (0,)))

    steps = n // width
    total = lax.fori_loop(
        0, steps, step, jnp.zeros((2 * rows, WIDE), jnp.float32), unroll=min(steps, 8)
    )
    return total[:rows] + total[rows:]


def category_spread(values, cats, h):
    place = cats % LANES
    group = cats // LANES
    found = []
    for g in range(0, values.shape[0], PAD):
        for lane in range(0, WIDE, LANES):
            row = jnp.broadcast_to(values[g + h : g + h + 1, lane : lane + LANES], cats.shape)
            found.append(jnp.take_along_axis(row, place, axis=1))
    bit = 1
    while len(found) > 1:
        odd = (group & bit) != 0
        pairs = [found[i : i + 2] for i in range(0, len(found), 2)]
        found = [jnp.where(odd, pair[1], pair[0]) if len(pair) == 2 else pair[0] for pair in pairs]
        bit *= 2
    return found[0]


def region_sums(load, same, n, horizon):
    high, low = split(jnp.concatenate([load(h) for h in range(horizon)], axis=1))
    total = product(same, high, ((1,), (0,))) + product(same, low, ((1,), (0,)))
    return [total[:, h * LANES : (h + 1) * LANES] for h in range(horizon)]


def pack_body(base_hbm, out_ref, base_ref, sem):
    copy = pltpu.make_async_copy(base_hbm, base_ref, sem)
    copy.start()
    copy.wait()
    n = base_ref.shape[1]
    for h in range(base_ref.shape[0]):
        put_rows(out_ref, n, h, base_ref[h])


def prepare_body(
    base_hbm, base_cat_hbm, weight_cat_hbm, base_reg_hbm, weight_reg_hbm, cats_hbm, map_hbm,
    spread_out, wcat_out, wstore_out, bstore_out, same_out, table_out, mask_out,
    cats_ref,
    field, values, base_ref, base_cat_ref, weight_cat_ref, base_reg_ref, weight_reg_ref, map_ref, sems,
):
    copies = [
        pltpu.make_async_copy(source, target, sems.at[i])
        for i, (source, target) in enumerate(
            (
                (cats_hbm, cats_ref),
                (base_hbm, base_ref),
                (weight_cat_hbm, weight_cat_ref),
                (base_cat_hbm, base_cat_ref),
                (map_hbm, map_ref),
                (weight_reg_hbm, weight_reg_ref),
                (base_reg_hbm, base_reg_ref),
            )
        )
    ]
    for copy in copies:
        copy.start()
    for copy in copies:
        copy.wait()
    horizon, n, _ = base_ref.shape
    n_regions = weight_reg_ref.shape[1]
    square = jnp.concatenate([cats_ref[...].astype(jnp.float32)] * (LANES // min(n, LANES)), axis=0)
    labels = lax.broadcasted_iota(jnp.int32, (LANES, WIDE), 1)
    columns = [
        jnp.transpose(square[i : i + LANES]).astype(jnp.int32) % WIDE
        for i in range(0, square.shape[0], LANES)
    ]
    for j in range(n):
        column = jnp.broadcast_to(columns[j // LANES][:, j % LANES : j % LANES + 1], (LANES, WIDE))
        table_out[j * LANES : (j + 1) * LANES, :] = jnp.where(
            column == labels, 1.0, 0.0
        ).astype(jnp.bfloat16)
        group = jnp.broadcast_to(cats_ref[j : j + 1, :] // WIDE, (PAD, LANES))
        for g in range(0, mask_out.shape[0], PAD):
            mask_out[g : g + PAD, j * LANES : (j + 1) * LANES] = jnp.where(
                group == g // PAD, 1.0, 0.0
            ).astype(jnp.bfloat16)

    field[...] = jnp.zeros_like(field)
    for h in range(horizon):
        field[h * n : (h + 1) * n, :] = base_ref[h]
    sums = category_sums(field, table_out, mask_out, n)
    wcat_out[...] = jnp.zeros_like(wcat_out)
    values[...] = jnp.zeros_like(values)
    for g in range(0, wcat_out.shape[0], PAD):
        for lane in range(0, WIDE, LANES):
            tile = (g // PAD * WIDE + lane) // LANES
            lanes = slice(lane, lane + LANES)
            weight = weight_cat_ref[:, tile, :]
            wcat_out[g : g + horizon, lanes] = weight
            values[g : g + horizon, lanes] = weight * (
                base_cat_ref[:, tile, :] - sums[g : g + horizon, lanes]
            )
    cats = cats_ref[...]
    for h in range(horizon):
        spread_out[h] = category_spread(values, cats, h)

    labels = lax.broadcasted_iota(jnp.int32, (n_regions, n), 0)
    table = jnp.where(labels == map_ref[...], 1.0, 0.0).astype(jnp.bfloat16)
    same_out[...] = product(table, table, ((0,), (0,))).astype(jnp.bfloat16)
    for source, target in ((weight_reg_ref, wstore_out), (base_reg_ref, bstore_out)):
        for h in range(horizon):
            high, low = split(source[h])
            rest = source[h] - high.astype(jnp.float32) - low.astype(jnp.float32)
            target[h] = (
                product(table, high, ((0,), (0,)))
                + product(table, low, ((0,), (0,)))
                + product(table, rest.astype(jnp.bfloat16), ((0,), (0,)))
            )


def region_start_body(got_ref, spread_ref, wstore_ref, bstore_ref, same_ref, reg_out, send_ref):
    horizon, n, _ = spread_ref.shape
    sums = region_sums(lambda h: rows_of(got_ref, n, h), same_ref[...], n, horizon)
    for h in range(horizon):
        put_rows(send_ref, n, h, spread_ref[h])
        part = wstore_ref[h] * (bstore_ref[h] - sums[h])
        reg_out[h] = part
        put_rows(send_ref, n, horizon + h, part)


def operate(r_ref, rs, eps, diag_ref, wcat_ref, wstore_ref, table_ref, mask_ref, cats_ref, same_ref, a_put, reg_put, sum_put, values):
    horizon, n, _ = diag_ref.shape
    gamma = jnp.zeros((n, LANES), jnp.float32)
    delta = jnp.zeros((n, LANES), jnp.float32)
    sums = region_sums(lambda h: rs[h], same_ref[...], n, horizon)
    for h in range(horizon):
        reg = wstore_ref[h] * sums[h]
        delta = delta + reg * rs[h]
        reg_put(h, reg)

    sums = category_sums(r_ref, table_ref, mask_ref, n)
    scaled = wcat_ref[...] * sums
    values[...] = scaled
    cats = cats_ref[...]
    for h in range(horizon):
        r = r_ref[h * n : (h + 1) * n, :]
        scaled_r = diag_ref[h] * r
        gamma = gamma + r * r
        delta = delta + scaled_r * r
        a_put(h, scaled_r + category_spread(values, cats, h))

    square = scaled * sums
    delta = jnp.sum(delta, axis=0, keepdims=True)
    for lane in range(0, WIDE, LANES):
        delta = delta + jnp.sum(square[:, lane : lane + LANES], axis=0, keepdims=True)
    lane = lax.broadcasted_iota(jnp.int32, (1, LANES), 1)
    line = jnp.zeros((1, LANES), jnp.float32)
    for i, part in enumerate((gamma, delta, eps)):
        if part is not None:
            whole = jnp.sum(jnp.sum(part, axis=0, keepdims=True), axis=1, keepdims=True)
            line = jnp.where(lane == i, whole, line)
    sum_put(jnp.broadcast_to(line, (n, LANES)))


def totals(got_ref, n, row):
    total = jnp.sum(rows_of(got_ref, n, row), axis=0, keepdims=True)
    total = jnp.broadcast_to(total, (8, LANES))
    return [
        jnp.take_along_axis(total, jnp.full((8, LANES), i, jnp.int32), axis=1)[0:1] for i in range(3)
    ]


def sender(ref, n, first, keep):
    def put(h, value):
        keep[h] = value
        put_rows(ref, n, first + h, value)

    return put


def clear_tail(r_ref, horizon, n):
    r_ref[horizon * n :, :] = jnp.zeros((r_ref.shape[0] - horizon * n, LANES), jnp.float32)


def first_body(
    a_ref, reg_ref, got_ref, diag_ref, wcat_ref, wstore_ref, table_ref, mask_ref, cats_ref, same_ref,
    r_ref, rs_ref, a_out, reg_out, send_ref, values,
):
    horizon, n, _ = diag_ref.shape
    clear_tail(r_ref, horizon, n)
    for h in range(horizon):
        r_ref[h * n : (h + 1) * n, :] = a_ref[h] + rows_of(got_ref, n, horizon + h)
        rs_ref[h] = rows_of(got_ref, n, h) + reg_ref[h]
    operate(
        r_ref, rs_ref, None, diag_ref, wcat_ref, wstore_ref, table_ref, mask_ref, cats_ref, same_ref,
        sender(send_ref, n, 0, a_out), sender(send_ref, n, horizon, reg_out),
        lambda line: put_rows(send_ref, n, 2 * horizon, line), values,
    )


def second_body(
    a_ref, reg_ref, got_ref, x_ref, r_ref, rs_ref, diag_ref, wcat_ref, wstore_ref, table_ref, mask_ref, cats_ref, same_ref,
    x_out, r_out, rs_out, s_out, ss_out, scal_ref, a_out, reg_out, send_ref, values,
):
    horizon, n, _ = diag_ref.shape
    gamma, delta, _ = totals(got_ref, n, 2 * horizon)
    alpha = gamma / delta
    scal_ref[0:1, :] = gamma
    scal_ref[1:2, :] = delta
    clear_tail(r_out, horizon, n)
    eps = jnp.zeros((n, LANES), jnp.float32)
    for h in range(horizon):
        ws = rows_of(got_ref, n, h) + reg_ref[h]
        ss_out[h] = ws
        rs_out[h] = rs_ref[h] - alpha * ws
        w = a_ref[h] + rows_of(got_ref, n, horizon + h)
        s_out[h] = w
        r = r_ref[h * n : (h + 1) * n, :]
        x_out[h] = x_ref[h] + alpha * r
        r = r - alpha * w
        r_out[h * n : (h + 1) * n, :] = r
        eps = eps + r * w
    operate(
        r_out, rs_out, eps, diag_ref, wcat_ref, wstore_ref, table_ref, mask_ref, cats_ref, same_ref,
        sender(send_ref, n, 0, a_out), sender(send_ref, n, horizon, reg_out),
        lambda line: put_rows(send_ref, n, 2 * horizon, line), values,
    )


def third_body(
    a_ref, reg_ref, got_ref, x_ref, r_ref, rs_ref, p_ref, s_ref, ss_ref, scal_ref,
    diag_ref, wcat_ref, wstore_ref, table_ref, mask_ref, cats_ref, same_ref,
    x_out, r_out, p_out, s_out, scal_out, a_out, send_ref, values, rs_out,
):
    horizon, n, _ = diag_ref.shape
    gamma, delta, eps = totals(got_ref, n, 2 * horizon)
    beta = gamma / scal_ref[0:1, :]
    curve = delta + 2.0 * beta * eps + beta * beta * scal_ref[1:2, :]
    alpha = gamma / curve
    scal_out[0:1, :] = gamma
    scal_out[1:2, :] = curve
    clear_tail(r_out, horizon, n)
    eps = jnp.zeros((n, LANES), jnp.float32)
    for h in range(horizon):
        ws = rows_of(got_ref, n, h) + reg_ref[h]
        rs_out[h] = rs_ref[h] - alpha * (ws + beta * ss_ref[h])
        w = a_ref[h] + rows_of(got_ref, n, horizon + h)
        s = w + beta * s_ref[h]
        s_out[h] = s
        r = r_ref[h * n : (h + 1) * n, :]
        p = r + beta * p_ref[h * n : (h + 1) * n, :]
        p_out[h] = p
        x_out[h] = x_ref[h] + alpha * p
        r = r - alpha * s
        r_out[h * n : (h + 1) * n, :] = r
        eps = eps + r * s

    def keep(h, value):
        a_out[h] = value

    operate(
        r_out, rs_out, eps, diag_ref, wcat_ref, wstore_ref, table_ref, mask_ref, cats_ref, same_ref,
        keep, lambda h, value: put_rows(send_ref, n, h, value),
        lambda line: put_rows(send_ref, n, horizon, line), values,
    )


def last_body(a_ref, got_ref, x_ref, r_ref, p_ref, s_ref, scal_ref, x_out, r_out):
    horizon, n, _ = a_ref.shape
    gamma, delta, eps = totals(got_ref, n, horizon)
    beta = gamma / scal_ref[0:1, :]
    alpha = gamma / (delta + 2.0 * beta * eps + beta * beta * scal_ref[1:2, :])
    for h in range(horizon):
        r = r_ref[h * n : (h + 1) * n, :]
        s = a_ref[h] + rows_of(got_ref, n, h) + beta * s_ref[h]
        x_out[h] = x_ref[h] + alpha * (r + beta * p_ref[h])
        r_out[h] = r - alpha * s


def on_device(
    base_bottom,
    weight_bottom,
    base_category,
    weight_category,
    base_region,
    weight_region,
    category_map,
    region_map,
):
    stores, horizon, skus = base_bottom.shape
    n = region_map.shape[0]
    groups = weight_category.shape[2] // WIDE
    tiles = weight_category.shape[2] // LANES
    field = (horizon, n, LANES)
    padded = (PAD * n, LANES)
    by_category = (horizon, tiles, LANES)
    scal = (2, LANES)
    values = pltpu.VMEM((groups * PAD, WIDE), jnp.float32)

    x = base_bottom.reshape(field)
    diag = weight_bottom.reshape(field)
    (sent,) = call(
        pack_body,
        [(n * horizon, LANES)],
        [pltpu.VMEM(field, jnp.float32), pltpu.SemaphoreType.DMA],
        (x,),
        [HBM],
    )
    got = exchange(sent, n)
    arguments = (
        x,
        base_category.reshape(by_category),
        weight_category.reshape(by_category),
        jnp.transpose(base_region, (1, 0, 2)),
        jnp.transpose(weight_region, (1, 0, 2)),
        category_map.reshape(n, LANES),
        region_map.reshape(1, n),
    )
    held = [pltpu.VMEM(arguments[i].shape, arguments[i].dtype) for i in (0, 1, 2, 3, 4, 6)]
    spread, wcat, wstore, bstore, same, table, mask, cats = call(
        prepare_body,
        [
            field,
            (groups * PAD, WIDE),
            field,
            field,
            jax.ShapeDtypeStruct((n, n), jnp.bfloat16),
            jax.ShapeDtypeStruct((skus, WIDE), jnp.bfloat16),
            jax.ShapeDtypeStruct((groups * PAD, skus), jnp.bfloat16),
            jax.ShapeDtypeStruct((n, LANES), jnp.int32),
        ],
        [
            pltpu.VMEM(padded, jnp.float32),
            values,
            *held,
            pltpu.SemaphoreType.DMA((len(arguments),)),
        ],
        arguments,
        [HBM] * len(arguments),
    )
    reg, sent = call(
        region_start_body,
        [field, (n * 2 * horizon, LANES)],
        [],
        (got, spread, wstore, bstore, same),
    )
    got = exchange(sent, n)
    fixed = (diag, wcat, wstore, table, mask, cats, same)
    both = (n * (2 * horizon + 1), LANES)
    r, rs, a, reg, sent = call(
        first_body, [padded, field, field, field, both], [values], (spread, reg, got) + fixed
    )
    got = exchange(sent, n)
    p = r
    x, r, rs, s, ss, scalars, a, reg, sent = call(
        second_body,
        [field, padded, field, field, field, scal, field, field, both],
        [values],
        (a, reg, got, x, r, rs) + fixed,
    )
    got = exchange(sent, n)
    x, r, p, s, scalars, a, sent = call(
        third_body,
        [field, padded, field, field, scal, field, (n * (horizon + 1), LANES)],
        [values, pltpu.VMEM(field, jnp.float32)],
        (a, reg, got, x, r, rs, p, s, ss, scalars) + fixed,
    )
    got = exchange(sent, n)
    x, r = call(last_body, [field, field], [], (a, got, x, r, p, s, scalars))
    return x.reshape(base_bottom.shape), r.reshape(base_bottom.shape)


def solution(mesh):
    in_specs = (
        P(("store", "sku"), None, None),
        P(("store", "sku"), None, None),
        P(("store", "sku"), None, None),
        P(("store", "sku"), None, None),
        P(None, None, ("store", "sku")),
        P(None, None, ("store", "sku")),
        P(),
        P(),
    )
    out_specs = (P(("store", "sku"), None, None), P(("store", "sku"), None, None))
    return jax.shard_map(
        on_device, mesh=mesh, in_specs=in_specs, out_specs=out_specs, check_vma=False
    )
```

```python
import jax
import jax.numpy as jnp
from jax import lax
from jax.experimental import pallas as pl
from jax.experimental.pallas import tpu as pltpu
from jax.sharding import PartitionSpec as P

LANES = 128
PAD = 16
WIDE = 256
VMEM = pl.BlockSpec(memory_space=pltpu.VMEM)
HBM = pl.BlockSpec(memory_space=pltpu.HBM)


def exchange(blocks, n):
    moved = lax.all_to_all(
        blocks.reshape(n, 1, -1), ("store", "sku"), split_axis=0, concat_axis=0, tiled=True
    )
    return moved.reshape(blocks.shape)


def call(body, outs, scratch, args, specs=None, held=False):
    outs = [
        out if isinstance(out, jax.ShapeDtypeStruct) else jax.ShapeDtypeStruct(out, jnp.float32)
        for out in outs
    ]
    specs = specs or [VMEM] * len(args)
    args = [
        pltpu.with_memory_space_constraint(arg, spec.memory_space) for arg, spec in zip(args, specs)
    ]
    return pl.pallas_call(
        body,
        out_shape=tuple(pltpu.VMEM(out.shape, out.dtype) if held else out for out in outs),
        in_specs=specs,
        out_specs=tuple(VMEM for _ in outs),
        scratch_shapes=scratch,
        compiler_params=pltpu.CompilerParams(vmem_limit_bytes=24 << 20),
    )(*args)


def split(value):
    high = value.astype(jnp.bfloat16)
    return high, (value - high.astype(jnp.float32)).astype(jnp.bfloat16)


def product(left, right, contract):
    return lax.dot_general(left, right, (contract, ((), ())), preferred_element_type=jnp.float32)


def rows_of(ref, n, h):
    return ref[pl.ds(h, n, stride=ref.shape[0] // n), :]


def put_rows(ref, n, h, value):
    ref[pl.ds(h, n, stride=ref.shape[0] // n), :] = value


def category_sums(field, table_ref, group_ref, n, rows):
    width = 4 if n % 4 == 0 else 1
    lanes = width * LANES

    def step(c, total):
        pieces = [field[pl.ds(c * width + i, PAD, stride=n), :] for i in range(width)]
        parts = split(jnp.concatenate(pieces, axis=1))
        start = pl.multiple_of(c * lanes, lanes)
        group = group_ref[:, pl.ds(start, lanes)]
        masks = [group == g for g in range(rows // PAD)]
        none = jnp.zeros((PAD, lanes), jnp.bfloat16)
        spread = jnp.concatenate(
            [jnp.where(mask, part, none) for part in parts for mask in masks], axis=0
        )
        return total + product(spread, table_ref[pl.ds(start, lanes), :], ((1,), (0,)))

    steps = n // width
    total = lax.fori_loop(
        0, steps, step, jnp.zeros((2 * rows, WIDE), jnp.float32), unroll=min(steps, 8)
    )
    return total[:rows] + total[rows:]


def category_spread(values, cats, h):
    place = cats % LANES
    group = cats // LANES
    found = []
    for g in range(0, values.shape[0], PAD):
        for lane in range(0, WIDE, LANES):
            row = jnp.broadcast_to(values[g + h : g + h + 1, lane : lane + LANES], cats.shape)
            found.append(jnp.take_along_axis(row, place, axis=1))
    bit = 1
    while len(found) > 1:
        odd = (group & bit) != 0
        pairs = [found[i : i + 2] for i in range(0, len(found), 2)]
        found = [jnp.where(odd, pair[1], pair[0]) if len(pair) == 2 else pair[0] for pair in pairs]
        bit *= 2
    return found[0]


def region_sums(load, same, n, horizon):
    high, low = split(jnp.concatenate([load(h) for h in range(horizon)], axis=1))
    total = product(same, high, ((1,), (0,))) + product(same, low, ((1,), (0,)))
    return [total[:, h * LANES : (h + 1) * LANES] for h in range(horizon)]


def pack_body(base_hbm, out_ref, base_ref, sem):
    copy = pltpu.make_async_copy(base_hbm, base_ref, sem)
    copy.start()
    copy.wait()
    n = base_ref.shape[1]
    for h in range(base_ref.shape[0]):
        put_rows(out_ref, n, h, base_ref[h])


def prepare_body(
    base_hbm, base_cat_hbm, weight_cat_hbm, base_reg_hbm, weight_reg_hbm, cats_hbm, map_hbm,
    spread_out, wcat_out, wstore_out, bstore_out, same_out, table_out, group_out,
    cats_ref,
    field, values, base_ref, base_cat_ref, weight_cat_ref, base_reg_ref, weight_reg_ref, map_ref, sems,
):
    copies = [
        pltpu.make_async_copy(source, target, sems.at[i])
        for i, (source, target) in enumerate(
            (
                (cats_hbm, cats_ref),
                (base_hbm, base_ref),
                (weight_cat_hbm, weight_cat_ref),
                (base_cat_hbm, base_cat_ref),
                (map_hbm, map_ref),
                (weight_reg_hbm, weight_reg_ref),
                (base_reg_hbm, base_reg_ref),
            )
        )
    ]
    for copy in copies:
        copy.start()
    for copy in copies:
        copy.wait()
    horizon, n, _ = base_ref.shape
    n_regions = weight_reg_ref.shape[1]
    square = jnp.concatenate([cats_ref[...].astype(jnp.float32)] * (LANES // min(n, LANES)), axis=0)
    labels = lax.broadcasted_iota(jnp.int32, (LANES, WIDE), 1)
    columns = [
        jnp.transpose(square[i : i + LANES]).astype(jnp.int32) % WIDE
        for i in range(0, square.shape[0], LANES)
    ]
    for j in range(n):
        column = jnp.broadcast_to(columns[j // LANES][:, j % LANES : j % LANES + 1], (LANES, WIDE))
        table_out[j * LANES : (j + 1) * LANES, :] = jnp.where(
            column == labels, 1.0, 0.0
        ).astype(jnp.bfloat16)
        group = jnp.broadcast_to(cats_ref[j : j + 1, :] // WIDE, (PAD, LANES))
        group_out[:, j * LANES : (j + 1) * LANES] = group.astype(jnp.float32).astype(jnp.bfloat16)

    field[...] = jnp.zeros_like(field)
    for h in range(horizon):
        field[h * n : (h + 1) * n, :] = base_ref[h]
    sums = category_sums(field, table_out, group_out, n, wcat_out.shape[0])
    wcat_out[...] = jnp.zeros_like(wcat_out)
    values[...] = jnp.zeros_like(values)
    for g in range(0, wcat_out.shape[0], PAD):
        for lane in range(0, WIDE, LANES):
            tile = (g // PAD * WIDE + lane) // LANES
            lanes = slice(lane, lane + LANES)
            weight = weight_cat_ref[:, tile, :]
            wcat_out[g : g + horizon, lanes] = weight
            values[g : g + horizon, lanes] = weight * (
                base_cat_ref[:, tile, :] - sums[g : g + horizon, lanes]
            )
    cats = cats_ref[...]
    for h in range(horizon):
        spread_out[h] = category_spread(values, cats, h)

    labels = lax.broadcasted_iota(jnp.int32, (n_regions, n), 0)
    table = jnp.where(labels == map_ref[...], 1.0, 0.0).astype(jnp.bfloat16)
    same_out[...] = product(table, table, ((0,), (0,))).astype(jnp.bfloat16)
    for source, target in ((weight_reg_ref, wstore_out), (base_reg_ref, bstore_out)):
        for h in range(horizon):
            high, low = split(source[h])
            rest = source[h] - high.astype(jnp.float32) - low.astype(jnp.float32)
            target[h] = (
                product(table, high, ((0,), (0,)))
                + product(table, low, ((0,), (0,)))
                + product(table, rest.astype(jnp.bfloat16), ((0,), (0,)))
            )


def region_start_body(got_ref, spread_ref, wstore_ref, bstore_ref, same_ref, reg_out, send_ref):
    horizon, n, _ = spread_ref.shape
    sums = region_sums(lambda h: rows_of(got_ref, n, h), same_ref[...], n, horizon)
    for h in range(horizon):
        put_rows(send_ref, n, h, spread_ref[h])
        part = wstore_ref[h] * (bstore_ref[h] - sums[h])
        reg_out[h] = part
        put_rows(send_ref, n, horizon + h, part)


def operate(r_ref, rs, eps, diag_ref, wcat_ref, wstore_ref, table_ref, group_ref, cats_ref, same_ref, a_put, reg_put, sum_put, values):
    horizon, n, _ = diag_ref.shape
    gamma = jnp.zeros((n, LANES), jnp.float32)
    delta = jnp.zeros((n, LANES), jnp.float32)
    sums = region_sums(lambda h: rs[h], same_ref[...], n, horizon)
    for h in range(horizon):
        reg = wstore_ref[h] * sums[h]
        delta = delta + reg * rs[h]
        reg_put(h, reg)

    sums = category_sums(r_ref, table_ref, group_ref, n, wcat_ref.shape[0])
    scaled = wcat_ref[...] * sums
    values[...] = scaled
    cats = cats_ref[...]
    for h in range(horizon):
        r = r_ref[h * n : (h + 1) * n, :]
        scaled_r = diag_ref[h] * r
        gamma = gamma + r * r
        delta = delta + scaled_r * r
        a_put(h, scaled_r + category_spread(values, cats, h))

    square = scaled * sums
    delta = jnp.sum(delta, axis=0, keepdims=True)
    for lane in range(0, WIDE, LANES):
        delta = delta + jnp.sum(square[:, lane : lane + LANES], axis=0, keepdims=True)
    lane = lax.broadcasted_iota(jnp.int32, (1, LANES), 1)
    line = jnp.zeros((1, LANES), jnp.float32)
    for i, part in enumerate((gamma, delta, eps)):
        if part is not None:
            whole = jnp.sum(jnp.sum(part, axis=0, keepdims=True), axis=1, keepdims=True)
            line = jnp.where(lane == i, whole, line)
    sum_put(jnp.broadcast_to(line, (n, LANES)))


def totals(got_ref, n, row):
    total = jnp.sum(rows_of(got_ref, n, row), axis=0, keepdims=True)
    total = jnp.broadcast_to(total, (8, LANES))
    return [
        jnp.take_along_axis(total, jnp.full((8, LANES), i, jnp.int32), axis=1)[0:1] for i in range(3)
    ]


def sender(ref, n, first, keep):
    def put(h, value):
        keep[h] = value
        put_rows(ref, n, first + h, value)

    return put


def clear_tail(r_ref, horizon, n):
    r_ref[horizon * n :, :] = jnp.zeros((r_ref.shape[0] - horizon * n, LANES), jnp.float32)


def first_body(
    a_ref, reg_ref, got_ref, diag_ref, wcat_ref, wstore_ref, table_ref, group_ref, cats_ref, same_ref,
    r_ref, rs_ref, a_out, reg_out, send_ref, values,
):
    horizon, n, _ = diag_ref.shape
    clear_tail(r_ref, horizon, n)
    for h in range(horizon):
        r_ref[h * n : (h + 1) * n, :] = a_ref[h] + rows_of(got_ref, n, horizon + h)
        rs_ref[h] = rows_of(got_ref, n, h) + reg_ref[h]
    operate(
        r_ref, rs_ref, None, diag_ref, wcat_ref, wstore_ref, table_ref, group_ref, cats_ref, same_ref,
        sender(send_ref, n, 0, a_out), sender(send_ref, n, horizon, reg_out),
        lambda line: put_rows(send_ref, n, 2 * horizon, line), values,
    )


def second_body(
    a_ref, reg_ref, got_ref, x_ref, r_ref, rs_ref, diag_ref, wcat_ref, wstore_ref, table_ref, group_ref, cats_ref, same_ref,
    x_out, r_out, rs_out, s_out, ss_out, scal_ref, a_out, reg_out, send_ref, values,
):
    horizon, n, _ = diag_ref.shape
    gamma, delta, _ = totals(got_ref, n, 2 * horizon)
    alpha = gamma / delta
    scal_ref[0:1, :] = gamma
    scal_ref[1:2, :] = delta
    clear_tail(r_out, horizon, n)
    eps = jnp.zeros((n, LANES), jnp.float32)
    for h in range(horizon):
        ws = rows_of(got_ref, n, h) + reg_ref[h]
        ss_out[h] = ws
        rs_out[h] = rs_ref[h] - alpha * ws
        w = a_ref[h] + rows_of(got_ref, n, horizon + h)
        s_out[h] = w
        r = r_ref[h * n : (h + 1) * n, :]
        x_out[h] = x_ref[h] + alpha * r
        r = r - alpha * w
        r_out[h * n : (h + 1) * n, :] = r
        eps = eps + r * w
    operate(
        r_out, rs_out, eps, diag_ref, wcat_ref, wstore_ref, table_ref, group_ref, cats_ref, same_ref,
        sender(send_ref, n, 0, a_out), sender(send_ref, n, horizon, reg_out),
        lambda line: put_rows(send_ref, n, 2 * horizon, line), values,
    )


def third_body(
    a_ref, reg_ref, got_ref, x_ref, r_ref, rs_ref, p_ref, s_ref, ss_ref, scal_ref,
    diag_ref, wcat_ref, wstore_ref, table_ref, group_ref, cats_ref, same_ref,
    x_out, r_out, p_out, s_out, scal_out, a_out, send_ref, values, rs_out,
):
    horizon, n, _ = diag_ref.shape
    gamma, delta, eps = totals(got_ref, n, 2 * horizon)
    beta = gamma / scal_ref[0:1, :]
    curve = delta + 2.0 * beta * eps + beta * beta * scal_ref[1:2, :]
    alpha = gamma / curve
    scal_out[0:1, :] = gamma
    scal_out[1:2, :] = curve
    clear_tail(r_out, horizon, n)
    eps = jnp.zeros((n, LANES), jnp.float32)
    for h in range(horizon):
        ws = rows_of(got_ref, n, h) + reg_ref[h]
        rs_out[h] = rs_ref[h] - alpha * (ws + beta * ss_ref[h])
        w = a_ref[h] + rows_of(got_ref, n, horizon + h)
        s = w + beta * s_ref[h]
        s_out[h] = s
        r = r_ref[h * n : (h + 1) * n, :]
        p = r + beta * p_ref[h * n : (h + 1) * n, :]
        p_out[h] = p
        x_out[h] = x_ref[h] + alpha * p
        r = r - alpha * s
        r_out[h * n : (h + 1) * n, :] = r
        eps = eps + r * s

    def keep(h, value):
        a_out[h] = value

    operate(
        r_out, rs_out, eps, diag_ref, wcat_ref, wstore_ref, table_ref, group_ref, cats_ref, same_ref,
        keep, lambda h, value: put_rows(send_ref, n, h, value),
        lambda line: put_rows(send_ref, n, horizon, line), values,
    )


def last_body(a_ref, got_ref, x_ref, r_ref, p_ref, s_ref, scal_ref, x_out, r_out):
    horizon, n, _ = a_ref.shape
    gamma, delta, eps = totals(got_ref, n, horizon)
    beta = gamma / scal_ref[0:1, :]
    alpha = gamma / (delta + 2.0 * beta * eps + beta * beta * scal_ref[1:2, :])
    for h in range(horizon):
        r = r_ref[h * n : (h + 1) * n, :]
        s = a_ref[h] + rows_of(got_ref, n, h) + beta * s_ref[h]
        x_out[h] = x_ref[h] + alpha * (r + beta * p_ref[h])
        r_out[h] = r - alpha * s


def on_device(
    base_bottom,
    weight_bottom,
    base_category,
    weight_category,
    base_region,
    weight_region,
    category_map,
    region_map,
):
    stores, horizon, skus = base_bottom.shape
    n = region_map.shape[0]
    groups = weight_category.shape[2] // WIDE
    tiles = weight_category.shape[2] // LANES
    field = (horizon, n, LANES)
    padded = (PAD * n, LANES)
    by_category = (horizon, tiles, LANES)
    scal = (2, LANES)
    values = pltpu.VMEM((groups * PAD, WIDE), jnp.float32)

    x = base_bottom.reshape(field)
    diag = weight_bottom.reshape(field)
    (sent,) = call(
        pack_body,
        [(n * horizon, LANES)],
        [pltpu.VMEM(field, jnp.float32), pltpu.SemaphoreType.DMA],
        (x,),
        [HBM],
        True,
    )
    got = exchange(sent, n)
    arguments = (
        x,
        base_category.reshape(by_category),
        weight_category.reshape(by_category),
        jnp.transpose(base_region, (1, 0, 2)),
        jnp.transpose(weight_region, (1, 0, 2)),
        category_map.reshape(n, LANES),
        region_map.reshape(1, n),
    )
    held = [pltpu.VMEM(arguments[i].shape, arguments[i].dtype) for i in (0, 1, 2, 3, 4, 6)]
    spread, wcat, wstore, bstore, same, table, group, cats = call(
        prepare_body,
        [
            field,
            (groups * PAD, WIDE),
            field,
            field,
            jax.ShapeDtypeStruct((n, n), jnp.bfloat16),
            jax.ShapeDtypeStruct((skus, WIDE), jnp.bfloat16),
            jax.ShapeDtypeStruct((PAD, skus), jnp.bfloat16),
            jax.ShapeDtypeStruct((n, LANES), jnp.int32),
        ],
        [
            pltpu.VMEM(padded, jnp.float32),
            values,
            *held,
            pltpu.SemaphoreType.DMA((len(arguments),)),
        ],
        arguments,
        [HBM] * len(arguments),
    )
    reg, sent = call(
        region_start_body,
        [field, (n * 2 * horizon, LANES)],
        [],
        (got, spread, wstore, bstore, same),
    )
    got = exchange(sent, n)
    fixed = (diag, wcat, wstore, table, group, cats, same)
    both = (n * (2 * horizon + 1), LANES)
    r, rs, a, reg, sent = call(
        first_body, [padded, field, field, field, both], [values], (spread, reg, got) + fixed
    )
    got = exchange(sent, n)
    p = r
    x, r, rs, s, ss, scalars, a, reg, sent = call(
        second_body,
        [field, padded, field, field, field, scal, field, field, both],
        [values],
        (a, reg, got, x, r, rs) + fixed,
    )
    got = exchange(sent, n)
    x, r, p, s, scalars, a, sent = call(
        third_body,
        [field, padded, field, field, scal, field, (n * (horizon + 1), LANES)],
        [values, pltpu.VMEM(field, jnp.float32)],
        (a, reg, got, x, r, rs, p, s, ss, scalars) + fixed,
    )
    got = exchange(sent, n)
    x, r = call(last_body, [field, field], [], (a, got, x, r, p, s, scalars))
    return x.reshape(base_bottom.shape), r.reshape(base_bottom.shape)


def solution(mesh):
    in_specs = (
        P(("store", "sku"), None, None),
        P(("store", "sku"), None, None),
        P(("store", "sku"), None, None),
        P(("store", "sku"), None, None),
        P(None, None, ("store", "sku")),
        P(None, None, ("store", "sku")),
        P(),
        P(),
    )
    out_specs = (P(("store", "sku"), None, None), P(("store", "sku"), None, None))
    return jax.shard_map(
        on_device, mesh=mesh, in_specs=in_specs, out_specs=out_specs, check_vma=False
    )
```

```python
import jax
import jax.numpy as jnp
from jax import lax
from jax.experimental import pallas as pl
from jax.experimental.pallas import tpu as pltpu
from jax.sharding import PartitionSpec as P

LANES = 128
PAD = 16
WIDE = 256
VMEM = pl.BlockSpec(memory_space=pltpu.VMEM)
HBM = pl.BlockSpec(memory_space=pltpu.HBM)


def exchange(blocks, n):
    moved = lax.all_to_all(
        blocks.reshape(n, 1, -1), ("store", "sku"), split_axis=0, concat_axis=0, tiled=True
    )
    return moved.reshape(blocks.shape)


def call(body, outs, scratch, args, specs=None, held=False):
    outs = [
        out if isinstance(out, jax.ShapeDtypeStruct) else jax.ShapeDtypeStruct(out, jnp.float32)
        for out in outs
    ]
    specs = specs or [VMEM] * len(args)
    args = [
        pltpu.with_memory_space_constraint(arg, spec.memory_space) for arg, spec in zip(args, specs)
    ]
    return pl.pallas_call(
        body,
        out_shape=tuple(pltpu.VMEM(out.shape, out.dtype) if held else out for out in outs),
        in_specs=specs,
        out_specs=tuple(VMEM for _ in outs),
        scratch_shapes=scratch,
        compiler_params=pltpu.CompilerParams(vmem_limit_bytes=24 << 20),
    )(*args)


def split(value):
    high = value.astype(jnp.bfloat16)
    return high, (value - high.astype(jnp.float32)).astype(jnp.bfloat16)


def split_all(value):
    high, low = split(value)
    rest = value - high.astype(jnp.float32) - low.astype(jnp.float32)
    return high, low, rest.astype(jnp.bfloat16)


def product(left, right, contract):
    return lax.dot_general(left, right, (contract, ((), ())), preferred_element_type=jnp.float32)


def rows_of(ref, n, h):
    return ref[pl.ds(h, n, stride=ref.shape[0] // n), :]


def put_rows(ref, n, h, value):
    ref[pl.ds(h, n, stride=ref.shape[0] // n), :] = value


def category_sums(field, table_ref, group_ref, n, rows):
    width = 4 if n % 4 == 0 else 1
    lanes = width * LANES

    def step(c, total):
        pieces = [field[pl.ds(c * width + i, PAD, stride=n), :] for i in range(width)]
        parts = split_all(jnp.concatenate(pieces, axis=1))
        start = pl.multiple_of(c * lanes, lanes)
        group = group_ref[:, pl.ds(start, lanes)]
        masks = [group == g for g in range(rows // PAD)]
        none = jnp.zeros((PAD, lanes), jnp.bfloat16)
        spread = jnp.concatenate(
            [jnp.where(mask, part, none) for part in parts for mask in masks], axis=0
        )
        return total + product(spread, table_ref[pl.ds(start, lanes), :], ((1,), (0,)))

    steps = n // width
    total = lax.fori_loop(
        0, steps, step, jnp.zeros((3 * rows, WIDE), jnp.float32), unroll=min(steps, 8)
    )
    return total[:rows] + (total[rows : 2 * rows] + total[2 * rows :])


def category_spread(values, cats, horizon, put):
    place = cats % LANES
    group = cats // LANES
    odd = [(group >> bit) & 1 != 0 for bit in range(3)]
    for h in range(horizon):
        found = []
        for g in range(0, values.shape[0], PAD):
            for lane in range(0, WIDE, LANES):
                row = jnp.broadcast_to(values[g + h : g + h + 1, lane : lane + LANES], cats.shape)
                found.append(jnp.take_along_axis(row, place, axis=1))
        for bit in range((len(found) - 1).bit_length()):
            mask = odd[bit] if bit < 3 else (group >> bit) & 1 != 0
            pairs = [found[i : i + 2] for i in range(0, len(found), 2)]
            found = [jnp.where(mask, pair[1], pair[0]) if len(pair) == 2 else pair[0] for pair in pairs]
        put(h, found[0])


def tiles_of(n):
    return [slice(t, t + 8) for t in range(0, n, 8)]


def put_tile(ref, n, h, tile, value):
    rows = ref.shape[0] // n
    ref[pl.ds(tile.start * rows + h, 8, stride=rows), :] = value


def region_sums(load, same, n, horizon):
    high, low = split(jnp.concatenate([load(h) for h in range(horizon)], axis=1))
    total = product(same, high, ((1,), (0,))) + product(same, low, ((1,), (0,)))
    return [total[:, h * LANES : (h + 1) * LANES] for h in range(horizon)]


def pack_body(base_hbm, out_ref, base_ref, sem):
    copy = pltpu.make_async_copy(base_hbm, base_ref, sem)
    copy.start()
    copy.wait()
    n = base_ref.shape[1]
    for h in range(base_ref.shape[0]):
        put_rows(out_ref, n, h, base_ref[h])


def prepare_body(
    base_hbm, base_cat_hbm, weight_cat_hbm, base_reg_hbm, weight_reg_hbm, cats_hbm, map_hbm,
    spread_out, wcat_out, wstore_out, bstore_out, same_out, table_out, group_out,
    cats_ref,
    field, values, base_ref, base_cat_ref, weight_cat_ref, base_reg_ref, weight_reg_ref, map_ref, sems,
):
    copies = [
        pltpu.make_async_copy(source, target, sems.at[i])
        for i, (source, target) in enumerate(
            (
                (cats_hbm, cats_ref),
                (base_hbm, base_ref),
                (weight_cat_hbm, weight_cat_ref),
                (base_cat_hbm, base_cat_ref),
                (map_hbm, map_ref),
                (weight_reg_hbm, weight_reg_ref),
                (base_reg_hbm, base_reg_ref),
            )
        )
    ]
    for copy in copies:
        copy.start()
    for copy in copies:
        copy.wait()
    horizon, n, _ = base_ref.shape
    n_regions = weight_reg_ref.shape[1]
    square = jnp.concatenate([cats_ref[...].astype(jnp.float32)] * (LANES // min(n, LANES)), axis=0)
    labels = lax.broadcasted_iota(jnp.int32, (LANES, WIDE), 1)
    columns = [
        jnp.transpose(square[i : i + LANES]).astype(jnp.int32) % WIDE
        for i in range(0, square.shape[0], LANES)
    ]
    for j in range(n):
        column = jnp.broadcast_to(columns[j // LANES][:, j % LANES : j % LANES + 1], (LANES, WIDE))
        table_out[j * LANES : (j + 1) * LANES, :] = jnp.where(
            column == labels, 1.0, 0.0
        ).astype(jnp.bfloat16)
        group = jnp.broadcast_to(cats_ref[j : j + 1, :] // WIDE, (PAD, LANES))
        group_out[:, j * LANES : (j + 1) * LANES] = group.astype(jnp.float32).astype(jnp.bfloat16)

    field[...] = jnp.zeros_like(field)
    for h in range(horizon):
        field[h * n : (h + 1) * n, :] = base_ref[h]
    sums = category_sums(field, table_out, group_out, n, wcat_out.shape[0])
    wcat_out[...] = jnp.zeros_like(wcat_out)
    values[...] = jnp.zeros_like(values)
    for g in range(0, wcat_out.shape[0], PAD):
        for lane in range(0, WIDE, LANES):
            tile = (g // PAD * WIDE + lane) // LANES
            lanes = slice(lane, lane + LANES)
            weight = weight_cat_ref[:, tile, :]
            wcat_out[g : g + horizon, lanes] = weight
            values[g : g + horizon, lanes] = weight * (
                base_cat_ref[:, tile, :] - sums[g : g + horizon, lanes]
            )
    for tile in tiles_of(n):

        def put(h, value):
            spread_out[h, tile, :] = value

        category_spread(values, cats_ref[tile, :], horizon, put)

    labels = lax.broadcasted_iota(jnp.int32, (n_regions, n), 0)
    table = jnp.where(labels == map_ref[...], 1.0, 0.0).astype(jnp.bfloat16)
    same_out[...] = product(table, table, ((0,), (0,))).astype(jnp.bfloat16)
    for source, target in ((weight_reg_ref, wstore_out), (base_reg_ref, bstore_out)):
        for h in range(horizon):
            high, low = split(source[h])
            rest = source[h] - high.astype(jnp.float32) - low.astype(jnp.float32)
            target[h] = (
                product(table, high, ((0,), (0,)))
                + product(table, low, ((0,), (0,)))
                + product(table, rest.astype(jnp.bfloat16), ((0,), (0,)))
            )


def region_start_body(got_ref, spread_ref, wstore_ref, bstore_ref, same_ref, reg_out, send_ref):
    horizon, n, _ = spread_ref.shape
    sums = region_sums(lambda h: rows_of(got_ref, n, h), same_ref[...], n, horizon)
    for h in range(horizon):
        put_rows(send_ref, n, h, spread_ref[h])
        part = wstore_ref[h] * (bstore_ref[h] - sums[h])
        reg_out[h] = part
        put_rows(send_ref, n, horizon + h, part)


def region_part(rs, wstore_ref, same_ref, put):
    horizon, n, _ = wstore_ref.shape
    sums = region_sums(lambda h: rs[h], same_ref[...], n, horizon)
    share = jnp.zeros((n, LANES), jnp.float32)
    for h in range(horizon):
        part = wstore_ref[h] * sums[h]
        share = share + part * rs[h]
        put(h, part)
    return share


def store_part(r_ref, sums, gamma, delta, eps, diag_ref, wcat_ref, cats_ref, put, put_line, values):
    horizon, n, _ = diag_ref.shape
    scaled = wcat_ref[...] * sums
    values[...] = scaled
    square = scaled * sums
    delta = jnp.sum(delta, axis=0, keepdims=True)
    for lane in range(0, WIDE, LANES):
        delta = delta + jnp.sum(square[:, lane : lane + LANES], axis=0, keepdims=True)
    lane = lax.broadcasted_iota(jnp.int32, (1, LANES), 1)
    line = jnp.zeros((1, LANES), jnp.float32)
    for i, part in enumerate((gamma, delta, eps)):
        if part is not None:
            whole = jnp.sum(jnp.sum(part, axis=0, keepdims=True), axis=1, keepdims=True)
            line = jnp.where(lane == i, whole, line)
    put_line(jnp.broadcast_to(line, (n, LANES)))
    for tile in tiles_of(n):

        def finish(h, value):
            put(h, tile, value + diag_ref[h, tile, :] * r_ref[h, tile, :])

        category_spread(values, cats_ref[tile, :], horizon, finish)


def totals(got_ref, n, row):
    total = jnp.sum(rows_of(got_ref, n, row), axis=0, keepdims=True)
    total = jnp.broadcast_to(total, (8, LANES))
    return [
        jnp.take_along_axis(total, jnp.full((8, LANES), i, jnp.int32), axis=1)[0:1] for i in range(3)
    ]


def wide(line):
    return jnp.concatenate([line] * (WIDE // LANES), axis=1)


def region_sender(ref, n, first, keep):
    def put(h, value):
        if keep is not None:
            keep[h] = value
        put_rows(ref, n, first + h, value)

    return put


def store_sender(ref, n, keep):
    def put(h, tile, value):
        keep[h, tile, :] = value
        if ref is not None:
            put_tile(ref, n, h, tile, value)

    return put


def clear_tail(field, horizon, n):
    field[horizon * n :, :] = jnp.zeros((field.shape[0] - horizon * n, LANES), jnp.float32)


def first_body(
    a_ref, reg_ref, got_ref, diag_ref, wcat_ref, wstore_ref, table_ref, group_ref, cats_ref, same_ref,
    r_out, rs_out, cr_out, a_out, reg_out, send_ref, values, field,
):
    horizon, n, _ = diag_ref.shape
    clear_tail(field, horizon, n)
    gamma = jnp.zeros((n, LANES), jnp.float32)
    delta = jnp.zeros((n, LANES), jnp.float32)
    for h in range(horizon):
        r = a_ref[h] + rows_of(got_ref, n, horizon + h)
        r_out[h] = r
        field[h * n : (h + 1) * n, :] = r
        gamma = gamma + r * r
        delta = delta + diag_ref[h] * r * r
    sums = category_sums(field, table_ref, group_ref, n, wcat_ref.shape[0])
    cr_out[...] = sums
    for h in range(horizon):
        rs_out[h] = rows_of(got_ref, n, h) + reg_ref[h]
    delta = delta + region_part(
        rs_out, wstore_ref, same_ref, region_sender(send_ref, n, horizon, reg_out)
    )
    store_part(
        r_out, sums, gamma, delta, None, diag_ref, wcat_ref, cats_ref,
        store_sender(send_ref, n, a_out),
        lambda line: put_rows(send_ref, n, 2 * horizon, line), values,
    )


def second_body(
    a_ref, reg_ref, got_ref, x_ref, r_ref, rs_ref, cr_ref,
    diag_ref, wcat_ref, wstore_ref, table_ref, group_ref, cats_ref, same_ref,
    x_out, r_out, rs_out, s_out, ss_out, cr_out, cs_out, scal_ref, a_out, reg_out, send_ref,
    values, field,
):
    horizon, n, _ = diag_ref.shape
    clear_tail(field, horizon, n)
    for h in range(horizon):
        field[h * n : (h + 1) * n, :] = a_ref[h] + rows_of(got_ref, n, horizon + h)
    sums = category_sums(field, table_ref, group_ref, n, wcat_ref.shape[0])
    cs_out[...] = sums
    gamma, delta, _ = totals(got_ref, n, 2 * horizon)
    alpha = gamma / delta
    scal_ref[0:1, :] = gamma
    scal_ref[1:2, :] = delta
    for h in range(horizon):
        ws = rows_of(got_ref, n, h) + reg_ref[h]
        ss_out[h] = ws
        rs_out[h] = rs_ref[h] - alpha * ws
    delta = region_part(
        rs_out, wstore_ref, same_ref, region_sender(send_ref, n, horizon, reg_out)
    )
    gamma = jnp.zeros((n, LANES), jnp.float32)
    eps = jnp.zeros((n, LANES), jnp.float32)
    for h in range(horizon):
        s = field[h * n : (h + 1) * n, :]
        s_out[h] = s
        r = r_ref[h]
        x_out[h] = x_ref[h] + alpha * r
        r = r - alpha * s
        r_out[h] = r
        gamma = gamma + r * r
        delta = delta + diag_ref[h] * r * r
        eps = eps + r * s
    sums = cr_ref[...] - wide(alpha) * sums
    cr_out[...] = sums
    store_part(
        r_out, sums, gamma, delta, eps, diag_ref, wcat_ref, cats_ref,
        store_sender(send_ref, n, a_out),
        lambda line: put_rows(send_ref, n, 2 * horizon, line), values,
    )


def third_body(
    a_ref, reg_ref, got_ref, x_ref, r_ref, rs_ref, p_ref, s_ref, ss_ref, cr_ref, cs_ref, scal_ref,
    diag_ref, wcat_ref, wstore_ref, table_ref, group_ref, cats_ref, same_ref,
    x_out, r_out, p_out, s_out, scal_out, a_out, send_ref, values, field, rs_out,
):
    horizon, n, _ = diag_ref.shape
    clear_tail(field, horizon, n)
    for h in range(horizon):
        field[h * n : (h + 1) * n, :] = a_ref[h] + rows_of(got_ref, n, horizon + h)
    sums = category_sums(field, table_ref, group_ref, n, wcat_ref.shape[0])
    gamma, delta, eps = totals(got_ref, n, 2 * horizon)
    beta = gamma / scal_ref[0:1, :]
    curve = delta + 2.0 * beta * eps + beta * beta * scal_ref[1:2, :]
    alpha = gamma / curve
    scal_out[0:1, :] = gamma
    scal_out[1:2, :] = curve
    for h in range(horizon):
        ws = rows_of(got_ref, n, h) + reg_ref[h]
        rs_out[h] = rs_ref[h] - alpha * (ws + beta * ss_ref[h])
    delta = region_part(rs_out, wstore_ref, same_ref, region_sender(send_ref, n, 0, None))
    gamma = jnp.zeros((n, LANES), jnp.float32)
    eps = jnp.zeros((n, LANES), jnp.float32)
    for h in range(horizon):
        s = field[h * n : (h + 1) * n, :] + beta * s_ref[h]
        s_out[h] = s
        r = r_ref[h]
        p = r + beta * p_ref[h]
        p_out[h] = p
        x_out[h] = x_ref[h] + alpha * p
        r = r - alpha * s
        r_out[h] = r
        gamma = gamma + r * r
        delta = delta + diag_ref[h] * r * r
        eps = eps + r * s
    sums = cr_ref[...] - wide(alpha) * (sums + wide(beta) * cs_ref[...])
    store_part(
        r_out, sums, gamma, delta, eps, diag_ref, wcat_ref, cats_ref,
        store_sender(None, n, a_out), lambda line: put_rows(send_ref, n, horizon, line), values,
    )


def last_body(a_ref, got_ref, x_ref, r_ref, p_ref, s_ref, scal_ref, x_out, r_out):
    horizon, n, _ = a_ref.shape
    gamma, delta, eps = totals(got_ref, n, horizon)
    beta = gamma / scal_ref[0:1, :]
    alpha = gamma / (delta + 2.0 * beta * eps + beta * beta * scal_ref[1:2, :])
    for h in range(horizon):
        r = r_ref[h]
        s = a_ref[h] + rows_of(got_ref, n, h) + beta * s_ref[h]
        x_out[h] = x_ref[h] + alpha * (r + beta * p_ref[h])
        r_out[h] = r - alpha * s


def on_device(
    base_bottom,
    weight_bottom,
    base_category,
    weight_category,
    base_region,
    weight_region,
    category_map,
    region_map,
):
    stores, horizon, skus = base_bottom.shape
    n = region_map.shape[0]
    groups = weight_category.shape[2] // WIDE
    tiles = weight_category.shape[2] // LANES
    field = (horizon, n, LANES)
    padded = (PAD * n, LANES)
    by_category = (horizon, tiles, LANES)
    scal = (2, LANES)
    values = pltpu.VMEM((groups * PAD, WIDE), jnp.float32)

    x = base_bottom.reshape(field)
    diag = weight_bottom.reshape(field)
    (sent,) = call(
        pack_body,
        [(n * horizon, LANES)],
        [pltpu.VMEM(field, jnp.float32), pltpu.SemaphoreType.DMA],
        (x,),
        [HBM],
        True,
    )
    got = exchange(sent, n)
    arguments = (
        x,
        base_category.reshape(by_category),
        weight_category.reshape(by_category),
        jnp.transpose(base_region, (1, 0, 2)),
        jnp.transpose(weight_region, (1, 0, 2)),
        category_map.reshape(n, LANES),
        region_map.reshape(1, n),
    )
    held = [pltpu.VMEM(arguments[i].shape, arguments[i].dtype) for i in (0, 1, 2, 3, 4, 6)]
    spread, wcat, wstore, bstore, same, table, group, cats = call(
        prepare_body,
        [
            field,
            (groups * PAD, WIDE),
            field,
            field,
            jax.ShapeDtypeStruct((n, n), jnp.bfloat16),
            jax.ShapeDtypeStruct((skus, WIDE), jnp.bfloat16),
            jax.ShapeDtypeStruct((PAD, skus), jnp.bfloat16),
            jax.ShapeDtypeStruct((n, LANES), jnp.int32),
        ],
        [
            pltpu.VMEM(padded, jnp.float32),
            values,
            *held,
            pltpu.SemaphoreType.DMA((len(arguments),)),
        ],
        arguments,
        [HBM] * len(arguments),
    )
    reg, sent = call(
        region_start_body,
        [field, (n * 2 * horizon, LANES)],
        [],
        (got, spread, wstore, bstore, same),
    )
    got = exchange(sent, n)
    fixed = (diag, wcat, wstore, table, group, cats, same)
    both = (n * (2 * horizon + 1), LANES)
    work = [values, pltpu.VMEM(padded, jnp.float32)]
    sums = (groups * PAD, WIDE)
    r, rs, cr, a, reg, sent = call(
        first_body, [field, field, sums, field, field, both], work, (spread, reg, got) + fixed
    )
    got = exchange(sent, n)
    p = r
    x, r, rs, s, ss, cr, cs, scalars, a, reg, sent = call(
        second_body,
        [field, field, field, field, field, sums, sums, scal, field, field, both],
        work,
        (a, reg, got, x, r, rs, cr) + fixed,
    )
    got = exchange(sent, n)
    x, r, p, s, scalars, a, sent = call(
        third_body,
        [field, field, field, field, scal, field, (n * (horizon + 1), LANES)],
        work + [pltpu.VMEM(field, jnp.float32)],
        (a, reg, got, x, r, rs, p, s, ss, cr, cs, scalars) + fixed,
    )
    got = exchange(sent, n)
    x, r = call(last_body, [field, field], [], (a, got, x, r, p, s, scalars))
    return x.reshape(base_bottom.shape), r.reshape(base_bottom.shape)


def solution(mesh):
    in_specs = (
        P(("store", "sku"), None, None),
        P(("store", "sku"), None, None),
        P(("store", "sku"), None, None),
        P(("store", "sku"), None, None),
        P(None, None, ("store", "sku")),
        P(None, None, ("store", "sku")),
        P(),
        P(),
    )
    out_specs = (P(("store", "sku"), None, None), P(("store", "sku"), None, None))
    return jax.shard_map(
        on_device, mesh=mesh, in_specs=in_specs, out_specs=out_specs, check_vma=False
    )
```

```python
import jax
import jax.numpy as jnp
from jax import lax
from jax.experimental import pallas as pl
from jax.experimental.pallas import tpu as pltpu
from jax.sharding import Mesh
from jax.sharding import PartitionSpec as P

LANES = 128
PAD = 16
WIDE = 256
VMEM = pl.BlockSpec(memory_space=pltpu.VMEM)
HBM = pl.BlockSpec(memory_space=pltpu.HBM)
SMEM = pl.BlockSpec(memory_space=pltpu.SMEM)
CORES = 2


def exchange(blocks, n):
    moved = lax.all_to_all(
        blocks.reshape(n, 1, -1), ("store", "sku"), split_axis=0, concat_axis=0, tiled=True
    )
    return moved.reshape(blocks.shape)


def call(body, outs, scratch, args, specs=None, held=False, out_specs=None):
    outs = [
        out if isinstance(out, jax.ShapeDtypeStruct) else jax.ShapeDtypeStruct(out, jnp.float32)
        for out in outs
    ]
    specs = specs or [VMEM] * len(args)
    args = [
        arg if spec is SMEM else pltpu.with_memory_space_constraint(arg, spec.memory_space)
        for arg, spec in zip(args, specs)
    ]
    return pl.pallas_call(
        body,
        out_shape=tuple(pltpu.VMEM(out.shape, out.dtype) if held else out for out in outs),
        in_specs=specs,
        out_specs=out_specs or tuple(VMEM for _ in outs),
        scratch_shapes=scratch,
        compiler_params=pltpu.CompilerParams(vmem_limit_bytes=24 << 20),
    )(*args)


def split(value):
    high = value.astype(jnp.bfloat16)
    return high, (value - high.astype(jnp.float32)).astype(jnp.bfloat16)


def split_all(value):
    high, low = split(value)
    rest = value - high.astype(jnp.float32) - low.astype(jnp.float32)
    return high, low, rest.astype(jnp.bfloat16)


def product(left, right, contract):
    return lax.dot_general(left, right, (contract, ((), ())), preferred_element_type=jnp.float32)


def rows_of(ref, n, h):
    return ref[pl.ds(h, n, stride=ref.shape[0] // n), :]


def put_rows(ref, n, h, value):
    ref[pl.ds(h, n, stride=ref.shape[0] // n), :] = value


def category_sums(field, table_ref, group_ref, n, rows):
    width = 4 if n % 4 == 0 else 1
    lanes = width * LANES

    def step(c, total):
        pieces = [field[pl.ds(c * width + i, PAD, stride=n), :] for i in range(width)]
        parts = split_all(jnp.concatenate(pieces, axis=1))
        start = pl.multiple_of(c * lanes, lanes)
        group = group_ref[:, pl.ds(start, lanes)]
        masks = [group == g for g in range(rows // PAD)]
        none = jnp.zeros((PAD, lanes), jnp.bfloat16)
        spread = jnp.concatenate(
            [jnp.where(mask, part, none) for part in parts for mask in masks], axis=0
        )
        return total + product(spread, table_ref[pl.ds(start, lanes), :], ((1,), (0,)))

    steps = n // width
    total = lax.fori_loop(
        0, steps, step, jnp.zeros((3 * rows, WIDE), jnp.float32), unroll=min(steps, 8)
    )
    return total[:rows] + (total[rows : 2 * rows] + total[2 * rows :])


def category_spread(values, cats, horizon, put):
    place = cats % LANES
    group = cats // LANES
    odd = [(group >> bit) & 1 != 0 for bit in range(3)]
    for h in range(horizon):
        found = []
        for g in range(0, values.shape[0], PAD):
            for lane in range(0, WIDE, LANES):
                row = jnp.broadcast_to(values[g + h : g + h + 1, lane : lane + LANES], cats.shape)
                found.append(jnp.take_along_axis(row, place, axis=1))
        for bit in range((len(found) - 1).bit_length()):
            mask = odd[bit] if bit < 3 else (group >> bit) & 1 != 0
            pairs = [found[i : i + 2] for i in range(0, len(found), 2)]
            found = [jnp.where(mask, pair[1], pair[0]) if len(pair) == 2 else pair[0] for pair in pairs]
        put(h, found[0])


def tiles_of(n):
    return [slice(t, t + 8) for t in range(0, n, 8)]


def put_tile(ref, n, h, tile, value):
    rows = ref.shape[0] // n
    ref[pl.ds(tile.start * rows + h, 8, stride=rows), :] = value


def region_sums(load, same, n, horizon):
    high, low = split(jnp.concatenate([load(h) for h in range(horizon)], axis=1))
    total = product(same, high, ((1,), (0,))) + product(same, low, ((1,), (0,)))
    return [total[:, h * LANES : (h + 1) * LANES] for h in range(horizon)]


def pack_body(base_hbm, out_ref, base_ref, sem):
    copy = pltpu.make_async_copy(base_hbm, base_ref, sem)
    copy.start()
    copy.wait()
    n = base_ref.shape[1]
    for h in range(base_ref.shape[0]):
        put_rows(out_ref, n, h, base_ref[h])


def prepare_body(
    base_hbm, base_cat_hbm, weight_cat_hbm, base_reg_hbm, weight_reg_hbm, cats_hbm, map_hbm,
    spread_out, wcat_out, wstore_out, bstore_out, same_out, table_out, group_out,
    cats_ref,
    field, values, base_ref, base_cat_ref, weight_cat_ref, base_reg_ref, weight_reg_ref, map_ref, sems,
):
    copies = [
        pltpu.make_async_copy(source, target, sems.at[i])
        for i, (source, target) in enumerate(
            (
                (cats_hbm, cats_ref),
                (base_hbm, base_ref),
                (weight_cat_hbm, weight_cat_ref),
                (base_cat_hbm, base_cat_ref),
                (map_hbm, map_ref),
                (weight_reg_hbm, weight_reg_ref),
                (base_reg_hbm, base_reg_ref),
            )
        )
    ]
    for copy in copies:
        copy.start()
    for copy in copies:
        copy.wait()
    horizon, n, _ = base_ref.shape
    n_regions = weight_reg_ref.shape[1]
    square = jnp.concatenate([cats_ref[...].astype(jnp.float32)] * (LANES // min(n, LANES)), axis=0)
    labels = lax.broadcasted_iota(jnp.int32, (LANES, WIDE), 1)
    columns = [
        jnp.transpose(square[i : i + LANES]).astype(jnp.int32) % WIDE
        for i in range(0, square.shape[0], LANES)
    ]
    for j in range(n):
        column = jnp.broadcast_to(columns[j // LANES][:, j % LANES : j % LANES + 1], (LANES, WIDE))
        table_out[j * LANES : (j + 1) * LANES, :] = jnp.where(
            column == labels, 1.0, 0.0
        ).astype(jnp.bfloat16)
        group = jnp.broadcast_to(cats_ref[j : j + 1, :] // WIDE, (PAD, LANES))
        group_out[:, j * LANES : (j + 1) * LANES] = group.astype(jnp.float32).astype(jnp.bfloat16)

    field[...] = jnp.zeros_like(field)
    for h in range(horizon):
        field[h * n : (h + 1) * n, :] = base_ref[h]
    sums = category_sums(field, table_out, group_out, n, wcat_out.shape[0])
    wcat_out[...] = jnp.zeros_like(wcat_out)
    values[...] = jnp.zeros_like(values)
    for g in range(0, wcat_out.shape[0], PAD):
        for lane in range(0, WIDE, LANES):
            tile = (g // PAD * WIDE + lane) // LANES
            lanes = slice(lane, lane + LANES)
            weight = weight_cat_ref[:, tile, :]
            wcat_out[g : g + horizon, lanes] = weight
            values[g : g + horizon, lanes] = weight * (
                base_cat_ref[:, tile, :] - sums[g : g + horizon, lanes]
            )
    for tile in tiles_of(n):

        def put(h, value):
            spread_out[h, tile, :] = value

        category_spread(values, cats_ref[tile, :], horizon, put)

    labels = lax.broadcasted_iota(jnp.int32, (n_regions, n), 0)
    table = jnp.where(labels == map_ref[...], 1.0, 0.0).astype(jnp.bfloat16)
    same_out[...] = product(table, table, ((0,), (0,))).astype(jnp.bfloat16)
    for source, target in ((weight_reg_ref, wstore_out), (base_reg_ref, bstore_out)):
        for h in range(horizon):
            high, low = split(source[h])
            rest = source[h] - high.astype(jnp.float32) - low.astype(jnp.float32)
            target[h] = (
                product(table, high, ((0,), (0,)))
                + product(table, low, ((0,), (0,)))
                + product(table, rest.astype(jnp.bfloat16), ((0,), (0,)))
            )


def region_start_body(got_ref, spread_ref, wstore_ref, bstore_ref, same_ref, reg_out, send_ref):
    horizon, n, _ = spread_ref.shape
    sums = region_sums(lambda h: rows_of(got_ref, n, h), same_ref[...], n, horizon)
    for h in range(horizon):
        put_rows(send_ref, n, h, spread_ref[h])
        part = wstore_ref[h] * (bstore_ref[h] - sums[h])
        reg_out[h] = part
        put_rows(send_ref, n, horizon + h, part)


def region_part(rs, wstore_ref, same_ref, put):
    horizon, n, _ = wstore_ref.shape
    sums = region_sums(lambda h: rs[h], same_ref[...], n, horizon)
    share = jnp.zeros((n, LANES), jnp.float32)
    for h in range(horizon):
        part = wstore_ref[h] * sums[h]
        share = share + part * rs[h]
        put(h, part)
    return share


def store_part(r_ref, sums, gamma, delta, eps, diag_ref, wcat_ref, cats_ref, put, put_line, values):
    horizon, n, _ = diag_ref.shape
    scaled = wcat_ref[...] * sums
    values[...] = scaled
    square = scaled * sums
    delta = jnp.sum(delta, axis=0, keepdims=True)
    for lane in range(0, WIDE, LANES):
        delta = delta + jnp.sum(square[:, lane : lane + LANES], axis=0, keepdims=True)
    lane = lax.broadcasted_iota(jnp.int32, (1, LANES), 1)
    line = jnp.zeros((1, LANES), jnp.float32)
    for i, part in enumerate((gamma, delta, eps)):
        if part is not None:
            whole = jnp.sum(jnp.sum(part, axis=0, keepdims=True), axis=1, keepdims=True)
            line = jnp.where(lane == i, whole, line)
    put_line(jnp.broadcast_to(line, (n, LANES)))
    for tile in tiles_of(n):

        def finish(h, value):
            put(h, tile, value + diag_ref[h, tile, :] * r_ref[h, tile, :])

        category_spread(values, cats_ref[tile, :], horizon, finish)


def totals(got_ref, n, row):
    total = jnp.sum(rows_of(got_ref, n, row), axis=0, keepdims=True)
    total = jnp.broadcast_to(total, (8, LANES))
    return [
        jnp.take_along_axis(total, jnp.full((8, LANES), i, jnp.int32), axis=1)[0:1] for i in range(3)
    ]


def wide(line):
    return jnp.concatenate([line] * (WIDE // LANES), axis=1)


def region_sender(ref, n, first, keep):
    def put(h, value):
        if keep is not None:
            keep[h] = value
        put_rows(ref, n, first + h, value)

    return put


def store_sender(ref, n, keep):
    def put(h, tile, value):
        keep[h, tile, :] = value
        if ref is not None:
            put_tile(ref, n, h, tile, value)

    return put


def clear_tail(field, horizon, n):
    field[horizon * n :, :] = jnp.zeros((field.shape[0] - horizon * n, LANES), jnp.float32)


def first_body(
    a_ref, reg_ref, got_ref, diag_ref, wcat_ref, wstore_ref, table_ref, group_ref, cats_ref, same_ref,
    r_out, rs_out, cr_out, a_out, reg_out, send_ref, values, field,
):
    horizon, n, _ = diag_ref.shape
    clear_tail(field, horizon, n)
    gamma = jnp.zeros((n, LANES), jnp.float32)
    delta = jnp.zeros((n, LANES), jnp.float32)
    for h in range(horizon):
        r = a_ref[h] + rows_of(got_ref, n, horizon + h)
        r_out[h] = r
        field[h * n : (h + 1) * n, :] = r
        gamma = gamma + r * r
        delta = delta + diag_ref[h] * r * r
    sums = category_sums(field, table_ref, group_ref, n, wcat_ref.shape[0])
    cr_out[...] = sums
    for h in range(horizon):
        rs_out[h] = rows_of(got_ref, n, h) + reg_ref[h]
    delta = delta + region_part(
        rs_out, wstore_ref, same_ref, region_sender(send_ref, n, horizon, reg_out)
    )
    store_part(
        r_out, sums, gamma, delta, None, diag_ref, wcat_ref, cats_ref,
        store_sender(send_ref, n, a_out),
        lambda line: put_rows(send_ref, n, 2 * horizon, line), values,
    )


def second_body(
    a_ref, reg_ref, got_ref, x_ref, r_ref, rs_ref, cr_ref,
    diag_ref, wcat_ref, wstore_ref, table_ref, group_ref, cats_ref, same_ref,
    x_out, r_out, rs_out, s_out, ss_out, cr_out, cs_out, scal_ref, a_out, reg_out, send_ref,
    values, field,
):
    horizon, n, _ = diag_ref.shape
    clear_tail(field, horizon, n)
    for h in range(horizon):
        field[h * n : (h + 1) * n, :] = a_ref[h] + rows_of(got_ref, n, horizon + h)
    sums = category_sums(field, table_ref, group_ref, n, wcat_ref.shape[0])
    cs_out[...] = sums
    gamma, delta, _ = totals(got_ref, n, 2 * horizon)
    alpha = gamma / delta
    scal_ref[0:1, :] = gamma
    scal_ref[1:2, :] = delta
    for h in range(horizon):
        ws = rows_of(got_ref, n, h) + reg_ref[h]
        ss_out[h] = ws
        rs_out[h] = rs_ref[h] - alpha * ws
    delta = region_part(
        rs_out, wstore_ref, same_ref, region_sender(send_ref, n, horizon, reg_out)
    )
    gamma = jnp.zeros((n, LANES), jnp.float32)
    eps = jnp.zeros((n, LANES), jnp.float32)
    for h in range(horizon):
        s = field[h * n : (h + 1) * n, :]
        s_out[h] = s
        r = r_ref[h]
        x_out[h] = x_ref[h] + alpha * r
        r = r - alpha * s
        r_out[h] = r
        gamma = gamma + r * r
        delta = delta + diag_ref[h] * r * r
        eps = eps + r * s
    sums = cr_ref[...] - wide(alpha) * sums
    cr_out[...] = sums
    store_part(
        r_out, sums, gamma, delta, eps, diag_ref, wcat_ref, cats_ref,
        store_sender(send_ref, n, a_out),
        lambda line: put_rows(send_ref, n, 2 * horizon, line), values,
    )


def third_body(
    a_ref, reg_ref, got_ref, x_ref, r_ref, rs_ref, p_ref, s_ref, ss_ref, cr_ref, cs_ref, scal_ref,
    diag_ref, wcat_ref, wstore_ref, table_ref, group_ref, cats_ref, same_ref,
    x_out, r_out, p_out, s_out, scal_out, a_out, send_ref, values, field, rs_out,
):
    horizon, n, _ = diag_ref.shape
    clear_tail(field, horizon, n)
    for h in range(horizon):
        field[h * n : (h + 1) * n, :] = a_ref[h] + rows_of(got_ref, n, horizon + h)
    sums = category_sums(field, table_ref, group_ref, n, wcat_ref.shape[0])
    gamma, delta, eps = totals(got_ref, n, 2 * horizon)
    beta = gamma / scal_ref[0:1, :]
    curve = delta + 2.0 * beta * eps + beta * beta * scal_ref[1:2, :]
    alpha = gamma / curve
    scal_out[0:1, :] = gamma
    scal_out[1:2, :] = curve
    for h in range(horizon):
        ws = rows_of(got_ref, n, h) + reg_ref[h]
        rs_out[h] = rs_ref[h] - alpha * (ws + beta * ss_ref[h])
    delta = region_part(rs_out, wstore_ref, same_ref, region_sender(send_ref, n, 0, None))
    gamma = jnp.zeros((n, LANES), jnp.float32)
    eps = jnp.zeros((n, LANES), jnp.float32)
    for h in range(horizon):
        s = field[h * n : (h + 1) * n, :] + beta * s_ref[h]
        s_out[h] = s
        r = r_ref[h]
        p = r + beta * p_ref[h]
        p_out[h] = p
        x_out[h] = x_ref[h] + alpha * p
        r = r - alpha * s
        r_out[h] = r
        gamma = gamma + r * r
        delta = delta + diag_ref[h] * r * r
        eps = eps + r * s
    sums = cr_ref[...] - wide(alpha) * (sums + wide(beta) * cs_ref[...])
    store_part(
        r_out, sums, gamma, delta, eps, diag_ref, wcat_ref, cats_ref,
        store_sender(None, n, a_out), lambda line: put_rows(send_ref, n, horizon, line), values,
    )


def last_body(a_ref, got_ref, x_ref, r_ref, p_ref, s_ref, scal_ref, x_out, r_out):
    horizon, n, _ = a_ref.shape
    gamma, delta, eps = totals(got_ref, n, horizon)
    beta = gamma / scal_ref[0:1, :]
    alpha = gamma / (delta + 2.0 * beta * eps + beta * beta * scal_ref[1:2, :])
    for h in range(horizon):
        r = r_ref[h]
        s = a_ref[h] + rows_of(got_ref, n, h) + beta * s_ref[h]
        x_out[h] = x_ref[h] + alpha * (r + beta * p_ref[h])
        r_out[h] = r - alpha * s


def on_device(
    base_bottom,
    weight_bottom,
    base_category,
    weight_category,
    base_region,
    weight_region,
    category_map,
    region_map,
):
    stores, horizon, skus = base_bottom.shape
    n = region_map.shape[0]
    groups = weight_category.shape[2] // WIDE
    tiles = weight_category.shape[2] // LANES
    field = (horizon, n, LANES)
    padded = (PAD * n, LANES)
    by_category = (horizon, tiles, LANES)
    scal = (2, LANES)
    values = pltpu.VMEM((groups * PAD, WIDE), jnp.float32)

    x = base_bottom.reshape(field)
    diag = weight_bottom.reshape(field)
    (sent,) = call(
        pack_body,
        [(n * horizon, LANES)],
        [pltpu.VMEM(field, jnp.float32), pltpu.SemaphoreType.DMA],
        (x,),
        [HBM],
        True,
    )
    got = exchange(sent, n)
    arguments = (
        x,
        base_category.reshape(by_category),
        weight_category.reshape(by_category),
        jnp.transpose(base_region, (1, 0, 2)),
        jnp.transpose(weight_region, (1, 0, 2)),
        category_map.reshape(n, LANES),
        region_map.reshape(1, n),
    )
    held = [pltpu.VMEM(arguments[i].shape, arguments[i].dtype) for i in (0, 1, 2, 3, 4, 6)]
    spread, wcat, wstore, bstore, same, table, group, cats = call(
        prepare_body,
        [
            field,
            (groups * PAD, WIDE),
            field,
            field,
            jax.ShapeDtypeStruct((n, n), jnp.bfloat16),
            jax.ShapeDtypeStruct((skus, WIDE), jnp.bfloat16),
            jax.ShapeDtypeStruct((PAD, skus), jnp.bfloat16),
            jax.ShapeDtypeStruct((n, LANES), jnp.int32),
        ],
        [
            pltpu.VMEM(padded, jnp.float32),
            values,
            *held,
            pltpu.SemaphoreType.DMA((len(arguments),)),
        ],
        arguments,
        [HBM] * len(arguments),
    )
    reg, sent = call(
        region_start_body,
        [field, (n * 2 * horizon, LANES)],
        [],
        (got, spread, wstore, bstore, same),
    )
    got = exchange(sent, n)
    fixed = (diag, wcat, wstore, table, group, cats, same)
    both = (n * (2 * horizon + 1), LANES)
    work = [values, pltpu.VMEM(padded, jnp.float32)]
    sums = (groups * PAD, WIDE)
    r, rs, cr, a, reg, sent = call(
        first_body, [field, field, sums, field, field, both], work, (spread, reg, got) + fixed
    )
    got = exchange(sent, n)
    p = r
    x, r, rs, s, ss, cr, cs, scalars, a, reg, sent = call(
        second_body,
        [field, field, field, field, field, sums, sums, scal, field, field, both],
        work,
        (a, reg, got, x, r, rs, cr) + fixed,
    )
    got = exchange(sent, n)
    x, r, p, s, scalars, a, sent = call(
        third_body,
        [field, field, field, field, scal, field, (n * (horizon + 1), LANES)],
        work + [pltpu.VMEM(field, jnp.float32)],
        (a, reg, got, x, r, rs, p, s, ss, cr, cs, scalars) + fixed,
    )
    got = exchange(sent, n)
    x, r = call(last_body, [field, field], [], (a, got, x, r, p, s, scalars))
    return x.reshape(base_bottom.shape), r.reshape(base_bottom.shape)


def week_rows(tiles, n, regions):
    sizes = (n, n, tiles, tiles, regions, regions)
    return [sum(sizes[:i]) for i in range(len(sizes) + 1)]


def week_pack_body(*refs):
    sources, out, sems = refs[:-2], refs[-2], refs[-1]
    horizon = sources[0].shape[0]
    copies, start = [], 0
    for i, source in enumerate(sources):
        rows = source.shape[1]
        target = out.at[pl.ds(0, horizon), pl.ds(start, rows)]
        copies.append(pltpu.make_async_copy(source, target, sems.at[i]))
        start += rows
    for copy in copies:
        copy.start()
    for copy in copies:
        copy.wait()


def week_table_body(cats_ref, table_out, group_out):
    n = cats_ref.shape[0]
    square = jnp.concatenate([cats_ref[...].astype(jnp.float32)] * (LANES // min(n, LANES)), axis=0)
    labels = lax.broadcasted_iota(jnp.int32, (LANES, WIDE), 1)
    columns = [
        jnp.transpose(square[i : i + LANES]).astype(jnp.int32) % WIDE
        for i in range(0, square.shape[0], LANES)
    ]
    for j in range(n):
        column = jnp.broadcast_to(columns[j // LANES][:, j % LANES : j % LANES + 1], (LANES, WIDE))
        table_out[j * LANES : (j + 1) * LANES, :] = jnp.where(
            column == labels, 1.0, 0.0
        ).astype(jnp.bfloat16)
        group = jnp.broadcast_to(cats_ref[j : j + 1, :] // WIDE, (group_out.shape[0], LANES))
        group_out[:, j * LANES : (j + 1) * LANES] = group.astype(jnp.float32).astype(jnp.bfloat16)


def ratio(top, bottom):
    return jnp.where(bottom > 0.0, top / bottom, 0.0)


def whole_sum(part):
    total = jnp.sum(jnp.sum(part, axis=0, keepdims=True), axis=1, keepdims=True)
    return jnp.broadcast_to(total, (1, LANES))


def week_body(
    ids_ref, own_ref, other_ref, table_ref, group_ref, cats_ref, map_ref,
    base_out, basis_out, line_out,
    diag, wstore, bstore, wcat, bcat, raw_weight, raw_base,
):
    core = ids_ref[0]
    n, skus = base_out.shape
    per = own_ref.shape[0] // line_out.shape[0]
    regions = raw_weight.shape[0]
    side = ids_ref.shape[0] - 2
    tiles = wcat.shape[0] // n * (WIDE // LANES)
    starts = week_rows(tiles, n, regions)
    chunk = min(skus, 8 * LANES)
    chunks = [slice(c, c + chunk) for c in range(0, skus, chunk)]

    for ref, c in ((own_ref, core), (other_ref, 1 - core)):
        for x in range(n // (CORES * side)):
            for t in range(0, side, 8):
                first = (x * side + t) * per
                top = pl.multiple_of(x * CORES * side + c * side + t, 8)

                def rows(row):
                    return ref[pl.ds(first + row, 8, stride=per), :]

                for j in range(n):
                    lanes = slice(j * LANES, (j + 1) * LANES)
                    base_out[pl.ds(top, 8), lanes] = rows(starts[0] + j)
                    diag[pl.ds(top, 8), lanes] = rows(starts[1] + j)
                for g in range(tiles):
                    lane = g * LANES % WIDE
                    down = pl.multiple_of(g * LANES // WIDE * n + top, 8)
                    wcat[pl.ds(down, 8), lane : lane + LANES] = rows(starts[2] + g)
                    bcat[pl.ds(down, 8), lane : lane + LANES] = rows(starts[3] + g)
            for k in range(side):
                first = (x * side + k) * per
                j = x * CORES * side + c * side + k
                lanes = pl.ds(pl.multiple_of(j * LANES, LANES), LANES)
                raw_base[:, lanes] = ref[first + starts[4] : first + starts[5], :]
                raw_weight[:, lanes] = ref[first + starts[5] : first + starts[6], :]

    labels = lax.broadcasted_iota(jnp.int32, (regions, n), 0)
    table = jnp.where(labels == map_ref[...], 1.0, 0.0).astype(jnp.bfloat16)
    same = product(table, table, ((0,), (0,))).astype(jnp.bfloat16)
    for source, target in ((raw_weight, wstore), (raw_base, bstore)):
        for lanes in chunks:
            parts = [product(table, part, ((0,), (0,))) for part in split_all(source[:, lanes])]
            target[:, lanes] = parts[0] + parts[1] + parts[2]

    def by_category(field):
        rows = wcat.shape[0]
        total = None
        for lanes in chunks:
            group = group_ref[:, lanes]
            masks = [group == g for g in range(rows // n)]
            none = jnp.zeros(group.shape, jnp.bfloat16)
            spread = jnp.concatenate(
                [jnp.where(mask, part, none) for part in split(field[:, lanes]) for mask in masks],
                axis=0,
            )
            part = product(spread, table_ref[lanes, :], ((1,), (0,)))
            total = part if total is None else total + part
        return total[:rows] + total[rows:]

    def spread_tile(values, j):
        members = jnp.broadcast_to(cats_ref[j : j + 1, :], (n, LANES))
        place = members % LANES
        group = members // LANES
        found = [
            jnp.take_along_axis(values[g : g + n, lane : lane + LANES], place, axis=1)
            for g in range(0, values.shape[0], n)
            for lane in range(0, WIDE, LANES)
        ]
        bit = 0
        while len(found) > 1:
            mask = (group >> bit) & 1 != 0
            pairs = [found[i : i + 2] for i in range(0, len(found), 2)]
            found = [jnp.where(mask, pair[1], pair[0]) if len(pair) == 2 else pair[0] for pair in pairs]
            bit += 1
        return found[0]

    def by_region(part):
        high, low = split(part)
        return product(same, high, ((1,), (0,))) + product(same, low, ((1,), (0,)))

    zero = jnp.zeros((n, LANES), jnp.float32)
    values = wcat[...] * (bcat[...] - by_category(base_out))
    norm = zero
    for lanes in chunks:
        sums = by_region(base_out[:, lanes])
        for t in range(0, chunk, LANES):
            tile = slice(lanes.start + t, lanes.start + t + LANES)
            part = wstore[:, tile] * (bstore[:, tile] - sums[:, t : t + LANES])
            part = part + spread_tile(values, tile.start // LANES)
            basis_out[0, :, tile] = part
            norm = norm + part * part
    norms, quotients = [whole_sum(norm)], []
    for k in range(3):
        field = basis_out.at[k]
        image = basis_out.at[k + 1]
        values = wcat[...] * by_category(field)
        dot = zero
        for lanes in chunks:
            sums = by_region(field[:, lanes])
            for t in range(0, chunk, LANES):
                tile = slice(lanes.start + t, lanes.start + t + LANES)
                part = field[:, tile]
                result = diag[:, tile] * part + wstore[:, tile] * sums[:, t : t + LANES]
                result = result + spread_tile(values, tile.start // LANES)
                image[:, tile] = result
                dot = dot + part * result
        quotients.append(ratio(whole_sum(dot), norms[k]))
        back = ratio(norms[k], norms[k - 1]) if k else None
        norm = zero
        for t in range(0, skus, LANES):
            tile = slice(t, t + LANES)
            result = image[:, tile] - quotients[k] * field[:, tile]
            if k:
                result = result - back * basis_out[k - 1, :, tile]
            image[:, tile] = result
            norm = norm + result * result
        norms.append(whole_sum(norm))
    lane = lax.broadcasted_iota(jnp.int32, (1, LANES), 1)
    line = jnp.zeros((1, LANES), jnp.float32)
    for i, value in enumerate(norms[:3] + quotients):
        line = jnp.where(lane == i, value, line)
    line_out[...] = jnp.broadcast_to(line, line_out.shape)


def week_combine_body(ids_ref, lines_ref, base_ref, basis_ref, send_ref, horizon):
    core = ids_ref[0]
    weeks = lines_ref.shape[0]
    n, skus = base_ref.shape
    side = ids_ref.shape[0] - 2
    week = lax.broadcasted_iota(jnp.int32, (weeks, LANES), 0)
    lines = jnp.where(week < horizon, lines_ref[...], 0.0)
    n1, n2, n3, a1, a2, a3 = [
        jnp.take_along_axis(lines, jnp.full((weeks, LANES), i, jnp.int32), axis=1) for i in range(6)
    ]
    e2, e3 = ratio(n2, n1), ratio(n3, n2)

    def dot(left, right):
        terms = n1 * left[0] * right[0] + n2 * left[1] * right[1] + n3 * left[2] * right[2]
        return jnp.sum(terms, axis=0, keepdims=True)

    zero = jnp.zeros((weeks, LANES), jnp.float32)
    x = [zero, zero, zero]
    r = [zero + 1.0, zero, zero, zero]
    p = r[:3]
    rr = dot(r, r)
    for k in range(3):
        image = [
            a1 * p[0] + e2 * p[1],
            p[0] + a2 * p[1] + e3 * p[2],
            p[1] + a3 * p[2],
            p[2],
        ]
        alpha = rr / dot(p, image)
        x = [left + alpha * right for left, right in zip(x, p)]
        r = [left - alpha * right for left, right in zip(r, image)]
        if k < 2:
            new = dot(r, r)
            p = [left + new / rr * right for left, right in zip(r[:3], p)]
            rr = new
    mine = week == ids_ref[1]
    x = [jnp.sum(jnp.where(mine, value, 0.0), axis=0, keepdims=True) for value in x]
    r = [jnp.sum(jnp.where(mine, value, 0.0), axis=0, keepdims=True) for value in r]
    rows = send_ref.shape[0] // weeks
    for i in range(n // (CORES * side)):
        for t in range(0, side, 8):
            top = pl.multiple_of(i * CORES * side + core * side + t, 8)
            for j in range(n):
                lanes = slice(j * LANES, (j + 1) * LANES)
                parts = [basis_ref[k, pl.ds(top, 8), lanes] for k in range(4)]
                left = base_ref[pl.ds(top, 8), lanes]
                right = r[3] * parts[3]
                for k in range(3):
                    left = left + x[k] * parts[k]
                    right = right + r[k] * parts[k]
                first = (i * side + t) * rows + j
                send_ref[pl.ds(first, 8, stride=rows), :] = left
                send_ref[pl.ds(first + n, 8, stride=rows), :] = right


def week_last_body(got_ref, x_out, r_out, sems):
    horizon, n, _ = x_out.shape
    copies = [
        pltpu.make_async_copy(
            got_ref.at[pl.ds(0, horizon), pl.ds(i * n, n)], target, sems.at[i]
        )
        for i, target in enumerate((x_out, r_out))
    ]
    for copy in copies:
        copy.start()
    for copy in copies:
        copy.wait()


def exchange_weeks(blocks):
    return lax.all_to_all(blocks, ("x", "sku"), split_axis=0, concat_axis=0, tiled=True)


def by_weeks(
    base_bottom,
    weight_bottom,
    base_category,
    weight_category,
    base_region,
    weight_region,
    category_map,
    region_map,
):
    stores, horizon, skus = base_bottom.shape
    n = region_map.shape[0]
    regions = weight_region.shape[0]
    tiles = weight_category.shape[2] // LANES
    groups = weight_category.shape[2] // WIDE
    side = lax.axis_size("sku")
    weeks = lax.axis_size("x") * side
    place = lax.axis_index("x") * side + lax.axis_index("sku")
    ids = jnp.stack([lax.axis_index("core"), place] + [place] * side).astype(jnp.int32)
    sources = (
        base_bottom.reshape(horizon, n, LANES),
        weight_bottom.reshape(horizon, n, LANES),
        weight_category.reshape(horizon, tiles, LANES),
        base_category.reshape(horizon, tiles, LANES),
        jnp.transpose(base_region, (1, 0, 2)),
        jnp.transpose(weight_region, (1, 0, 2)),
    )
    per = week_rows(tiles, n, regions)[-1]
    (sent,) = call(
        week_pack_body,
        [(weeks, per, LANES)],
        [pltpu.SemaphoreType.DMA((len(sources),))],
        sources,
        [HBM] * len(sources),
        out_specs=(HBM,),
    )
    own = exchange_weeks(sent)
    other = lax.ppermute(own, "core", [(0, 1), (1, 0)])
    table, group = call(
        week_table_body,
        [
            jax.ShapeDtypeStruct((skus, WIDE), jnp.bfloat16),
            jax.ShapeDtypeStruct((n, skus), jnp.bfloat16),
        ],
        [],
        (category_map.reshape(n, LANES),),
    )
    full = pltpu.VMEM((n, skus), jnp.float32)
    raw = pltpu.VMEM((regions, skus), jnp.float32)
    cat = pltpu.VMEM((groups * n, WIDE), jnp.float32)
    base, basis, line = call(
        week_body,
        [(n, skus), (4, n, skus), (weeks, LANES)],
        [full, full, full, cat, cat, raw, raw],
        (
            ids,
            own.reshape(-1, LANES),
            other.reshape(-1, LANES),
            table,
            group,
            category_map.reshape(n, LANES),
            region_map.reshape(1, n),
        ),
        [SMEM] + [VMEM] * 6,
    )
    lines = exchange_weeks(line.reshape(weeks, 1, LANES)).reshape(weeks, LANES)
    (sent,) = call(
        lambda *refs: week_combine_body(*refs, horizon),
        [(weeks * 2 * n, LANES)],
        [],
        (ids, lines, base, basis),
        [SMEM] + [VMEM] * 3,
    )
    got = exchange_weeks(sent.reshape(weeks, 2 * n, LANES))
    x, r = call(
        week_last_body,
        [(horizon, n, LANES)] * 2,
        [pltpu.SemaphoreType.DMA((2,))],
        (got,),
        [VMEM],
        out_specs=(HBM, HBM),
    )
    return x.reshape(base_bottom.shape), r.reshape(base_bottom.shape)


def solution(mesh):
    def mapped(device_mesh, body, stores):
        split_stores = P(stores, None, None)
        split_skus = P(None, None, stores)
        return jax.shard_map(
            body,
            mesh=device_mesh,
            in_specs=(split_stores,) * 4 + (split_skus,) * 2 + (P(), P()),
            out_specs=(split_stores,) * 2,
            check_vma=False,
        )

    side = mesh.shape["sku"]
    chips = mesh.devices.reshape(-1, CORES, side)

    def program(base_bottom, *others):
        stores, horizon, skus = base_bottom.shape
        fits = 16 * stores * skus * 4 <= 16 << 20
        if fits and horizon <= chips.shape[0] * side and side % 8 == 0:
            device_mesh = Mesh(chips, ("x", "core", "sku"))
            return mapped(device_mesh, by_weeks, ("x", "core", "sku"))(base_bottom, *others)
        return mapped(mesh, on_device, ("store", "sku"))(base_bottom, *others)

    return program
```

```python
import jax
import jax.numpy as jnp
from jax import lax
from jax.experimental import pallas as pl
from jax.experimental.pallas import tpu as pltpu
from jax.sharding import Mesh
from jax.sharding import PartitionSpec as P

LANES = 128
PAD = 16
WIDE = 256
VMEM = pl.BlockSpec(memory_space=pltpu.VMEM)
HBM = pl.BlockSpec(memory_space=pltpu.HBM)
SMEM = pl.BlockSpec(memory_space=pltpu.SMEM)
CORES = 2


def exchange(blocks, n):
    moved = lax.all_to_all(
        blocks.reshape(n, 1, -1), ("store", "sku"), split_axis=0, concat_axis=0, tiled=True
    )
    return moved.reshape(blocks.shape)


def call(body, outs, scratch, args, specs=None, held=False, out_specs=None):
    outs = [
        out if isinstance(out, jax.ShapeDtypeStruct) else jax.ShapeDtypeStruct(out, jnp.float32)
        for out in outs
    ]
    specs = specs or [VMEM] * len(args)
    args = [
        arg if spec is SMEM else pltpu.with_memory_space_constraint(arg, spec.memory_space)
        for arg, spec in zip(args, specs)
    ]
    return pl.pallas_call(
        body,
        out_shape=tuple(pltpu.VMEM(out.shape, out.dtype) if held else out for out in outs),
        in_specs=specs,
        out_specs=out_specs or tuple(VMEM for _ in outs),
        scratch_shapes=scratch,
        compiler_params=pltpu.CompilerParams(vmem_limit_bytes=24 << 20),
    )(*args)


def split(value):
    high = value.astype(jnp.bfloat16)
    return high, (value - high.astype(jnp.float32)).astype(jnp.bfloat16)


def split_all(value):
    high, low = split(value)
    rest = value - high.astype(jnp.float32) - low.astype(jnp.float32)
    return high, low, rest.astype(jnp.bfloat16)


def product(left, right, contract):
    return lax.dot_general(left, right, (contract, ((), ())), preferred_element_type=jnp.float32)


def rows_of(ref, n, h):
    return ref[pl.ds(h, n, stride=ref.shape[0] // n), :]


def put_rows(ref, n, h, value):
    ref[pl.ds(h, n, stride=ref.shape[0] // n), :] = value


def category_sums(field, table_ref, group_ref, n, rows):
    width = 4 if n % 4 == 0 else 1
    lanes = width * LANES

    def step(c, total):
        pieces = [field[pl.ds(c * width + i, PAD, stride=n), :] for i in range(width)]
        parts = split_all(jnp.concatenate(pieces, axis=1))
        start = pl.multiple_of(c * lanes, lanes)
        group = group_ref[:, pl.ds(start, lanes)]
        masks = [group == g for g in range(rows // PAD)]
        none = jnp.zeros((PAD, lanes), jnp.bfloat16)
        spread = jnp.concatenate(
            [jnp.where(mask, part, none) for part in parts for mask in masks], axis=0
        )
        return total + product(spread, table_ref[pl.ds(start, lanes), :], ((1,), (0,)))

    steps = n // width
    total = lax.fori_loop(
        0, steps, step, jnp.zeros((3 * rows, WIDE), jnp.float32), unroll=min(steps, 8)
    )
    return total[:rows] + (total[rows : 2 * rows] + total[2 * rows :])


def category_spread(values, cats, horizon, put):
    place = cats % LANES
    group = cats // LANES
    odd = [(group >> bit) & 1 != 0 for bit in range(3)]
    for h in range(horizon):
        found = []
        for g in range(0, values.shape[0], PAD):
            for lane in range(0, WIDE, LANES):
                row = jnp.broadcast_to(values[g + h : g + h + 1, lane : lane + LANES], cats.shape)
                found.append(jnp.take_along_axis(row, place, axis=1))
        for bit in range((len(found) - 1).bit_length()):
            mask = odd[bit] if bit < 3 else (group >> bit) & 1 != 0
            pairs = [found[i : i + 2] for i in range(0, len(found), 2)]
            found = [jnp.where(mask, pair[1], pair[0]) if len(pair) == 2 else pair[0] for pair in pairs]
        put(h, found[0])


def tiles_of(n):
    return [slice(t, t + 8) for t in range(0, n, 8)]


def put_tile(ref, n, h, tile, value):
    rows = ref.shape[0] // n
    ref[pl.ds(tile.start * rows + h, 8, stride=rows), :] = value


def region_sums(load, same, n, horizon):
    high, low = split(jnp.concatenate([load(h) for h in range(horizon)], axis=1))
    total = product(same, high, ((1,), (0,))) + product(same, low, ((1,), (0,)))
    return [total[:, h * LANES : (h + 1) * LANES] for h in range(horizon)]


def pack_body(base_hbm, out_ref, base_ref, sem):
    copy = pltpu.make_async_copy(base_hbm, base_ref, sem)
    copy.start()
    copy.wait()
    n = base_ref.shape[1]
    for h in range(base_ref.shape[0]):
        put_rows(out_ref, n, h, base_ref[h])


def prepare_body(
    base_hbm, base_cat_hbm, weight_cat_hbm, base_reg_hbm, weight_reg_hbm, cats_hbm, map_hbm,
    spread_out, wcat_out, wstore_out, bstore_out, same_out, table_out, group_out,
    cats_ref,
    field, values, base_ref, base_cat_ref, weight_cat_ref, base_reg_ref, weight_reg_ref, map_ref, sems,
):
    copies = [
        pltpu.make_async_copy(source, target, sems.at[i])
        for i, (source, target) in enumerate(
            (
                (cats_hbm, cats_ref),
                (base_hbm, base_ref),
                (weight_cat_hbm, weight_cat_ref),
                (base_cat_hbm, base_cat_ref),
                (map_hbm, map_ref),
                (weight_reg_hbm, weight_reg_ref),
                (base_reg_hbm, base_reg_ref),
            )
        )
    ]
    for copy in copies:
        copy.start()
    for copy in copies:
        copy.wait()
    horizon, n, _ = base_ref.shape
    n_regions = weight_reg_ref.shape[1]
    square = jnp.concatenate([cats_ref[...].astype(jnp.float32)] * (LANES // min(n, LANES)), axis=0)
    labels = lax.broadcasted_iota(jnp.int32, (LANES, WIDE), 1)
    columns = [
        jnp.transpose(square[i : i + LANES]).astype(jnp.int32) % WIDE
        for i in range(0, square.shape[0], LANES)
    ]
    for j in range(n):
        column = jnp.broadcast_to(columns[j // LANES][:, j % LANES : j % LANES + 1], (LANES, WIDE))
        table_out[j * LANES : (j + 1) * LANES, :] = jnp.where(
            column == labels, 1.0, 0.0
        ).astype(jnp.bfloat16)
        group = jnp.broadcast_to(cats_ref[j : j + 1, :] // WIDE, (PAD, LANES))
        group_out[:, j * LANES : (j + 1) * LANES] = group.astype(jnp.float32).astype(jnp.bfloat16)

    field[...] = jnp.zeros_like(field)
    for h in range(horizon):
        field[h * n : (h + 1) * n, :] = base_ref[h]
    sums = category_sums(field, table_out, group_out, n, wcat_out.shape[0])
    wcat_out[...] = jnp.zeros_like(wcat_out)
    values[...] = jnp.zeros_like(values)
    for g in range(0, wcat_out.shape[0], PAD):
        for lane in range(0, WIDE, LANES):
            tile = (g // PAD * WIDE + lane) // LANES
            lanes = slice(lane, lane + LANES)
            weight = weight_cat_ref[:, tile, :]
            wcat_out[g : g + horizon, lanes] = weight
            values[g : g + horizon, lanes] = weight * (
                base_cat_ref[:, tile, :] - sums[g : g + horizon, lanes]
            )
    for tile in tiles_of(n):

        def put(h, value):
            spread_out[h, tile, :] = value

        category_spread(values, cats_ref[tile, :], horizon, put)

    labels = lax.broadcasted_iota(jnp.int32, (n_regions, n), 0)
    table = jnp.where(labels == map_ref[...], 1.0, 0.0).astype(jnp.bfloat16)
    same_out[...] = product(table, table, ((0,), (0,))).astype(jnp.bfloat16)
    for source, target in ((weight_reg_ref, wstore_out), (base_reg_ref, bstore_out)):
        for h in range(horizon):
            high, low = split(source[h])
            rest = source[h] - high.astype(jnp.float32) - low.astype(jnp.float32)
            target[h] = (
                product(table, high, ((0,), (0,)))
                + product(table, low, ((0,), (0,)))
                + product(table, rest.astype(jnp.bfloat16), ((0,), (0,)))
            )


def region_start_body(got_ref, spread_ref, wstore_ref, bstore_ref, same_ref, reg_out, send_ref):
    horizon, n, _ = spread_ref.shape
    sums = region_sums(lambda h: rows_of(got_ref, n, h), same_ref[...], n, horizon)
    for h in range(horizon):
        put_rows(send_ref, n, h, spread_ref[h])
        part = wstore_ref[h] * (bstore_ref[h] - sums[h])
        reg_out[h] = part
        put_rows(send_ref, n, horizon + h, part)


def region_part(rs, wstore_ref, same_ref, put):
    horizon, n, _ = wstore_ref.shape
    sums = region_sums(lambda h: rs[h], same_ref[...], n, horizon)
    share = jnp.zeros((n, LANES), jnp.float32)
    for h in range(horizon):
        part = wstore_ref[h] * sums[h]
        share = share + part * rs[h]
        put(h, part)
    return share


def store_part(r_ref, sums, gamma, delta, eps, diag_ref, wcat_ref, cats_ref, put, put_line, values):
    horizon, n, _ = diag_ref.shape
    scaled = wcat_ref[...] * sums
    values[...] = scaled
    square = scaled * sums
    delta = jnp.sum(delta, axis=0, keepdims=True)
    for lane in range(0, WIDE, LANES):
        delta = delta + jnp.sum(square[:, lane : lane + LANES], axis=0, keepdims=True)
    lane = lax.broadcasted_iota(jnp.int32, (1, LANES), 1)
    line = jnp.zeros((1, LANES), jnp.float32)
    for i, part in enumerate((gamma, delta, eps)):
        if part is not None:
            whole = jnp.sum(jnp.sum(part, axis=0, keepdims=True), axis=1, keepdims=True)
            line = jnp.where(lane == i, whole, line)
    put_line(jnp.broadcast_to(line, (n, LANES)))
    for tile in tiles_of(n):

        def finish(h, value):
            put(h, tile, value + diag_ref[h, tile, :] * r_ref[h, tile, :])

        category_spread(values, cats_ref[tile, :], horizon, finish)


def totals(got_ref, n, row):
    total = jnp.sum(rows_of(got_ref, n, row), axis=0, keepdims=True)
    total = jnp.broadcast_to(total, (8, LANES))
    return [
        jnp.take_along_axis(total, jnp.full((8, LANES), i, jnp.int32), axis=1)[0:1] for i in range(3)
    ]


def wide(line):
    return jnp.concatenate([line] * (WIDE // LANES), axis=1)


def region_sender(ref, n, first, keep):
    def put(h, value):
        if keep is not None:
            keep[h] = value
        put_rows(ref, n, first + h, value)

    return put


def store_sender(ref, n, keep):
    def put(h, tile, value):
        keep[h, tile, :] = value
        if ref is not None:
            put_tile(ref, n, h, tile, value)

    return put


def clear_tail(field, horizon, n):
    field[horizon * n :, :] = jnp.zeros((field.shape[0] - horizon * n, LANES), jnp.float32)


def first_body(
    a_ref, reg_ref, got_ref, diag_ref, wcat_ref, wstore_ref, table_ref, group_ref, cats_ref, same_ref,
    r_out, rs_out, cr_out, a_out, reg_out, send_ref, values, field,
):
    horizon, n, _ = diag_ref.shape
    clear_tail(field, horizon, n)
    gamma = jnp.zeros((n, LANES), jnp.float32)
    delta = jnp.zeros((n, LANES), jnp.float32)
    for h in range(horizon):
        r = a_ref[h] + rows_of(got_ref, n, horizon + h)
        r_out[h] = r
        field[h * n : (h + 1) * n, :] = r
        gamma = gamma + r * r
        delta = delta + diag_ref[h] * r * r
    sums = category_sums(field, table_ref, group_ref, n, wcat_ref.shape[0])
    cr_out[...] = sums
    for h in range(horizon):
        rs_out[h] = rows_of(got_ref, n, h) + reg_ref[h]
    delta = delta + region_part(
        rs_out, wstore_ref, same_ref, region_sender(send_ref, n, horizon, reg_out)
    )
    store_part(
        r_out, sums, gamma, delta, None, diag_ref, wcat_ref, cats_ref,
        store_sender(send_ref, n, a_out),
        lambda line: put_rows(send_ref, n, 2 * horizon, line), values,
    )


def second_body(
    a_ref, reg_ref, got_ref, x_ref, r_ref, rs_ref, cr_ref,
    diag_ref, wcat_ref, wstore_ref, table_ref, group_ref, cats_ref, same_ref,
    x_out, r_out, rs_out, s_out, ss_out, cr_out, cs_out, scal_ref, a_out, reg_out, send_ref,
    values, field,
):
    horizon, n, _ = diag_ref.shape
    clear_tail(field, horizon, n)
    for h in range(horizon):
        field[h * n : (h + 1) * n, :] = a_ref[h] + rows_of(got_ref, n, horizon + h)
    sums = category_sums(field, table_ref, group_ref, n, wcat_ref.shape[0])
    cs_out[...] = sums
    gamma, delta, _ = totals(got_ref, n, 2 * horizon)
    alpha = gamma / delta
    scal_ref[0:1, :] = gamma
    scal_ref[1:2, :] = delta
    for h in range(horizon):
        ws = rows_of(got_ref, n, h) + reg_ref[h]
        ss_out[h] = ws
        rs_out[h] = rs_ref[h] - alpha * ws
    delta = region_part(
        rs_out, wstore_ref, same_ref, region_sender(send_ref, n, horizon, reg_out)
    )
    gamma = jnp.zeros((n, LANES), jnp.float32)
    eps = jnp.zeros((n, LANES), jnp.float32)
    for h in range(horizon):
        s = field[h * n : (h + 1) * n, :]
        s_out[h] = s
        r = r_ref[h]
        x_out[h] = x_ref[h] + alpha * r
        r = r - alpha * s
        r_out[h] = r
        gamma = gamma + r * r
        delta = delta + diag_ref[h] * r * r
        eps = eps + r * s
    sums = cr_ref[...] - wide(alpha) * sums
    cr_out[...] = sums
    store_part(
        r_out, sums, gamma, delta, eps, diag_ref, wcat_ref, cats_ref,
        store_sender(send_ref, n, a_out),
        lambda line: put_rows(send_ref, n, 2 * horizon, line), values,
    )


def third_body(
    a_ref, reg_ref, got_ref, x_ref, r_ref, rs_ref, p_ref, s_ref, ss_ref, cr_ref, cs_ref, scal_ref,
    diag_ref, wcat_ref, wstore_ref, table_ref, group_ref, cats_ref, same_ref,
    x_out, r_out, p_out, s_out, scal_out, a_out, send_ref, values, field, rs_out,
):
    horizon, n, _ = diag_ref.shape
    clear_tail(field, horizon, n)
    for h in range(horizon):
        field[h * n : (h + 1) * n, :] = a_ref[h] + rows_of(got_ref, n, horizon + h)
    sums = category_sums(field, table_ref, group_ref, n, wcat_ref.shape[0])
    gamma, delta, eps = totals(got_ref, n, 2 * horizon)
    beta = gamma / scal_ref[0:1, :]
    curve = delta + 2.0 * beta * eps + beta * beta * scal_ref[1:2, :]
    alpha = gamma / curve
    scal_out[0:1, :] = gamma
    scal_out[1:2, :] = curve
    for h in range(horizon):
        ws = rows_of(got_ref, n, h) + reg_ref[h]
        rs_out[h] = rs_ref[h] - alpha * (ws + beta * ss_ref[h])
    delta = region_part(rs_out, wstore_ref, same_ref, region_sender(send_ref, n, 0, None))
    gamma = jnp.zeros((n, LANES), jnp.float32)
    eps = jnp.zeros((n, LANES), jnp.float32)
    for h in range(horizon):
        s = field[h * n : (h + 1) * n, :] + beta * s_ref[h]
        s_out[h] = s
        r = r_ref[h]
        p = r + beta * p_ref[h]
        p_out[h] = p
        x_out[h] = x_ref[h] + alpha * p
        r = r - alpha * s
        r_out[h] = r
        gamma = gamma + r * r
        delta = delta + diag_ref[h] * r * r
        eps = eps + r * s
    sums = cr_ref[...] - wide(alpha) * (sums + wide(beta) * cs_ref[...])
    store_part(
        r_out, sums, gamma, delta, eps, diag_ref, wcat_ref, cats_ref,
        store_sender(None, n, a_out), lambda line: put_rows(send_ref, n, horizon, line), values,
    )


def last_body(a_ref, got_ref, x_ref, r_ref, p_ref, s_ref, scal_ref, x_out, r_out):
    horizon, n, _ = a_ref.shape
    gamma, delta, eps = totals(got_ref, n, horizon)
    beta = gamma / scal_ref[0:1, :]
    alpha = gamma / (delta + 2.0 * beta * eps + beta * beta * scal_ref[1:2, :])
    for h in range(horizon):
        r = r_ref[h]
        s = a_ref[h] + rows_of(got_ref, n, h) + beta * s_ref[h]
        x_out[h] = x_ref[h] + alpha * (r + beta * p_ref[h])
        r_out[h] = r - alpha * s


def on_device(
    base_bottom,
    weight_bottom,
    base_category,
    weight_category,
    base_region,
    weight_region,
    category_map,
    region_map,
):
    stores, horizon, skus = base_bottom.shape
    n = region_map.shape[0]
    groups = weight_category.shape[2] // WIDE
    tiles = weight_category.shape[2] // LANES
    field = (horizon, n, LANES)
    padded = (PAD * n, LANES)
    by_category = (horizon, tiles, LANES)
    scal = (2, LANES)
    values = pltpu.VMEM((groups * PAD, WIDE), jnp.float32)

    x = base_bottom.reshape(field)
    diag = weight_bottom.reshape(field)
    (sent,) = call(
        pack_body,
        [(n * horizon, LANES)],
        [pltpu.VMEM(field, jnp.float32), pltpu.SemaphoreType.DMA],
        (x,),
        [HBM],
        True,
    )
    got = exchange(sent, n)
    arguments = (
        x,
        base_category.reshape(by_category),
        weight_category.reshape(by_category),
        jnp.transpose(base_region, (1, 0, 2)),
        jnp.transpose(weight_region, (1, 0, 2)),
        category_map.reshape(n, LANES),
        region_map.reshape(1, n),
    )
    held = [pltpu.VMEM(arguments[i].shape, arguments[i].dtype) for i in (0, 1, 2, 3, 4, 6)]
    spread, wcat, wstore, bstore, same, table, group, cats = call(
        prepare_body,
        [
            field,
            (groups * PAD, WIDE),
            field,
            field,
            jax.ShapeDtypeStruct((n, n), jnp.bfloat16),
            jax.ShapeDtypeStruct((skus, WIDE), jnp.bfloat16),
            jax.ShapeDtypeStruct((PAD, skus), jnp.bfloat16),
            jax.ShapeDtypeStruct((n, LANES), jnp.int32),
        ],
        [
            pltpu.VMEM(padded, jnp.float32),
            values,
            *held,
            pltpu.SemaphoreType.DMA((len(arguments),)),
        ],
        arguments,
        [HBM] * len(arguments),
    )
    reg, sent = call(
        region_start_body,
        [field, (n * 2 * horizon, LANES)],
        [],
        (got, spread, wstore, bstore, same),
    )
    got = exchange(sent, n)
    fixed = (diag, wcat, wstore, table, group, cats, same)
    both = (n * (2 * horizon + 1), LANES)
    work = [values, pltpu.VMEM(padded, jnp.float32)]
    sums = (groups * PAD, WIDE)
    r, rs, cr, a, reg, sent = call(
        first_body, [field, field, sums, field, field, both], work, (spread, reg, got) + fixed
    )
    got = exchange(sent, n)
    p = r
    x, r, rs, s, ss, cr, cs, scalars, a, reg, sent = call(
        second_body,
        [field, field, field, field, field, sums, sums, scal, field, field, both],
        work,
        (a, reg, got, x, r, rs, cr) + fixed,
    )
    got = exchange(sent, n)
    x, r, p, s, scalars, a, sent = call(
        third_body,
        [field, field, field, field, scal, field, (n * (horizon + 1), LANES)],
        work + [pltpu.VMEM(field, jnp.float32)],
        (a, reg, got, x, r, rs, p, s, ss, cr, cs, scalars) + fixed,
    )
    got = exchange(sent, n)
    x, r = call(last_body, [field, field], [], (a, got, x, r, p, s, scalars))
    return x.reshape(base_bottom.shape), r.reshape(base_bottom.shape)


def week_rows(tiles, n, regions):
    sizes = (n, n, tiles, tiles, regions, regions)
    return [sum(sizes[:i]) for i in range(len(sizes) + 1)]


def week_pack_body(*refs):
    sources, out, sems = refs[:-2], refs[-2], refs[-1]
    horizon = sources[0].shape[0]
    copies, start = [], 0
    for i, source in enumerate(sources):
        rows = source.shape[1]
        target = out.at[pl.ds(0, horizon), pl.ds(start, rows)]
        copies.append(pltpu.make_async_copy(source, target, sems.at[i]))
        start += rows
    for copy in copies:
        copy.start()
    for copy in copies:
        copy.wait()


def week_table_body(map_ref, cats_ref, table_out, group_out, same_out, region_out, regions):
    n = cats_ref.shape[0]
    lane = lax.broadcasted_iota(jnp.int32, (n, LANES), 1)
    line = lax.broadcasted_iota(jnp.int32, (n, LANES), 0)
    across = jnp.zeros((n, LANES), jnp.int32)
    down = jnp.zeros((n, LANES), jnp.int32)
    for s in range(n):
        across = jnp.where(lane % n == s, map_ref[s], across)
        down = jnp.where(line == s, map_ref[s], down)
    same_out[...] = jnp.where(across == down, 1.0, 0.0).astype(jnp.bfloat16)
    region_out[...] = jnp.where(lane % regions == down, 1.0, 0.0).astype(jnp.bfloat16)
    square = jnp.concatenate([cats_ref[...].astype(jnp.float32)] * (LANES // min(n, LANES)), axis=0)
    labels = lax.broadcasted_iota(jnp.int32, (LANES, WIDE), 1)
    columns = [
        jnp.transpose(square[i : i + LANES]).astype(jnp.int32) % WIDE
        for i in range(0, square.shape[0], LANES)
    ]
    for j in range(n):
        column = jnp.broadcast_to(columns[j // LANES][:, j % LANES : j % LANES + 1], (LANES, WIDE))
        table_out[j * LANES : (j + 1) * LANES, :] = jnp.where(
            column == labels, 1.0, 0.0
        ).astype(jnp.bfloat16)
        group = jnp.broadcast_to(cats_ref[j : j + 1, :] // WIDE, (group_out.shape[0], LANES))
        group_out[:, j * LANES : (j + 1) * LANES] = group.astype(jnp.float32).astype(jnp.bfloat16)


def ratio(top, bottom):
    return jnp.where(bottom > 0.0, top / bottom, 0.0)


def whole_sum(part):
    total = jnp.sum(jnp.sum(part, axis=0, keepdims=True), axis=1, keepdims=True)
    return jnp.broadcast_to(total, (1, LANES))


def week_body(
    core_ref, own_ref, other_hbm, table_ref, group_ref, same_ref, region_ref, cats_ref,
    base_out, basis_out, line_out,
    diag, wstore, bstore, wcat, bcat, raw_weight, raw_base, other_ref, sem,
    side,
):
    core = core_ref[0]
    n, skus = base_out.shape
    per = own_ref.shape[0] // line_out.shape[0]
    regions = raw_weight.shape[0]
    tiles = wcat.shape[0] // n * (WIDE // LANES)
    starts = week_rows(tiles, n, regions)
    chunk = min(skus, 8 * LANES)
    chunks = [slice(c, c + chunk) for c in range(0, skus, chunk)]
    copy = pltpu.make_async_copy(other_hbm, other_ref, sem)
    copy.start()

    for ref, c in ((own_ref, core), (other_ref, 1 - core)):
        if ref is other_ref:
            copy.wait()
        for x in range(n // (CORES * side)):
            for t in range(0, side, 8):
                first = (x * side + t) * per
                top = pl.multiple_of(x * CORES * side + c * side + t, 8)

                def rows(row):
                    return ref[pl.ds(first + row, 8, stride=per), :]

                for j in range(n):
                    lanes = slice(j * LANES, (j + 1) * LANES)
                    base_out[pl.ds(top, 8), lanes] = rows(starts[0] + j)
                    diag[pl.ds(top, 8), lanes] = rows(starts[1] + j)
                for g in range(tiles):
                    lane = g * LANES % WIDE
                    down = pl.multiple_of(g * LANES // WIDE * n + top, 8)
                    wcat[pl.ds(down, 8), lane : lane + LANES] = rows(starts[2] + g)
                    bcat[pl.ds(down, 8), lane : lane + LANES] = rows(starts[3] + g)
            for k in range(side):
                first = (x * side + k) * per
                j = x * CORES * side + c * side + k
                lanes = pl.ds(pl.multiple_of(j * LANES, LANES), LANES)
                raw_base[:, lanes] = ref[first + starts[4] : first + starts[5], :]
                raw_weight[:, lanes] = ref[first + starts[5] : first + starts[6], :]

    region_table = region_ref[:, : 3 * regions]
    same = same_ref[:, : 2 * n]
    for source, target in ((raw_weight, wstore), (raw_base, bstore)):
        for lanes in chunks:
            parts = jnp.concatenate(split_all(source[:, lanes]), axis=0)
            target[:, lanes] = product(region_table, parts, ((1,), (0,)))

    def by_category(field):
        rows = wcat.shape[0]
        total = None
        for lanes in chunks:
            group = group_ref[:, lanes]
            masks = [group == g for g in range(rows // n)]
            none = jnp.zeros(group.shape, jnp.bfloat16)
            spread = jnp.concatenate(
                [jnp.where(mask, part, none) for part in split(field[:, lanes]) for mask in masks],
                axis=0,
            )
            part = product(spread, table_ref[lanes, :], ((1,), (0,)))
            total = part if total is None else total + part
        return total[:rows] + total[rows:]

    def spread_tile(values, j):
        members = jnp.broadcast_to(cats_ref[j : j + 1, :], (n, LANES))
        place = members % LANES
        group = members // LANES
        found = [
            jnp.take_along_axis(values[g : g + n, lane : lane + LANES], place, axis=1)
            for g in range(0, values.shape[0], n)
            for lane in range(0, WIDE, LANES)
        ]
        bit = 0
        while len(found) > 1:
            mask = (group >> bit) & 1 != 0
            pairs = [found[i : i + 2] for i in range(0, len(found), 2)]
            found = [jnp.where(mask, pair[1], pair[0]) if len(pair) == 2 else pair[0] for pair in pairs]
            bit += 1
        return found[0]

    def by_region(part):
        return product(same, jnp.concatenate(split(part), axis=0), ((1,), (0,)))

    zero = jnp.zeros((n, LANES), jnp.float32)
    values = wcat[...] * (bcat[...] - by_category(base_out))
    norm = zero
    for lanes in chunks:
        sums = by_region(base_out[:, lanes])
        for t in range(0, chunk, LANES):
            tile = slice(lanes.start + t, lanes.start + t + LANES)
            part = wstore[:, tile] * (bstore[:, tile] - sums[:, t : t + LANES])
            part = part + spread_tile(values, tile.start // LANES)
            basis_out[0, :, tile] = part
            norm = norm + part * part
    norms, quotients = [whole_sum(norm)], []
    for k in range(3):
        field = basis_out.at[k]
        image = basis_out.at[k + 1]
        values = wcat[...] * by_category(field)
        dot = zero
        for lanes in chunks:
            sums = by_region(field[:, lanes])
            for t in range(0, chunk, LANES):
                tile = slice(lanes.start + t, lanes.start + t + LANES)
                part = field[:, tile]
                result = diag[:, tile] * part + wstore[:, tile] * sums[:, t : t + LANES]
                result = result + spread_tile(values, tile.start // LANES)
                image[:, tile] = result
                dot = dot + part * result
        quotients.append(ratio(whole_sum(dot), norms[k]))
        back = ratio(norms[k], norms[k - 1]) if k else None
        norm = zero
        for t in range(0, skus, LANES):
            tile = slice(t, t + LANES)
            result = image[:, tile] - quotients[k] * field[:, tile]
            if k:
                result = result - back * basis_out[k - 1, :, tile]
            image[:, tile] = result
            norm = norm + result * result
        norms.append(whole_sum(norm))
    lane = lax.broadcasted_iota(jnp.int32, (1, LANES), 1)
    line = jnp.zeros((1, LANES), jnp.float32)
    for i, value in enumerate(norms[:3] + quotients):
        line = jnp.where(lane == i, value, line)
    line_out[...] = jnp.broadcast_to(line, line_out.shape)


def week_combine_body(core_ref, place_ref, lines_ref, base_ref, basis_ref, send_ref, horizon, side):
    core = core_ref[0]
    weeks = lines_ref.shape[0]
    n, skus = base_ref.shape
    week = lax.broadcasted_iota(jnp.int32, (weeks, LANES), 0)
    lines = jnp.where(week < horizon, lines_ref[...], 0.0)
    n1, n2, n3, a1, a2, a3 = [
        jnp.take_along_axis(lines, jnp.full((weeks, LANES), i, jnp.int32), axis=1) for i in range(6)
    ]
    e2, e3 = ratio(n2, n1), ratio(n3, n2)

    def dot(left, right):
        terms = n1 * left[0] * right[0] + n2 * left[1] * right[1] + n3 * left[2] * right[2]
        return jnp.sum(terms, axis=0, keepdims=True)

    zero = jnp.zeros((weeks, LANES), jnp.float32)
    x = [zero, zero, zero]
    r = [zero + 1.0, zero, zero, zero]
    p = r[:3]
    rr = dot(r, r)
    for k in range(3):
        image = [
            a1 * p[0] + e2 * p[1],
            p[0] + a2 * p[1] + e3 * p[2],
            p[1] + a3 * p[2],
            p[2],
        ]
        alpha = rr / dot(p, image)
        x = [left + alpha * right for left, right in zip(x, p)]
        r = [left - alpha * right for left, right in zip(r, image)]
        if k < 2:
            new = dot(r, r)
            p = [left + new / rr * right for left, right in zip(r[:3], p)]
            rr = new
    mine = week == place_ref[0]
    x = [jnp.sum(jnp.where(mine, value, 0.0), axis=0, keepdims=True) for value in x]
    r = [jnp.sum(jnp.where(mine, value, 0.0), axis=0, keepdims=True) for value in r]
    rows = send_ref.shape[0] // weeks
    for i in range(n // (CORES * side)):
        for t in range(0, side, 8):
            top = pl.multiple_of(i * CORES * side + core * side + t, 8)
            for j in range(n):
                lanes = slice(j * LANES, (j + 1) * LANES)
                parts = [basis_ref[k, pl.ds(top, 8), lanes] for k in range(4)]
                left = base_ref[pl.ds(top, 8), lanes]
                right = r[3] * parts[3]
                for k in range(3):
                    left = left + x[k] * parts[k]
                    right = right + r[k] * parts[k]
                first = (i * side + t) * rows + j
                send_ref[pl.ds(first, 8, stride=rows), :] = left
                send_ref[pl.ds(first + n, 8, stride=rows), :] = right


def week_last_body(got_ref, x_out, r_out, sems):
    horizon, n, _ = x_out.shape
    copies = [
        pltpu.make_async_copy(
            got_ref.at[pl.ds(0, horizon), pl.ds(i * n, n)], target, sems.at[i]
        )
        for i, target in enumerate((x_out, r_out))
    ]
    for copy in copies:
        copy.start()
    for copy in copies:
        copy.wait()


def exchange_weeks(blocks):
    return lax.all_to_all(blocks, ("x", "sku"), split_axis=0, concat_axis=0, tiled=True)


def by_weeks(
    base_bottom,
    weight_bottom,
    base_category,
    weight_category,
    base_region,
    weight_region,
    category_map,
    region_map,
):
    stores, horizon, skus = base_bottom.shape
    n = region_map.shape[0]
    regions = weight_region.shape[0]
    tiles = weight_category.shape[2] // LANES
    groups = weight_category.shape[2] // WIDE
    side = lax.axis_size("sku")
    weeks = lax.axis_size("x") * side
    place = lax.axis_index("x") * side + lax.axis_index("sku")
    place = place.astype(jnp.int32).reshape(1)
    core = lax.axis_index("core").astype(jnp.int32).reshape(1)
    cats = category_map.reshape(n, LANES)
    sources = (
        base_bottom.reshape(horizon, n, LANES),
        weight_bottom.reshape(horizon, n, LANES),
        weight_category.reshape(horizon, tiles, LANES),
        base_category.reshape(horizon, tiles, LANES),
        jnp.transpose(base_region, (1, 0, 2)),
        jnp.transpose(weight_region, (1, 0, 2)),
    )
    per = week_rows(tiles, n, regions)[-1]
    (sent,) = call(
        week_pack_body,
        [(weeks, per, LANES)],
        [pltpu.SemaphoreType.DMA((len(sources),))],
        sources,
        [HBM] * len(sources),
        out_specs=(HBM,),
    )
    own = exchange_weeks(sent)
    other = lax.ppermute(own, "core", [(0, 1), (1, 0)])
    table, group, same, region = call(
        lambda *refs: week_table_body(*refs, regions),
        [
            jax.ShapeDtypeStruct((skus, WIDE), jnp.bfloat16),
            jax.ShapeDtypeStruct((n, skus), jnp.bfloat16),
            jax.ShapeDtypeStruct((n, LANES), jnp.bfloat16),
            jax.ShapeDtypeStruct((n, LANES), jnp.bfloat16),
        ],
        [],
        (region_map, cats),
        [SMEM, VMEM],
    )
    full = pltpu.VMEM((n, skus), jnp.float32)
    raw = pltpu.VMEM((regions, skus), jnp.float32)
    cat = pltpu.VMEM((groups * n, WIDE), jnp.float32)
    base, basis, line = call(
        lambda *refs: week_body(*refs, side),
        [(n, skus), (4, n, skus), (weeks, LANES)],
        [
            full, full, full, cat, cat, raw, raw,
            pltpu.VMEM((weeks * per, LANES), jnp.float32),
            pltpu.SemaphoreType.DMA,
        ],
        (
            core, own.reshape(-1, LANES), other.reshape(-1, LANES),
            table, group, same, region, cats,
        ),
        [SMEM, VMEM, HBM] + [VMEM] * 5,
    )
    lines = exchange_weeks(line.reshape(weeks, 1, LANES)).reshape(weeks, LANES)
    (sent,) = call(
        lambda *refs: week_combine_body(*refs, horizon, side),
        [(weeks * 2 * n, LANES)],
        [],
        (core, place, lines, base, basis),
        [SMEM] * 2 + [VMEM] * 3,
    )
    got = exchange_weeks(sent.reshape(weeks, 2 * n, LANES))
    x, r = call(
        week_last_body,
        [(horizon, n, LANES)] * 2,
        [pltpu.SemaphoreType.DMA((2,))],
        (got,),
        [VMEM],
        out_specs=(HBM, HBM),
    )
    return x.reshape(base_bottom.shape), r.reshape(base_bottom.shape)


def solution(mesh):
    def mapped(device_mesh, body, stores):
        split_stores = P(stores, None, None)
        split_skus = P(None, None, stores)
        return jax.shard_map(
            body,
            mesh=device_mesh,
            in_specs=(split_stores,) * 4 + (split_skus,) * 2 + (P(), P()),
            out_specs=(split_stores,) * 2,
            check_vma=False,
        )

    side = mesh.shape["sku"]
    chips = mesh.devices.reshape(-1, CORES, side)

    def program(base_bottom, *others):
        stores, horizon, skus = base_bottom.shape
        fits = 16 * stores * skus * 4 <= 16 << 20
        fits = fits and 3 * others[3].shape[0] <= LANES and LANES % stores == 0
        if fits and horizon <= chips.shape[0] * side and side % 8 == 0:
            device_mesh = Mesh(chips, ("x", "core", "sku"))
            return mapped(device_mesh, by_weeks, ("x", "core", "sku"))(base_bottom, *others)
        return mapped(mesh, on_device, ("store", "sku"))(base_bottom, *others)

    return program
```

```python
import jax
import jax.numpy as jnp
from jax import lax
from jax.experimental import pallas as pl
from jax.experimental.pallas import tpu as pltpu
from jax.sharding import Mesh
from jax.sharding import PartitionSpec as P

LANES = 128
PAD = 16
WIDE = 256
VMEM = pl.BlockSpec(memory_space=pltpu.VMEM)
HBM = pl.BlockSpec(memory_space=pltpu.HBM)
SMEM = pl.BlockSpec(memory_space=pltpu.SMEM)
ANY = pl.BlockSpec(memory_space=pl.ANY)
CORES = 2


def exchange(blocks, n):
    moved = lax.all_to_all(
        blocks.reshape(n, 1, -1), ("store", "sku"), split_axis=0, concat_axis=0, tiled=True
    )
    return moved.reshape(blocks.shape)


def call(body, outs, scratch, args, specs=None, held=False, out_specs=None):
    outs = [
        out if isinstance(out, jax.ShapeDtypeStruct) else jax.ShapeDtypeStruct(out, jnp.float32)
        for out in outs
    ]
    specs = specs or [VMEM] * len(args)
    args = [
        arg if spec in (SMEM, ANY) else pltpu.with_memory_space_constraint(arg, spec.memory_space)
        for arg, spec in zip(args, specs)
    ]
    return pl.pallas_call(
        body,
        out_shape=tuple(pltpu.VMEM(out.shape, out.dtype) if held else out for out in outs),
        in_specs=specs,
        out_specs=out_specs or tuple(VMEM for _ in outs),
        scratch_shapes=scratch,
        compiler_params=pltpu.CompilerParams(vmem_limit_bytes=24 << 20),
    )(*args)


def split(value):
    high = value.astype(jnp.bfloat16)
    return high, (value - high.astype(jnp.float32)).astype(jnp.bfloat16)


def split_all(value):
    high, low = split(value)
    rest = value - high.astype(jnp.float32) - low.astype(jnp.float32)
    return high, low, rest.astype(jnp.bfloat16)


def product(left, right, contract):
    return lax.dot_general(left, right, (contract, ((), ())), preferred_element_type=jnp.float32)


def rows_of(ref, n, h):
    return ref[pl.ds(h, n, stride=ref.shape[0] // n), :]


def put_rows(ref, n, h, value):
    ref[pl.ds(h, n, stride=ref.shape[0] // n), :] = value


def category_sums(field, table_ref, group_ref, n, rows):
    width = 4 if n % 4 == 0 else 1
    lanes = width * LANES

    def step(c, total):
        pieces = [field[pl.ds(c * width + i, PAD, stride=n), :] for i in range(width)]
        parts = split_all(jnp.concatenate(pieces, axis=1))
        start = pl.multiple_of(c * lanes, lanes)
        group = group_ref[:, pl.ds(start, lanes)]
        masks = [group == g for g in range(rows // PAD)]
        none = jnp.zeros((PAD, lanes), jnp.bfloat16)
        spread = jnp.concatenate(
            [jnp.where(mask, part, none) for part in parts for mask in masks], axis=0
        )
        return total + product(spread, table_ref[pl.ds(start, lanes), :], ((1,), (0,)))

    steps = n // width
    total = lax.fori_loop(
        0, steps, step, jnp.zeros((3 * rows, WIDE), jnp.float32), unroll=min(steps, 8)
    )
    return total[:rows] + (total[rows : 2 * rows] + total[2 * rows :])


def category_spread(values, cats, horizon, put):
    place = cats & (LANES - 1)
    group = cats >> (LANES.bit_length() - 1)
    for h in range(horizon):
        found = []
        for g in range(0, values.shape[0], PAD):
            for lane in range(0, WIDE, LANES):
                row = jnp.broadcast_to(values[g + h : g + h + 1, lane : lane + LANES], cats.shape)
                found.append(jnp.take_along_axis(row, place, axis=1))
        for bit in range((len(found) - 1).bit_length()):
            mask = group & (1 << bit) != 0
            pairs = [found[i : i + 2] for i in range(0, len(found), 2)]
            found = [jnp.where(mask, pair[1], pair[0]) if len(pair) == 2 else pair[0] for pair in pairs]
        put(h, found[0])


def tiles_of(n):
    return [slice(t, t + 8) for t in range(0, n, 8)]


def put_tile(ref, n, h, tile, value):
    rows = ref.shape[0] // n
    ref[pl.ds(tile.start * rows + h, 8, stride=rows), :] = value


def region_sums(load, same, n, horizon):
    high, low = split(jnp.concatenate([load(h) for h in range(horizon)], axis=1))
    total = product(same, high, ((1,), (0,))) + product(same, low, ((1,), (0,)))
    return [total[:, h * LANES : (h + 1) * LANES] for h in range(horizon)]


def pack_body(base_hbm, out_ref, base_ref, sem):
    copy = pltpu.make_async_copy(base_hbm, base_ref, sem)
    copy.start()
    copy.wait()
    n = base_ref.shape[1]
    for h in range(base_ref.shape[0]):
        put_rows(out_ref, n, h, base_ref[h])


def prepare_body(
    base_hbm, base_cat_hbm, weight_cat_hbm, base_reg_hbm, weight_reg_hbm, cats_hbm, map_hbm,
    spread_out, wcat_out, wstore_out, bstore_out, same_out, table_out, group_out,
    cats_ref,
    field, values, base_ref, base_cat_ref, weight_cat_ref, base_reg_ref, weight_reg_ref, map_ref, sems,
):
    copies = [
        pltpu.make_async_copy(source, target, sems.at[i])
        for i, (source, target) in enumerate(
            (
                (cats_hbm, cats_ref),
                (base_hbm, base_ref),
                (weight_cat_hbm, weight_cat_ref),
                (base_cat_hbm, base_cat_ref),
                (map_hbm, map_ref),
                (weight_reg_hbm, weight_reg_ref),
                (base_reg_hbm, base_reg_ref),
            )
        )
    ]
    for copy in copies:
        copy.start()
    for copy in copies:
        copy.wait()
    horizon, n, _ = base_ref.shape
    n_regions = weight_reg_ref.shape[1]
    square = jnp.concatenate([cats_ref[...].astype(jnp.float32)] * (LANES // min(n, LANES)), axis=0)
    labels = lax.broadcasted_iota(jnp.int32, (LANES, WIDE), 1)
    columns = [
        jnp.transpose(square[i : i + LANES]).astype(jnp.int32) % WIDE
        for i in range(0, square.shape[0], LANES)
    ]
    for j in range(n):
        column = jnp.broadcast_to(columns[j // LANES][:, j % LANES : j % LANES + 1], (LANES, WIDE))
        table_out[j * LANES : (j + 1) * LANES, :] = jnp.where(
            column == labels, 1.0, 0.0
        ).astype(jnp.bfloat16)
        group = jnp.broadcast_to(cats_ref[j : j + 1, :] // WIDE, (PAD, LANES))
        group_out[:, j * LANES : (j + 1) * LANES] = group.astype(jnp.float32).astype(jnp.bfloat16)

    field[...] = jnp.zeros_like(field)
    for h in range(horizon):
        field[h * n : (h + 1) * n, :] = base_ref[h]
    sums = category_sums(field, table_out, group_out, n, wcat_out.shape[0])
    wcat_out[...] = jnp.zeros_like(wcat_out)
    values[...] = jnp.zeros_like(values)
    for g in range(0, wcat_out.shape[0], PAD):
        for lane in range(0, WIDE, LANES):
            tile = (g // PAD * WIDE + lane) // LANES
            lanes = slice(lane, lane + LANES)
            weight = weight_cat_ref[:, tile, :]
            wcat_out[g : g + horizon, lanes] = weight
            values[g : g + horizon, lanes] = weight * (
                base_cat_ref[:, tile, :] - sums[g : g + horizon, lanes]
            )
    for tile in tiles_of(n):

        def put(h, value):
            spread_out[h, tile, :] = value

        category_spread(values, cats_ref[tile, :], horizon, put)

    labels = lax.broadcasted_iota(jnp.int32, (n_regions, n), 0)
    table = jnp.where(labels == map_ref[...], 1.0, 0.0).astype(jnp.bfloat16)
    same_out[...] = product(table, table, ((0,), (0,))).astype(jnp.bfloat16)
    for source, target in ((weight_reg_ref, wstore_out), (base_reg_ref, bstore_out)):
        for h in range(horizon):
            high, low = split(source[h])
            rest = source[h] - high.astype(jnp.float32) - low.astype(jnp.float32)
            target[h] = (
                product(table, high, ((0,), (0,)))
                + product(table, low, ((0,), (0,)))
                + product(table, rest.astype(jnp.bfloat16), ((0,), (0,)))
            )


def region_start_body(got_ref, spread_ref, wstore_ref, bstore_ref, same_ref, reg_out, send_ref):
    horizon, n, _ = spread_ref.shape
    sums = region_sums(lambda h: rows_of(got_ref, n, h), same_ref[...], n, horizon)
    for h in range(horizon):
        put_rows(send_ref, n, h, spread_ref[h])
        part = wstore_ref[h] * (bstore_ref[h] - sums[h])
        reg_out[h] = part
        put_rows(send_ref, n, horizon + h, part)


def region_part(rs, wstore_ref, same_ref, put):
    horizon, n, _ = wstore_ref.shape
    sums = region_sums(lambda h: rs[h], same_ref[...], n, horizon)
    share = jnp.zeros((n, LANES), jnp.float32)
    for h in range(horizon):
        part = wstore_ref[h] * sums[h]
        share = share + part * rs[h]
        put(h, part)
    return share


def store_part(r_ref, sums, gamma, delta, eps, diag_ref, wcat_ref, cats_ref, put, put_line, values):
    horizon, n, _ = diag_ref.shape
    scaled = wcat_ref[...] * sums
    values[...] = scaled
    square = scaled * sums
    delta = jnp.sum(delta, axis=0, keepdims=True)
    for lane in range(0, WIDE, LANES):
        delta = delta + jnp.sum(square[:, lane : lane + LANES], axis=0, keepdims=True)
    lane = lax.broadcasted_iota(jnp.int32, (1, LANES), 1)
    line = jnp.zeros((1, LANES), jnp.float32)
    for i, part in enumerate((gamma, delta, eps)):
        if part is not None:
            whole = jnp.sum(jnp.sum(part, axis=0, keepdims=True), axis=1, keepdims=True)
            line = jnp.where(lane == i, whole, line)
    put_line(jnp.broadcast_to(line, (n, LANES)))
    for tile in tiles_of(n):

        def finish(h, value):
            put(h, tile, value + diag_ref[h, tile, :] * r_ref[h, tile, :])

        category_spread(values, cats_ref[tile, :], horizon, finish)


def totals(got_ref, n, row):
    total = jnp.sum(rows_of(got_ref, n, row), axis=0, keepdims=True)
    total = jnp.broadcast_to(total, (8, LANES))
    return [
        jnp.take_along_axis(total, jnp.full((8, LANES), i, jnp.int32), axis=1)[0:1] for i in range(3)
    ]


def wide(line):
    return jnp.concatenate([line] * (WIDE // LANES), axis=1)


def region_sender(ref, n, first, keep):
    def put(h, value):
        if keep is not None:
            keep[h] = value
        put_rows(ref, n, first + h, value)

    return put


def store_sender(ref, n, keep):
    def put(h, tile, value):
        keep[h, tile, :] = value
        if ref is not None:
            put_tile(ref, n, h, tile, value)

    return put


def clear_tail(field, horizon, n):
    field[horizon * n :, :] = jnp.zeros((field.shape[0] - horizon * n, LANES), jnp.float32)


def first_body(
    a_ref, reg_ref, got_ref, diag_ref, wcat_ref, wstore_ref, table_ref, group_ref, cats_ref, same_ref,
    r_out, rs_out, cr_out, a_out, reg_out, send_ref, values, field,
):
    horizon, n, _ = diag_ref.shape
    clear_tail(field, horizon, n)
    gamma = jnp.zeros((n, LANES), jnp.float32)
    delta = jnp.zeros((n, LANES), jnp.float32)
    for h in range(horizon):
        r = a_ref[h] + rows_of(got_ref, n, horizon + h)
        r_out[h] = r
        field[h * n : (h + 1) * n, :] = r
        gamma = gamma + r * r
        delta = delta + diag_ref[h] * r * r
    sums = category_sums(field, table_ref, group_ref, n, wcat_ref.shape[0])
    cr_out[...] = sums
    for h in range(horizon):
        rs_out[h] = rows_of(got_ref, n, h) + reg_ref[h]
    delta = delta + region_part(
        rs_out, wstore_ref, same_ref, region_sender(send_ref, n, horizon, reg_out)
    )
    store_part(
        r_out, sums, gamma, delta, None, diag_ref, wcat_ref, cats_ref,
        store_sender(send_ref, n, a_out),
        lambda line: put_rows(send_ref, n, 2 * horizon, line), values,
    )


def second_body(
    a_ref, reg_ref, got_ref, x_ref, r_ref, rs_ref, cr_ref,
    diag_ref, wcat_ref, wstore_ref, table_ref, group_ref, cats_ref, same_ref,
    x_out, r_out, rs_out, s_out, ss_out, cr_out, cs_out, scal_ref, a_out, reg_out, send_ref,
    values, field,
):
    horizon, n, _ = diag_ref.shape
    clear_tail(field, horizon, n)
    for h in range(horizon):
        field[h * n : (h + 1) * n, :] = a_ref[h] + rows_of(got_ref, n, horizon + h)
    sums = category_sums(field, table_ref, group_ref, n, wcat_ref.shape[0])
    cs_out[...] = sums
    gamma, delta, _ = totals(got_ref, n, 2 * horizon)
    alpha = gamma / delta
    scal_ref[0:1, :] = gamma
    scal_ref[1:2, :] = delta
    for h in range(horizon):
        ws = rows_of(got_ref, n, h) + reg_ref[h]
        ss_out[h] = ws
        rs_out[h] = rs_ref[h] - alpha * ws
    delta = region_part(
        rs_out, wstore_ref, same_ref, region_sender(send_ref, n, horizon, reg_out)
    )
    gamma = jnp.zeros((n, LANES), jnp.float32)
    eps = jnp.zeros((n, LANES), jnp.float32)
    for h in range(horizon):
        s = field[h * n : (h + 1) * n, :]
        s_out[h] = s
        r = r_ref[h]
        x_out[h] = x_ref[h] + alpha * r
        r = r - alpha * s
        r_out[h] = r
        gamma = gamma + r * r
        delta = delta + diag_ref[h] * r * r
        eps = eps + r * s
    sums = cr_ref[...] - wide(alpha) * sums
    cr_out[...] = sums
    store_part(
        r_out, sums, gamma, delta, eps, diag_ref, wcat_ref, cats_ref,
        store_sender(send_ref, n, a_out),
        lambda line: put_rows(send_ref, n, 2 * horizon, line), values,
    )


def third_body(
    a_ref, reg_ref, got_ref, x_ref, r_ref, rs_ref, p_ref, s_ref, ss_ref, cr_ref, cs_ref, scal_ref,
    diag_ref, wcat_ref, wstore_ref, table_ref, group_ref, cats_ref, same_ref,
    x_out, r_out, p_out, s_out, scal_out, a_out, send_ref, values, field, rs_out,
):
    horizon, n, _ = diag_ref.shape
    clear_tail(field, horizon, n)
    for h in range(horizon):
        field[h * n : (h + 1) * n, :] = a_ref[h] + rows_of(got_ref, n, horizon + h)
    sums = category_sums(field, table_ref, group_ref, n, wcat_ref.shape[0])
    gamma, delta, eps = totals(got_ref, n, 2 * horizon)
    beta = gamma / scal_ref[0:1, :]
    curve = delta + 2.0 * beta * eps + beta * beta * scal_ref[1:2, :]
    alpha = gamma / curve
    scal_out[0:1, :] = gamma
    scal_out[1:2, :] = curve
    for h in range(horizon):
        ws = rows_of(got_ref, n, h) + reg_ref[h]
        rs_out[h] = rs_ref[h] - alpha * (ws + beta * ss_ref[h])
    delta = region_part(rs_out, wstore_ref, same_ref, region_sender(send_ref, n, 0, None))
    gamma = jnp.zeros((n, LANES), jnp.float32)
    eps = jnp.zeros((n, LANES), jnp.float32)
    for h in range(horizon):
        s = field[h * n : (h + 1) * n, :] + beta * s_ref[h]
        s_out[h] = s
        r = r_ref[h]
        p = r + beta * p_ref[h]
        p_out[h] = p
        x_out[h] = x_ref[h] + alpha * p
        r = r - alpha * s
        r_out[h] = r
        gamma = gamma + r * r
        delta = delta + diag_ref[h] * r * r
        eps = eps + r * s
    sums = cr_ref[...] - wide(alpha) * (sums + wide(beta) * cs_ref[...])
    store_part(
        r_out, sums, gamma, delta, eps, diag_ref, wcat_ref, cats_ref,
        store_sender(None, n, a_out), lambda line: put_rows(send_ref, n, horizon, line), values,
    )


def last_body(a_ref, got_ref, x_ref, r_ref, p_ref, s_ref, scal_ref, x_out, r_out):
    horizon, n, _ = a_ref.shape
    gamma, delta, eps = totals(got_ref, n, horizon)
    beta = gamma / scal_ref[0:1, :]
    alpha = gamma / (delta + 2.0 * beta * eps + beta * beta * scal_ref[1:2, :])
    for h in range(horizon):
        r = r_ref[h]
        s = a_ref[h] + rows_of(got_ref, n, h) + beta * s_ref[h]
        x_out[h] = x_ref[h] + alpha * (r + beta * p_ref[h])
        r_out[h] = r - alpha * s


def on_device(
    base_bottom,
    weight_bottom,
    base_category,
    weight_category,
    base_region,
    weight_region,
    category_map,
    region_map,
):
    stores, horizon, skus = base_bottom.shape
    n = region_map.shape[0]
    groups = weight_category.shape[2] // WIDE
    tiles = weight_category.shape[2] // LANES
    field = (horizon, n, LANES)
    padded = (PAD * n, LANES)
    by_category = (horizon, tiles, LANES)
    scal = (2, LANES)
    values = pltpu.VMEM((groups * PAD, WIDE), jnp.float32)

    x = base_bottom.reshape(field)
    diag = weight_bottom.reshape(field)
    (sent,) = call(
        pack_body,
        [(n * horizon, LANES)],
        [pltpu.VMEM(field, jnp.float32), pltpu.SemaphoreType.DMA],
        (x,),
        [HBM],
        True,
    )
    got = exchange(sent, n)
    arguments = (
        x,
        base_category.reshape(by_category),
        weight_category.reshape(by_category),
        jnp.transpose(base_region, (1, 0, 2)),
        jnp.transpose(weight_region, (1, 0, 2)),
        category_map.reshape(n, LANES),
        region_map.reshape(1, n),
    )
    held = [pltpu.VMEM(arguments[i].shape, arguments[i].dtype) for i in (0, 1, 2, 3, 4, 6)]
    spread, wcat, wstore, bstore, same, table, group, cats = call(
        prepare_body,
        [
            field,
            (groups * PAD, WIDE),
            field,
            field,
            jax.ShapeDtypeStruct((n, n), jnp.bfloat16),
            jax.ShapeDtypeStruct((skus, WIDE), jnp.bfloat16),
            jax.ShapeDtypeStruct((PAD, skus), jnp.bfloat16),
            jax.ShapeDtypeStruct((n, LANES), jnp.int32),
        ],
        [
            pltpu.VMEM(padded, jnp.float32),
            values,
            *held,
            pltpu.SemaphoreType.DMA((len(arguments),)),
        ],
        arguments,
        [HBM] * len(arguments),
    )
    reg, sent = call(
        region_start_body,
        [field, (n * 2 * horizon, LANES)],
        [],
        (got, spread, wstore, bstore, same),
    )
    got = exchange(sent, n)
    fixed = (diag, wcat, wstore, table, group, cats, same)
    both = (n * (2 * horizon + 1), LANES)
    work = [values, pltpu.VMEM(padded, jnp.float32)]
    sums = (groups * PAD, WIDE)
    r, rs, cr, a, reg, sent = call(
        first_body, [field, field, sums, field, field, both], work, (spread, reg, got) + fixed
    )
    got = exchange(sent, n)
    p = r
    x, r, rs, s, ss, cr, cs, scalars, a, reg, sent = call(
        second_body,
        [field, field, field, field, field, sums, sums, scal, field, field, both],
        work,
        (a, reg, got, x, r, rs, cr) + fixed,
    )
    got = exchange(sent, n)
    x, r, p, s, scalars, a, sent = call(
        third_body,
        [field, field, field, field, scal, field, (n * (horizon + 1), LANES)],
        work + [pltpu.VMEM(field, jnp.float32)],
        (a, reg, got, x, r, rs, p, s, ss, cr, cs, scalars) + fixed,
    )
    got = exchange(sent, n)
    x, r = call(last_body, [field, field], [], (a, got, x, r, p, s, scalars))
    return x.reshape(base_bottom.shape), r.reshape(base_bottom.shape)


def week_rows(tiles, n, regions):
    sizes = (n, n, tiles, tiles, regions, regions)
    return [sum(sizes[:i]) for i in range(len(sizes) + 1)]


def week_pack_body(*refs):
    sources, out, sems = refs[:-2], refs[-2], refs[-1]
    horizon = sources[0].shape[0]
    copies, start = [], 0
    for i, source in enumerate(sources):
        rows = source.shape[1]
        target = out.at[pl.ds(0, horizon), pl.ds(start, rows)]
        copies.append(pltpu.make_async_copy(source, target, sems.at[i]))
        start += rows
    for copy in copies:
        copy.start()
    for copy in copies:
        copy.wait()


def week_table_body(map_ref, cats_ref, table_out, group_out, same_out, region_out, regions):
    n = cats_ref.shape[0]
    lane = lax.broadcasted_iota(jnp.int32, (n, LANES), 1)
    line = lax.broadcasted_iota(jnp.int32, (n, LANES), 0)
    across = jnp.zeros((n, LANES), jnp.int32)
    down = jnp.zeros((n, LANES), jnp.int32)
    for s in range(n):
        across = jnp.where(lane % n == s, map_ref[s], across)
        down = jnp.where(line == s, map_ref[s], down)
    same_out[...] = jnp.where(across == down, 1.0, 0.0).astype(jnp.bfloat16)
    region_out[...] = jnp.where(lane % regions == down, 1.0, 0.0).astype(jnp.bfloat16)
    square = jnp.concatenate([cats_ref[...].astype(jnp.float32)] * (LANES // min(n, LANES)), axis=0)
    labels = lax.broadcasted_iota(jnp.int32, (LANES, WIDE), 1)
    columns = [
        jnp.transpose(square[i : i + LANES]).astype(jnp.int32) % WIDE
        for i in range(0, square.shape[0], LANES)
    ]
    for j in range(n):
        column = jnp.broadcast_to(columns[j // LANES][:, j % LANES : j % LANES + 1], (LANES, WIDE))
        table_out[j * LANES : (j + 1) * LANES, :] = jnp.where(
            column == labels, 1.0, 0.0
        ).astype(jnp.bfloat16)
        group = jnp.broadcast_to(cats_ref[j : j + 1, :] // WIDE, (group_out.shape[0], LANES))
        group_out[:, j * LANES : (j + 1) * LANES] = group.astype(jnp.float32).astype(jnp.bfloat16)


def ratio(top, bottom):
    return jnp.where(bottom > 0.0, top / bottom, 0.0)


def whole_sum(part):
    total = jnp.sum(jnp.sum(part, axis=0, keepdims=True), axis=1, keepdims=True)
    return jnp.broadcast_to(total, (1, LANES))


def week_body(
    core_ref, own_ref, other_hbm, table_ref, group_ref, same_ref, region_ref, cats_ref,
    base_out, basis_out, line_out,
    base, basis, diag, wstore, bstore, wcat, bcat, raw_weight, raw_base, other_ref, sem,
    side,
):
    core = core_ref[0]
    n, skus = base.shape
    per = own_ref.shape[0] // line_out.shape[0]
    regions = raw_weight.shape[0]
    tiles = wcat.shape[0] // n * (WIDE // LANES)
    starts = week_rows(tiles, n, regions)
    chunk = min(skus, 8 * LANES)
    chunks = [slice(c, c + chunk) for c in range(0, skus, chunk)]
    copy = pltpu.make_async_copy(other_hbm, other_ref, sem)
    copy.start()

    for ref, c in ((own_ref, core), (other_ref, 1 - core)):
        if ref is other_ref:
            copy.wait()
        for x in range(n // (CORES * side)):
            for t in range(0, side, 8):
                first = (x * side + t) * per
                top = pl.multiple_of(x * CORES * side + c * side + t, 8)

                def rows(row):
                    return ref[pl.ds(first + row, 8, stride=per), :]

                for j in range(n):
                    lanes = slice(j * LANES, (j + 1) * LANES)
                    base[pl.ds(top, 8), lanes] = rows(starts[0] + j)
                    diag[pl.ds(top, 8), lanes] = rows(starts[1] + j)
                for g in range(tiles):
                    lane = g * LANES % WIDE
                    down = pl.multiple_of(g * LANES // WIDE * n + top, 8)
                    wcat[pl.ds(down, 8), lane : lane + LANES] = rows(starts[2] + g)
                    bcat[pl.ds(down, 8), lane : lane + LANES] = rows(starts[3] + g)
            for k in range(side):
                first = (x * side + k) * per
                j = x * CORES * side + c * side + k
                lanes = pl.ds(pl.multiple_of(j * LANES, LANES), LANES)
                raw_base[:, lanes] = ref[first + starts[4] : first + starts[5], :]
                raw_weight[:, lanes] = ref[first + starts[5] : first + starts[6], :]

    region_table = region_ref[:, : 3 * regions]
    same = same_ref[:, : 2 * n]
    for source, target in ((raw_weight, wstore), (raw_base, bstore)):
        for lanes in chunks:
            parts = jnp.concatenate(split_all(source[:, lanes]), axis=0)
            target[:, lanes] = product(region_table, parts, ((1,), (0,)))

    def by_category(field):
        rows = wcat.shape[0]
        total = None
        for lanes in chunks:
            group = group_ref[:, lanes]
            masks = [group == g for g in range(rows // n)]
            none = jnp.zeros(group.shape, jnp.bfloat16)
            spread = jnp.concatenate(
                [jnp.where(mask, part, none) for part in split(field[:, lanes]) for mask in masks],
                axis=0,
            )
            part = product(spread, table_ref[lanes, :], ((1,), (0,)))
            total = part if total is None else total + part
        return total[:rows] + total[rows:]

    def spread_tile(values, j):
        members = cats_ref[j : j + 1, :]
        place = jnp.broadcast_to(members & (LANES - 1), (n, LANES))
        group = jnp.broadcast_to(members >> (LANES.bit_length() - 1), (n, LANES))
        found = [
            jnp.take_along_axis(values[g : g + n, lane : lane + LANES], place, axis=1)
            for g in range(0, values.shape[0], n)
            for lane in range(0, WIDE, LANES)
        ]
        bit = 0
        while len(found) > 1:
            mask = group & (1 << bit) != 0
            pairs = [found[i : i + 2] for i in range(0, len(found), 2)]
            found = [jnp.where(mask, pair[1], pair[0]) if len(pair) == 2 else pair[0] for pair in pairs]
            bit += 1
        return found[0]

    def by_region(part):
        return product(same, jnp.concatenate(split(part), axis=0), ((1,), (0,)))

    zero = jnp.zeros((n, LANES), jnp.float32)
    values = wcat[...] * (bcat[...] - by_category(base))
    norm = zero
    for lanes in chunks:
        sums = by_region(base[:, lanes])
        for t in range(0, chunk, LANES):
            tile = slice(lanes.start + t, lanes.start + t + LANES)
            part = wstore[:, tile] * (bstore[:, tile] - sums[:, t : t + LANES])
            part = part + spread_tile(values, tile.start // LANES)
            basis[0, :, tile] = part
            norm = norm + part * part
    norms, quotients = [whole_sum(norm)], []
    for k in range(3):
        field = basis.at[k]
        image = basis.at[k + 1]
        values = wcat[...] * by_category(field)
        dot = zero
        for lanes in chunks:
            sums = by_region(field[:, lanes])
            for t in range(0, chunk, LANES):
                tile = slice(lanes.start + t, lanes.start + t + LANES)
                part = field[:, tile]
                result = diag[:, tile] * part + wstore[:, tile] * sums[:, t : t + LANES]
                result = result + spread_tile(values, tile.start // LANES)
                image[:, tile] = result
                dot = dot + part * result
        quotients.append(ratio(whole_sum(dot), norms[k]))
        back = ratio(norms[k], norms[k - 1]) if k else None
        norm = zero
        for t in range(0, skus, LANES):
            tile = slice(t, t + LANES)
            result = image[:, tile] - quotients[k] * field[:, tile]
            if k:
                result = result - back * basis[k - 1, :, tile]
            image[:, tile] = result
            norm = norm + result * result
        norms.append(whole_sum(norm))
    lane = lax.broadcasted_iota(jnp.int32, (1, LANES), 1)
    line = jnp.zeros((1, LANES), jnp.float32)
    for i, value in enumerate(norms[:3] + quotients):
        line = jnp.where(lane == i, value, line)
    line_out[...] = jnp.broadcast_to(line, line_out.shape)
    for x in range(n // (CORES * side)):
        for t in range(0, side, 8):
            top = pl.multiple_of(x * CORES * side + core * side + t, 8)
            target = slice(x * side + t, x * side + t + 8)
            base_out[target, :] = base[pl.ds(top, 8), :]
            for k in range(4):
                basis_out[k, target, :] = basis[k, pl.ds(top, 8), :]


def week_combine_body(place_ref, lines_ref, base_ref, basis_ref, send_ref, horizon):
    weeks = lines_ref.shape[0]
    n = base_ref.shape[1] // LANES
    week = lax.broadcasted_iota(jnp.int32, (weeks, LANES), 0)
    lines = jnp.where(week < horizon, lines_ref[...], 0.0)
    n1, n2, n3, a1, a2, a3 = [
        jnp.take_along_axis(lines, jnp.full((weeks, LANES), i, jnp.int32), axis=1) for i in range(6)
    ]
    e2, e3 = ratio(n2, n1), ratio(n3, n2)

    def dot(left, right):
        terms = n1 * left[0] * right[0] + n2 * left[1] * right[1] + n3 * left[2] * right[2]
        return jnp.sum(terms, axis=0, keepdims=True)

    zero = jnp.zeros((weeks, LANES), jnp.float32)
    x = [zero, zero, zero]
    r = [zero + 1.0, zero, zero, zero]
    p = r[:3]
    rr = dot(r, r)
    for k in range(3):
        image = [
            a1 * p[0] + e2 * p[1],
            p[0] + a2 * p[1] + e3 * p[2],
            p[1] + a3 * p[2],
            p[2],
        ]
        alpha = rr / dot(p, image)
        x = [left + alpha * right for left, right in zip(x, p)]
        r = [left - alpha * right for left, right in zip(r, image)]
        if k < 2:
            new = dot(r, r)
            p = [left + new / rr * right for left, right in zip(r[:3], p)]
            rr = new
    mine = week == place_ref[0]
    x = [jnp.sum(jnp.where(mine, value, 0.0), axis=0, keepdims=True) for value in x]
    r = [jnp.sum(jnp.where(mine, value, 0.0), axis=0, keepdims=True) for value in r]
    rows = send_ref.shape[0] // weeks
    for t in range(0, weeks, 8):
        for j in range(n):
            lanes = slice(j * LANES, (j + 1) * LANES)
            parts = [basis_ref[k, t : t + 8, lanes] for k in range(4)]
            left = base_ref[t : t + 8, lanes]
            right = r[3] * parts[3]
            for k in range(3):
                left = left + x[k] * parts[k]
                right = right + r[k] * parts[k]
            first = t * rows + j
            send_ref[pl.ds(first, 8, stride=rows), :] = left
            send_ref[pl.ds(first + n, 8, stride=rows), :] = right


def week_last_body(got_ref, x_out, r_out, sems):
    horizon, n, _ = x_out.shape
    copies = [
        pltpu.make_async_copy(
            got_ref.at[pl.ds(0, horizon), pl.ds(i * n, n)], target, sems.at[i]
        )
        for i, target in enumerate((x_out, r_out))
    ]
    for copy in copies:
        copy.start()
    for copy in copies:
        copy.wait()


def exchange_weeks(blocks):
    return lax.all_to_all(blocks, ("x", "sku"), split_axis=0, concat_axis=0, tiled=True)


def by_weeks(
    base_bottom,
    weight_bottom,
    base_category,
    weight_category,
    base_region,
    weight_region,
    category_map,
    region_map,
):
    stores, horizon, skus = base_bottom.shape
    n = region_map.shape[0]
    regions = weight_region.shape[0]
    tiles = weight_category.shape[2] // LANES
    groups = weight_category.shape[2] // WIDE
    side = lax.axis_size("sku")
    weeks = lax.axis_size("x") * side
    place = lax.axis_index("x") * side + lax.axis_index("sku")
    place = place.astype(jnp.int32).reshape(1)
    core = lax.axis_index("core").astype(jnp.int32).reshape(1)
    cats = category_map.reshape(n, LANES)
    sources = (
        base_bottom.reshape(horizon, n, LANES),
        weight_bottom.reshape(horizon, n, LANES),
        weight_category.reshape(horizon, tiles, LANES),
        base_category.reshape(horizon, tiles, LANES),
        jnp.transpose(base_region, (1, 0, 2)),
        jnp.transpose(weight_region, (1, 0, 2)),
    )
    per = week_rows(tiles, n, regions)[-1]
    (sent,) = call(
        week_pack_body,
        [(weeks, per, LANES)],
        [pltpu.SemaphoreType.DMA((len(sources),))],
        sources,
        [HBM] * len(sources),
        out_specs=(HBM,),
    )
    own = exchange_weeks(sent)
    other = lax.ppermute(own, "core", [(0, 1), (1, 0)])
    table, group, same, region = call(
        lambda *refs: week_table_body(*refs, regions),
        [
            jax.ShapeDtypeStruct((skus, WIDE), jnp.bfloat16),
            jax.ShapeDtypeStruct((n, skus), jnp.bfloat16),
            jax.ShapeDtypeStruct((n, LANES), jnp.bfloat16),
            jax.ShapeDtypeStruct((n, LANES), jnp.bfloat16),
        ],
        [],
        (region_map, cats),
        [SMEM, VMEM],
    )
    full = pltpu.VMEM((n, skus), jnp.float32)
    raw = pltpu.VMEM((regions, skus), jnp.float32)
    cat = pltpu.VMEM((groups * n, WIDE), jnp.float32)
    base, basis, line = call(
        lambda *refs: week_body(*refs, side),
        [(weeks, skus), (4, weeks, skus), (weeks, LANES)],
        [
            full, pltpu.VMEM((4, n, skus), jnp.float32),
            full, full, full, cat, cat, raw, raw,
            pltpu.VMEM((weeks * per, LANES), jnp.float32),
            pltpu.SemaphoreType.DMA,
        ],
        (
            core, own.reshape(-1, LANES), other.reshape(-1, LANES),
            table, group, same, region, cats,
        ),
        [SMEM, VMEM, ANY] + [VMEM] * 5,
    )
    lines = exchange_weeks(line.reshape(weeks, 1, LANES)).reshape(weeks, LANES)
    (sent,) = call(
        lambda *refs: week_combine_body(*refs, horizon),
        [(weeks * 2 * n, LANES)],
        [],
        (place, lines, base, basis),
        [SMEM] + [VMEM] * 3,
    )
    got = exchange_weeks(sent.reshape(weeks, 2 * n, LANES))
    x, r = call(
        week_last_body,
        [(horizon, n, LANES)] * 2,
        [pltpu.SemaphoreType.DMA((2,))],
        (got,),
        [VMEM],
        out_specs=(HBM, HBM),
    )
    return x.reshape(base_bottom.shape), r.reshape(base_bottom.shape)


def solution(mesh):
    def mapped(device_mesh, body, stores):
        split_stores = P(stores, None, None)
        split_skus = P(None, None, stores)
        return jax.shard_map(
            body,
            mesh=device_mesh,
            in_specs=(split_stores,) * 4 + (split_skus,) * 2 + (P(), P()),
            out_specs=(split_stores,) * 2,
            check_vma=False,
        )

    side = mesh.shape["sku"]
    chips = mesh.devices.reshape(-1, CORES, side)

    def program(base_bottom, *others):
        stores, horizon, skus = base_bottom.shape
        fits = 16 * stores * skus * 4 <= 16 << 20
        fits = fits and 3 * others[3].shape[0] <= LANES and LANES % stores == 0
        if fits and horizon <= chips.shape[0] * side and side % 8 == 0:
            device_mesh = Mesh(chips, ("x", "core", "sku"))
            return mapped(device_mesh, by_weeks, ("x", "core", "sku"))(base_bottom, *others)
        return mapped(mesh, on_device, ("store", "sku"))(base_bottom, *others)

    return program
```

```python
import jax
import jax.numpy as jnp
from jax import lax
from jax.experimental import pallas as pl
from jax.experimental.pallas import tpu as pltpu
from jax.sharding import Mesh
from jax.sharding import PartitionSpec as P

LANES = 128
PAD = 16
WIDE = 256
VMEM = pl.BlockSpec(memory_space=pltpu.VMEM)
HBM = pl.BlockSpec(memory_space=pltpu.HBM)
SMEM = pl.BlockSpec(memory_space=pltpu.SMEM)
ANY = pl.BlockSpec(memory_space=pl.ANY)
CORES = 2


def exchange(blocks, n):
    moved = lax.all_to_all(
        blocks.reshape(n, 1, -1), ("store", "sku"), split_axis=0, concat_axis=0, tiled=True
    )
    return moved.reshape(blocks.shape)


def call(body, outs, scratch, args, specs=None, held=False, out_specs=None):
    outs = [
        out if isinstance(out, jax.ShapeDtypeStruct) else jax.ShapeDtypeStruct(out, jnp.float32)
        for out in outs
    ]
    specs = specs or [VMEM] * len(args)
    args = [
        arg if spec in (SMEM, ANY) else pltpu.with_memory_space_constraint(arg, spec.memory_space)
        for arg, spec in zip(args, specs)
    ]
    return pl.pallas_call(
        body,
        out_shape=tuple(pltpu.VMEM(out.shape, out.dtype) if held else out for out in outs),
        in_specs=specs,
        out_specs=out_specs or tuple(VMEM for _ in outs),
        scratch_shapes=scratch,
        compiler_params=pltpu.CompilerParams(vmem_limit_bytes=24 << 20),
    )(*args)


def split(value):
    high = value.astype(jnp.bfloat16)
    return high, (value - high.astype(jnp.float32)).astype(jnp.bfloat16)


def split_all(value):
    high, low = split(value)
    rest = value - high.astype(jnp.float32) - low.astype(jnp.float32)
    return high, low, rest.astype(jnp.bfloat16)


def product(left, right, contract):
    return lax.dot_general(left, right, (contract, ((), ())), preferred_element_type=jnp.float32)


def rows_of(ref, n, h):
    return ref[pl.ds(h, n, stride=ref.shape[0] // n), :]


def put_rows(ref, n, h, value):
    ref[pl.ds(h, n, stride=ref.shape[0] // n), :] = value


def category_sums(field, table_ref, group_ref, n, rows):
    width = 4 if n % 4 == 0 else 1
    lanes = width * LANES

    def step(c, total):
        pieces = [field[pl.ds(c * width + i, PAD, stride=n), :] for i in range(width)]
        parts = split_all(jnp.concatenate(pieces, axis=1))
        start = pl.multiple_of(c * lanes, lanes)
        group = group_ref[:, pl.ds(start, lanes)]
        masks = [group == g for g in range(rows // PAD)]
        none = jnp.zeros((PAD, lanes), jnp.bfloat16)
        spread = jnp.concatenate(
            [jnp.where(mask, part, none) for part in parts for mask in masks], axis=0
        )
        return total + product(spread, table_ref[pl.ds(start, lanes), :], ((1,), (0,)))

    steps = n // width
    total = lax.fori_loop(
        0, steps, step, jnp.zeros((3 * rows, WIDE), jnp.float32), unroll=min(steps, 8)
    )
    return total[:rows] + (total[rows : 2 * rows] + total[2 * rows :])


def category_spread(values, cats, horizon, put):
    place = cats & (LANES - 1)
    group = cats >> (LANES.bit_length() - 1)
    for h in range(horizon):
        found = []
        for g in range(0, values.shape[0], PAD):
            for lane in range(0, WIDE, LANES):
                row = jnp.broadcast_to(values[g + h : g + h + 1, lane : lane + LANES], cats.shape)
                found.append(jnp.take_along_axis(row, place, axis=1))
        for bit in range((len(found) - 1).bit_length()):
            mask = group & (1 << bit) != 0
            pairs = [found[i : i + 2] for i in range(0, len(found), 2)]
            found = [jnp.where(mask, pair[1], pair[0]) if len(pair) == 2 else pair[0] for pair in pairs]
        put(h, found[0])


def tiles_of(n):
    return [slice(t, t + 8) for t in range(0, n, 8)]


def put_tile(ref, n, h, tile, value):
    rows = ref.shape[0] // n
    ref[pl.ds(tile.start * rows + h, 8, stride=rows), :] = value


def region_sums(load, same, n, horizon):
    high, low = split(jnp.concatenate([load(h) for h in range(horizon)], axis=1))
    total = product(same, high, ((1,), (0,))) + product(same, low, ((1,), (0,)))
    return [total[:, h * LANES : (h + 1) * LANES] for h in range(horizon)]


def pack_body(base_hbm, out_ref, base_ref, sem):
    copy = pltpu.make_async_copy(base_hbm, base_ref, sem)
    copy.start()
    copy.wait()
    n = base_ref.shape[1]
    for h in range(base_ref.shape[0]):
        put_rows(out_ref, n, h, base_ref[h])


def prepare_body(
    base_hbm, base_cat_hbm, weight_cat_hbm, base_reg_hbm, weight_reg_hbm, cats_hbm, map_hbm,
    spread_out, wcat_out, wstore_out, bstore_out, same_out, table_out, group_out,
    cats_ref,
    field, values, base_ref, base_cat_ref, weight_cat_ref, base_reg_ref, weight_reg_ref, map_ref, sems,
):
    copies = [
        pltpu.make_async_copy(source, target, sems.at[i])
        for i, (source, target) in enumerate(
            (
                (cats_hbm, cats_ref),
                (base_hbm, base_ref),
                (weight_cat_hbm, weight_cat_ref),
                (base_cat_hbm, base_cat_ref),
                (map_hbm, map_ref),
                (weight_reg_hbm, weight_reg_ref),
                (base_reg_hbm, base_reg_ref),
            )
        )
    ]
    for copy in copies:
        copy.start()
    for copy in copies:
        copy.wait()
    horizon, n, _ = base_ref.shape
    n_regions = weight_reg_ref.shape[1]
    square = jnp.concatenate([cats_ref[...].astype(jnp.float32)] * (LANES // min(n, LANES)), axis=0)
    labels = lax.broadcasted_iota(jnp.int32, (LANES, WIDE), 1)
    columns = [
        jnp.transpose(square[i : i + LANES]).astype(jnp.int32) % WIDE
        for i in range(0, square.shape[0], LANES)
    ]
    for j in range(n):
        column = jnp.broadcast_to(columns[j // LANES][:, j % LANES : j % LANES + 1], (LANES, WIDE))
        table_out[j * LANES : (j + 1) * LANES, :] = jnp.where(
            column == labels, 1.0, 0.0
        ).astype(jnp.bfloat16)
        group = jnp.broadcast_to(cats_ref[j : j + 1, :] // WIDE, (PAD, LANES))
        group_out[:, j * LANES : (j + 1) * LANES] = group.astype(jnp.float32).astype(jnp.bfloat16)

    field[...] = jnp.zeros_like(field)
    for h in range(horizon):
        field[h * n : (h + 1) * n, :] = base_ref[h]
    sums = category_sums(field, table_out, group_out, n, wcat_out.shape[0])
    wcat_out[...] = jnp.zeros_like(wcat_out)
    values[...] = jnp.zeros_like(values)
    for g in range(0, wcat_out.shape[0], PAD):
        for lane in range(0, WIDE, LANES):
            tile = (g // PAD * WIDE + lane) // LANES
            lanes = slice(lane, lane + LANES)
            weight = weight_cat_ref[:, tile, :]
            wcat_out[g : g + horizon, lanes] = weight
            values[g : g + horizon, lanes] = weight * (
                base_cat_ref[:, tile, :] - sums[g : g + horizon, lanes]
            )
    for tile in tiles_of(n):

        def put(h, value):
            spread_out[h, tile, :] = value

        category_spread(values, cats_ref[tile, :], horizon, put)

    labels = lax.broadcasted_iota(jnp.int32, (n_regions, n), 0)
    table = jnp.where(labels == map_ref[...], 1.0, 0.0).astype(jnp.bfloat16)
    same_out[...] = product(table, table, ((0,), (0,))).astype(jnp.bfloat16)
    for source, target in ((weight_reg_ref, wstore_out), (base_reg_ref, bstore_out)):
        for h in range(horizon):
            high, low = split(source[h])
            rest = source[h] - high.astype(jnp.float32) - low.astype(jnp.float32)
            target[h] = (
                product(table, high, ((0,), (0,)))
                + product(table, low, ((0,), (0,)))
                + product(table, rest.astype(jnp.bfloat16), ((0,), (0,)))
            )


def region_start_body(got_ref, spread_ref, wstore_ref, bstore_ref, same_ref, reg_out, send_ref):
    horizon, n, _ = spread_ref.shape
    sums = region_sums(lambda h: rows_of(got_ref, n, h), same_ref[...], n, horizon)
    for h in range(horizon):
        put_rows(send_ref, n, h, spread_ref[h])
        part = wstore_ref[h] * (bstore_ref[h] - sums[h])
        reg_out[h] = part
        put_rows(send_ref, n, horizon + h, part)


def region_part(rs, wstore_ref, same_ref, put):
    horizon, n, _ = wstore_ref.shape
    sums = region_sums(lambda h: rs[h], same_ref[...], n, horizon)
    share = jnp.zeros((n, LANES), jnp.float32)
    for h in range(horizon):
        part = wstore_ref[h] * sums[h]
        share = share + part * rs[h]
        put(h, part)
    return share


def store_part(r_ref, sums, gamma, delta, eps, diag_ref, wcat_ref, cats_ref, put, put_line, values):
    horizon, n, _ = diag_ref.shape
    scaled = wcat_ref[...] * sums
    values[...] = scaled
    square = scaled * sums
    delta = jnp.sum(delta, axis=0, keepdims=True)
    for lane in range(0, WIDE, LANES):
        delta = delta + jnp.sum(square[:, lane : lane + LANES], axis=0, keepdims=True)
    lane = lax.broadcasted_iota(jnp.int32, (1, LANES), 1)
    line = jnp.zeros((1, LANES), jnp.float32)
    for i, part in enumerate((gamma, delta, eps)):
        if part is not None:
            whole = jnp.sum(jnp.sum(part, axis=0, keepdims=True), axis=1, keepdims=True)
            line = jnp.where(lane == i, whole, line)
    put_line(jnp.broadcast_to(line, (n, LANES)))
    for tile in tiles_of(n):

        def finish(h, value):
            put(h, tile, value + diag_ref[h, tile, :] * r_ref[h, tile, :])

        category_spread(values, cats_ref[tile, :], horizon, finish)


def totals(got_ref, n, row):
    total = jnp.sum(rows_of(got_ref, n, row), axis=0, keepdims=True)
    total = jnp.broadcast_to(total, (8, LANES))
    return [
        jnp.take_along_axis(total, jnp.full((8, LANES), i, jnp.int32), axis=1)[0:1] for i in range(3)
    ]


def wide(line):
    return jnp.concatenate([line] * (WIDE // LANES), axis=1)


def region_sender(ref, n, first, keep):
    def put(h, value):
        if keep is not None:
            keep[h] = value
        put_rows(ref, n, first + h, value)

    return put


def store_sender(ref, n, keep):
    def put(h, tile, value):
        keep[h, tile, :] = value
        if ref is not None:
            put_tile(ref, n, h, tile, value)

    return put


def clear_tail(field, horizon, n):
    field[horizon * n :, :] = jnp.zeros((field.shape[0] - horizon * n, LANES), jnp.float32)


def first_body(
    a_ref, reg_ref, got_ref, diag_ref, wcat_ref, wstore_ref, table_ref, group_ref, cats_ref, same_ref,
    r_out, rs_out, cr_out, a_out, reg_out, send_ref, values, field,
):
    horizon, n, _ = diag_ref.shape
    clear_tail(field, horizon, n)
    gamma = jnp.zeros((n, LANES), jnp.float32)
    delta = jnp.zeros((n, LANES), jnp.float32)
    for h in range(horizon):
        r = a_ref[h] + rows_of(got_ref, n, horizon + h)
        r_out[h] = r
        field[h * n : (h + 1) * n, :] = r
        gamma = gamma + r * r
        delta = delta + diag_ref[h] * r * r
    sums = category_sums(field, table_ref, group_ref, n, wcat_ref.shape[0])
    cr_out[...] = sums
    for h in range(horizon):
        rs_out[h] = rows_of(got_ref, n, h) + reg_ref[h]
    delta = delta + region_part(
        rs_out, wstore_ref, same_ref, region_sender(send_ref, n, horizon, reg_out)
    )
    store_part(
        r_out, sums, gamma, delta, None, diag_ref, wcat_ref, cats_ref,
        store_sender(send_ref, n, a_out),
        lambda line: put_rows(send_ref, n, 2 * horizon, line), values,
    )


def second_body(
    a_ref, reg_ref, got_ref, x_ref, r_ref, rs_ref, cr_ref,
    diag_ref, wcat_ref, wstore_ref, table_ref, group_ref, cats_ref, same_ref,
    x_out, r_out, rs_out, s_out, ss_out, cr_out, cs_out, scal_ref, a_out, reg_out, send_ref,
    values, field,
):
    horizon, n, _ = diag_ref.shape
    clear_tail(field, horizon, n)
    for h in range(horizon):
        field[h * n : (h + 1) * n, :] = a_ref[h] + rows_of(got_ref, n, horizon + h)
    sums = category_sums(field, table_ref, group_ref, n, wcat_ref.shape[0])
    cs_out[...] = sums
    gamma, delta, _ = totals(got_ref, n, 2 * horizon)
    alpha = gamma / delta
    scal_ref[0:1, :] = gamma
    scal_ref[1:2, :] = delta
    for h in range(horizon):
        ws = rows_of(got_ref, n, h) + reg_ref[h]
        ss_out[h] = ws
        rs_out[h] = rs_ref[h] - alpha * ws
    delta = region_part(
        rs_out, wstore_ref, same_ref, region_sender(send_ref, n, horizon, reg_out)
    )
    gamma = jnp.zeros((n, LANES), jnp.float32)
    eps = jnp.zeros((n, LANES), jnp.float32)
    for h in range(horizon):
        s = field[h * n : (h + 1) * n, :]
        s_out[h] = s
        r = r_ref[h]
        x_out[h] = x_ref[h] + alpha * r
        r = r - alpha * s
        r_out[h] = r
        gamma = gamma + r * r
        delta = delta + diag_ref[h] * r * r
        eps = eps + r * s
    sums = cr_ref[...] - wide(alpha) * sums
    cr_out[...] = sums
    store_part(
        r_out, sums, gamma, delta, eps, diag_ref, wcat_ref, cats_ref,
        store_sender(send_ref, n, a_out),
        lambda line: put_rows(send_ref, n, 2 * horizon, line), values,
    )


def third_body(
    a_ref, reg_ref, got_ref, x_ref, r_ref, rs_ref, p_ref, s_ref, ss_ref, cr_ref, cs_ref, scal_ref,
    diag_ref, wcat_ref, wstore_ref, table_ref, group_ref, cats_ref, same_ref,
    x_out, r_out, p_out, s_out, scal_out, a_out, send_ref, values, field, rs_out,
):
    horizon, n, _ = diag_ref.shape
    clear_tail(field, horizon, n)
    for h in range(horizon):
        field[h * n : (h + 1) * n, :] = a_ref[h] + rows_of(got_ref, n, horizon + h)
    sums = category_sums(field, table_ref, group_ref, n, wcat_ref.shape[0])
    gamma, delta, eps = totals(got_ref, n, 2 * horizon)
    beta = gamma / scal_ref[0:1, :]
    curve = delta + 2.0 * beta * eps + beta * beta * scal_ref[1:2, :]
    alpha = gamma / curve
    scal_out[0:1, :] = gamma
    scal_out[1:2, :] = curve
    for h in range(horizon):
        ws = rows_of(got_ref, n, h) + reg_ref[h]
        rs_out[h] = rs_ref[h] - alpha * (ws + beta * ss_ref[h])
    delta = region_part(rs_out, wstore_ref, same_ref, region_sender(send_ref, n, 0, None))
    gamma = jnp.zeros((n, LANES), jnp.float32)
    eps = jnp.zeros((n, LANES), jnp.float32)
    for h in range(horizon):
        s = field[h * n : (h + 1) * n, :] + beta * s_ref[h]
        s_out[h] = s
        r = r_ref[h]
        p = r + beta * p_ref[h]
        p_out[h] = p
        x_out[h] = x_ref[h] + alpha * p
        r = r - alpha * s
        r_out[h] = r
        gamma = gamma + r * r
        delta = delta + diag_ref[h] * r * r
        eps = eps + r * s
    sums = cr_ref[...] - wide(alpha) * (sums + wide(beta) * cs_ref[...])
    store_part(
        r_out, sums, gamma, delta, eps, diag_ref, wcat_ref, cats_ref,
        store_sender(None, n, a_out), lambda line: put_rows(send_ref, n, horizon, line), values,
    )


def last_body(a_ref, got_ref, x_ref, r_ref, p_ref, s_ref, scal_ref, x_out, r_out):
    horizon, n, _ = a_ref.shape
    gamma, delta, eps = totals(got_ref, n, horizon)
    beta = gamma / scal_ref[0:1, :]
    alpha = gamma / (delta + 2.0 * beta * eps + beta * beta * scal_ref[1:2, :])
    for h in range(horizon):
        r = r_ref[h]
        s = a_ref[h] + rows_of(got_ref, n, h) + beta * s_ref[h]
        x_out[h] = x_ref[h] + alpha * (r + beta * p_ref[h])
        r_out[h] = r - alpha * s


def on_device(
    base_bottom,
    weight_bottom,
    base_category,
    weight_category,
    base_region,
    weight_region,
    category_map,
    region_map,
):
    stores, horizon, skus = base_bottom.shape
    n = region_map.shape[0]
    groups = weight_category.shape[2] // WIDE
    tiles = weight_category.shape[2] // LANES
    field = (horizon, n, LANES)
    padded = (PAD * n, LANES)
    by_category = (horizon, tiles, LANES)
    scal = (2, LANES)
    values = pltpu.VMEM((groups * PAD, WIDE), jnp.float32)

    x = base_bottom.reshape(field)
    diag = weight_bottom.reshape(field)
    (sent,) = call(
        pack_body,
        [(n * horizon, LANES)],
        [pltpu.VMEM(field, jnp.float32), pltpu.SemaphoreType.DMA],
        (x,),
        [HBM],
        True,
    )
    got = exchange(sent, n)
    arguments = (
        x,
        base_category.reshape(by_category),
        weight_category.reshape(by_category),
        jnp.transpose(base_region, (1, 0, 2)),
        jnp.transpose(weight_region, (1, 0, 2)),
        category_map.reshape(n, LANES),
        region_map.reshape(1, n),
    )
    held = [pltpu.VMEM(arguments[i].shape, arguments[i].dtype) for i in (0, 1, 2, 3, 4, 6)]
    spread, wcat, wstore, bstore, same, table, group, cats = call(
        prepare_body,
        [
            field,
            (groups * PAD, WIDE),
            field,
            field,
            jax.ShapeDtypeStruct((n, n), jnp.bfloat16),
            jax.ShapeDtypeStruct((skus, WIDE), jnp.bfloat16),
            jax.ShapeDtypeStruct((PAD, skus), jnp.bfloat16),
            jax.ShapeDtypeStruct((n, LANES), jnp.int32),
        ],
        [
            pltpu.VMEM(padded, jnp.float32),
            values,
            *held,
            pltpu.SemaphoreType.DMA((len(arguments),)),
        ],
        arguments,
        [HBM] * len(arguments),
    )
    reg, sent = call(
        region_start_body,
        [field, (n * 2 * horizon, LANES)],
        [],
        (got, spread, wstore, bstore, same),
    )
    got = exchange(sent, n)
    fixed = (diag, wcat, wstore, table, group, cats, same)
    both = (n * (2 * horizon + 1), LANES)
    work = [values, pltpu.VMEM(padded, jnp.float32)]
    sums = (groups * PAD, WIDE)
    r, rs, cr, a, reg, sent = call(
        first_body, [field, field, sums, field, field, both], work, (spread, reg, got) + fixed
    )
    got = exchange(sent, n)
    p = r
    x, r, rs, s, ss, cr, cs, scalars, a, reg, sent = call(
        second_body,
        [field, field, field, field, field, sums, sums, scal, field, field, both],
        work,
        (a, reg, got, x, r, rs, cr) + fixed,
    )
    got = exchange(sent, n)
    x, r, p, s, scalars, a, sent = call(
        third_body,
        [field, field, field, field, scal, field, (n * (horizon + 1), LANES)],
        work + [pltpu.VMEM(field, jnp.float32)],
        (a, reg, got, x, r, rs, p, s, ss, cr, cs, scalars) + fixed,
    )
    got = exchange(sent, n)
    x, r = call(last_body, [field, field], [], (a, got, x, r, p, s, scalars))
    return x.reshape(base_bottom.shape), r.reshape(base_bottom.shape)


def week_rows(tiles, n, regions):
    sizes = (n, n, tiles, tiles, regions, regions)
    return [sum(sizes[:i]) for i in range(len(sizes) + 1)]


def week_pack_body(*refs):
    sources, out, sems = refs[:-2], refs[-2], refs[-1]
    horizon = sources[0].shape[0]
    copies, start = [], 0
    for i, source in enumerate(sources):
        rows = source.shape[1]
        target = out.at[pl.ds(0, horizon), pl.ds(start, rows)]
        copies.append(pltpu.make_async_copy(source, target, sems.at[i]))
        start += rows
    for copy in copies:
        copy.start()
    for copy in copies:
        copy.wait()


def week_table_body(
    map_ref, cats_ref, table_out, flipped_out, group_out, same_out, region_out, regions
):
    n = cats_ref.shape[0]
    lane = lax.broadcasted_iota(jnp.int32, (n, LANES), 1)
    line = lax.broadcasted_iota(jnp.int32, (n, LANES), 0)
    across = jnp.zeros((n, LANES), jnp.int32)
    down = jnp.zeros((n, LANES), jnp.int32)
    for s in range(n):
        across = jnp.where(lane % n == s, map_ref[s], across)
        down = jnp.where(line == s, map_ref[s], down)
    same_out[...] = jnp.where(across == down, 1.0, 0.0).astype(jnp.bfloat16)
    region_out[...] = jnp.where(lane % regions == down, 1.0, 0.0).astype(jnp.bfloat16)
    square = jnp.concatenate([cats_ref[...].astype(jnp.float32)] * (LANES // min(n, LANES)), axis=0)
    labels = lax.broadcasted_iota(jnp.int32, (LANES, WIDE), 1)
    downward = lax.broadcasted_iota(jnp.int32, (WIDE, LANES), 0)
    columns = [
        jnp.transpose(square[i : i + LANES]).astype(jnp.int32) & (WIDE - 1)
        for i in range(0, square.shape[0], LANES)
    ]
    for j in range(n):
        column = jnp.broadcast_to(columns[j // LANES][:, j % LANES : j % LANES + 1], (LANES, WIDE))
        table_out[j * LANES : (j + 1) * LANES, :] = jnp.where(
            column == labels, 1.0, 0.0
        ).astype(jnp.bfloat16)
        flipped_out[:, j * LANES : (j + 1) * LANES] = jnp.where(
            (cats_ref[j : j + 1, :] & (WIDE - 1)) == downward, 1.0, 0.0
        ).astype(jnp.bfloat16)
        group = cats_ref[j : j + 1, :] >> (WIDE.bit_length() - 1)
        group = jnp.broadcast_to(group, (group_out.shape[0], LANES))
        group_out[:, j * LANES : (j + 1) * LANES] = group.astype(jnp.float32).astype(jnp.bfloat16)


def ratio(top, bottom):
    return jnp.where(bottom > 0.0, top / bottom, 0.0)


def whole_sum(part):
    total = jnp.sum(jnp.sum(part, axis=0, keepdims=True), axis=1, keepdims=True)
    return jnp.broadcast_to(total, (1, LANES))


def week_body(
    core_ref, place_ref, own_ref, other_hbm, table_ref, flipped_ref, group_ref, same_ref, region_ref,
    cats_ref, kept_out, line_out,
    base, basis, diag, wstore, bstore, wcat, bcat, raw_weight, raw_base, held, other_ref, sem,
    side,
):
    core = core_ref[0]
    n, skus = base.shape
    per = own_ref.shape[0] // line_out.shape[0]
    regions = raw_weight.shape[0]
    tiles = wcat.shape[0] // n * (WIDE // LANES)
    starts = week_rows(tiles, n, regions)
    chunk = min(skus, 8 * LANES)
    chunks = [slice(c, c + chunk) for c in range(0, skus, chunk)]
    copy = pltpu.make_async_copy(other_hbm, other_ref, sem)
    copy.start()

    for ref, c in ((own_ref, core), (other_ref, 1 - core)):
        if ref is other_ref:
            copy.wait()
        for x in range(n // (CORES * side)):
            for t in range(0, side, 8):
                first = (x * side + t) * per
                top = pl.multiple_of(x * CORES * side + c * side + t, 8)

                def rows(row):
                    return ref[pl.ds(first + row, 8, stride=per), :]

                for j in range(n):
                    lanes = slice(j * LANES, (j + 1) * LANES)
                    base[pl.ds(top, 8), lanes] = rows(starts[0] + j)
                    diag[pl.ds(top, 8), lanes] = rows(starts[1] + j)
                for g in range(tiles):
                    lane = g * LANES % WIDE
                    down = pl.multiple_of(g * LANES // WIDE * n + top, 8)
                    wcat[pl.ds(down, 8), lane : lane + LANES] = rows(starts[2] + g)
                    bcat[pl.ds(down, 8), lane : lane + LANES] = rows(starts[3] + g)
            for k in range(side):
                first = (x * side + k) * per
                j = x * CORES * side + c * side + k
                lanes = pl.ds(pl.multiple_of(j * LANES, LANES), LANES)
                raw_base[:, lanes] = ref[first + starts[4] : first + starts[5], :]
                raw_weight[:, lanes] = ref[first + starts[5] : first + starts[6], :]

    region_table = region_ref[:, : 3 * regions]
    same = same_ref[:, : 2 * n]
    for source, target in ((raw_weight, wstore), (raw_base, bstore)):
        for lanes in chunks:
            parts = jnp.concatenate(split_all(source[:, lanes]), axis=0)
            target[:, lanes] = product(region_table, parts, ((1,), (0,)))

    def by_category(field):
        rows = wcat.shape[0]
        total = None
        for lanes in chunks:
            group = group_ref[:, lanes]
            masks = [group == g for g in range(rows // n)]
            none = jnp.zeros(group.shape, jnp.bfloat16)
            spread = jnp.concatenate(
                [jnp.where(mask, part, none) for part in split(field[:, lanes]) for mask in masks],
                axis=0,
            )
            part = product(spread, table_ref[lanes, :], ((1,), (0,)))
            total = part if total is None else total + part
        return total[:rows] + total[rows:]

    def spread(values, m, put):
        parts = jnp.concatenate(split(values), axis=0)
        groups = values.shape[0] // m
        for lanes in chunks:
            found = product(parts, flipped_ref[:, lanes], ((1,), (0,)))
            for t in range(0, chunk, LANES):
                tile = slice(lanes.start + t, lanes.start + t + LANES)
                members = cats_ref[tile.start // LANES : tile.start // LANES + 1, :]
                group = jnp.broadcast_to(members >> (WIDE.bit_length() - 1), (m, LANES))
                high, low = found[: groups * m, t : t + LANES], found[groups * m :, t : t + LANES]
                one = [
                    high[g * m : (g + 1) * m] + low[g * m : (g + 1) * m] for g in range(groups)
                ]
                bit = 1
                while len(one) > 1:
                    odd = group & bit != 0
                    pairs = [one[i : i + 2] for i in range(0, len(one), 2)]
                    one = [jnp.where(odd, *pair[::-1]) if len(pair) == 2 else pair[0] for pair in pairs]
                    bit *= 2
                put(tile, one[0])

    def by_region(part):
        return product(same, jnp.concatenate(split(part), axis=0), ((1,), (0,)))

    def tiles_in(lanes):
        for t in range(0, chunk, LANES):
            yield slice(lanes.start + t, lanes.start + t + LANES), slice(t, t + LANES)

    zero = jnp.zeros((n, LANES), jnp.float32)
    for lanes in chunks:
        sums = by_region(base[:, lanes])
        for tile, inner in tiles_in(lanes):
            basis[0, :, tile] = wstore[:, tile] * (bstore[:, tile] - sums[:, inner])
    norm = [zero]

    def start(tile, value):
        result = basis[0, :, tile] + value
        basis[0, :, tile] = result
        norm[0] = norm[0] + result * result

    spread(wcat[...] * (bcat[...] - by_category(base)), n, start)
    norms, quotients = [whole_sum(norm[0])], []
    for k in range(3):
        field, image = basis.at[k], basis.at[k + 1]
        sums = by_category(field)
        values = wcat[...] * sums
        square = values * sums
        dot = zero
        for lane in range(0, WIDE, LANES):
            for g in range(0, square.shape[0], n):
                dot = dot + square[g : g + n, lane : lane + LANES]
        for lanes in chunks:
            sums = by_region(field[:, lanes])
            for tile, inner in tiles_in(lanes):
                part = field[:, tile]
                result = diag[:, tile] * part + wstore[:, tile] * sums[:, inner]
                image[:, tile] = result
                dot = dot + part * result
        quotients.append(ratio(whole_sum(dot), norms[k]))
        back = ratio(norms[k], norms[k - 1]) if k else None
        if k == 2:
            break
        norm = [zero]

        def step(tile, value):
            result = image[:, tile] + value - quotients[k] * field[:, tile]
            if k:
                result = result - back * basis[k - 1, :, tile]
            image[:, tile] = result
            norm[0] = norm[0] + result * result

        spread(values, n, step)
        norms.append(whole_sum(norm[0]))

    lane = lax.broadcasted_iota(jnp.int32, line_out.shape, 1)
    place = lax.broadcasted_iota(jnp.int32, line_out.shape, 0)
    line = jnp.where((lane == 6) & (place == place_ref[0]), 1.0, 0.0)
    for i, value in enumerate(norms + quotients):
        line = jnp.where(lane == i, jnp.broadcast_to(value, line.shape), line)
    line_out[...] = line

    held[...] = values
    weeks = line_out.shape[0]
    tops = [
        pl.multiple_of(x * CORES * side + core * side + t, 8)
        for x in range(n // (CORES * side))
        for t in range(0, side, 8)
    ]
    for i, top in enumerate(tops):
        kept_out[4, i * 8 : i * 8 + 8, :] = base[pl.ds(top, 8), :]
        for k in range(4):
            kept_out[k, i * 8 : i * 8 + 8, :] = basis[k, pl.ds(top, 8), :]
    mine = jnp.concatenate(
        [held[pl.ds(g + top, 8), :] for g in range(0, held.shape[0], n) for top in tops], axis=0
    )

    def finish(tile, value):
        result = kept_out[3, :, tile] + value - quotients[2] * kept_out[2, :, tile]
        kept_out[3, :, tile] = result - back * kept_out[1, :, tile]

    spread(mine, weeks, finish)


def week_combine_body(lines_ref, kept_ref, send_ref, horizon):
    weeks = lines_ref.shape[0]
    n = kept_ref.shape[2] // LANES
    week = lax.broadcasted_iota(jnp.int32, (weeks, LANES), 0)
    lines = jnp.where(week < horizon, lines_ref[...], 0.0)
    n1, n2, n3, a1, a2, a3, mark = [
        jnp.take_along_axis(lines, jnp.full((weeks, LANES), i, jnp.int32), axis=1) for i in range(7)
    ]
    e2, e3 = ratio(n2, n1), ratio(n3, n2)

    def dot(left, right):
        terms = n1 * left[0] * right[0] + n2 * left[1] * right[1] + n3 * left[2] * right[2]
        return jnp.sum(terms, axis=0, keepdims=True)

    zero = jnp.zeros((weeks, LANES), jnp.float32)
    x = [zero, zero, zero]
    r = [zero + 1.0, zero, zero, zero]
    p = r[:3]
    rr = dot(r, r)
    for k in range(3):
        image = [
            a1 * p[0] + e2 * p[1],
            p[0] + a2 * p[1] + e3 * p[2],
            p[1] + a3 * p[2],
            p[2],
        ]
        alpha = rr / dot(p, image)
        x = [left + alpha * right for left, right in zip(x, p)]
        r = [left - alpha * right for left, right in zip(r, image)]
        if k < 2:
            new = dot(r, r)
            p = [left + new / rr * right for left, right in zip(r[:3], p)]
            rr = new
    mine = mark > 0.0
    x = [jnp.sum(jnp.where(mine, value, 0.0), axis=0, keepdims=True) for value in x]
    r = [jnp.sum(jnp.where(mine, value, 0.0), axis=0, keepdims=True) for value in r]
    rows = send_ref.shape[0] // weeks
    for t in range(0, weeks, 8):
        for j in range(n):
            lanes = slice(j * LANES, (j + 1) * LANES)
            parts = [kept_ref[k, t : t + 8, lanes] for k in range(4)]
            left = kept_ref[4, t : t + 8, lanes]
            right = r[3] * parts[3]
            for k in range(3):
                left = left + x[k] * parts[k]
                right = right + r[k] * parts[k]
            first = t * rows + j
            send_ref[pl.ds(first, 8, stride=rows), :] = left
            send_ref[pl.ds(first + n, 8, stride=rows), :] = right


def week_last_body(got_ref, x_out, r_out, sems):
    horizon, n, _ = x_out.shape
    copies = [
        pltpu.make_async_copy(
            got_ref.at[pl.ds(0, horizon), pl.ds(i * n, n)], target, sems.at[i]
        )
        for i, target in enumerate((x_out, r_out))
    ]
    for copy in copies:
        copy.start()
    for copy in copies:
        copy.wait()


def exchange_weeks(blocks):
    return lax.all_to_all(blocks, ("x", "sku"), split_axis=0, concat_axis=0, tiled=True)


def by_weeks(
    base_bottom,
    weight_bottom,
    base_category,
    weight_category,
    base_region,
    weight_region,
    category_map,
    region_map,
):
    stores, horizon, skus = base_bottom.shape
    n = region_map.shape[0]
    regions = weight_region.shape[0]
    tiles = weight_category.shape[2] // LANES
    groups = weight_category.shape[2] // WIDE
    side = lax.axis_size("sku")
    weeks = lax.axis_size("x") * side
    place = lax.axis_index("x") * side + lax.axis_index("sku")
    place = place.astype(jnp.int32).reshape(1)
    core = lax.axis_index("core").astype(jnp.int32).reshape(1)
    cats = category_map.reshape(n, LANES)
    sources = (
        base_bottom.reshape(horizon, n, LANES),
        weight_bottom.reshape(horizon, n, LANES),
        weight_category.reshape(horizon, tiles, LANES),
        base_category.reshape(horizon, tiles, LANES),
        jnp.transpose(base_region, (1, 0, 2)),
        jnp.transpose(weight_region, (1, 0, 2)),
    )
    per = week_rows(tiles, n, regions)[-1]
    (sent,) = call(
        week_pack_body,
        [(weeks, per, LANES)],
        [pltpu.SemaphoreType.DMA((len(sources),))],
        sources,
        [HBM] * len(sources),
        out_specs=(HBM,),
    )
    own = exchange_weeks(sent)
    other = lax.ppermute(own, "core", [(0, 1), (1, 0)])
    table, flipped, group, same, region = call(
        lambda *refs: week_table_body(*refs, regions),
        [
            jax.ShapeDtypeStruct((skus, WIDE), jnp.bfloat16),
            jax.ShapeDtypeStruct((WIDE, skus), jnp.bfloat16),
            jax.ShapeDtypeStruct((n, skus), jnp.bfloat16),
            jax.ShapeDtypeStruct((n, LANES), jnp.bfloat16),
            jax.ShapeDtypeStruct((n, LANES), jnp.bfloat16),
        ],
        [],
        (region_map, cats),
        [SMEM, VMEM],
    )
    full = pltpu.VMEM((n, skus), jnp.float32)
    raw = pltpu.VMEM((regions, skus), jnp.float32)
    cat = pltpu.VMEM((groups * n, WIDE), jnp.float32)
    kept, line = call(
        lambda *refs: week_body(*refs, side),
        [(5, weeks, skus), (weeks, LANES)],
        [
            full, pltpu.VMEM((4, n, skus), jnp.float32),
            full, full, full, cat, cat, raw, raw, cat,
            pltpu.VMEM((weeks * per, LANES), jnp.float32),
            pltpu.SemaphoreType.DMA,
        ],
        (
            core, place, own.reshape(-1, LANES), other.reshape(-1, LANES),
            table, flipped, group, same, region, cats,
        ),
        [SMEM, SMEM, VMEM, ANY] + [VMEM] * 6,
    )
    lines = exchange_weeks(line.reshape(weeks, 1, LANES)).reshape(weeks, LANES)
    (sent,) = call(
        lambda *refs: week_combine_body(*refs, horizon),
        [(weeks * 2 * n, LANES)],
        [],
        (lines, kept),
        [VMEM] * 2,
    )
    got = exchange_weeks(sent.reshape(weeks, 2 * n, LANES))
    x, r = call(
        week_last_body,
        [(horizon, n, LANES)] * 2,
        [pltpu.SemaphoreType.DMA((2,))],
        (got,),
        [VMEM],
        out_specs=(HBM, HBM),
    )
    return x.reshape(base_bottom.shape), r.reshape(base_bottom.shape)


def solution(mesh):
    def mapped(device_mesh, body, stores):
        split_stores = P(stores, None, None)
        split_skus = P(None, None, stores)
        return jax.shard_map(
            body,
            mesh=device_mesh,
            in_specs=(split_stores,) * 4 + (split_skus,) * 2 + (P(), P()),
            out_specs=(split_stores,) * 2,
            check_vma=False,
        )

    side = mesh.shape["sku"]
    chips = mesh.devices.reshape(-1, CORES, side)

    def program(base_bottom, *others):
        stores, horizon, skus = base_bottom.shape
        fits = 16 * stores * skus * 4 <= 16 << 20
        fits = fits and 3 * others[3].shape[0] <= LANES and LANES % stores == 0
        if fits and horizon <= chips.shape[0] * side and side % 8 == 0:
            device_mesh = Mesh(chips, ("x", "core", "sku"))
            return mapped(device_mesh, by_weeks, ("x", "core", "sku"))(base_bottom, *others)
        return mapped(mesh, on_device, ("store", "sku"))(base_bottom, *others)

    return program
```

```python
import jax
import jax.numpy as jnp
from jax import lax
from jax.experimental import pallas as pl
from jax.experimental.pallas import tpu as pltpu
from jax.sharding import Mesh
from jax.sharding import PartitionSpec as P

LANES = 128
PAD = 16
WIDE = 256
VMEM = pl.BlockSpec(memory_space=pltpu.VMEM)
HBM = pl.BlockSpec(memory_space=pltpu.HBM)
SMEM = pl.BlockSpec(memory_space=pltpu.SMEM)
FREE = pl.BlockSpec(memory_space=pltpu.VMEM)
CORES = 2


def exchange(blocks, n):
    moved = lax.all_to_all(
        blocks.reshape(n, 1, -1), ("store", "sku"), split_axis=0, concat_axis=0, tiled=True
    )
    return moved.reshape(blocks.shape)


def call(body, outs, scratch, args, specs=None, held=False, out_specs=None):
    outs = [
        out if isinstance(out, jax.ShapeDtypeStruct) else jax.ShapeDtypeStruct(out, jnp.float32)
        for out in outs
    ]
    specs = specs or [VMEM] * len(args)
    args = [
        arg if spec is SMEM or spec is FREE else pltpu.with_memory_space_constraint(arg, spec.memory_space)
        for arg, spec in zip(args, specs)
    ]
    return pl.pallas_call(
        body,
        out_shape=tuple(pltpu.VMEM(out.shape, out.dtype) if held else out for out in outs),
        in_specs=specs,
        out_specs=out_specs or tuple(VMEM for _ in outs),
        scratch_shapes=scratch,
        compiler_params=pltpu.CompilerParams(vmem_limit_bytes=24 << 20),
    )(*args)


def split(value):
    high = value.astype(jnp.bfloat16)
    return high, (value - high.astype(jnp.float32)).astype(jnp.bfloat16)


def split_all(value):
    high, low = split(value)
    rest = value - high.astype(jnp.float32) - low.astype(jnp.float32)
    return high, low, rest.astype(jnp.bfloat16)


def product(left, right, contract):
    return lax.dot_general(left, right, (contract, ((), ())), preferred_element_type=jnp.float32)


def rows_of(ref, n, h):
    return ref[pl.ds(h, n, stride=ref.shape[0] // n), :]


def put_rows(ref, n, h, value):
    ref[pl.ds(h, n, stride=ref.shape[0] // n), :] = value


def category_sums(field, table_ref, group_ref, n, rows):
    width = 4 if n % 4 == 0 else 1
    lanes = width * LANES

    def step(c, total):
        pieces = [field[pl.ds(c * width + i, PAD, stride=n), :] for i in range(width)]
        parts = split_all(jnp.concatenate(pieces, axis=1))
        start = pl.multiple_of(c * lanes, lanes)
        group = group_ref[:, pl.ds(start, lanes)]
        masks = [group == g for g in range(rows // PAD)]
        none = jnp.zeros((PAD, lanes), jnp.bfloat16)
        spread = jnp.concatenate(
            [jnp.where(mask, part, none) for part in parts for mask in masks], axis=0
        )
        return total + product(spread, table_ref[pl.ds(start, lanes), :], ((1,), (0,)))

    steps = n // width
    total = lax.fori_loop(
        0, steps, step, jnp.zeros((3 * rows, WIDE), jnp.float32), unroll=min(steps, 8)
    )
    return total[:rows] + (total[rows : 2 * rows] + total[2 * rows :])


def category_spread(values, cats, horizon, put):
    place = cats & (LANES - 1)
    group = cats >> (LANES.bit_length() - 1)
    for h in range(horizon):
        found = []
        for g in range(0, values.shape[0], PAD):
            for lane in range(0, WIDE, LANES):
                row = jnp.broadcast_to(values[g + h : g + h + 1, lane : lane + LANES], cats.shape)
                found.append(jnp.take_along_axis(row, place, axis=1))
        for bit in range((len(found) - 1).bit_length()):
            mask = group & (1 << bit) != 0
            pairs = [found[i : i + 2] for i in range(0, len(found), 2)]
            found = [jnp.where(mask, pair[1], pair[0]) if len(pair) == 2 else pair[0] for pair in pairs]
        put(h, found[0])


def tiles_of(n):
    return [slice(t, t + 8) for t in range(0, n, 8)]


def put_tile(ref, n, h, tile, value):
    rows = ref.shape[0] // n
    ref[pl.ds(tile.start * rows + h, 8, stride=rows), :] = value


def region_sums(load, same, n, horizon):
    high, low = split(jnp.concatenate([load(h) for h in range(horizon)], axis=1))
    total = product(same, high, ((1,), (0,))) + product(same, low, ((1,), (0,)))
    return [total[:, h * LANES : (h + 1) * LANES] for h in range(horizon)]


def pack_body(base_hbm, out_ref, base_ref, sem):
    copy = pltpu.make_async_copy(base_hbm, base_ref, sem)
    copy.start()
    copy.wait()
    n = base_ref.shape[1]
    for h in range(base_ref.shape[0]):
        put_rows(out_ref, n, h, base_ref[h])


def prepare_body(
    base_hbm, base_cat_hbm, weight_cat_hbm, base_reg_hbm, weight_reg_hbm, cats_hbm, map_hbm,
    spread_out, wcat_out, wstore_out, bstore_out, same_out, table_out, group_out,
    cats_ref,
    field, values, base_ref, base_cat_ref, weight_cat_ref, base_reg_ref, weight_reg_ref, map_ref, sems,
):
    copies = [
        pltpu.make_async_copy(source, target, sems.at[i])
        for i, (source, target) in enumerate(
            (
                (cats_hbm, cats_ref),
                (base_hbm, base_ref),
                (weight_cat_hbm, weight_cat_ref),
                (base_cat_hbm, base_cat_ref),
                (map_hbm, map_ref),
                (weight_reg_hbm, weight_reg_ref),
                (base_reg_hbm, base_reg_ref),
            )
        )
    ]
    for copy in copies:
        copy.start()
    for copy in copies:
        copy.wait()
    horizon, n, _ = base_ref.shape
    n_regions = weight_reg_ref.shape[1]
    square = jnp.concatenate([cats_ref[...].astype(jnp.float32)] * (LANES // min(n, LANES)), axis=0)
    labels = lax.broadcasted_iota(jnp.int32, (LANES, WIDE), 1)
    columns = [
        jnp.transpose(square[i : i + LANES]).astype(jnp.int32) % WIDE
        for i in range(0, square.shape[0], LANES)
    ]
    for j in range(n):
        column = jnp.broadcast_to(columns[j // LANES][:, j % LANES : j % LANES + 1], (LANES, WIDE))
        table_out[j * LANES : (j + 1) * LANES, :] = jnp.where(
            column == labels, 1.0, 0.0
        ).astype(jnp.bfloat16)
        group = jnp.broadcast_to(cats_ref[j : j + 1, :] // WIDE, (PAD, LANES))
        group_out[:, j * LANES : (j + 1) * LANES] = group.astype(jnp.float32).astype(jnp.bfloat16)

    field[...] = jnp.zeros_like(field)
    for h in range(horizon):
        field[h * n : (h + 1) * n, :] = base_ref[h]
    sums = category_sums(field, table_out, group_out, n, wcat_out.shape[0])
    wcat_out[...] = jnp.zeros_like(wcat_out)
    values[...] = jnp.zeros_like(values)
    for g in range(0, wcat_out.shape[0], PAD):
        for lane in range(0, WIDE, LANES):
            tile = (g // PAD * WIDE + lane) // LANES
            lanes = slice(lane, lane + LANES)
            weight = weight_cat_ref[:, tile, :]
            wcat_out[g : g + horizon, lanes] = weight
            values[g : g + horizon, lanes] = weight * (
                base_cat_ref[:, tile, :] - sums[g : g + horizon, lanes]
            )
    for tile in tiles_of(n):

        def put(h, value):
            spread_out[h, tile, :] = value

        category_spread(values, cats_ref[tile, :], horizon, put)

    labels = lax.broadcasted_iota(jnp.int32, (n_regions, n), 0)
    table = jnp.where(labels == map_ref[...], 1.0, 0.0).astype(jnp.bfloat16)
    same_out[...] = product(table, table, ((0,), (0,))).astype(jnp.bfloat16)
    for source, target in ((weight_reg_ref, wstore_out), (base_reg_ref, bstore_out)):
        for h in range(horizon):
            high, low = split(source[h])
            rest = source[h] - high.astype(jnp.float32) - low.astype(jnp.float32)
            target[h] = (
                product(table, high, ((0,), (0,)))
                + product(table, low, ((0,), (0,)))
                + product(table, rest.astype(jnp.bfloat16), ((0,), (0,)))
            )


def region_start_body(got_ref, spread_ref, wstore_ref, bstore_ref, same_ref, reg_out, send_ref):
    horizon, n, _ = spread_ref.shape
    sums = region_sums(lambda h: rows_of(got_ref, n, h), same_ref[...], n, horizon)
    for h in range(horizon):
        put_rows(send_ref, n, h, spread_ref[h])
        part = wstore_ref[h] * (bstore_ref[h] - sums[h])
        reg_out[h] = part
        put_rows(send_ref, n, horizon + h, part)


def region_part(rs, wstore_ref, same_ref, put):
    horizon, n, _ = wstore_ref.shape
    sums = region_sums(lambda h: rs[h], same_ref[...], n, horizon)
    share = jnp.zeros((n, LANES), jnp.float32)
    for h in range(horizon):
        part = wstore_ref[h] * sums[h]
        share = share + part * rs[h]
        put(h, part)
    return share


def store_part(r_ref, sums, gamma, delta, eps, diag_ref, wcat_ref, cats_ref, put, put_line, values):
    horizon, n, _ = diag_ref.shape
    scaled = wcat_ref[...] * sums
    values[...] = scaled
    square = scaled * sums
    delta = jnp.sum(delta, axis=0, keepdims=True)
    for lane in range(0, WIDE, LANES):
        delta = delta + jnp.sum(square[:, lane : lane + LANES], axis=0, keepdims=True)
    lane = lax.broadcasted_iota(jnp.int32, (1, LANES), 1)
    line = jnp.zeros((1, LANES), jnp.float32)
    for i, part in enumerate((gamma, delta, eps)):
        if part is not None:
            whole = jnp.sum(jnp.sum(part, axis=0, keepdims=True), axis=1, keepdims=True)
            line = jnp.where(lane == i, whole, line)
    put_line(jnp.broadcast_to(line, (n, LANES)))
    for tile in tiles_of(n):

        def finish(h, value):
            put(h, tile, value + diag_ref[h, tile, :] * r_ref[h, tile, :])

        category_spread(values, cats_ref[tile, :], horizon, finish)


def totals(got_ref, n, row):
    total = jnp.sum(rows_of(got_ref, n, row), axis=0, keepdims=True)
    total = jnp.broadcast_to(total, (8, LANES))
    return [
        jnp.take_along_axis(total, jnp.full((8, LANES), i, jnp.int32), axis=1)[0:1] for i in range(3)
    ]


def wide(line):
    return jnp.concatenate([line] * (WIDE // LANES), axis=1)


def region_sender(ref, n, first, keep):
    def put(h, value):
        if keep is not None:
            keep[h] = value
        put_rows(ref, n, first + h, value)

    return put


def store_sender(ref, n, keep):
    def put(h, tile, value):
        keep[h, tile, :] = value
        if ref is not None:
            put_tile(ref, n, h, tile, value)

    return put


def clear_tail(field, horizon, n):
    field[horizon * n :, :] = jnp.zeros((field.shape[0] - horizon * n, LANES), jnp.float32)


def first_body(
    a_ref, reg_ref, got_ref, diag_ref, wcat_ref, wstore_ref, table_ref, group_ref, cats_ref, same_ref,
    r_out, rs_out, cr_out, a_out, reg_out, send_ref, values, field,
):
    horizon, n, _ = diag_ref.shape
    clear_tail(field, horizon, n)
    gamma = jnp.zeros((n, LANES), jnp.float32)
    delta = jnp.zeros((n, LANES), jnp.float32)
    for h in range(horizon):
        r = a_ref[h] + rows_of(got_ref, n, horizon + h)
        r_out[h] = r
        field[h * n : (h + 1) * n, :] = r
        gamma = gamma + r * r
        delta = delta + diag_ref[h] * r * r
    sums = category_sums(field, table_ref, group_ref, n, wcat_ref.shape[0])
    cr_out[...] = sums
    for h in range(horizon):
        rs_out[h] = rows_of(got_ref, n, h) + reg_ref[h]
    delta = delta + region_part(
        rs_out, wstore_ref, same_ref, region_sender(send_ref, n, horizon, reg_out)
    )
    store_part(
        r_out, sums, gamma, delta, None, diag_ref, wcat_ref, cats_ref,
        store_sender(send_ref, n, a_out),
        lambda line: put_rows(send_ref, n, 2 * horizon, line), values,
    )


def second_body(
    a_ref, reg_ref, got_ref, x_ref, r_ref, rs_ref, cr_ref,
    diag_ref, wcat_ref, wstore_ref, table_ref, group_ref, cats_ref, same_ref,
    x_out, r_out, rs_out, s_out, ss_out, cr_out, cs_out, scal_ref, a_out, reg_out, send_ref,
    values, field,
):
    horizon, n, _ = diag_ref.shape
    clear_tail(field, horizon, n)
    for h in range(horizon):
        field[h * n : (h + 1) * n, :] = a_ref[h] + rows_of(got_ref, n, horizon + h)
    sums = category_sums(field, table_ref, group_ref, n, wcat_ref.shape[0])
    cs_out[...] = sums
    gamma, delta, _ = totals(got_ref, n, 2 * horizon)
    alpha = gamma / delta
    scal_ref[0:1, :] = gamma
    scal_ref[1:2, :] = delta
    for h in range(horizon):
        ws = rows_of(got_ref, n, h) + reg_ref[h]
        ss_out[h] = ws
        rs_out[h] = rs_ref[h] - alpha * ws
    delta = region_part(
        rs_out, wstore_ref, same_ref, region_sender(send_ref, n, horizon, reg_out)
    )
    gamma = jnp.zeros((n, LANES), jnp.float32)
    eps = jnp.zeros((n, LANES), jnp.float32)
    for h in range(horizon):
        s = field[h * n : (h + 1) * n, :]
        s_out[h] = s
        r = r_ref[h]
        x_out[h] = x_ref[h] + alpha * r
        r = r - alpha * s
        r_out[h] = r
        gamma = gamma + r * r
        delta = delta + diag_ref[h] * r * r
        eps = eps + r * s
    sums = cr_ref[...] - wide(alpha) * sums
    cr_out[...] = sums
    store_part(
        r_out, sums, gamma, delta, eps, diag_ref, wcat_ref, cats_ref,
        store_sender(send_ref, n, a_out),
        lambda line: put_rows(send_ref, n, 2 * horizon, line), values,
    )


def third_body(
    a_ref, reg_ref, got_ref, x_ref, r_ref, rs_ref, p_ref, s_ref, ss_ref, cr_ref, cs_ref, scal_ref,
    diag_ref, wcat_ref, wstore_ref, table_ref, group_ref, cats_ref, same_ref,
    x_out, r_out, p_out, s_out, scal_out, a_out, send_ref, values, field, rs_out,
):
    horizon, n, _ = diag_ref.shape
    clear_tail(field, horizon, n)
    for h in range(horizon):
        field[h * n : (h + 1) * n, :] = a_ref[h] + rows_of(got_ref, n, horizon + h)
    sums = category_sums(field, table_ref, group_ref, n, wcat_ref.shape[0])
    gamma, delta, eps = totals(got_ref, n, 2 * horizon)
    beta = gamma / scal_ref[0:1, :]
    curve = delta + 2.0 * beta * eps + beta * beta * scal_ref[1:2, :]
    alpha = gamma / curve
    scal_out[0:1, :] = gamma
    scal_out[1:2, :] = curve
    for h in range(horizon):
        ws = rows_of(got_ref, n, h) + reg_ref[h]
        rs_out[h] = rs_ref[h] - alpha * (ws + beta * ss_ref[h])
    delta = region_part(rs_out, wstore_ref, same_ref, region_sender(send_ref, n, 0, None))
    gamma = jnp.zeros((n, LANES), jnp.float32)
    eps = jnp.zeros((n, LANES), jnp.float32)
    for h in range(horizon):
        s = field[h * n : (h + 1) * n, :] + beta * s_ref[h]
        s_out[h] = s
        r = r_ref[h]
        p = r + beta * p_ref[h]
        p_out[h] = p
        x_out[h] = x_ref[h] + alpha * p
        r = r - alpha * s
        r_out[h] = r
        gamma = gamma + r * r
        delta = delta + diag_ref[h] * r * r
        eps = eps + r * s
    sums = cr_ref[...] - wide(alpha) * (sums + wide(beta) * cs_ref[...])
    store_part(
        r_out, sums, gamma, delta, eps, diag_ref, wcat_ref, cats_ref,
        store_sender(None, n, a_out), lambda line: put_rows(send_ref, n, horizon, line), values,
    )


def last_body(a_ref, got_ref, x_ref, r_ref, p_ref, s_ref, scal_ref, x_out, r_out):
    horizon, n, _ = a_ref.shape
    gamma, delta, eps = totals(got_ref, n, horizon)
    beta = gamma / scal_ref[0:1, :]
    alpha = gamma / (delta + 2.0 * beta * eps + beta * beta * scal_ref[1:2, :])
    for h in range(horizon):
        r = r_ref[h]
        s = a_ref[h] + rows_of(got_ref, n, h) + beta * s_ref[h]
        x_out[h] = x_ref[h] + alpha * (r + beta * p_ref[h])
        r_out[h] = r - alpha * s


def on_device(
    base_bottom,
    weight_bottom,
    base_category,
    weight_category,
    base_region,
    weight_region,
    category_map,
    region_map,
):
    stores, horizon, skus = base_bottom.shape
    n = region_map.shape[0]
    groups = weight_category.shape[2] // WIDE
    tiles = weight_category.shape[2] // LANES
    field = (horizon, n, LANES)
    padded = (PAD * n, LANES)
    by_category = (horizon, tiles, LANES)
    scal = (2, LANES)
    values = pltpu.VMEM((groups * PAD, WIDE), jnp.float32)

    x = base_bottom.reshape(field)
    diag = weight_bottom.reshape(field)
    (sent,) = call(
        pack_body,
        [(n * horizon, LANES)],
        [pltpu.VMEM(field, jnp.float32), pltpu.SemaphoreType.DMA],
        (x,),
        [HBM],
        True,
    )
    got = exchange(sent, n)
    arguments = (
        x,
        base_category.reshape(by_category),
        weight_category.reshape(by_category),
        jnp.transpose(base_region, (1, 0, 2)),
        jnp.transpose(weight_region, (1, 0, 2)),
        category_map.reshape(n, LANES),
        region_map.reshape(1, n),
    )
    held = [pltpu.VMEM(arguments[i].shape, arguments[i].dtype) for i in (0, 1, 2, 3, 4, 6)]
    spread, wcat, wstore, bstore, same, table, group, cats = call(
        prepare_body,
        [
            field,
            (groups * PAD, WIDE),
            field,
            field,
            jax.ShapeDtypeStruct((n, n), jnp.bfloat16),
            jax.ShapeDtypeStruct((skus, WIDE), jnp.bfloat16),
            jax.ShapeDtypeStruct((PAD, skus), jnp.bfloat16),
            jax.ShapeDtypeStruct((n, LANES), jnp.int32),
        ],
        [
            pltpu.VMEM(padded, jnp.float32),
            values,
            *held,
            pltpu.SemaphoreType.DMA((len(arguments),)),
        ],
        arguments,
        [HBM] * len(arguments),
    )
    reg, sent = call(
        region_start_body,
        [field, (n * 2 * horizon, LANES)],
        [],
        (got, spread, wstore, bstore, same),
    )
    got = exchange(sent, n)
    fixed = (diag, wcat, wstore, table, group, cats, same)
    both = (n * (2 * horizon + 1), LANES)
    work = [values, pltpu.VMEM(padded, jnp.float32)]
    sums = (groups * PAD, WIDE)
    r, rs, cr, a, reg, sent = call(
        first_body, [field, field, sums, field, field, both], work, (spread, reg, got) + fixed
    )
    got = exchange(sent, n)
    p = r
    x, r, rs, s, ss, cr, cs, scalars, a, reg, sent = call(
        second_body,
        [field, field, field, field, field, sums, sums, scal, field, field, both],
        work,
        (a, reg, got, x, r, rs, cr) + fixed,
    )
    got = exchange(sent, n)
    x, r, p, s, scalars, a, sent = call(
        third_body,
        [field, field, field, field, scal, field, (n * (horizon + 1), LANES)],
        work + [pltpu.VMEM(field, jnp.float32)],
        (a, reg, got, x, r, rs, p, s, ss, cr, cs, scalars) + fixed,
    )
    got = exchange(sent, n)
    x, r = call(last_body, [field, field], [], (a, got, x, r, p, s, scalars))
    return x.reshape(base_bottom.shape), r.reshape(base_bottom.shape)


def week_rows(tiles, n, regions):
    sizes = (n, n, tiles, tiles, regions, regions)
    return [sum(sizes[:i]) for i in range(len(sizes) + 1)]


def week_pack_body(*refs):
    sources, cats_hbm, out, table_out, group_out, cats, sems = refs[:-6], *refs[-6:]
    horizon = sources[0].shape[0]
    cats_copy = pltpu.make_async_copy(cats_hbm, cats, sems.at[len(sources)])
    cats_copy.start()
    copies, start = [], 0
    for i, source in enumerate(sources):
        rows = source.shape[1]
        target = out.at[pl.ds(0, horizon), pl.ds(start, rows)]
        copies.append(pltpu.make_async_copy(source, target, sems.at[i]))
        start += rows
    for copy in copies:
        copy.start()
    cats_copy.wait()
    downward = lax.broadcasted_iota(jnp.int32, (WIDE, LANES), 0)
    for j in range(cats.shape[0]):
        lanes = slice(j * LANES, (j + 1) * LANES)
        members = cats[j : j + 1, :]
        table_out[:, lanes] = jnp.where(
            (members & (WIDE - 1)) == downward, 1.0, 0.0
        ).astype(jnp.bfloat16)
        group = jnp.broadcast_to(members >> (WIDE.bit_length() - 1), (group_out.shape[0], LANES))
        group_out[:, lanes] = group.astype(jnp.float32).astype(jnp.bfloat16)
    for copy in copies:
        copy.wait()


def ratio(top, bottom):
    return jnp.where(bottom > 0.0, top / bottom, 0.0)


def whole_sum(part):
    total = jnp.sum(jnp.sum(part, axis=0, keepdims=True), axis=1, keepdims=True)
    return jnp.broadcast_to(total, (1, LANES))


def week_body(
    core_ref, place_ref, map_ref, own_ref, other_ref, table_ref, group_ref, cats_ref,
    kept_out, line_out,
    base, basis, diag, wstore, bstore, wcat, bcat, raw_weight, raw_base, held,
    side,
):
    core = core_ref[0]
    n, skus = base.shape
    per = own_ref.shape[0] // line_out.shape[0]
    regions = raw_weight.shape[0]
    tiles = wcat.shape[0] // n * (WIDE // LANES)
    starts = week_rows(tiles, n, regions)
    chunk = min(skus, 8 * LANES)
    chunks = [slice(c, c + chunk) for c in range(0, skus, chunk)]
    for ref, c in ((own_ref, core), (other_ref, 1 - core)):
        for x in range(n // (CORES * side)):
            for t in range(0, side, 8):
                first = (x * side + t) * per
                top = pl.multiple_of(x * CORES * side + c * side + t, 8)

                def rows(row):
                    return ref[pl.ds(first + row, 8, stride=per), :]

                for j in range(n):
                    lanes = slice(j * LANES, (j + 1) * LANES)
                    base[pl.ds(top, 8), lanes] = rows(starts[0] + j)
                    diag[pl.ds(top, 8), lanes] = rows(starts[1] + j)
                for g in range(tiles):
                    lane = g * LANES % WIDE
                    down = pl.multiple_of(g * LANES // WIDE * n + top, 8)
                    wcat[pl.ds(down, 8), lane : lane + LANES] = rows(starts[2] + g)
                    bcat[pl.ds(down, 8), lane : lane + LANES] = rows(starts[3] + g)
            for k in range(side):
                first = (x * side + k) * per
                j = x * CORES * side + c * side + k
                lanes = pl.ds(pl.multiple_of(j * LANES, LANES), LANES)
                raw_base[:, lanes] = ref[first + starts[4] : first + starts[5], :]
                raw_weight[:, lanes] = ref[first + starts[5] : first + starts[6], :]

    lane = lax.broadcasted_iota(jnp.int32, (n, LANES), 1)
    line = lax.broadcasted_iota(jnp.int32, (n, LANES), 0)
    across = jnp.zeros((n, LANES), jnp.int32)
    down = jnp.zeros((n, LANES), jnp.int32)
    for s in range(n):
        across = jnp.where(lane % n == s, map_ref[s], across)
        down = jnp.where(line == s, map_ref[s], down)
    same = jnp.where(across == down, 1.0, 0.0).astype(jnp.bfloat16)[:, : 2 * n]
    region_table = jnp.where(lane % regions == down, 1.0, 0.0)
    region_table = region_table.astype(jnp.bfloat16)[:, : 3 * regions]
    for source, target in ((raw_weight, wstore), (raw_base, bstore)):
        for lanes in chunks:
            parts = jnp.concatenate(split_all(source[:, lanes]), axis=0)
            target[:, lanes] = product(region_table, parts, ((1,), (0,)))

    def by_category(field):
        rows = wcat.shape[0]
        total = None
        for lanes in chunks:
            group = group_ref[:, lanes]
            masks = [group == g for g in range(rows // n)]
            none = jnp.zeros(group.shape, jnp.bfloat16)
            spread = jnp.concatenate(
                [jnp.where(mask, part, none) for part in split(field[:, lanes]) for mask in masks],
                axis=0,
            )
            part = product(spread, table_ref[:, lanes], ((1,), (1,)))
            total = part if total is None else total + part
        return total[:rows] + total[rows:]

    def spread(values, m, put):
        parts = jnp.concatenate(split(values), axis=0)
        groups = values.shape[0] // m
        for lanes in chunks:
            found = product(parts, table_ref[:, lanes], ((1,), (0,)))
            for t in range(0, chunk, LANES):
                tile = slice(lanes.start + t, lanes.start + t + LANES)
                members = cats_ref[tile.start // LANES : tile.start // LANES + 1, :]
                group = jnp.broadcast_to(members >> (WIDE.bit_length() - 1), (m, LANES))
                high, low = found[: groups * m, t : t + LANES], found[groups * m :, t : t + LANES]
                one = [
                    high[g * m : (g + 1) * m] + low[g * m : (g + 1) * m] for g in range(groups)
                ]
                bit = 1
                while len(one) > 1:
                    odd = group & bit != 0
                    pairs = [one[i : i + 2] for i in range(0, len(one), 2)]
                    one = [jnp.where(odd, *pair[::-1]) if len(pair) == 2 else pair[0] for pair in pairs]
                    bit *= 2
                put(tile, one[0])

    def by_region(part):
        return product(same, jnp.concatenate(split(part), axis=0), ((1,), (0,)))

    def tiles_in(lanes):
        for t in range(0, chunk, LANES):
            yield slice(lanes.start + t, lanes.start + t + LANES), slice(t, t + LANES)

    zero = jnp.zeros((n, LANES), jnp.float32)
    for lanes in chunks:
        sums = by_region(base[:, lanes])
        for tile, inner in tiles_in(lanes):
            basis[0, :, tile] = wstore[:, tile] * (bstore[:, tile] - sums[:, inner])
    norm = [zero]

    def start(tile, value):
        result = basis[0, :, tile] + value
        basis[0, :, tile] = result
        norm[0] = norm[0] + result * result

    spread(wcat[...] * (bcat[...] - by_category(base)), n, start)
    norms, quotients = [whole_sum(norm[0])], []
    for k in range(3):
        field, image = basis.at[k], basis.at[k + 1]
        sums = by_category(field)
        values = wcat[...] * sums
        square = values * sums
        dot = zero
        for lane in range(0, WIDE, LANES):
            for g in range(0, square.shape[0], n):
                dot = dot + square[g : g + n, lane : lane + LANES]
        for lanes in chunks:
            sums = by_region(field[:, lanes])
            for tile, inner in tiles_in(lanes):
                part = field[:, tile]
                result = diag[:, tile] * part + wstore[:, tile] * sums[:, inner]
                image[:, tile] = result
                dot = dot + part * result
        quotients.append(ratio(whole_sum(dot), norms[k]))
        back = ratio(norms[k], norms[k - 1]) if k else None
        if k == 2:
            break
        norm = [zero]

        def step(tile, value):
            result = image[:, tile] + value - quotients[k] * field[:, tile]
            if k:
                result = result - back * basis[k - 1, :, tile]
            image[:, tile] = result
            norm[0] = norm[0] + result * result

        spread(values, n, step)
        norms.append(whole_sum(norm[0]))

    lane = lax.broadcasted_iota(jnp.int32, line_out.shape, 1)
    place = lax.broadcasted_iota(jnp.int32, line_out.shape, 0)
    line = jnp.where((lane == 6) & (place == place_ref[0]), 1.0, 0.0)
    for i, value in enumerate(norms + quotients):
        line = jnp.where(lane == i, jnp.broadcast_to(value, line.shape), line)
    line_out[...] = line

    held[...] = values
    weeks = line_out.shape[0]
    tops = [
        pl.multiple_of(x * CORES * side + core * side + t, 8)
        for x in range(n // (CORES * side))
        for t in range(0, side, 8)
    ]
    for i, top in enumerate(tops):
        kept_out[4, i * 8 : i * 8 + 8, :] = base[pl.ds(top, 8), :]
        for k in range(4):
            kept_out[k, i * 8 : i * 8 + 8, :] = basis[k, pl.ds(top, 8), :]
    mine = jnp.concatenate(
        [held[pl.ds(g + top, 8), :] for g in range(0, held.shape[0], n) for top in tops], axis=0
    )

    def finish(tile, value):
        result = kept_out[3, :, tile] + value - quotients[2] * kept_out[2, :, tile]
        kept_out[3, :, tile] = result - back * kept_out[1, :, tile]

    spread(mine, weeks, finish)


def week_combine_body(lines_ref, kept_ref, send_ref, horizon):
    weeks = lines_ref.shape[0]
    n = kept_ref.shape[2] // LANES
    week = lax.broadcasted_iota(jnp.int32, (weeks, LANES), 0)
    lines = jnp.where(week < horizon, lines_ref[...], 0.0)
    n1, n2, n3, a1, a2, a3, mark = [
        jnp.take_along_axis(lines, jnp.full((weeks, LANES), i, jnp.int32), axis=1) for i in range(7)
    ]
    e2, e3 = ratio(n2, n1), ratio(n3, n2)

    def dot(left, right):
        terms = n1 * left[0] * right[0] + n2 * left[1] * right[1] + n3 * left[2] * right[2]
        return jnp.sum(terms, axis=0, keepdims=True)

    zero = jnp.zeros((weeks, LANES), jnp.float32)
    x = [zero, zero, zero]
    r = [zero + 1.0, zero, zero, zero]
    p = r[:3]
    rr = dot(r, r)
    for k in range(3):
        image = [
            a1 * p[0] + e2 * p[1],
            p[0] + a2 * p[1] + e3 * p[2],
            p[1] + a3 * p[2],
            p[2],
        ]
        alpha = rr / dot(p, image)
        x = [left + alpha * right for left, right in zip(x, p)]
        r = [left - alpha * right for left, right in zip(r, image)]
        if k < 2:
            new = dot(r, r)
            p = [left + new / rr * right for left, right in zip(r[:3], p)]
            rr = new
    mine = mark > 0.0
    x = [jnp.sum(jnp.where(mine, value, 0.0), axis=0, keepdims=True) for value in x]
    r = [jnp.sum(jnp.where(mine, value, 0.0), axis=0, keepdims=True) for value in r]
    rows = send_ref.shape[0] // weeks
    for t in range(0, weeks, 8):
        for j in range(n):
            lanes = slice(j * LANES, (j + 1) * LANES)
            parts = [kept_ref[k, t : t + 8, lanes] for k in range(4)]
            left = kept_ref[4, t : t + 8, lanes]
            right = r[3] * parts[3]
            for k in range(3):
                left = left + x[k] * parts[k]
                right = right + r[k] * parts[k]
            first = t * rows + j
            send_ref[pl.ds(first, 8, stride=rows), :] = left
            send_ref[pl.ds(first + n, 8, stride=rows), :] = right


def week_last_body(got_ref, x_out, r_out, sems):
    horizon, n, _ = x_out.shape
    copies = [
        pltpu.make_async_copy(
            got_ref.at[pl.ds(0, horizon), pl.ds(i * n, n)], target, sems.at[i]
        )
        for i, target in enumerate((x_out, r_out))
    ]
    for copy in copies:
        copy.start()
    for copy in copies:
        copy.wait()


def exchange_weeks(blocks):
    return lax.all_to_all(blocks, ("x", "sku"), split_axis=0, concat_axis=0, tiled=True)


def by_weeks(
    base_bottom,
    weight_bottom,
    base_category,
    weight_category,
    base_region,
    weight_region,
    category_map,
    region_map,
):
    stores, horizon, skus = base_bottom.shape
    n = region_map.shape[0]
    regions = weight_region.shape[0]
    tiles = weight_category.shape[2] // LANES
    groups = weight_category.shape[2] // WIDE
    side = lax.axis_size("sku")
    weeks = lax.axis_size("x") * side
    place = lax.axis_index("x") * side + lax.axis_index("sku")
    place = place.astype(jnp.int32).reshape(1)
    core = lax.axis_index("core").astype(jnp.int32).reshape(1)
    cats = category_map.reshape(n, LANES)
    sources = (
        base_bottom.reshape(horizon, n, LANES),
        weight_bottom.reshape(horizon, n, LANES),
        weight_category.reshape(horizon, tiles, LANES),
        base_category.reshape(horizon, tiles, LANES),
        jnp.transpose(base_region, (1, 0, 2)),
        jnp.transpose(weight_region, (1, 0, 2)),
    )
    per = week_rows(tiles, n, regions)[-1]
    sent, table, group = call(
        week_pack_body,
        [
            (weeks, per, LANES),
            jax.ShapeDtypeStruct((WIDE, skus), jnp.bfloat16),
            jax.ShapeDtypeStruct((n, skus), jnp.bfloat16),
        ],
        [pltpu.VMEM(cats.shape, jnp.int32), pltpu.SemaphoreType.DMA((len(sources) + 1,))],
        sources + (cats,),
        [HBM] * (len(sources) + 1),
        out_specs=(HBM, VMEM, VMEM),
    )
    own = exchange_weeks(sent)
    other = lax.ppermute(own, "core", [(0, 1), (1, 0)])
    full = pltpu.VMEM((n, skus), jnp.float32)
    raw = pltpu.VMEM((regions, skus), jnp.float32)
    cat = pltpu.VMEM((groups * n, WIDE), jnp.float32)
    kept, line = call(
        lambda *refs: week_body(*refs, side),
        [(5, weeks, skus), (weeks, LANES)],
        [
            full, pltpu.VMEM((4, n, skus), jnp.float32),
            full, full, full, cat, cat, raw, raw, cat,
        ],
        (
            core, place, region_map, own.reshape(-1, LANES), other.reshape(-1, LANES),
            table, group, cats,
        ),
        [SMEM] * 3 + [VMEM, FREE] + [VMEM] * 3,
    )
    lines = exchange_weeks(line.reshape(weeks, 1, LANES)).reshape(weeks, LANES)
    (sent,) = call(
        lambda *refs: week_combine_body(*refs, horizon),
        [(weeks * 2 * n, LANES)],
        [],
        (lines, kept),
        [VMEM] * 2,
    )
    got = exchange_weeks(sent.reshape(weeks, 2 * n, LANES))
    x, r = call(
        week_last_body,
        [(horizon, n, LANES)] * 2,
        [pltpu.SemaphoreType.DMA((2,))],
        (got,),
        [VMEM],
        out_specs=(HBM, HBM),
    )
    return x.reshape(base_bottom.shape), r.reshape(base_bottom.shape)


def solution(mesh):
    def mapped(device_mesh, body, stores):
        split_stores = P(stores, None, None)
        split_skus = P(None, None, stores)
        return jax.shard_map(
            body,
            mesh=device_mesh,
            in_specs=(split_stores,) * 4 + (split_skus,) * 2 + (P(), P()),
            out_specs=(split_stores,) * 2,
            check_vma=False,
        )

    side = mesh.shape["sku"]
    chips = mesh.devices.reshape(-1, CORES, side)

    def program(base_bottom, *others):
        stores, horizon, skus = base_bottom.shape
        fits = 16 * stores * skus * 4 <= 16 << 20
        fits = fits and 3 * others[3].shape[0] <= LANES and LANES % stores == 0
        if fits and horizon <= chips.shape[0] * side and side % 8 == 0:
            device_mesh = Mesh(chips, ("x", "core", "sku"))
            return mapped(device_mesh, by_weeks, ("x", "core", "sku"))(base_bottom, *others)
        return mapped(mesh, on_device, ("store", "sku"))(base_bottom, *others)

    return program
```

```python
import jax
import jax.numpy as jnp
from jax import lax
from jax.experimental import pallas as pl
from jax.experimental.pallas import tpu as pltpu
from jax.sharding import Mesh
from jax.sharding import PartitionSpec as P

LANES = 128
PAD = 16
WIDE = 256
VMEM = pl.BlockSpec(memory_space=pltpu.VMEM)
HBM = pl.BlockSpec(memory_space=pltpu.HBM)
SMEM = pl.BlockSpec(memory_space=pltpu.SMEM)
FREE = pl.BlockSpec(memory_space=pltpu.VMEM)
CORES = 2


def exchange(blocks, n):
    moved = lax.all_to_all(
        blocks.reshape(n, 1, -1), ("store", "sku"), split_axis=0, concat_axis=0, tiled=True
    )
    return moved.reshape(blocks.shape)


def call(body, outs, scratch, args, specs=None, held=False, out_specs=None):
    outs = [
        out if isinstance(out, jax.ShapeDtypeStruct) else jax.ShapeDtypeStruct(out, jnp.float32)
        for out in outs
    ]
    specs = specs or [VMEM] * len(args)
    args = [
        arg if spec is SMEM or spec is FREE else pltpu.with_memory_space_constraint(arg, spec.memory_space)
        for arg, spec in zip(args, specs)
    ]
    return pl.pallas_call(
        body,
        out_shape=tuple(pltpu.VMEM(out.shape, out.dtype) if held else out for out in outs),
        in_specs=specs,
        out_specs=out_specs or tuple(VMEM for _ in outs),
        scratch_shapes=scratch,
        compiler_params=pltpu.CompilerParams(vmem_limit_bytes=24 << 20),
    )(*args)


def split(value):
    high = value.astype(jnp.bfloat16)
    return high, (value - high.astype(jnp.float32)).astype(jnp.bfloat16)


def split_all(value):
    high, low = split(value)
    rest = value - high.astype(jnp.float32) - low.astype(jnp.float32)
    return high, low, rest.astype(jnp.bfloat16)


def product(left, right, contract):
    return lax.dot_general(left, right, (contract, ((), ())), preferred_element_type=jnp.float32)


def rows_of(ref, n, h):
    return ref[pl.ds(h, n, stride=ref.shape[0] // n), :]


def put_rows(ref, n, h, value):
    ref[pl.ds(h, n, stride=ref.shape[0] // n), :] = value


def category_sums(field, table_ref, group_ref, n, rows):
    width = 4 if n % 4 == 0 else 1
    lanes = width * LANES

    def step(c, total):
        pieces = [field[pl.ds(c * width + i, PAD, stride=n), :] for i in range(width)]
        parts = split_all(jnp.concatenate(pieces, axis=1))
        start = pl.multiple_of(c * lanes, lanes)
        group = group_ref[:, pl.ds(start, lanes)]
        masks = [group == g for g in range(rows // PAD)]
        none = jnp.zeros((PAD, lanes), jnp.bfloat16)
        spread = jnp.concatenate(
            [jnp.where(mask, part, none) for part in parts for mask in masks], axis=0
        )
        return total + product(spread, table_ref[pl.ds(start, lanes), :], ((1,), (0,)))

    steps = n // width
    total = lax.fori_loop(
        0, steps, step, jnp.zeros((3 * rows, WIDE), jnp.float32), unroll=min(steps, 8)
    )
    return total[:rows] + (total[rows : 2 * rows] + total[2 * rows :])


def category_spread(values, cats, horizon, put):
    place = cats & (LANES - 1)
    group = cats >> (LANES.bit_length() - 1)
    for h in range(horizon):
        found = []
        for g in range(0, values.shape[0], PAD):
            for lane in range(0, WIDE, LANES):
                row = jnp.broadcast_to(values[g + h : g + h + 1, lane : lane + LANES], cats.shape)
                found.append(jnp.take_along_axis(row, place, axis=1))
        for bit in range((len(found) - 1).bit_length()):
            mask = group & (1 << bit) != 0
            pairs = [found[i : i + 2] for i in range(0, len(found), 2)]
            found = [jnp.where(mask, pair[1], pair[0]) if len(pair) == 2 else pair[0] for pair in pairs]
        put(h, found[0])


def tiles_of(n):
    return [slice(t, t + 8) for t in range(0, n, 8)]


def put_tile(ref, n, h, tile, value):
    rows = ref.shape[0] // n
    ref[pl.ds(tile.start * rows + h, 8, stride=rows), :] = value


def region_sums(load, same, n, horizon):
    high, low = split(jnp.concatenate([load(h) for h in range(horizon)], axis=1))
    total = product(same, high, ((1,), (0,))) + product(same, low, ((1,), (0,)))
    return [total[:, h * LANES : (h + 1) * LANES] for h in range(horizon)]


def pack_body(base_hbm, out_ref, base_ref, sem):
    copy = pltpu.make_async_copy(base_hbm, base_ref, sem)
    copy.start()
    copy.wait()
    n = base_ref.shape[1]
    for h in range(base_ref.shape[0]):
        put_rows(out_ref, n, h, base_ref[h])


def prepare_body(
    base_hbm, base_cat_hbm, weight_cat_hbm, base_reg_hbm, weight_reg_hbm, cats_hbm, map_hbm,
    spread_out, wcat_out, wstore_out, bstore_out, same_out, table_out, group_out,
    cats_ref,
    field, values, base_ref, base_cat_ref, weight_cat_ref, base_reg_ref, weight_reg_ref, map_ref, sems,
):
    copies = [
        pltpu.make_async_copy(source, target, sems.at[i])
        for i, (source, target) in enumerate(
            (
                (cats_hbm, cats_ref),
                (base_hbm, base_ref),
                (weight_cat_hbm, weight_cat_ref),
                (base_cat_hbm, base_cat_ref),
                (map_hbm, map_ref),
                (weight_reg_hbm, weight_reg_ref),
                (base_reg_hbm, base_reg_ref),
            )
        )
    ]
    for copy in copies:
        copy.start()
    for copy in copies:
        copy.wait()
    horizon, n, _ = base_ref.shape
    n_regions = weight_reg_ref.shape[1]
    square = jnp.concatenate([cats_ref[...].astype(jnp.float32)] * (LANES // min(n, LANES)), axis=0)
    labels = lax.broadcasted_iota(jnp.int32, (LANES, WIDE), 1)
    columns = [
        jnp.transpose(square[i : i + LANES]).astype(jnp.int32) % WIDE
        for i in range(0, square.shape[0], LANES)
    ]
    for j in range(n):
        column = jnp.broadcast_to(columns[j // LANES][:, j % LANES : j % LANES + 1], (LANES, WIDE))
        table_out[j * LANES : (j + 1) * LANES, :] = jnp.where(
            column == labels, 1.0, 0.0
        ).astype(jnp.bfloat16)
        group = jnp.broadcast_to(cats_ref[j : j + 1, :] // WIDE, (PAD, LANES))
        group_out[:, j * LANES : (j + 1) * LANES] = group.astype(jnp.float32).astype(jnp.bfloat16)

    field[...] = jnp.zeros_like(field)
    for h in range(horizon):
        field[h * n : (h + 1) * n, :] = base_ref[h]
    sums = category_sums(field, table_out, group_out, n, wcat_out.shape[0])
    wcat_out[...] = jnp.zeros_like(wcat_out)
    values[...] = jnp.zeros_like(values)
    for g in range(0, wcat_out.shape[0], PAD):
        for lane in range(0, WIDE, LANES):
            tile = (g // PAD * WIDE + lane) // LANES
            lanes = slice(lane, lane + LANES)
            weight = weight_cat_ref[:, tile, :]
            wcat_out[g : g + horizon, lanes] = weight
            values[g : g + horizon, lanes] = weight * (
                base_cat_ref[:, tile, :] - sums[g : g + horizon, lanes]
            )
    for tile in tiles_of(n):

        def put(h, value):
            spread_out[h, tile, :] = value

        category_spread(values, cats_ref[tile, :], horizon, put)

    labels = lax.broadcasted_iota(jnp.int32, (n_regions, n), 0)
    table = jnp.where(labels == map_ref[...], 1.0, 0.0).astype(jnp.bfloat16)
    same_out[...] = product(table, table, ((0,), (0,))).astype(jnp.bfloat16)
    for source, target in ((weight_reg_ref, wstore_out), (base_reg_ref, bstore_out)):
        for h in range(horizon):
            high, low = split(source[h])
            rest = source[h] - high.astype(jnp.float32) - low.astype(jnp.float32)
            target[h] = (
                product(table, high, ((0,), (0,)))
                + product(table, low, ((0,), (0,)))
                + product(table, rest.astype(jnp.bfloat16), ((0,), (0,)))
            )


def region_start_body(got_ref, spread_ref, wstore_ref, bstore_ref, same_ref, reg_out, send_ref):
    horizon, n, _ = spread_ref.shape
    sums = region_sums(lambda h: rows_of(got_ref, n, h), same_ref[...], n, horizon)
    for h in range(horizon):
        put_rows(send_ref, n, h, spread_ref[h])
        part = wstore_ref[h] * (bstore_ref[h] - sums[h])
        reg_out[h] = part
        put_rows(send_ref, n, horizon + h, part)


def region_part(rs, wstore_ref, same_ref, put):
    horizon, n, _ = wstore_ref.shape
    sums = region_sums(lambda h: rs[h], same_ref[...], n, horizon)
    share = jnp.zeros((n, LANES), jnp.float32)
    for h in range(horizon):
        part = wstore_ref[h] * sums[h]
        share = share + part * rs[h]
        put(h, part)
    return share


def store_part(r_ref, sums, gamma, delta, eps, diag_ref, wcat_ref, cats_ref, put, put_line, values):
    horizon, n, _ = diag_ref.shape
    scaled = wcat_ref[...] * sums
    values[...] = scaled
    square = scaled * sums
    delta = jnp.sum(delta, axis=0, keepdims=True)
    for lane in range(0, WIDE, LANES):
        delta = delta + jnp.sum(square[:, lane : lane + LANES], axis=0, keepdims=True)
    lane = lax.broadcasted_iota(jnp.int32, (1, LANES), 1)
    line = jnp.zeros((1, LANES), jnp.float32)
    for i, part in enumerate((gamma, delta, eps)):
        if part is not None:
            whole = jnp.sum(jnp.sum(part, axis=0, keepdims=True), axis=1, keepdims=True)
            line = jnp.where(lane == i, whole, line)
    put_line(jnp.broadcast_to(line, (n, LANES)))
    for tile in tiles_of(n):

        def finish(h, value):
            put(h, tile, value + diag_ref[h, tile, :] * r_ref[h, tile, :])

        category_spread(values, cats_ref[tile, :], horizon, finish)


def totals(got_ref, n, row):
    total = jnp.sum(rows_of(got_ref, n, row), axis=0, keepdims=True)
    total = jnp.broadcast_to(total, (8, LANES))
    return [
        jnp.take_along_axis(total, jnp.full((8, LANES), i, jnp.int32), axis=1)[0:1] for i in range(3)
    ]


def wide(line):
    return jnp.concatenate([line] * (WIDE // LANES), axis=1)


def region_sender(ref, n, first, keep):
    def put(h, value):
        if keep is not None:
            keep[h] = value
        put_rows(ref, n, first + h, value)

    return put


def store_sender(ref, n, keep):
    def put(h, tile, value):
        keep[h, tile, :] = value
        if ref is not None:
            put_tile(ref, n, h, tile, value)

    return put


def clear_tail(field, horizon, n):
    field[horizon * n :, :] = jnp.zeros((field.shape[0] - horizon * n, LANES), jnp.float32)


def first_body(
    a_ref, reg_ref, got_ref, diag_ref, wcat_ref, wstore_ref, table_ref, group_ref, cats_ref, same_ref,
    r_out, rs_out, cr_out, a_out, reg_out, send_ref, values, field,
):
    horizon, n, _ = diag_ref.shape
    clear_tail(field, horizon, n)
    gamma = jnp.zeros((n, LANES), jnp.float32)
    delta = jnp.zeros((n, LANES), jnp.float32)
    for h in range(horizon):
        r = a_ref[h] + rows_of(got_ref, n, horizon + h)
        r_out[h] = r
        field[h * n : (h + 1) * n, :] = r
        gamma = gamma + r * r
        delta = delta + diag_ref[h] * r * r
    sums = category_sums(field, table_ref, group_ref, n, wcat_ref.shape[0])
    cr_out[...] = sums
    for h in range(horizon):
        rs_out[h] = rows_of(got_ref, n, h) + reg_ref[h]
    delta = delta + region_part(
        rs_out, wstore_ref, same_ref, region_sender(send_ref, n, horizon, reg_out)
    )
    store_part(
        r_out, sums, gamma, delta, None, diag_ref, wcat_ref, cats_ref,
        store_sender(send_ref, n, a_out),
        lambda line: put_rows(send_ref, n, 2 * horizon, line), values,
    )


def second_body(
    a_ref, reg_ref, got_ref, x_ref, r_ref, rs_ref, cr_ref,
    diag_ref, wcat_ref, wstore_ref, table_ref, group_ref, cats_ref, same_ref,
    x_out, r_out, rs_out, s_out, ss_out, cr_out, cs_out, scal_ref, a_out, reg_out, send_ref,
    values, field,
):
    horizon, n, _ = diag_ref.shape
    clear_tail(field, horizon, n)
    for h in range(horizon):
        field[h * n : (h + 1) * n, :] = a_ref[h] + rows_of(got_ref, n, horizon + h)
    sums = category_sums(field, table_ref, group_ref, n, wcat_ref.shape[0])
    cs_out[...] = sums
    gamma, delta, _ = totals(got_ref, n, 2 * horizon)
    alpha = gamma / delta
    scal_ref[0:1, :] = gamma
    scal_ref[1:2, :] = delta
    for h in range(horizon):
        ws = rows_of(got_ref, n, h) + reg_ref[h]
        ss_out[h] = ws
        rs_out[h] = rs_ref[h] - alpha * ws
    delta = region_part(
        rs_out, wstore_ref, same_ref, region_sender(send_ref, n, horizon, reg_out)
    )
    gamma = jnp.zeros((n, LANES), jnp.float32)
    eps = jnp.zeros((n, LANES), jnp.float32)
    for h in range(horizon):
        s = field[h * n : (h + 1) * n, :]
        s_out[h] = s
        r = r_ref[h]
        x_out[h] = x_ref[h] + alpha * r
        r = r - alpha * s
        r_out[h] = r
        gamma = gamma + r * r
        delta = delta + diag_ref[h] * r * r
        eps = eps + r * s
    sums = cr_ref[...] - wide(alpha) * sums
    cr_out[...] = sums
    store_part(
        r_out, sums, gamma, delta, eps, diag_ref, wcat_ref, cats_ref,
        store_sender(send_ref, n, a_out),
        lambda line: put_rows(send_ref, n, 2 * horizon, line), values,
    )


def third_body(
    a_ref, reg_ref, got_ref, x_ref, r_ref, rs_ref, p_ref, s_ref, ss_ref, cr_ref, cs_ref, scal_ref,
    diag_ref, wcat_ref, wstore_ref, table_ref, group_ref, cats_ref, same_ref,
    x_out, r_out, p_out, s_out, scal_out, a_out, send_ref, values, field, rs_out,
):
    horizon, n, _ = diag_ref.shape
    clear_tail(field, horizon, n)
    for h in range(horizon):
        field[h * n : (h + 1) * n, :] = a_ref[h] + rows_of(got_ref, n, horizon + h)
    sums = category_sums(field, table_ref, group_ref, n, wcat_ref.shape[0])
    gamma, delta, eps = totals(got_ref, n, 2 * horizon)
    beta = gamma / scal_ref[0:1, :]
    curve = delta + 2.0 * beta * eps + beta * beta * scal_ref[1:2, :]
    alpha = gamma / curve
    scal_out[0:1, :] = gamma
    scal_out[1:2, :] = curve
    for h in range(horizon):
        ws = rows_of(got_ref, n, h) + reg_ref[h]
        rs_out[h] = rs_ref[h] - alpha * (ws + beta * ss_ref[h])
    delta = region_part(rs_out, wstore_ref, same_ref, region_sender(send_ref, n, 0, None))
    gamma = jnp.zeros((n, LANES), jnp.float32)
    eps = jnp.zeros((n, LANES), jnp.float32)
    for h in range(horizon):
        s = field[h * n : (h + 1) * n, :] + beta * s_ref[h]
        s_out[h] = s
        r = r_ref[h]
        p = r + beta * p_ref[h]
        p_out[h] = p
        x_out[h] = x_ref[h] + alpha * p
        r = r - alpha * s
        r_out[h] = r
        gamma = gamma + r * r
        delta = delta + diag_ref[h] * r * r
        eps = eps + r * s
    sums = cr_ref[...] - wide(alpha) * (sums + wide(beta) * cs_ref[...])
    store_part(
        r_out, sums, gamma, delta, eps, diag_ref, wcat_ref, cats_ref,
        store_sender(None, n, a_out), lambda line: put_rows(send_ref, n, horizon, line), values,
    )


def last_body(a_ref, got_ref, x_ref, r_ref, p_ref, s_ref, scal_ref, x_out, r_out):
    horizon, n, _ = a_ref.shape
    gamma, delta, eps = totals(got_ref, n, horizon)
    beta = gamma / scal_ref[0:1, :]
    alpha = gamma / (delta + 2.0 * beta * eps + beta * beta * scal_ref[1:2, :])
    for h in range(horizon):
        r = r_ref[h]
        s = a_ref[h] + rows_of(got_ref, n, h) + beta * s_ref[h]
        x_out[h] = x_ref[h] + alpha * (r + beta * p_ref[h])
        r_out[h] = r - alpha * s


def on_device(
    base_bottom,
    weight_bottom,
    base_category,
    weight_category,
    base_region,
    weight_region,
    category_map,
    region_map,
):
    stores, horizon, skus = base_bottom.shape
    n = region_map.shape[0]
    groups = weight_category.shape[2] // WIDE
    tiles = weight_category.shape[2] // LANES
    field = (horizon, n, LANES)
    padded = (PAD * n, LANES)
    by_category = (horizon, tiles, LANES)
    scal = (2, LANES)
    values = pltpu.VMEM((groups * PAD, WIDE), jnp.float32)

    x = base_bottom.reshape(field)
    diag = weight_bottom.reshape(field)
    (sent,) = call(
        pack_body,
        [(n * horizon, LANES)],
        [pltpu.VMEM(field, jnp.float32), pltpu.SemaphoreType.DMA],
        (x,),
        [HBM],
        True,
    )
    got = exchange(sent, n)
    arguments = (
        x,
        base_category.reshape(by_category),
        weight_category.reshape(by_category),
        jnp.transpose(base_region, (1, 0, 2)),
        jnp.transpose(weight_region, (1, 0, 2)),
        category_map.reshape(n, LANES),
        region_map.reshape(1, n),
    )
    held = [pltpu.VMEM(arguments[i].shape, arguments[i].dtype) for i in (0, 1, 2, 3, 4, 6)]
    spread, wcat, wstore, bstore, same, table, group, cats = call(
        prepare_body,
        [
            field,
            (groups * PAD, WIDE),
            field,
            field,
            jax.ShapeDtypeStruct((n, n), jnp.bfloat16),
            jax.ShapeDtypeStruct((skus, WIDE), jnp.bfloat16),
            jax.ShapeDtypeStruct((PAD, skus), jnp.bfloat16),
            jax.ShapeDtypeStruct((n, LANES), jnp.int32),
        ],
        [
            pltpu.VMEM(padded, jnp.float32),
            values,
            *held,
            pltpu.SemaphoreType.DMA((len(arguments),)),
        ],
        arguments,
        [HBM] * len(arguments),
    )
    reg, sent = call(
        region_start_body,
        [field, (n * 2 * horizon, LANES)],
        [],
        (got, spread, wstore, bstore, same),
    )
    got = exchange(sent, n)
    fixed = (diag, wcat, wstore, table, group, cats, same)
    both = (n * (2 * horizon + 1), LANES)
    work = [values, pltpu.VMEM(padded, jnp.float32)]
    sums = (groups * PAD, WIDE)
    r, rs, cr, a, reg, sent = call(
        first_body, [field, field, sums, field, field, both], work, (spread, reg, got) + fixed
    )
    got = exchange(sent, n)
    p = r
    x, r, rs, s, ss, cr, cs, scalars, a, reg, sent = call(
        second_body,
        [field, field, field, field, field, sums, sums, scal, field, field, both],
        work,
        (a, reg, got, x, r, rs, cr) + fixed,
    )
    got = exchange(sent, n)
    x, r, p, s, scalars, a, sent = call(
        third_body,
        [field, field, field, field, scal, field, (n * (horizon + 1), LANES)],
        work + [pltpu.VMEM(field, jnp.float32)],
        (a, reg, got, x, r, rs, p, s, ss, cr, cs, scalars) + fixed,
    )
    got = exchange(sent, n)
    x, r = call(last_body, [field, field], [], (a, got, x, r, p, s, scalars))
    return x.reshape(base_bottom.shape), r.reshape(base_bottom.shape)


def week_rows(tiles, n, regions):
    sizes = (n, n, tiles, tiles, regions, regions)
    return [sum(sizes[:i]) for i in range(len(sizes) + 1)]


def week_pack_body(*refs):
    sources, out, sems = refs[:-2], refs[-2], refs[-1]
    horizon = sources[0].shape[0]
    copies, start = [], 0
    for i, source in enumerate(sources):
        rows = source.shape[1]
        target = out.at[pl.ds(0, horizon), pl.ds(start, rows)]
        copies.append(pltpu.make_async_copy(source, target, sems.at[i]))
        start += rows
    for copy in copies:
        copy.start()
    for copy in copies:
        copy.wait()


def week_table_body(
    map_ref, cats_ref, table_out, flipped_out, group_out, same_out, region_out, regions
):
    n = cats_ref.shape[0]
    lane = lax.broadcasted_iota(jnp.int32, (n, LANES), 1)
    line = lax.broadcasted_iota(jnp.int32, (n, LANES), 0)
    across = jnp.zeros((n, LANES), jnp.int32)
    down = jnp.zeros((n, LANES), jnp.int32)
    for s in range(n):
        across = jnp.where(lane % n == s, map_ref[s], across)
        down = jnp.where(line == s, map_ref[s], down)
    same_out[...] = jnp.where(across == down, 1.0, 0.0).astype(jnp.bfloat16)
    region_out[...] = jnp.where(lane % regions == down, 1.0, 0.0).astype(jnp.bfloat16)
    square = jnp.concatenate([cats_ref[...].astype(jnp.float32)] * (LANES // min(n, LANES)), axis=0)
    labels = lax.broadcasted_iota(jnp.int32, (LANES, WIDE), 1)
    downward = lax.broadcasted_iota(jnp.int32, (WIDE, LANES), 0)
    columns = [
        jnp.transpose(square[i : i + LANES]).astype(jnp.int32) & (WIDE - 1)
        for i in range(0, square.shape[0], LANES)
    ]
    for j in range(n):
        column = jnp.broadcast_to(columns[j // LANES][:, j % LANES : j % LANES + 1], (LANES, WIDE))
        table_out[j * LANES : (j + 1) * LANES, :] = jnp.where(
            column == labels, 1.0, 0.0
        ).astype(jnp.bfloat16)
        flipped_out[:, j * LANES : (j + 1) * LANES] = jnp.where(
            (cats_ref[j : j + 1, :] & (WIDE - 1)) == downward, 1.0, 0.0
        ).astype(jnp.bfloat16)
        group = cats_ref[j : j + 1, :] >> (WIDE.bit_length() - 1)
        group = jnp.broadcast_to(group, (group_out.shape[0], LANES))
        group_out[:, j * LANES : (j + 1) * LANES] = group.astype(jnp.float32).astype(jnp.bfloat16)


def ratio(top, bottom):
    return jnp.where(bottom > 0.0, top / bottom, 0.0)


def whole_sum(part):
    total = jnp.sum(jnp.sum(part, axis=0, keepdims=True), axis=1, keepdims=True)
    return jnp.broadcast_to(total, (1, LANES))


def week_body(
    core_ref, place_ref, own_ref, other_ref, table_ref, flipped_ref, group_ref, same_ref, region_ref,
    cats_ref, kept_out, line_out,
    base, basis, diag, wstore, bstore, wcat, bcat, raw_weight, raw_base, held,
    side,
):
    core = core_ref[0]
    n, skus = base.shape
    per = own_ref.shape[0] // line_out.shape[0]
    regions = raw_weight.shape[0]
    tiles = wcat.shape[0] // n * (WIDE // LANES)
    starts = week_rows(tiles, n, regions)
    chunk = min(skus, 8 * LANES)
    chunks = [slice(c, c + chunk) for c in range(0, skus, chunk)]
    for ref, c in ((own_ref, core), (other_ref, 1 - core)):
        for x in range(n // (CORES * side)):
            for t in range(0, side, 8):
                first = (x * side + t) * per
                top = pl.multiple_of(x * CORES * side + c * side + t, 8)

                def rows(row):
                    return ref[pl.ds(first + row, 8, stride=per), :]

                for j in range(n):
                    lanes = slice(j * LANES, (j + 1) * LANES)
                    base[pl.ds(top, 8), lanes] = rows(starts[0] + j)
                    diag[pl.ds(top, 8), lanes] = rows(starts[1] + j)
                for g in range(tiles):
                    lane = g * LANES % WIDE
                    down = pl.multiple_of(g * LANES // WIDE * n + top, 8)
                    wcat[pl.ds(down, 8), lane : lane + LANES] = rows(starts[2] + g)
                    bcat[pl.ds(down, 8), lane : lane + LANES] = rows(starts[3] + g)
            for k in range(side):
                first = (x * side + k) * per
                j = x * CORES * side + c * side + k
                lanes = pl.ds(pl.multiple_of(j * LANES, LANES), LANES)
                raw_base[:, lanes] = ref[first + starts[4] : first + starts[5], :]
                raw_weight[:, lanes] = ref[first + starts[5] : first + starts[6], :]

    region_table = region_ref[:, : 3 * regions]
    same = same_ref[:, : 2 * n]
    for source, target in ((raw_weight, wstore), (raw_base, bstore)):
        for lanes in chunks:
            parts = jnp.concatenate(split_all(source[:, lanes]), axis=0)
            target[:, lanes] = product(region_table, parts, ((1,), (0,)))

    def by_category(field, lanes, total):
        group = group_ref[:, lanes]
        masks = [group == g for g in range(wcat.shape[0] // n)]
        none = jnp.zeros(group.shape, jnp.bfloat16)
        rows = [jnp.where(mask, part, none) for part in split(field) for mask in masks]
        part = product(jnp.concatenate(rows, axis=0), table_ref[lanes, :], ((1,), (0,)))
        return part if total is None else total + part

    def both_parts(total):
        return total[: wcat.shape[0]] + total[wcat.shape[0] :]

    def by_region(part):
        return product(same, jnp.concatenate(split(part), axis=0), ((1,), (0,)))

    def tiles_in(lanes):
        for t in range(0, chunk, LANES):
            yield slice(lanes.start + t, lanes.start + t + LANES), slice(t, t + LANES)

    def spread(parts, m, lanes):
        groups = parts.shape[0] // (2 * m)
        found = product(parts, flipped_ref[:, lanes], ((1,), (0,)))
        for tile, inner in tiles_in(lanes):
            members = cats_ref[tile.start // LANES : tile.start // LANES + 1, :]
            group = jnp.broadcast_to(members >> (WIDE.bit_length() - 1), (m, LANES))
            high, low = found[: groups * m, inner], found[groups * m :, inner]
            one = [high[g * m : (g + 1) * m] + low[g * m : (g + 1) * m] for g in range(groups)]
            bit = 1
            while len(one) > 1:
                odd = group & bit != 0
                pairs = [one[i : i + 2] for i in range(0, len(one), 2)]
                one = [jnp.where(odd, *pair[::-1]) if len(pair) == 2 else pair[0] for pair in pairs]
                bit *= 2
            yield tile, one[0]

    zero = jnp.zeros((n, LANES), jnp.float32)
    total = None
    for lanes in chunks:
        total = by_category(base[:, lanes], lanes, total)
        sums = by_region(base[:, lanes])
        for tile, inner in tiles_in(lanes):
            basis[0, :, tile] = wstore[:, tile] * (bstore[:, tile] - sums[:, inner])
    values = wcat[...] * (bcat[...] - both_parts(total))
    norms, quotients = [], []
    for k in range(3):
        field, image = basis.at[k], basis.at[k + 1]
        parts = jnp.concatenate(split(values), axis=0)
        back = ratio(norms[k - 1], norms[k - 2]) if k > 1 else None
        norm, dot, total = zero, zero, None
        for lanes in chunks:
            for tile, value in spread(parts, n, lanes):
                result = field[:, tile] + value
                if k > 0:
                    result = result - quotients[k - 1] * basis[k - 1, :, tile]
                if k > 1:
                    result = result - back * basis[k - 2, :, tile]
                field[:, tile] = result
                norm = norm + result * result
            total = by_category(field[:, lanes], lanes, total)
            sums = by_region(field[:, lanes])
            for tile, inner in tiles_in(lanes):
                part = field[:, tile]
                result = diag[:, tile] * part + wstore[:, tile] * sums[:, inner]
                image[:, tile] = result
                dot = dot + part * result
        norms.append(whole_sum(norm))
        sums = both_parts(total)
        values = wcat[...] * sums
        square = values * sums
        for lane in range(0, WIDE, LANES):
            for g in range(0, square.shape[0], n):
                dot = dot + square[g : g + n, lane : lane + LANES]
        quotients.append(ratio(whole_sum(dot), norms[k]))
    back = ratio(norms[2], norms[1])

    lane = lax.broadcasted_iota(jnp.int32, line_out.shape, 1)
    place = lax.broadcasted_iota(jnp.int32, line_out.shape, 0)
    line = jnp.where((lane == 6) & (place == place_ref[0]), 1.0, 0.0)
    for i, value in enumerate(norms + quotients):
        line = jnp.where(lane == i, jnp.broadcast_to(value, line.shape), line)
    line_out[...] = line

    held[...] = values
    weeks = line_out.shape[0]
    tops = [
        pl.multiple_of(x * CORES * side + core * side + t, 8)
        for x in range(n // (CORES * side))
        for t in range(0, side, 8)
    ]
    for i, top in enumerate(tops):
        kept_out[4, i * 8 : i * 8 + 8, :] = base[pl.ds(top, 8), :]
        for k in range(4):
            kept_out[k, i * 8 : i * 8 + 8, :] = basis[k, pl.ds(top, 8), :]
    mine = jnp.concatenate(
        [held[pl.ds(g + top, 8), :] for g in range(0, held.shape[0], n) for top in tops], axis=0
    )

    parts = jnp.concatenate(split(mine), axis=0)
    for lanes in chunks:
        for tile, value in spread(parts, weeks, lanes):
            result = kept_out[3, :, tile] + value - quotients[2] * kept_out[2, :, tile]
            kept_out[3, :, tile] = result - back * kept_out[1, :, tile]


def week_combine_body(lines_ref, kept_ref, send_ref, horizon):
    weeks = lines_ref.shape[0]
    n = kept_ref.shape[2] // LANES
    week = lax.broadcasted_iota(jnp.int32, (weeks, LANES), 0)
    lines = jnp.where(week < horizon, lines_ref[...], 0.0)
    n1, n2, n3, a1, a2, a3, mark = [
        jnp.take_along_axis(lines, jnp.full((weeks, LANES), i, jnp.int32), axis=1) for i in range(7)
    ]
    e2, e3 = ratio(n2, n1), ratio(n3, n2)

    def dot(left, right):
        terms = n1 * left[0] * right[0] + n2 * left[1] * right[1] + n3 * left[2] * right[2]
        return jnp.sum(terms, axis=0, keepdims=True)

    zero = jnp.zeros((weeks, LANES), jnp.float32)
    x = [zero, zero, zero]
    r = [zero + 1.0, zero, zero, zero]
    p = r[:3]
    rr = dot(r, r)
    for k in range(3):
        image = [
            a1 * p[0] + e2 * p[1],
            p[0] + a2 * p[1] + e3 * p[2],
            p[1] + a3 * p[2],
            p[2],
        ]
        alpha = rr / dot(p, image)
        x = [left + alpha * right for left, right in zip(x, p)]
        r = [left - alpha * right for left, right in zip(r, image)]
        if k < 2:
            new = dot(r, r)
            p = [left + new / rr * right for left, right in zip(r[:3], p)]
            rr = new
    mine = mark > 0.0
    x = [jnp.sum(jnp.where(mine, value, 0.0), axis=0, keepdims=True) for value in x]
    r = [jnp.sum(jnp.where(mine, value, 0.0), axis=0, keepdims=True) for value in r]
    rows = send_ref.shape[0] // weeks
    for t in range(0, weeks, 8):
        for j in range(n):
            lanes = slice(j * LANES, (j + 1) * LANES)
            parts = [kept_ref[k, t : t + 8, lanes] for k in range(4)]
            left = kept_ref[4, t : t + 8, lanes]
            right = r[3] * parts[3]
            for k in range(3):
                left = left + x[k] * parts[k]
                right = right + r[k] * parts[k]
            first = t * rows + j
            send_ref[pl.ds(first, 8, stride=rows), :] = left
            send_ref[pl.ds(first + n, 8, stride=rows), :] = right


def week_last_body(got_ref, x_out, r_out, sems):
    horizon, n, _ = x_out.shape
    copies = [
        pltpu.make_async_copy(
            got_ref.at[pl.ds(0, horizon), pl.ds(i * n, n)], target, sems.at[i]
        )
        for i, target in enumerate((x_out, r_out))
    ]
    for copy in copies:
        copy.start()
    for copy in copies:
        copy.wait()


def exchange_weeks(blocks):
    return lax.all_to_all(blocks, ("x", "sku"), split_axis=0, concat_axis=0, tiled=True)


def by_weeks(
    base_bottom,
    weight_bottom,
    base_category,
    weight_category,
    base_region,
    weight_region,
    category_map,
    region_map,
):
    stores, horizon, skus = base_bottom.shape
    n = region_map.shape[0]
    regions = weight_region.shape[0]
    tiles = weight_category.shape[2] // LANES
    groups = weight_category.shape[2] // WIDE
    side = lax.axis_size("sku")
    weeks = lax.axis_size("x") * side
    place = lax.axis_index("x") * side + lax.axis_index("sku")
    place = place.astype(jnp.int32).reshape(1)
    core = lax.axis_index("core").astype(jnp.int32).reshape(1)
    cats = category_map.reshape(n, LANES)
    sources = (
        base_bottom.reshape(horizon, n, LANES),
        weight_bottom.reshape(horizon, n, LANES),
        weight_category.reshape(horizon, tiles, LANES),
        base_category.reshape(horizon, tiles, LANES),
        jnp.transpose(base_region, (1, 0, 2)),
        jnp.transpose(weight_region, (1, 0, 2)),
    )
    per = week_rows(tiles, n, regions)[-1]
    (sent,) = call(
        week_pack_body,
        [(weeks, per, LANES)],
        [pltpu.SemaphoreType.DMA((len(sources),))],
        sources,
        [HBM] * len(sources),
        out_specs=(HBM,),
    )
    own = exchange_weeks(sent)
    other = lax.ppermute(own, "core", [(0, 1), (1, 0)])
    table, flipped, group, same, region = call(
        lambda *refs: week_table_body(*refs, regions),
        [
            jax.ShapeDtypeStruct((skus, WIDE), jnp.bfloat16),
            jax.ShapeDtypeStruct((WIDE, skus), jnp.bfloat16),
            jax.ShapeDtypeStruct((n, skus), jnp.bfloat16),
            jax.ShapeDtypeStruct((n, LANES), jnp.bfloat16),
            jax.ShapeDtypeStruct((n, LANES), jnp.bfloat16),
        ],
        [],
        (region_map, cats),
        [SMEM, VMEM],
    )
    full = pltpu.VMEM((n, skus), jnp.float32)
    raw = pltpu.VMEM((regions, skus), jnp.float32)
    cat = pltpu.VMEM((groups * n, WIDE), jnp.float32)
    kept, line = call(
        lambda *refs: week_body(*refs, side),
        [(5, weeks, skus), (weeks, LANES)],
        [
            full, pltpu.VMEM((4, n, skus), jnp.float32),
            full, full, full, cat, cat, raw, raw, cat,
        ],
        (
            core, place, own.reshape(-1, LANES), other.reshape(-1, LANES),
            table, flipped, group, same, region, cats,
        ),
        [SMEM, SMEM, VMEM, FREE] + [VMEM] * 6,
    )
    lines = exchange_weeks(line.reshape(weeks, 1, LANES)).reshape(weeks, LANES)
    (sent,) = call(
        lambda *refs: week_combine_body(*refs, horizon),
        [(weeks * 2 * n, LANES)],
        [],
        (lines, kept),
        [VMEM] * 2,
    )
    got = exchange_weeks(sent.reshape(weeks, 2 * n, LANES))
    x, r = call(
        week_last_body,
        [(horizon, n, LANES)] * 2,
        [pltpu.SemaphoreType.DMA((2,))],
        (got,),
        [VMEM],
        out_specs=(HBM, HBM),
    )
    return x.reshape(base_bottom.shape), r.reshape(base_bottom.shape)


def solution(mesh):
    def mapped(device_mesh, body, stores):
        split_stores = P(stores, None, None)
        split_skus = P(None, None, stores)
        return jax.shard_map(
            body,
            mesh=device_mesh,
            in_specs=(split_stores,) * 4 + (split_skus,) * 2 + (P(), P()),
            out_specs=(split_stores,) * 2,
            check_vma=False,
        )

    side = mesh.shape["sku"]
    chips = mesh.devices.reshape(-1, CORES, side)

    def program(base_bottom, *others):
        stores, horizon, skus = base_bottom.shape
        fits = 16 * stores * skus * 4 <= 16 << 20
        fits = fits and 3 * others[3].shape[0] <= LANES and LANES % stores == 0
        if fits and horizon <= chips.shape[0] * side and side % 8 == 0:
            device_mesh = Mesh(chips, ("x", "core", "sku"))
            return mapped(device_mesh, by_weeks, ("x", "core", "sku"))(base_bottom, *others)
        return mapped(mesh, on_device, ("store", "sku"))(base_bottom, *others)

    return program
```

```python
import jax
import jax.numpy as jnp
from jax import lax
from jax.experimental import pallas as pl
from jax.experimental.pallas import tpu as pltpu
from jax.sharding import Mesh
from jax.sharding import PartitionSpec as P

LANES = 128
PAD = 16
WIDE = 256
VMEM = pl.BlockSpec(memory_space=pltpu.VMEM)
HBM = pl.BlockSpec(memory_space=pltpu.HBM)
SMEM = pl.BlockSpec(memory_space=pltpu.SMEM)
FREE = pl.BlockSpec(memory_space=pltpu.VMEM)
CORES = 2


def exchange(blocks, n):
    moved = lax.all_to_all(
        blocks.reshape(n, 1, -1), ("store", "sku"), split_axis=0, concat_axis=0, tiled=True
    )
    return moved.reshape(blocks.shape)


def call(body, outs, scratch, args, specs=None, held=False, out_specs=None):
    outs = [
        out if isinstance(out, jax.ShapeDtypeStruct) else jax.ShapeDtypeStruct(out, jnp.float32)
        for out in outs
    ]
    specs = specs or [VMEM] * len(args)
    args = [
        arg if spec is SMEM or spec is FREE else pltpu.with_memory_space_constraint(arg, spec.memory_space)
        for arg, spec in zip(args, specs)
    ]
    return pl.pallas_call(
        body,
        out_shape=tuple(pltpu.VMEM(out.shape, out.dtype) if held else out for out in outs),
        in_specs=specs,
        out_specs=out_specs or tuple(VMEM for _ in outs),
        scratch_shapes=scratch,
        compiler_params=pltpu.CompilerParams(vmem_limit_bytes=24 << 20),
    )(*args)


def split(value):
    high = value.astype(jnp.bfloat16)
    return high, (value - high.astype(jnp.float32)).astype(jnp.bfloat16)


def split_all(value):
    high, low = split(value)
    rest = value - high.astype(jnp.float32) - low.astype(jnp.float32)
    return high, low, rest.astype(jnp.bfloat16)


def product(left, right, contract):
    return lax.dot_general(left, right, (contract, ((), ())), preferred_element_type=jnp.float32)


def rows_of(ref, n, h):
    return ref[pl.ds(h, n, stride=ref.shape[0] // n), :]


def put_rows(ref, n, h, value):
    ref[pl.ds(h, n, stride=ref.shape[0] // n), :] = value


def category_sums(field, table_ref, group_ref, n, rows):
    width = 4 if n % 4 == 0 else 1
    lanes = width * LANES

    def step(c, total):
        pieces = [field[pl.ds(c * width + i, PAD, stride=n), :] for i in range(width)]
        parts = split_all(jnp.concatenate(pieces, axis=1))
        start = pl.multiple_of(c * lanes, lanes)
        group = group_ref[:, pl.ds(start, lanes)]
        masks = [group == g for g in range(rows // PAD)]
        none = jnp.zeros((PAD, lanes), jnp.bfloat16)
        spread = jnp.concatenate(
            [jnp.where(mask, part, none) for part in parts for mask in masks], axis=0
        )
        return total + product(spread, table_ref[pl.ds(start, lanes), :], ((1,), (0,)))

    steps = n // width
    total = lax.fori_loop(
        0, steps, step, jnp.zeros((3 * rows, WIDE), jnp.float32), unroll=min(steps, 8)
    )
    return total[:rows] + (total[rows : 2 * rows] + total[2 * rows :])


def category_spread(values, cats, horizon, put):
    place = cats & (LANES - 1)
    group = cats >> (LANES.bit_length() - 1)
    for h in range(horizon):
        found = []
        for g in range(0, values.shape[0], PAD):
            for lane in range(0, WIDE, LANES):
                row = jnp.broadcast_to(values[g + h : g + h + 1, lane : lane + LANES], cats.shape)
                found.append(jnp.take_along_axis(row, place, axis=1))
        for bit in range((len(found) - 1).bit_length()):
            mask = group & (1 << bit) != 0
            pairs = [found[i : i + 2] for i in range(0, len(found), 2)]
            found = [jnp.where(mask, pair[1], pair[0]) if len(pair) == 2 else pair[0] for pair in pairs]
        put(h, found[0])


def tiles_of(n):
    return [slice(t, t + 8) for t in range(0, n, 8)]


def put_tile(ref, n, h, tile, value):
    rows = ref.shape[0] // n
    ref[pl.ds(tile.start * rows + h, 8, stride=rows), :] = value


def region_sums(load, same, n, horizon):
    high, low = split(jnp.concatenate([load(h) for h in range(horizon)], axis=1))
    total = product(same, high, ((1,), (0,))) + product(same, low, ((1,), (0,)))
    return [total[:, h * LANES : (h + 1) * LANES] for h in range(horizon)]


def pack_body(base_hbm, out_ref, base_ref, sem):
    copy = pltpu.make_async_copy(base_hbm, base_ref, sem)
    copy.start()
    copy.wait()
    n = base_ref.shape[1]
    for h in range(base_ref.shape[0]):
        put_rows(out_ref, n, h, base_ref[h])


def prepare_body(
    base_hbm, base_cat_hbm, weight_cat_hbm, base_reg_hbm, weight_reg_hbm, cats_hbm, map_hbm,
    spread_out, wcat_out, wstore_out, bstore_out, same_out, table_out, group_out,
    cats_ref,
    field, values, base_ref, base_cat_ref, weight_cat_ref, base_reg_ref, weight_reg_ref, map_ref, sems,
):
    copies = [
        pltpu.make_async_copy(source, target, sems.at[i])
        for i, (source, target) in enumerate(
            (
                (cats_hbm, cats_ref),
                (base_hbm, base_ref),
                (weight_cat_hbm, weight_cat_ref),
                (base_cat_hbm, base_cat_ref),
                (map_hbm, map_ref),
                (weight_reg_hbm, weight_reg_ref),
                (base_reg_hbm, base_reg_ref),
            )
        )
    ]
    for copy in copies:
        copy.start()
    for copy in copies:
        copy.wait()
    horizon, n, _ = base_ref.shape
    n_regions = weight_reg_ref.shape[1]
    square = jnp.concatenate([cats_ref[...].astype(jnp.float32)] * (LANES // min(n, LANES)), axis=0)
    labels = lax.broadcasted_iota(jnp.int32, (LANES, WIDE), 1)
    columns = [
        jnp.transpose(square[i : i + LANES]).astype(jnp.int32) % WIDE
        for i in range(0, square.shape[0], LANES)
    ]
    for j in range(n):
        column = jnp.broadcast_to(columns[j // LANES][:, j % LANES : j % LANES + 1], (LANES, WIDE))
        table_out[j * LANES : (j + 1) * LANES, :] = jnp.where(
            column == labels, 1.0, 0.0
        ).astype(jnp.bfloat16)
        group = jnp.broadcast_to(cats_ref[j : j + 1, :] // WIDE, (PAD, LANES))
        group_out[:, j * LANES : (j + 1) * LANES] = group.astype(jnp.float32).astype(jnp.bfloat16)

    field[...] = jnp.zeros_like(field)
    for h in range(horizon):
        field[h * n : (h + 1) * n, :] = base_ref[h]
    sums = category_sums(field, table_out, group_out, n, wcat_out.shape[0])
    wcat_out[...] = jnp.zeros_like(wcat_out)
    values[...] = jnp.zeros_like(values)
    for g in range(0, wcat_out.shape[0], PAD):
        for lane in range(0, WIDE, LANES):
            tile = (g // PAD * WIDE + lane) // LANES
            lanes = slice(lane, lane + LANES)
            weight = weight_cat_ref[:, tile, :]
            wcat_out[g : g + horizon, lanes] = weight
            values[g : g + horizon, lanes] = weight * (
                base_cat_ref[:, tile, :] - sums[g : g + horizon, lanes]
            )
    for tile in tiles_of(n):

        def put(h, value):
            spread_out[h, tile, :] = value

        category_spread(values, cats_ref[tile, :], horizon, put)

    labels = lax.broadcasted_iota(jnp.int32, (n_regions, n), 0)
    table = jnp.where(labels == map_ref[...], 1.0, 0.0).astype(jnp.bfloat16)
    same_out[...] = product(table, table, ((0,), (0,))).astype(jnp.bfloat16)
    for source, target in ((weight_reg_ref, wstore_out), (base_reg_ref, bstore_out)):
        for h in range(horizon):
            high, low = split(source[h])
            rest = source[h] - high.astype(jnp.float32) - low.astype(jnp.float32)
            target[h] = (
                product(table, high, ((0,), (0,)))
                + product(table, low, ((0,), (0,)))
                + product(table, rest.astype(jnp.bfloat16), ((0,), (0,)))
            )


def region_start_body(got_ref, spread_ref, wstore_ref, bstore_ref, same_ref, reg_out, send_ref):
    horizon, n, _ = spread_ref.shape
    sums = region_sums(lambda h: rows_of(got_ref, n, h), same_ref[...], n, horizon)
    for h in range(horizon):
        put_rows(send_ref, n, h, spread_ref[h])
        part = wstore_ref[h] * (bstore_ref[h] - sums[h])
        reg_out[h] = part
        put_rows(send_ref, n, horizon + h, part)


def region_part(rs, wstore_ref, same_ref, put):
    horizon, n, _ = wstore_ref.shape
    sums = region_sums(lambda h: rs[h], same_ref[...], n, horizon)
    share = jnp.zeros((n, LANES), jnp.float32)
    for h in range(horizon):
        part = wstore_ref[h] * sums[h]
        share = share + part * rs[h]
        put(h, part)
    return share


def store_part(r_ref, sums, gamma, delta, eps, diag_ref, wcat_ref, cats_ref, put, put_line, values):
    horizon, n, _ = diag_ref.shape
    scaled = wcat_ref[...] * sums
    values[...] = scaled
    square = scaled * sums
    delta = jnp.sum(delta, axis=0, keepdims=True)
    for lane in range(0, WIDE, LANES):
        delta = delta + jnp.sum(square[:, lane : lane + LANES], axis=0, keepdims=True)
    lane = lax.broadcasted_iota(jnp.int32, (1, LANES), 1)
    line = jnp.zeros((1, LANES), jnp.float32)
    for i, part in enumerate((gamma, delta, eps)):
        if part is not None:
            whole = jnp.sum(jnp.sum(part, axis=0, keepdims=True), axis=1, keepdims=True)
            line = jnp.where(lane == i, whole, line)
    put_line(jnp.broadcast_to(line, (n, LANES)))
    for tile in tiles_of(n):

        def finish(h, value):
            put(h, tile, value + diag_ref[h, tile, :] * r_ref[h, tile, :])

        category_spread(values, cats_ref[tile, :], horizon, finish)


def totals(got_ref, n, row):
    total = jnp.sum(rows_of(got_ref, n, row), axis=0, keepdims=True)
    total = jnp.broadcast_to(total, (8, LANES))
    return [
        jnp.take_along_axis(total, jnp.full((8, LANES), i, jnp.int32), axis=1)[0:1] for i in range(3)
    ]


def wide(line):
    return jnp.concatenate([line] * (WIDE // LANES), axis=1)


def region_sender(ref, n, first, keep):
    def put(h, value):
        if keep is not None:
            keep[h] = value
        put_rows(ref, n, first + h, value)

    return put


def store_sender(ref, n, keep):
    def put(h, tile, value):
        keep[h, tile, :] = value
        if ref is not None:
            put_tile(ref, n, h, tile, value)

    return put


def clear_tail(field, horizon, n):
    field[horizon * n :, :] = jnp.zeros((field.shape[0] - horizon * n, LANES), jnp.float32)


def first_body(
    a_ref, reg_ref, got_ref, diag_ref, wcat_ref, wstore_ref, table_ref, group_ref, cats_ref, same_ref,
    r_out, rs_out, cr_out, a_out, reg_out, send_ref, values, field,
):
    horizon, n, _ = diag_ref.shape
    clear_tail(field, horizon, n)
    gamma = jnp.zeros((n, LANES), jnp.float32)
    delta = jnp.zeros((n, LANES), jnp.float32)
    for h in range(horizon):
        r = a_ref[h] + rows_of(got_ref, n, horizon + h)
        r_out[h] = r
        field[h * n : (h + 1) * n, :] = r
        gamma = gamma + r * r
        delta = delta + diag_ref[h] * r * r
    sums = category_sums(field, table_ref, group_ref, n, wcat_ref.shape[0])
    cr_out[...] = sums
    for h in range(horizon):
        rs_out[h] = rows_of(got_ref, n, h) + reg_ref[h]
    delta = delta + region_part(
        rs_out, wstore_ref, same_ref, region_sender(send_ref, n, horizon, reg_out)
    )
    store_part(
        r_out, sums, gamma, delta, None, diag_ref, wcat_ref, cats_ref,
        store_sender(send_ref, n, a_out),
        lambda line: put_rows(send_ref, n, 2 * horizon, line), values,
    )


def second_body(
    a_ref, reg_ref, got_ref, x_ref, r_ref, rs_ref, cr_ref,
    diag_ref, wcat_ref, wstore_ref, table_ref, group_ref, cats_ref, same_ref,
    x_out, r_out, rs_out, s_out, ss_out, cr_out, cs_out, scal_ref, a_out, reg_out, send_ref,
    values, field,
):
    horizon, n, _ = diag_ref.shape
    clear_tail(field, horizon, n)
    for h in range(horizon):
        field[h * n : (h + 1) * n, :] = a_ref[h] + rows_of(got_ref, n, horizon + h)
    sums = category_sums(field, table_ref, group_ref, n, wcat_ref.shape[0])
    cs_out[...] = sums
    gamma, delta, _ = totals(got_ref, n, 2 * horizon)
    alpha = gamma / delta
    scal_ref[0:1, :] = gamma
    scal_ref[1:2, :] = delta
    for h in range(horizon):
        ws = rows_of(got_ref, n, h) + reg_ref[h]
        ss_out[h] = ws
        rs_out[h] = rs_ref[h] - alpha * ws
    delta = region_part(
        rs_out, wstore_ref, same_ref, region_sender(send_ref, n, horizon, reg_out)
    )
    gamma = jnp.zeros((n, LANES), jnp.float32)
    eps = jnp.zeros((n, LANES), jnp.float32)
    for h in range(horizon):
        s = field[h * n : (h + 1) * n, :]
        s_out[h] = s
        r = r_ref[h]
        x_out[h] = x_ref[h] + alpha * r
        r = r - alpha * s
        r_out[h] = r
        gamma = gamma + r * r
        delta = delta + diag_ref[h] * r * r
        eps = eps + r * s
    sums = cr_ref[...] - wide(alpha) * sums
    cr_out[...] = sums
    store_part(
        r_out, sums, gamma, delta, eps, diag_ref, wcat_ref, cats_ref,
        store_sender(send_ref, n, a_out),
        lambda line: put_rows(send_ref, n, 2 * horizon, line), values,
    )


def third_body(
    a_ref, reg_ref, got_ref, x_ref, r_ref, rs_ref, p_ref, s_ref, ss_ref, cr_ref, cs_ref, scal_ref,
    diag_ref, wcat_ref, wstore_ref, table_ref, group_ref, cats_ref, same_ref,
    x_out, r_out, p_out, s_out, scal_out, a_out, send_ref, values, field, rs_out,
):
    horizon, n, _ = diag_ref.shape
    clear_tail(field, horizon, n)
    for h in range(horizon):
        field[h * n : (h + 1) * n, :] = a_ref[h] + rows_of(got_ref, n, horizon + h)
    sums = category_sums(field, table_ref, group_ref, n, wcat_ref.shape[0])
    gamma, delta, eps = totals(got_ref, n, 2 * horizon)
    beta = gamma / scal_ref[0:1, :]
    curve = delta + 2.0 * beta * eps + beta * beta * scal_ref[1:2, :]
    alpha = gamma / curve
    scal_out[0:1, :] = gamma
    scal_out[1:2, :] = curve
    for h in range(horizon):
        ws = rows_of(got_ref, n, h) + reg_ref[h]
        rs_out[h] = rs_ref[h] - alpha * (ws + beta * ss_ref[h])
    delta = region_part(rs_out, wstore_ref, same_ref, region_sender(send_ref, n, 0, None))
    gamma = jnp.zeros((n, LANES), jnp.float32)
    eps = jnp.zeros((n, LANES), jnp.float32)
    for h in range(horizon):
        s = field[h * n : (h + 1) * n, :] + beta * s_ref[h]
        s_out[h] = s
        r = r_ref[h]
        p = r + beta * p_ref[h]
        p_out[h] = p
        x_out[h] = x_ref[h] + alpha * p
        r = r - alpha * s
        r_out[h] = r
        gamma = gamma + r * r
        delta = delta + diag_ref[h] * r * r
        eps = eps + r * s
    sums = cr_ref[...] - wide(alpha) * (sums + wide(beta) * cs_ref[...])
    store_part(
        r_out, sums, gamma, delta, eps, diag_ref, wcat_ref, cats_ref,
        store_sender(None, n, a_out), lambda line: put_rows(send_ref, n, horizon, line), values,
    )


def last_body(a_ref, got_ref, x_ref, r_ref, p_ref, s_ref, scal_ref, x_out, r_out):
    horizon, n, _ = a_ref.shape
    gamma, delta, eps = totals(got_ref, n, horizon)
    beta = gamma / scal_ref[0:1, :]
    alpha = gamma / (delta + 2.0 * beta * eps + beta * beta * scal_ref[1:2, :])
    for h in range(horizon):
        r = r_ref[h]
        s = a_ref[h] + rows_of(got_ref, n, h) + beta * s_ref[h]
        x_out[h] = x_ref[h] + alpha * (r + beta * p_ref[h])
        r_out[h] = r - alpha * s


def on_device(
    base_bottom,
    weight_bottom,
    base_category,
    weight_category,
    base_region,
    weight_region,
    category_map,
    region_map,
):
    stores, horizon, skus = base_bottom.shape
    n = region_map.shape[0]
    groups = weight_category.shape[2] // WIDE
    tiles = weight_category.shape[2] // LANES
    field = (horizon, n, LANES)
    padded = (PAD * n, LANES)
    by_category = (horizon, tiles, LANES)
    scal = (2, LANES)
    values = pltpu.VMEM((groups * PAD, WIDE), jnp.float32)

    x = base_bottom.reshape(field)
    diag = weight_bottom.reshape(field)
    (sent,) = call(
        pack_body,
        [(n * horizon, LANES)],
        [pltpu.VMEM(field, jnp.float32), pltpu.SemaphoreType.DMA],
        (x,),
        [HBM],
        True,
    )
    got = exchange(sent, n)
    arguments = (
        x,
        base_category.reshape(by_category),
        weight_category.reshape(by_category),
        jnp.transpose(base_region, (1, 0, 2)),
        jnp.transpose(weight_region, (1, 0, 2)),
        category_map.reshape(n, LANES),
        region_map.reshape(1, n),
    )
    held = [pltpu.VMEM(arguments[i].shape, arguments[i].dtype) for i in (0, 1, 2, 3, 4, 6)]
    spread, wcat, wstore, bstore, same, table, group, cats = call(
        prepare_body,
        [
            field,
            (groups * PAD, WIDE),
            field,
            field,
            jax.ShapeDtypeStruct((n, n), jnp.bfloat16),
            jax.ShapeDtypeStruct((skus, WIDE), jnp.bfloat16),
            jax.ShapeDtypeStruct((PAD, skus), jnp.bfloat16),
            jax.ShapeDtypeStruct((n, LANES), jnp.int32),
        ],
        [
            pltpu.VMEM(padded, jnp.float32),
            values,
            *held,
            pltpu.SemaphoreType.DMA((len(arguments),)),
        ],
        arguments,
        [HBM] * len(arguments),
    )
    reg, sent = call(
        region_start_body,
        [field, (n * 2 * horizon, LANES)],
        [],
        (got, spread, wstore, bstore, same),
    )
    got = exchange(sent, n)
    fixed = (diag, wcat, wstore, table, group, cats, same)
    both = (n * (2 * horizon + 1), LANES)
    work = [values, pltpu.VMEM(padded, jnp.float32)]
    sums = (groups * PAD, WIDE)
    r, rs, cr, a, reg, sent = call(
        first_body, [field, field, sums, field, field, both], work, (spread, reg, got) + fixed
    )
    got = exchange(sent, n)
    p = r
    x, r, rs, s, ss, cr, cs, scalars, a, reg, sent = call(
        second_body,
        [field, field, field, field, field, sums, sums, scal, field, field, both],
        work,
        (a, reg, got, x, r, rs, cr) + fixed,
    )
    got = exchange(sent, n)
    x, r, p, s, scalars, a, sent = call(
        third_body,
        [field, field, field, field, scal, field, (n * (horizon + 1), LANES)],
        work + [pltpu.VMEM(field, jnp.float32)],
        (a, reg, got, x, r, rs, p, s, ss, cr, cs, scalars) + fixed,
    )
    got = exchange(sent, n)
    x, r = call(last_body, [field, field], [], (a, got, x, r, p, s, scalars))
    return x.reshape(base_bottom.shape), r.reshape(base_bottom.shape)


def week_rows(tiles, n, regions):
    sizes = (n, n, tiles, tiles, regions, regions)
    return [sum(sizes[:i]) for i in range(len(sizes) + 1)]


def week_pack_body(*refs):
    sources, out, sems = refs[:-2], refs[-2], refs[-1]
    horizon = sources[0].shape[0]
    copies, start = [], 0
    for i, source in enumerate(sources):
        rows = source.shape[1]
        target = out.at[pl.ds(0, horizon), pl.ds(start, rows)]
        copies.append(pltpu.make_async_copy(source, target, sems.at[i]))
        start += rows
    for copy in copies:
        copy.start()
    for copy in copies:
        copy.wait()


def week_table_body(
    map_ref, cats_ref, table_out, flipped_out, group_out, same_out, region_out, regions
):
    n = cats_ref.shape[0]
    lane = lax.broadcasted_iota(jnp.int32, (n, LANES), 1)
    line = lax.broadcasted_iota(jnp.int32, (n, LANES), 0)
    across = jnp.zeros((n, LANES), jnp.int32)
    down = jnp.zeros((n, LANES), jnp.int32)
    for s in range(n):
        across = jnp.where(lane % n == s, map_ref[s], across)
        down = jnp.where(line == s, map_ref[s], down)
    same_out[...] = jnp.where(across == down, 1.0, 0.0).astype(jnp.bfloat16)
    region_out[...] = jnp.where(lane % regions == down, 1.0, 0.0).astype(jnp.bfloat16)
    square = jnp.concatenate([cats_ref[...].astype(jnp.float32)] * (LANES // min(n, LANES)), axis=0)
    labels = lax.broadcasted_iota(jnp.int32, (LANES, WIDE), 1)
    downward = lax.broadcasted_iota(jnp.int32, (WIDE, LANES), 0)
    columns = [
        jnp.transpose(square[i : i + LANES]).astype(jnp.int32) & (WIDE - 1)
        for i in range(0, square.shape[0], LANES)
    ]
    for j in range(n):
        column = jnp.broadcast_to(columns[j // LANES][:, j % LANES : j % LANES + 1], (LANES, WIDE))
        table_out[j * LANES : (j + 1) * LANES, :] = jnp.where(
            column == labels, 1.0, 0.0
        ).astype(jnp.bfloat16)
        flipped_out[:, j * LANES : (j + 1) * LANES] = jnp.where(
            (cats_ref[j : j + 1, :] & (WIDE - 1)) == downward, 1.0, 0.0
        ).astype(jnp.bfloat16)
        group = cats_ref[j : j + 1, :] >> (WIDE.bit_length() - 1)
        group = jnp.broadcast_to(group, (group_out.shape[0], LANES))
        group_out[:, j * LANES : (j + 1) * LANES] = group.astype(jnp.float32).astype(jnp.bfloat16)


def ratio(top, bottom):
    return jnp.where(bottom > 0.0, top / bottom, 0.0)


def whole_sum(part):
    total = jnp.sum(jnp.sum(part, axis=0, keepdims=True), axis=1, keepdims=True)
    return jnp.broadcast_to(total, (1, LANES))


def week_body(
    core_ref, place_ref, own_ref, other_ref, table_ref, flipped_ref, group_ref, same_ref, region_ref,
    cats_ref, kept_out, line_out,
    base, basis, diag, wstore, bstore, wcat, bcat, raw_weight, raw_base, held,
    side,
):
    core = core_ref[0]
    n, skus = base.shape
    per = own_ref.shape[0] // line_out.shape[0]
    regions = raw_weight.shape[0]
    tiles = wcat.shape[0] // n * (WIDE // LANES)
    starts = week_rows(tiles, n, regions)
    chunk = min(skus, 8 * LANES)
    chunks = [slice(c, c + chunk) for c in range(0, skus, chunk)]
    for ref, c in ((own_ref, core), (other_ref, 1 - core)):
        for x in range(n // (CORES * side)):
            for t in range(0, side, 8):
                first = (x * side + t) * per
                top = pl.multiple_of(x * CORES * side + c * side + t, 8)

                def rows(row):
                    return ref[pl.ds(first + row, 8, stride=per), :]

                for j in range(n):
                    lanes = slice(j * LANES, (j + 1) * LANES)
                    base[pl.ds(top, 8), lanes] = rows(starts[0] + j)
                    diag[pl.ds(top, 8), lanes] = rows(starts[1] + j)
                for g in range(tiles):
                    lane = g * LANES % WIDE
                    down = pl.multiple_of(g * LANES // WIDE * n + top, 8)
                    wcat[pl.ds(down, 8), lane : lane + LANES] = rows(starts[2] + g)
                    bcat[pl.ds(down, 8), lane : lane + LANES] = rows(starts[3] + g)
            for k in range(side):
                first = (x * side + k) * per
                j = x * CORES * side + c * side + k
                lanes = pl.ds(pl.multiple_of(j * LANES, LANES), LANES)
                raw_base[:, lanes] = ref[first + starts[4] : first + starts[5], :]
                raw_weight[:, lanes] = ref[first + starts[5] : first + starts[6], :]

    region_table = region_ref[:, : 3 * regions]
    same = same_ref[:, : 2 * n]
    for source, target in ((raw_weight, wstore), (raw_base, bstore)):
        for lanes in chunks:
            parts = jnp.concatenate(split_all(source[:, lanes]), axis=0)
            target[:, lanes] = product(region_table, parts, ((1,), (0,)))

    def by_category(field):
        rows = wcat.shape[0]
        total = None
        for lanes in chunks:
            group = group_ref[:, lanes]
            masks = [group == g for g in range(rows // n)]
            none = jnp.zeros(group.shape, jnp.bfloat16)
            spread = jnp.concatenate(
                [jnp.where(mask, part, none) for part in split(field[:, lanes]) for mask in masks],
                axis=0,
            )
            part = product(spread, table_ref[lanes, :], ((1,), (0,)))
            total = part if total is None else total + part
        return total[:rows] + total[rows:]

    def spread(values, m, put):
        parts = jnp.concatenate(split(values), axis=0)
        groups = values.shape[0] // m
        for lanes in chunks:
            found = product(parts, flipped_ref[:, lanes], ((1,), (0,)))
            for t in range(0, chunk, LANES):
                tile = slice(lanes.start + t, lanes.start + t + LANES)
                members = cats_ref[tile.start // LANES : tile.start // LANES + 1, :]
                group = jnp.broadcast_to(members >> (WIDE.bit_length() - 1), (m, LANES))
                high, low = found[: groups * m, t : t + LANES], found[groups * m :, t : t + LANES]
                one = [
                    high[g * m : (g + 1) * m] + low[g * m : (g + 1) * m] for g in range(groups)
                ]
                bit = 1
                while len(one) > 1:
                    odd = group & bit != 0
                    pairs = [one[i : i + 2] for i in range(0, len(one), 2)]
                    one = [jnp.where(odd, *pair[::-1]) if len(pair) == 2 else pair[0] for pair in pairs]
                    bit *= 2
                put(tile, one[0])

    def by_region(part):
        return product(same, jnp.concatenate(split(part), axis=0), ((1,), (0,)))

    def tiles_in(lanes):
        for t in range(0, chunk, LANES):
            yield slice(lanes.start + t, lanes.start + t + LANES), slice(t, t + LANES)

    zero = jnp.zeros((n, LANES), jnp.float32)
    for lanes in chunks:
        sums = by_region(base[:, lanes])
        for tile, inner in tiles_in(lanes):
            basis[0, :, tile] = wstore[:, tile] * (bstore[:, tile] - sums[:, inner])
    norm = [zero]

    def start(tile, value):
        result = basis[0, :, tile] + value
        basis[0, :, tile] = result
        norm[0] = norm[0] + result * result

    spread(wcat[...] * (bcat[...] - by_category(base)), n, start)
    norms, quotients = [whole_sum(norm[0])], []
    for k in range(3):
        field, image = basis.at[k], basis.at[k + 1]
        sums = by_category(field)
        values = wcat[...] * sums
        square = values * sums
        dot = zero
        for lane in range(0, WIDE, LANES):
            for g in range(0, square.shape[0], n):
                dot = dot + square[g : g + n, lane : lane + LANES]
        for lanes in chunks:
            sums = by_region(field[:, lanes])
            for tile, inner in tiles_in(lanes):
                part = field[:, tile]
                result = diag[:, tile] * part + wstore[:, tile] * sums[:, inner]
                image[:, tile] = result
                dot = dot + part * result
        quotients.append(ratio(whole_sum(dot), norms[k]))
        back = ratio(norms[k], norms[k - 1]) if k else None
        if k == 2:
            break
        norm = [zero]

        def step(tile, value):
            result = image[:, tile] + value - quotients[k] * field[:, tile]
            if k:
                result = result - back * basis[k - 1, :, tile]
            image[:, tile] = result
            norm[0] = norm[0] + result * result

        spread(values, n, step)
        norms.append(whole_sum(norm[0]))

    lane = lax.broadcasted_iota(jnp.int32, line_out.shape, 1)
    place = lax.broadcasted_iota(jnp.int32, line_out.shape, 0)
    line = jnp.where((lane == 6) & (place == place_ref[0]), 1.0, 0.0)
    for i, value in enumerate(norms + quotients):
        line = jnp.where(lane == i, jnp.broadcast_to(value, line.shape), line)
    line_out[...] = line

    held[...] = values
    weeks = line_out.shape[0]
    tops = [
        pl.multiple_of(x * CORES * side + core * side + t, 8)
        for x in range(n // (CORES * side))
        for t in range(0, side, 8)
    ]
    for i, top in enumerate(tops):
        kept_out[4, i * 8 : i * 8 + 8, :] = base[pl.ds(top, 8), :]
        for k in range(4):
            kept_out[k, i * 8 : i * 8 + 8, :] = basis[k, pl.ds(top, 8), :]
    mine = jnp.concatenate(
        [held[pl.ds(g + top, 8), :] for g in range(0, held.shape[0], n) for top in tops], axis=0
    )

    def finish(tile, value):
        result = kept_out[3, :, tile] + value - quotients[2] * kept_out[2, :, tile]
        kept_out[3, :, tile] = result - back * kept_out[1, :, tile]

    spread(mine, weeks, finish)


def week_combine_body(lines_ref, kept_ref, send_ref, horizon):
    weeks = lines_ref.shape[0]
    n = kept_ref.shape[2] // LANES
    week = lax.broadcasted_iota(jnp.int32, (weeks, LANES), 0)
    lines = jnp.where(week < horizon, lines_ref[...], 0.0)
    n1, n2, n3, a1, a2, a3, mark = [
        jnp.take_along_axis(lines, jnp.full((weeks, LANES), i, jnp.int32), axis=1) for i in range(7)
    ]
    e2, e3 = ratio(n2, n1), ratio(n3, n2)

    def dot(left, right):
        terms = n1 * left[0] * right[0] + n2 * left[1] * right[1] + n3 * left[2] * right[2]
        return jnp.sum(terms, axis=0, keepdims=True)

    zero = jnp.zeros((weeks, LANES), jnp.float32)
    x = [zero, zero, zero]
    r = [zero + 1.0, zero, zero, zero]
    p = r[:3]
    rr = dot(r, r)
    for k in range(3):
        image = [
            a1 * p[0] + e2 * p[1],
            p[0] + a2 * p[1] + e3 * p[2],
            p[1] + a3 * p[2],
            p[2],
        ]
        alpha = rr / dot(p, image)
        x = [left + alpha * right for left, right in zip(x, p)]
        r = [left - alpha * right for left, right in zip(r, image)]
        if k < 2:
            new = dot(r, r)
            p = [left + new / rr * right for left, right in zip(r[:3], p)]
            rr = new
    mine = mark > 0.0
    x = [jnp.sum(jnp.where(mine, value, 0.0), axis=0, keepdims=True) for value in x]
    r = [jnp.sum(jnp.where(mine, value, 0.0), axis=0, keepdims=True) for value in r]
    rows = send_ref.shape[0] // weeks
    for t in range(0, weeks, 8):
        for j in range(n):
            lanes = slice(j * LANES, (j + 1) * LANES)
            parts = [kept_ref[k, t : t + 8, lanes] for k in range(4)]
            left = kept_ref[4, t : t + 8, lanes]
            right = r[3] * parts[3]
            for k in range(3):
                left = left + x[k] * parts[k]
                right = right + r[k] * parts[k]
            first = t * rows + j
            send_ref[pl.ds(first, 8, stride=rows), :] = left
            send_ref[pl.ds(first + n, 8, stride=rows), :] = right


def week_last_body(got_ref, x_out, r_out, sems):
    horizon, n, _ = x_out.shape
    copies = [
        pltpu.make_async_copy(
            got_ref.at[pl.ds(0, horizon), pl.ds(i * n, n)], target, sems.at[i]
        )
        for i, target in enumerate((x_out, r_out))
    ]
    for copy in copies:
        copy.start()
    for copy in copies:
        copy.wait()


def exchange_weeks(blocks):
    return lax.all_to_all(blocks, ("x", "sku"), split_axis=0, concat_axis=0, tiled=True)


def by_weeks(
    base_bottom,
    weight_bottom,
    base_category,
    weight_category,
    base_region,
    weight_region,
    category_map,
    region_map,
):
    stores, horizon, skus = base_bottom.shape
    n = region_map.shape[0]
    regions = weight_region.shape[0]
    tiles = weight_category.shape[2] // LANES
    groups = weight_category.shape[2] // WIDE
    side = lax.axis_size("sku")
    weeks = lax.axis_size("x") * side
    place = lax.axis_index("x") * side + lax.axis_index("sku")
    place = place.astype(jnp.int32).reshape(1)
    core = lax.axis_index("core").astype(jnp.int32).reshape(1)
    cats = category_map.reshape(n, LANES)
    sources = (
        base_bottom.reshape(horizon, n, LANES),
        weight_bottom.reshape(horizon, n, LANES),
        weight_category.reshape(horizon, tiles, LANES),
        base_category.reshape(horizon, tiles, LANES),
        jnp.transpose(base_region, (1, 0, 2)),
        jnp.transpose(weight_region, (1, 0, 2)),
    )
    per = week_rows(tiles, n, regions)[-1]
    (sent,) = call(
        week_pack_body,
        [(weeks, per, LANES)],
        [pltpu.SemaphoreType.DMA((len(sources),))],
        sources,
        [HBM] * len(sources),
        out_specs=(HBM,),
    )
    own = exchange_weeks(sent)
    other = lax.ppermute(own, "core", [(0, 1), (1, 0)])
    table, flipped, group, same, region = call(
        lambda *refs: week_table_body(*refs, regions),
        [
            jax.ShapeDtypeStruct((skus, WIDE), jnp.bfloat16),
            jax.ShapeDtypeStruct((WIDE, skus), jnp.bfloat16),
            jax.ShapeDtypeStruct((n, skus), jnp.bfloat16),
            jax.ShapeDtypeStruct((n, LANES), jnp.bfloat16),
            jax.ShapeDtypeStruct((n, LANES), jnp.bfloat16),
        ],
        [],
        (region_map, cats),
        [SMEM, VMEM],
    )
    full = pltpu.VMEM((n, skus), jnp.float32)
    raw = pltpu.VMEM((regions, skus), jnp.float32)
    cat = pltpu.VMEM((groups * n, WIDE), jnp.float32)
    kept, line = call(
        lambda *refs: week_body(*refs, side),
        [(5, weeks, skus), (weeks, LANES)],
        [
            full, pltpu.VMEM((4, n, skus), jnp.float32),
            full, full, full, cat, cat, raw, raw, cat,
        ],
        (
            core, place, own.reshape(-1, LANES), other.reshape(-1, LANES),
            table, flipped, group, same, region, cats,
        ),
        [SMEM, SMEM, VMEM, FREE] + [VMEM] * 6,
    )
    lines = exchange_weeks(line.reshape(weeks, 1, LANES)).reshape(weeks, LANES)
    (sent,) = call(
        lambda *refs: week_combine_body(*refs, horizon),
        [(weeks * 2 * n, LANES)],
        [],
        (lines, kept),
        [VMEM] * 2,
    )
    got = exchange_weeks(sent.reshape(weeks, 2 * n, LANES))
    x, r = call(
        week_last_body,
        [(horizon, n, LANES)] * 2,
        [pltpu.SemaphoreType.DMA((2,))],
        (got,),
        [VMEM],
        out_specs=(HBM, HBM),
    )
    return x.reshape(base_bottom.shape), r.reshape(base_bottom.shape)


def solution(mesh):
    def mapped(device_mesh, body, stores):
        split_stores = P(stores, None, None)
        split_skus = P(None, None, stores)
        return jax.shard_map(
            body,
            mesh=device_mesh,
            in_specs=(split_stores,) * 4 + (split_skus,) * 2 + (P(), P()),
            out_specs=(split_stores,) * 2,
            check_vma=False,
        )

    side = mesh.shape["sku"]
    chips = mesh.devices.reshape(-1, CORES, side)

    def program(base_bottom, *others):
        stores, horizon, skus = base_bottom.shape
        fits = 16 * stores * skus * 4 <= 16 << 20
        fits = fits and 3 * others[3].shape[0] <= LANES and LANES % stores == 0
        if fits and horizon <= chips.shape[0] * side and side % 8 == 0:
            device_mesh = Mesh(chips, ("x", "core", "sku"))
            return mapped(device_mesh, by_weeks, ("x", "core", "sku"))(base_bottom, *others)
        return mapped(mesh, on_device, ("store", "sku"))(base_bottom, *others)

    return program
```

```python
import jax
import jax.numpy as jnp
from jax import lax
from jax.experimental import pallas as pl
from jax.experimental.pallas import tpu as pltpu
from jax.sharding import Mesh
from jax.sharding import PartitionSpec as P

LANES = 128
PAD = 16
WIDE = 256
VMEM = pl.BlockSpec(memory_space=pltpu.VMEM)
HBM = pl.BlockSpec(memory_space=pltpu.HBM)
SMEM = pl.BlockSpec(memory_space=pltpu.SMEM)
FREE = pl.BlockSpec(memory_space=pltpu.VMEM)
CORES = 2


def exchange(blocks, n):
    moved = lax.all_to_all(
        blocks.reshape(n, 1, -1), ("store", "sku"), split_axis=0, concat_axis=0, tiled=True
    )
    return moved.reshape(blocks.shape)


def call(body, outs, scratch, args, specs=None, held=False, out_specs=None):
    outs = [
        out if isinstance(out, jax.ShapeDtypeStruct) else jax.ShapeDtypeStruct(out, jnp.float32)
        for out in outs
    ]
    specs = specs or [VMEM] * len(args)
    args = [
        arg if spec is SMEM or spec is FREE else pltpu.with_memory_space_constraint(arg, spec.memory_space)
        for arg, spec in zip(args, specs)
    ]
    return pl.pallas_call(
        body,
        out_shape=tuple(pltpu.VMEM(out.shape, out.dtype) if held else out for out in outs),
        in_specs=specs,
        out_specs=out_specs or tuple(VMEM for _ in outs),
        scratch_shapes=scratch,
        compiler_params=pltpu.CompilerParams(vmem_limit_bytes=24 << 20),
    )(*args)


def split(value):
    high = value.astype(jnp.bfloat16)
    return high, (value - high.astype(jnp.float32)).astype(jnp.bfloat16)


def split_all(value):
    high, low = split(value)
    rest = value - high.astype(jnp.float32) - low.astype(jnp.float32)
    return high, low, rest.astype(jnp.bfloat16)


def product(left, right, contract):
    return lax.dot_general(left, right, (contract, ((), ())), preferred_element_type=jnp.float32)


def rows_of(ref, n, h):
    return ref[pl.ds(h, n, stride=ref.shape[0] // n), :]


def put_rows(ref, n, h, value):
    ref[pl.ds(h, n, stride=ref.shape[0] // n), :] = value


def category_sums(field, table_ref, group_ref, n, rows):
    width = 4 if n % 4 == 0 else 1
    lanes = width * LANES

    def step(c, total):
        pieces = [field[pl.ds(c * width + i, PAD, stride=n), :] for i in range(width)]
        parts = split_all(jnp.concatenate(pieces, axis=1))
        start = pl.multiple_of(c * lanes, lanes)
        group = group_ref[:, pl.ds(start, lanes)]
        masks = [group == g for g in range(rows // PAD)]
        none = jnp.zeros((PAD, lanes), jnp.bfloat16)
        spread = jnp.concatenate(
            [jnp.where(mask, part, none) for part in parts for mask in masks], axis=0
        )
        return total + product(spread, table_ref[pl.ds(start, lanes), :], ((1,), (0,)))

    steps = n // width
    total = lax.fori_loop(
        0, steps, step, jnp.zeros((3 * rows, WIDE), jnp.float32), unroll=min(steps, 8)
    )
    return total[:rows] + (total[rows : 2 * rows] + total[2 * rows :])


def category_spread(values, cats, horizon, put):
    place = cats & (LANES - 1)
    group = cats >> (LANES.bit_length() - 1)
    for h in range(horizon):
        found = []
        for g in range(0, values.shape[0], PAD):
            for lane in range(0, WIDE, LANES):
                row = jnp.broadcast_to(values[g + h : g + h + 1, lane : lane + LANES], cats.shape)
                found.append(jnp.take_along_axis(row, place, axis=1))
        for bit in range((len(found) - 1).bit_length()):
            mask = group & (1 << bit) != 0
            pairs = [found[i : i + 2] for i in range(0, len(found), 2)]
            found = [jnp.where(mask, pair[1], pair[0]) if len(pair) == 2 else pair[0] for pair in pairs]
        put(h, found[0])


def tiles_of(n):
    return [slice(t, t + 8) for t in range(0, n, 8)]


def put_tile(ref, n, h, tile, value):
    rows = ref.shape[0] // n
    ref[pl.ds(tile.start * rows + h, 8, stride=rows), :] = value


def region_sums(load, same, n, horizon):
    high, low = split(jnp.concatenate([load(h) for h in range(horizon)], axis=1))
    total = product(same, high, ((1,), (0,))) + product(same, low, ((1,), (0,)))
    return [total[:, h * LANES : (h + 1) * LANES] for h in range(horizon)]


def pack_body(base_hbm, out_ref, base_ref, sem):
    copy = pltpu.make_async_copy(base_hbm, base_ref, sem)
    copy.start()
    copy.wait()
    n = base_ref.shape[1]
    for h in range(base_ref.shape[0]):
        put_rows(out_ref, n, h, base_ref[h])


def prepare_body(
    base_hbm, base_cat_hbm, weight_cat_hbm, base_reg_hbm, weight_reg_hbm, cats_hbm, map_hbm,
    spread_out, wcat_out, wstore_out, bstore_out, same_out, table_out, group_out,
    cats_ref,
    field, values, base_ref, base_cat_ref, weight_cat_ref, base_reg_ref, weight_reg_ref, map_ref, sems,
):
    copies = [
        pltpu.make_async_copy(source, target, sems.at[i])
        for i, (source, target) in enumerate(
            (
                (cats_hbm, cats_ref),
                (base_hbm, base_ref),
                (weight_cat_hbm, weight_cat_ref),
                (base_cat_hbm, base_cat_ref),
                (map_hbm, map_ref),
                (weight_reg_hbm, weight_reg_ref),
                (base_reg_hbm, base_reg_ref),
            )
        )
    ]
    for copy in copies:
        copy.start()
    for copy in copies:
        copy.wait()
    horizon, n, _ = base_ref.shape
    n_regions = weight_reg_ref.shape[1]
    square = jnp.concatenate([cats_ref[...].astype(jnp.float32)] * (LANES // min(n, LANES)), axis=0)
    labels = lax.broadcasted_iota(jnp.int32, (LANES, WIDE), 1)
    columns = [
        jnp.transpose(square[i : i + LANES]).astype(jnp.int32) % WIDE
        for i in range(0, square.shape[0], LANES)
    ]
    for j in range(n):
        column = jnp.broadcast_to(columns[j // LANES][:, j % LANES : j % LANES + 1], (LANES, WIDE))
        table_out[j * LANES : (j + 1) * LANES, :] = jnp.where(
            column == labels, 1.0, 0.0
        ).astype(jnp.bfloat16)
        group = jnp.broadcast_to(cats_ref[j : j + 1, :] // WIDE, (PAD, LANES))
        group_out[:, j * LANES : (j + 1) * LANES] = group.astype(jnp.float32).astype(jnp.bfloat16)

    field[...] = jnp.zeros_like(field)
    for h in range(horizon):
        field[h * n : (h + 1) * n, :] = base_ref[h]
    sums = category_sums(field, table_out, group_out, n, wcat_out.shape[0])
    wcat_out[...] = jnp.zeros_like(wcat_out)
    values[...] = jnp.zeros_like(values)
    for g in range(0, wcat_out.shape[0], PAD):
        for lane in range(0, WIDE, LANES):
            tile = (g // PAD * WIDE + lane) // LANES
            lanes = slice(lane, lane + LANES)
            weight = weight_cat_ref[:, tile, :]
            wcat_out[g : g + horizon, lanes] = weight
            values[g : g + horizon, lanes] = weight * (
                base_cat_ref[:, tile, :] - sums[g : g + horizon, lanes]
            )
    for tile in tiles_of(n):

        def put(h, value):
            spread_out[h, tile, :] = value

        category_spread(values, cats_ref[tile, :], horizon, put)

    labels = lax.broadcasted_iota(jnp.int32, (n_regions, n), 0)
    table = jnp.where(labels == map_ref[...], 1.0, 0.0).astype(jnp.bfloat16)
    same_out[...] = product(table, table, ((0,), (0,))).astype(jnp.bfloat16)
    for source, target in ((weight_reg_ref, wstore_out), (base_reg_ref, bstore_out)):
        for h in range(horizon):
            high, low = split(source[h])
            rest = source[h] - high.astype(jnp.float32) - low.astype(jnp.float32)
            target[h] = (
                product(table, high, ((0,), (0,)))
                + product(table, low, ((0,), (0,)))
                + product(table, rest.astype(jnp.bfloat16), ((0,), (0,)))
            )


def region_start_body(got_ref, spread_ref, wstore_ref, bstore_ref, same_ref, reg_out, send_ref):
    horizon, n, _ = spread_ref.shape
    sums = region_sums(lambda h: rows_of(got_ref, n, h), same_ref[...], n, horizon)
    for h in range(horizon):
        put_rows(send_ref, n, h, spread_ref[h])
        part = wstore_ref[h] * (bstore_ref[h] - sums[h])
        reg_out[h] = part
        put_rows(send_ref, n, horizon + h, part)


def region_part(rs, wstore_ref, same_ref, put):
    horizon, n, _ = wstore_ref.shape
    sums = region_sums(lambda h: rs[h], same_ref[...], n, horizon)
    share = jnp.zeros((n, LANES), jnp.float32)
    for h in range(horizon):
        part = wstore_ref[h] * sums[h]
        share = share + part * rs[h]
        put(h, part)
    return share


def store_part(r_ref, sums, gamma, delta, eps, diag_ref, wcat_ref, cats_ref, put, put_line, values):
    horizon, n, _ = diag_ref.shape
    scaled = wcat_ref[...] * sums
    values[...] = scaled
    square = scaled * sums
    delta = jnp.sum(delta, axis=0, keepdims=True)
    for lane in range(0, WIDE, LANES):
        delta = delta + jnp.sum(square[:, lane : lane + LANES], axis=0, keepdims=True)
    lane = lax.broadcasted_iota(jnp.int32, (1, LANES), 1)
    line = jnp.zeros((1, LANES), jnp.float32)
    for i, part in enumerate((gamma, delta, eps)):
        if part is not None:
            whole = jnp.sum(jnp.sum(part, axis=0, keepdims=True), axis=1, keepdims=True)
            line = jnp.where(lane == i, whole, line)
    put_line(jnp.broadcast_to(line, (n, LANES)))
    for tile in tiles_of(n):

        def finish(h, value):
            put(h, tile, value + diag_ref[h, tile, :] * r_ref[h, tile, :])

        category_spread(values, cats_ref[tile, :], horizon, finish)


def totals(got_ref, n, row):
    total = jnp.sum(rows_of(got_ref, n, row), axis=0, keepdims=True)
    total = jnp.broadcast_to(total, (8, LANES))
    return [
        jnp.take_along_axis(total, jnp.full((8, LANES), i, jnp.int32), axis=1)[0:1] for i in range(3)
    ]


def wide(line):
    return jnp.concatenate([line] * (WIDE // LANES), axis=1)


def region_sender(ref, n, first, keep):
    def put(h, value):
        if keep is not None:
            keep[h] = value
        put_rows(ref, n, first + h, value)

    return put


def store_sender(ref, n, keep):
    def put(h, tile, value):
        keep[h, tile, :] = value
        if ref is not None:
            put_tile(ref, n, h, tile, value)

    return put


def clear_tail(field, horizon, n):
    field[horizon * n :, :] = jnp.zeros((field.shape[0] - horizon * n, LANES), jnp.float32)


def first_body(
    a_ref, reg_ref, got_ref, diag_ref, wcat_ref, wstore_ref, table_ref, group_ref, cats_ref, same_ref,
    r_out, rs_out, cr_out, a_out, reg_out, send_ref, values, field,
):
    horizon, n, _ = diag_ref.shape
    clear_tail(field, horizon, n)
    gamma = jnp.zeros((n, LANES), jnp.float32)
    delta = jnp.zeros((n, LANES), jnp.float32)
    for h in range(horizon):
        r = a_ref[h] + rows_of(got_ref, n, horizon + h)
        r_out[h] = r
        field[h * n : (h + 1) * n, :] = r
        gamma = gamma + r * r
        delta = delta + diag_ref[h] * r * r
    sums = category_sums(field, table_ref, group_ref, n, wcat_ref.shape[0])
    cr_out[...] = sums
    for h in range(horizon):
        rs_out[h] = rows_of(got_ref, n, h) + reg_ref[h]
    delta = delta + region_part(
        rs_out, wstore_ref, same_ref, region_sender(send_ref, n, horizon, reg_out)
    )
    store_part(
        r_out, sums, gamma, delta, None, diag_ref, wcat_ref, cats_ref,
        store_sender(send_ref, n, a_out),
        lambda line: put_rows(send_ref, n, 2 * horizon, line), values,
    )


def second_body(
    a_ref, reg_ref, got_ref, x_ref, r_ref, rs_ref, cr_ref,
    diag_ref, wcat_ref, wstore_ref, table_ref, group_ref, cats_ref, same_ref,
    x_out, r_out, rs_out, s_out, ss_out, cr_out, cs_out, scal_ref, a_out, reg_out, send_ref,
    values, field,
):
    horizon, n, _ = diag_ref.shape
    clear_tail(field, horizon, n)
    for h in range(horizon):
        field[h * n : (h + 1) * n, :] = a_ref[h] + rows_of(got_ref, n, horizon + h)
    sums = category_sums(field, table_ref, group_ref, n, wcat_ref.shape[0])
    cs_out[...] = sums
    gamma, delta, _ = totals(got_ref, n, 2 * horizon)
    alpha = gamma / delta
    scal_ref[0:1, :] = gamma
    scal_ref[1:2, :] = delta
    for h in range(horizon):
        ws = rows_of(got_ref, n, h) + reg_ref[h]
        ss_out[h] = ws
        rs_out[h] = rs_ref[h] - alpha * ws
    delta = region_part(
        rs_out, wstore_ref, same_ref, region_sender(send_ref, n, horizon, reg_out)
    )
    gamma = jnp.zeros((n, LANES), jnp.float32)
    eps = jnp.zeros((n, LANES), jnp.float32)
    for h in range(horizon):
        s = field[h * n : (h + 1) * n, :]
        s_out[h] = s
        r = r_ref[h]
        x_out[h] = x_ref[h] + alpha * r
        r = r - alpha * s
        r_out[h] = r
        gamma = gamma + r * r
        delta = delta + diag_ref[h] * r * r
        eps = eps + r * s
    sums = cr_ref[...] - wide(alpha) * sums
    cr_out[...] = sums
    store_part(
        r_out, sums, gamma, delta, eps, diag_ref, wcat_ref, cats_ref,
        store_sender(send_ref, n, a_out),
        lambda line: put_rows(send_ref, n, 2 * horizon, line), values,
    )


def third_body(
    a_ref, reg_ref, got_ref, x_ref, r_ref, rs_ref, p_ref, s_ref, ss_ref, cr_ref, cs_ref, scal_ref,
    diag_ref, wcat_ref, wstore_ref, table_ref, group_ref, cats_ref, same_ref,
    x_out, r_out, p_out, s_out, scal_out, a_out, send_ref, values, field, rs_out,
):
    horizon, n, _ = diag_ref.shape
    clear_tail(field, horizon, n)
    for h in range(horizon):
        field[h * n : (h + 1) * n, :] = a_ref[h] + rows_of(got_ref, n, horizon + h)
    sums = category_sums(field, table_ref, group_ref, n, wcat_ref.shape[0])
    gamma, delta, eps = totals(got_ref, n, 2 * horizon)
    beta = gamma / scal_ref[0:1, :]
    curve = delta + 2.0 * beta * eps + beta * beta * scal_ref[1:2, :]
    alpha = gamma / curve
    scal_out[0:1, :] = gamma
    scal_out[1:2, :] = curve
    for h in range(horizon):
        ws = rows_of(got_ref, n, h) + reg_ref[h]
        rs_out[h] = rs_ref[h] - alpha * (ws + beta * ss_ref[h])
    delta = region_part(rs_out, wstore_ref, same_ref, region_sender(send_ref, n, 0, None))
    gamma = jnp.zeros((n, LANES), jnp.float32)
    eps = jnp.zeros((n, LANES), jnp.float32)
    for h in range(horizon):
        s = field[h * n : (h + 1) * n, :] + beta * s_ref[h]
        s_out[h] = s
        r = r_ref[h]
        p = r + beta * p_ref[h]
        p_out[h] = p
        x_out[h] = x_ref[h] + alpha * p
        r = r - alpha * s
        r_out[h] = r
        gamma = gamma + r * r
        delta = delta + diag_ref[h] * r * r
        eps = eps + r * s
    sums = cr_ref[...] - wide(alpha) * (sums + wide(beta) * cs_ref[...])
    store_part(
        r_out, sums, gamma, delta, eps, diag_ref, wcat_ref, cats_ref,
        store_sender(None, n, a_out), lambda line: put_rows(send_ref, n, horizon, line), values,
    )


def last_body(a_ref, got_ref, x_ref, r_ref, p_ref, s_ref, scal_ref, x_out, r_out):
    horizon, n, _ = a_ref.shape
    gamma, delta, eps = totals(got_ref, n, horizon)
    beta = gamma / scal_ref[0:1, :]
    alpha = gamma / (delta + 2.0 * beta * eps + beta * beta * scal_ref[1:2, :])
    for h in range(horizon):
        r = r_ref[h]
        s = a_ref[h] + rows_of(got_ref, n, h) + beta * s_ref[h]
        x_out[h] = x_ref[h] + alpha * (r + beta * p_ref[h])
        r_out[h] = r - alpha * s


def on_device(
    base_bottom,
    weight_bottom,
    base_category,
    weight_category,
    base_region,
    weight_region,
    category_map,
    region_map,
):
    stores, horizon, skus = base_bottom.shape
    n = region_map.shape[0]
    groups = weight_category.shape[2] // WIDE
    tiles = weight_category.shape[2] // LANES
    field = (horizon, n, LANES)
    padded = (PAD * n, LANES)
    by_category = (horizon, tiles, LANES)
    scal = (2, LANES)
    values = pltpu.VMEM((groups * PAD, WIDE), jnp.float32)

    x = base_bottom.reshape(field)
    diag = weight_bottom.reshape(field)
    (sent,) = call(
        pack_body,
        [(n * horizon, LANES)],
        [pltpu.VMEM(field, jnp.float32), pltpu.SemaphoreType.DMA],
        (x,),
        [HBM],
        True,
    )
    got = exchange(sent, n)
    arguments = (
        x,
        base_category.reshape(by_category),
        weight_category.reshape(by_category),
        jnp.transpose(base_region, (1, 0, 2)),
        jnp.transpose(weight_region, (1, 0, 2)),
        category_map.reshape(n, LANES),
        region_map.reshape(1, n),
    )
    held = [pltpu.VMEM(arguments[i].shape, arguments[i].dtype) for i in (0, 1, 2, 3, 4, 6)]
    spread, wcat, wstore, bstore, same, table, group, cats = call(
        prepare_body,
        [
            field,
            (groups * PAD, WIDE),
            field,
            field,
            jax.ShapeDtypeStruct((n, n), jnp.bfloat16),
            jax.ShapeDtypeStruct((skus, WIDE), jnp.bfloat16),
            jax.ShapeDtypeStruct((PAD, skus), jnp.bfloat16),
            jax.ShapeDtypeStruct((n, LANES), jnp.int32),
        ],
        [
            pltpu.VMEM(padded, jnp.float32),
            values,
            *held,
            pltpu.SemaphoreType.DMA((len(arguments),)),
        ],
        arguments,
        [HBM] * len(arguments),
    )
    reg, sent = call(
        region_start_body,
        [field, (n * 2 * horizon, LANES)],
        [],
        (got, spread, wstore, bstore, same),
    )
    got = exchange(sent, n)
    fixed = (diag, wcat, wstore, table, group, cats, same)
    both = (n * (2 * horizon + 1), LANES)
    work = [values, pltpu.VMEM(padded, jnp.float32)]
    sums = (groups * PAD, WIDE)
    r, rs, cr, a, reg, sent = call(
        first_body, [field, field, sums, field, field, both], work, (spread, reg, got) + fixed
    )
    got = exchange(sent, n)
    p = r
    x, r, rs, s, ss, cr, cs, scalars, a, reg, sent = call(
        second_body,
        [field, field, field, field, field, sums, sums, scal, field, field, both],
        work,
        (a, reg, got, x, r, rs, cr) + fixed,
    )
    got = exchange(sent, n)
    x, r, p, s, scalars, a, sent = call(
        third_body,
        [field, field, field, field, scal, field, (n * (horizon + 1), LANES)],
        work + [pltpu.VMEM(field, jnp.float32)],
        (a, reg, got, x, r, rs, p, s, ss, cr, cs, scalars) + fixed,
    )
    got = exchange(sent, n)
    x, r = call(last_body, [field, field], [], (a, got, x, r, p, s, scalars))
    return x.reshape(base_bottom.shape), r.reshape(base_bottom.shape)


def week_rows(tiles, n, regions):
    sizes = (n, n, tiles, tiles, regions, regions)
    return [sum(sizes[:i]) for i in range(len(sizes) + 1)]


def week_pack_body(*refs):
    sources, out, sems = refs[:-2], refs[-2], refs[-1]
    horizon = sources[0].shape[0]
    copies, start = [], 0
    for i, source in enumerate(sources):
        rows = source.shape[1]
        target = out.at[pl.ds(0, horizon), pl.ds(start, rows)]
        copies.append(pltpu.make_async_copy(source, target, sems.at[i]))
        start += rows
    for copy in copies:
        copy.start()
    for copy in copies:
        copy.wait()


def week_table_body(
    map_ref, cats_ref, table_out, flipped_out, group_out, same_out, region_out, regions
):
    n = cats_ref.shape[0]
    lane = lax.broadcasted_iota(jnp.int32, (n, LANES), 1)
    line = lax.broadcasted_iota(jnp.int32, (n, LANES), 0)
    across = jnp.zeros((n, LANES), jnp.int32)
    down = jnp.zeros((n, LANES), jnp.int32)
    for s in range(n):
        across = jnp.where(lane % n == s, map_ref[s], across)
        down = jnp.where(line == s, map_ref[s], down)
    same_out[...] = jnp.where(across == down, 1.0, 0.0).astype(jnp.bfloat16)
    region_out[...] = jnp.where(lane % regions == down, 1.0, 0.0).astype(jnp.bfloat16)
    square = jnp.concatenate([cats_ref[...].astype(jnp.float32)] * (LANES // min(n, LANES)), axis=0)
    labels = lax.broadcasted_iota(jnp.int32, (LANES, WIDE), 1)
    downward = lax.broadcasted_iota(jnp.int32, (WIDE, LANES), 0)
    columns = [
        jnp.transpose(square[i : i + LANES]).astype(jnp.int32) & (WIDE - 1)
        for i in range(0, square.shape[0], LANES)
    ]
    for j in range(n):
        column = jnp.broadcast_to(columns[j // LANES][:, j % LANES : j % LANES + 1], (LANES, WIDE))
        table_out[j * LANES : (j + 1) * LANES, :] = jnp.where(
            column == labels, 1.0, 0.0
        ).astype(jnp.bfloat16)
        flipped_out[:, j * LANES : (j + 1) * LANES] = jnp.where(
            (cats_ref[j : j + 1, :] & (WIDE - 1)) == downward, 1.0, 0.0
        ).astype(jnp.bfloat16)
        group = cats_ref[j : j + 1, :] >> (WIDE.bit_length() - 1)
        group = jnp.broadcast_to(group, (group_out.shape[0], LANES))
        group_out[:, j * LANES : (j + 1) * LANES] = group.astype(jnp.float32).astype(jnp.bfloat16)


def ratio(top, bottom):
    return jnp.where(bottom > 0.0, top / bottom, 0.0)


def whole_sum(part):
    total = jnp.sum(jnp.sum(part, axis=0, keepdims=True), axis=1, keepdims=True)
    return jnp.broadcast_to(total, (1, LANES))


def week_body(
    core_ref, own_ref, other_ref, table_ref, flipped_ref, group_ref, same_ref, region_ref,
    cats_ref, kept_out, line_out,
    base, basis, diag, wstore, bstore, wcat, bcat, raw_weight, raw_base, held,
    side, weeks,
):
    core = core_ref[0]
    n, skus = base.shape
    per = own_ref.shape[0] // weeks
    regions = raw_weight.shape[0]
    tiles = wcat.shape[0] // n * (WIDE // LANES)
    starts = week_rows(tiles, n, regions)
    chunk = min(skus, 8 * LANES)
    chunks = [slice(c, c + chunk) for c in range(0, skus, chunk)]
    for ref, c in ((own_ref, core), (other_ref, 1 - core)):
        for x in range(n // (CORES * side)):
            for t in range(0, side, 8):
                first = (x * side + t) * per
                top = pl.multiple_of(x * CORES * side + c * side + t, 8)

                def rows(row):
                    return ref[pl.ds(first + row, 8, stride=per), :]

                for j in range(n):
                    lanes = slice(j * LANES, (j + 1) * LANES)
                    base[pl.ds(top, 8), lanes] = rows(starts[0] + j)
                    diag[pl.ds(top, 8), lanes] = rows(starts[1] + j)
                for g in range(tiles):
                    lane = g * LANES % WIDE
                    down = pl.multiple_of(g * LANES // WIDE * n + top, 8)
                    wcat[pl.ds(down, 8), lane : lane + LANES] = rows(starts[2] + g)
                    bcat[pl.ds(down, 8), lane : lane + LANES] = rows(starts[3] + g)
            for k in range(side):
                first = (x * side + k) * per
                j = x * CORES * side + c * side + k
                lanes = pl.ds(pl.multiple_of(j * LANES, LANES), LANES)
                raw_base[:, lanes] = ref[first + starts[4] : first + starts[5], :]
                raw_weight[:, lanes] = ref[first + starts[5] : first + starts[6], :]

    region_table = region_ref[:, : 3 * regions]
    same = same_ref[:, : 2 * n]
    for source, target in ((raw_weight, wstore), (raw_base, bstore)):
        for lanes in chunks:
            parts = jnp.concatenate(split_all(source[:, lanes]), axis=0)
            target[:, lanes] = product(region_table, parts, ((1,), (0,)))

    def by_category(field):
        rows = wcat.shape[0]
        group = group_ref[...]
        masks = [group == g for g in range(rows // n)]
        none = jnp.zeros(group.shape, jnp.bfloat16)
        spread = jnp.concatenate(
            [jnp.where(mask, part, none) for part in split(field[...]) for mask in masks], axis=0
        )
        total = product(spread, table_ref[...], ((1,), (0,)))
        return total[:rows] + total[rows:]

    def spread(values, m, put):
        parts = jnp.concatenate(split(values), axis=0)
        groups = values.shape[0] // m
        for lanes in chunks:
            found = product(parts, flipped_ref[:, lanes], ((1,), (0,)))
            for t in range(0, chunk, LANES):
                tile = slice(lanes.start + t, lanes.start + t + LANES)
                members = cats_ref[tile.start // LANES : tile.start // LANES + 1, :]
                group = jnp.broadcast_to(members >> (WIDE.bit_length() - 1), (m, LANES))
                high, low = found[: groups * m, t : t + LANES], found[groups * m :, t : t + LANES]
                one = [
                    high[g * m : (g + 1) * m] + low[g * m : (g + 1) * m] for g in range(groups)
                ]
                bit = 1
                while len(one) > 1:
                    odd = group & bit != 0
                    pairs = [one[i : i + 2] for i in range(0, len(one), 2)]
                    one = [jnp.where(odd, *pair[::-1]) if len(pair) == 2 else pair[0] for pair in pairs]
                    bit *= 2
                put(tile, one[0])

    def by_region(part):
        return product(same, jnp.concatenate(split(part), axis=0), ((1,), (0,)))

    def tiles_in(lanes):
        for t in range(0, chunk, LANES):
            yield slice(lanes.start + t, lanes.start + t + LANES), slice(t, t + LANES)

    zero = jnp.zeros((n, LANES), jnp.float32)
    for lanes in chunks:
        sums = by_region(base[:, lanes])
        for tile, inner in tiles_in(lanes):
            basis[0, :, tile] = wstore[:, tile] * (bstore[:, tile] - sums[:, inner])
    norm = [zero]

    def start(tile, value):
        result = basis[0, :, tile] + value
        basis[0, :, tile] = result
        norm[0] = norm[0] + result * result

    spread(wcat[...] * (bcat[...] - by_category(base)), n, start)
    norms, quotients = [whole_sum(norm[0])], []
    for k in range(3):
        field, image = basis.at[k], basis.at[k + 1]
        sums = by_category(field)
        values = wcat[...] * sums
        square = values * sums
        dot = zero
        for lane in range(0, WIDE, LANES):
            for g in range(0, square.shape[0], n):
                dot = dot + square[g : g + n, lane : lane + LANES]
        for lanes in chunks:
            sums = by_region(field[:, lanes])
            for tile, inner in tiles_in(lanes):
                part = field[:, tile]
                result = diag[:, tile] * part + wstore[:, tile] * sums[:, inner]
                image[:, tile] = result
                dot = dot + part * result
        quotients.append(ratio(whole_sum(dot), norms[k]))
        back = ratio(norms[k], norms[k - 1]) if k else None
        if k == 2:
            break
        norm = [zero]

        def step(tile, value):
            result = image[:, tile] + value - quotients[k] * field[:, tile]
            if k:
                result = result - back * basis[k - 1, :, tile]
            image[:, tile] = result
            norm[0] = norm[0] + result * result

        spread(values, n, step)
        norms.append(whole_sum(norm[0]))

    lane = lax.broadcasted_iota(jnp.int32, line_out.shape, 1)
    line = jnp.zeros(line_out.shape, jnp.float32)
    for i, value in enumerate(norms + quotients):
        line = jnp.where(lane == i, jnp.broadcast_to(value, line.shape), line)
    line_out[...] = line

    held[...] = values
    tops = [
        pl.multiple_of(x * CORES * side + core * side + t, 8)
        for x in range(n // (CORES * side))
        for t in range(0, side, 8)
    ]
    for i, top in enumerate(tops):
        kept_out[4, i * 8 : i * 8 + 8, :] = base[pl.ds(top, 8), :]
        for k in range(4):
            kept_out[k, i * 8 : i * 8 + 8, :] = basis[k, pl.ds(top, 8), :]
    mine = jnp.concatenate(
        [held[pl.ds(g + top, 8), :] for g in range(0, held.shape[0], n) for top in tops], axis=0
    )

    def finish(tile, value):
        result = kept_out[3, :, tile] + value - quotients[2] * kept_out[2, :, tile]
        kept_out[3, :, tile] = result - back * kept_out[1, :, tile]

    spread(mine, weeks, finish)


def week_combine_body(place_ref, lines_ref, kept_ref, send_ref, horizon):
    weeks = lines_ref.shape[0]
    n = kept_ref.shape[2] // LANES
    week = lax.broadcasted_iota(jnp.int32, (weeks, LANES), 0)
    lines = jnp.where(week < horizon, lines_ref[...], 0.0)
    n1, n2, n3, a1, a2, a3 = [
        jnp.take_along_axis(lines, jnp.full((weeks, LANES), i, jnp.int32), axis=1) for i in range(6)
    ]
    e2, e3 = ratio(n2, n1), ratio(n3, n2)

    def dot(left, right):
        terms = n1 * left[0] * right[0] + n2 * left[1] * right[1] + n3 * left[2] * right[2]
        return jnp.sum(terms, axis=0, keepdims=True)

    zero = jnp.zeros((weeks, LANES), jnp.float32)
    x = [zero, zero, zero]
    r = [zero + 1.0, zero, zero, zero]
    p = r[:3]
    rr = dot(r, r)
    for k in range(3):
        image = [
            a1 * p[0] + e2 * p[1],
            p[0] + a2 * p[1] + e3 * p[2],
            p[1] + a3 * p[2],
            p[2],
        ]
        alpha = rr / dot(p, image)
        x = [left + alpha * right for left, right in zip(x, p)]
        r = [left - alpha * right for left, right in zip(r, image)]
        if k < 2:
            new = dot(r, r)
            p = [left + new / rr * right for left, right in zip(r[:3], p)]
            rr = new
    mine = week == place_ref[0]
    x = [jnp.sum(jnp.where(mine, value, 0.0), axis=0, keepdims=True) for value in x]
    r = [jnp.sum(jnp.where(mine, value, 0.0), axis=0, keepdims=True) for value in r]
    rows = send_ref.shape[0] // weeks
    for t in range(0, weeks, 8):
        for j in range(n):
            lanes = slice(j * LANES, (j + 1) * LANES)
            parts = [kept_ref[k, t : t + 8, lanes] for k in range(4)]
            left = kept_ref[4, t : t + 8, lanes]
            right = r[3] * parts[3]
            for k in range(3):
                left = left + x[k] * parts[k]
                right = right + r[k] * parts[k]
            first = t * rows + j
            send_ref[pl.ds(first, 8, stride=rows), :] = left
            send_ref[pl.ds(first + n, 8, stride=rows), :] = right


def week_last_body(got_ref, x_out, r_out, sems):
    horizon, n, _ = x_out.shape
    copies = [
        pltpu.make_async_copy(
            got_ref.at[pl.ds(0, horizon), pl.ds(i * n, n)], target, sems.at[i]
        )
        for i, target in enumerate((x_out, r_out))
    ]
    for copy in copies:
        copy.start()
    for copy in copies:
        copy.wait()


def exchange_weeks(blocks):
    return lax.all_to_all(blocks, ("x", "sku"), split_axis=0, concat_axis=0, tiled=True)


def by_weeks(
    base_bottom,
    weight_bottom,
    base_category,
    weight_category,
    base_region,
    weight_region,
    category_map,
    region_map,
):
    stores, horizon, skus = base_bottom.shape
    n = region_map.shape[0]
    regions = weight_region.shape[0]
    tiles = weight_category.shape[2] // LANES
    groups = weight_category.shape[2] // WIDE
    side = lax.axis_size("sku")
    weeks = lax.axis_size("x") * side
    place = lax.axis_index("x") * side + lax.axis_index("sku")
    place = place.astype(jnp.int32).reshape(1)
    core = lax.axis_index("core").astype(jnp.int32).reshape(1)
    cats = category_map.reshape(n, LANES)
    sources = (
        base_bottom.reshape(horizon, n, LANES),
        weight_bottom.reshape(horizon, n, LANES),
        weight_category.reshape(horizon, tiles, LANES),
        base_category.reshape(horizon, tiles, LANES),
        jnp.transpose(base_region, (1, 0, 2)),
        jnp.transpose(weight_region, (1, 0, 2)),
    )
    per = week_rows(tiles, n, regions)[-1]
    (sent,) = call(
        week_pack_body,
        [(weeks, per, LANES)],
        [pltpu.SemaphoreType.DMA((len(sources),))],
        sources,
        [HBM] * len(sources),
        out_specs=(HBM,),
    )
    own = exchange_weeks(sent)
    other = lax.ppermute(own, "core", [(0, 1), (1, 0)])
    table, flipped, group, same, region = call(
        lambda *refs: week_table_body(*refs, regions),
        [
            jax.ShapeDtypeStruct((skus, WIDE), jnp.bfloat16),
            jax.ShapeDtypeStruct((WIDE, skus), jnp.bfloat16),
            jax.ShapeDtypeStruct((n, skus), jnp.bfloat16),
            jax.ShapeDtypeStruct((n, LANES), jnp.bfloat16),
            jax.ShapeDtypeStruct((n, LANES), jnp.bfloat16),
        ],
        [],
        (region_map, cats),
        [SMEM, VMEM],
    )
    full = pltpu.VMEM((n, skus), jnp.float32)
    raw = pltpu.VMEM((regions, skus), jnp.float32)
    cat = pltpu.VMEM((groups * n, WIDE), jnp.float32)
    kept, line = call(
        lambda *refs: week_body(*refs, side, weeks),
        [(5, weeks, skus), (1, LANES)],
        [
            full, pltpu.VMEM((4, n, skus), jnp.float32),
            full, full, full, cat, cat, raw, raw, cat,
        ],
        (
            core, own.reshape(-1, LANES), other.reshape(-1, LANES),
            table, flipped, group, same, region, cats,
        ),
        [SMEM, VMEM, FREE] + [VMEM] * 6,
    )
    lines = lax.all_gather(line, ("x", "sku"), axis=0, tiled=True)
    (sent,) = call(
        lambda *refs: week_combine_body(*refs, horizon),
        [(weeks * 2 * n, LANES)],
        [],
        (place, lines, kept),
        [SMEM] + [VMEM] * 2,
    )
    got = exchange_weeks(sent.reshape(weeks, 2 * n, LANES))
    x, r = call(
        week_last_body,
        [(horizon, n, LANES)] * 2,
        [pltpu.SemaphoreType.DMA((2,))],
        (got,),
        [VMEM],
        out_specs=(HBM, HBM),
    )
    return x.reshape(base_bottom.shape), r.reshape(base_bottom.shape)


def solution(mesh):
    def mapped(device_mesh, body, stores):
        split_stores = P(stores, None, None)
        split_skus = P(None, None, stores)
        return jax.shard_map(
            body,
            mesh=device_mesh,
            in_specs=(split_stores,) * 4 + (split_skus,) * 2 + (P(), P()),
            out_specs=(split_stores,) * 2,
            check_vma=False,
        )

    side = mesh.shape["sku"]
    chips = mesh.devices.reshape(-1, CORES, side)

    def program(base_bottom, *others):
        stores, horizon, skus = base_bottom.shape
        fits = 16 * stores * skus * 4 <= 16 << 20
        fits = fits and 3 * others[3].shape[0] <= LANES and LANES % stores == 0
        if fits and horizon <= chips.shape[0] * side and side % 8 == 0:
            device_mesh = Mesh(chips, ("x", "core", "sku"))
            return mapped(device_mesh, by_weeks, ("x", "core", "sku"))(base_bottom, *others)
        return mapped(mesh, on_device, ("store", "sku"))(base_bottom, *others)

    return program
```

```python
import jax
import jax.numpy as jnp
from jax import lax
from jax.experimental import pallas as pl
from jax.experimental.pallas import tpu as pltpu
from jax.sharding import Mesh
from jax.sharding import PartitionSpec as P

LANES = 128
PAD = 16
WIDE = 256
VMEM = pl.BlockSpec(memory_space=pltpu.VMEM)
HBM = pl.BlockSpec(memory_space=pltpu.HBM)
SMEM = pl.BlockSpec(memory_space=pltpu.SMEM)
FREE = pl.BlockSpec(memory_space=pltpu.VMEM)
CORES = 2


def exchange(blocks, n):
    moved = lax.all_to_all(
        blocks.reshape(n, 1, -1), ("store", "sku"), split_axis=0, concat_axis=0, tiled=True
    )
    return moved.reshape(blocks.shape)


def call(body, outs, scratch, args, specs=None, held=False, out_specs=None):
    outs = [
        out if isinstance(out, jax.ShapeDtypeStruct) else jax.ShapeDtypeStruct(out, jnp.float32)
        for out in outs
    ]
    specs = specs or [VMEM] * len(args)
    args = [
        arg if spec is SMEM or spec is FREE else pltpu.with_memory_space_constraint(arg, spec.memory_space)
        for arg, spec in zip(args, specs)
    ]
    return pl.pallas_call(
        body,
        out_shape=tuple(pltpu.VMEM(out.shape, out.dtype) if held else out for out in outs),
        in_specs=specs,
        out_specs=out_specs or tuple(VMEM for _ in outs),
        scratch_shapes=scratch,
        compiler_params=pltpu.CompilerParams(vmem_limit_bytes=24 << 20),
    )(*args)


def split(value):
    high = value.astype(jnp.bfloat16)
    return high, (value - high.astype(jnp.float32)).astype(jnp.bfloat16)


def split_all(value):
    high, low = split(value)
    rest = value - high.astype(jnp.float32) - low.astype(jnp.float32)
    return high, low, rest.astype(jnp.bfloat16)


def product(left, right, contract):
    return lax.dot_general(left, right, (contract, ((), ())), preferred_element_type=jnp.float32)


def rows_of(ref, n, h):
    return ref[pl.ds(h, n, stride=ref.shape[0] // n), :]


def put_rows(ref, n, h, value):
    ref[pl.ds(h, n, stride=ref.shape[0] // n), :] = value


def category_sums(field, table_ref, group_ref, n, rows):
    width = 4 if n % 4 == 0 else 1
    lanes = width * LANES

    def step(c, total):
        pieces = [field[pl.ds(c * width + i, PAD, stride=n), :] for i in range(width)]
        parts = split_all(jnp.concatenate(pieces, axis=1))
        start = pl.multiple_of(c * lanes, lanes)
        group = group_ref[:, pl.ds(start, lanes)]
        masks = [group == g for g in range(rows // PAD)]
        none = jnp.zeros((PAD, lanes), jnp.bfloat16)
        spread = jnp.concatenate(
            [jnp.where(mask, part, none) for part in parts for mask in masks], axis=0
        )
        return total + product(spread, table_ref[pl.ds(start, lanes), :], ((1,), (0,)))

    steps = n // width
    total = lax.fori_loop(
        0, steps, step, jnp.zeros((3 * rows, WIDE), jnp.float32), unroll=min(steps, 8)
    )
    return total[:rows] + (total[rows : 2 * rows] + total[2 * rows :])


def category_spread(values, cats, horizon, put):
    place = cats & (LANES - 1)
    group = cats >> (LANES.bit_length() - 1)
    for h in range(horizon):
        found = []
        for g in range(0, values.shape[0], PAD):
            for lane in range(0, WIDE, LANES):
                row = jnp.broadcast_to(values[g + h : g + h + 1, lane : lane + LANES], cats.shape)
                found.append(jnp.take_along_axis(row, place, axis=1))
        for bit in range((len(found) - 1).bit_length()):
            mask = group & (1 << bit) != 0
            pairs = [found[i : i + 2] for i in range(0, len(found), 2)]
            found = [jnp.where(mask, pair[1], pair[0]) if len(pair) == 2 else pair[0] for pair in pairs]
        put(h, found[0])


def tiles_of(n):
    return [slice(t, t + 8) for t in range(0, n, 8)]


def put_tile(ref, n, h, tile, value):
    rows = ref.shape[0] // n
    ref[pl.ds(tile.start * rows + h, 8, stride=rows), :] = value


def region_sums(load, same, n, horizon):
    high, low = split(jnp.concatenate([load(h) for h in range(horizon)], axis=1))
    total = product(same, high, ((1,), (0,))) + product(same, low, ((1,), (0,)))
    return [total[:, h * LANES : (h + 1) * LANES] for h in range(horizon)]


def pack_body(base_hbm, out_ref, base_ref, sem):
    copy = pltpu.make_async_copy(base_hbm, base_ref, sem)
    copy.start()
    copy.wait()
    n = base_ref.shape[1]
    for h in range(base_ref.shape[0]):
        put_rows(out_ref, n, h, base_ref[h])


def prepare_body(
    base_hbm, base_cat_hbm, weight_cat_hbm, base_reg_hbm, weight_reg_hbm, cats_hbm, map_hbm,
    spread_out, wcat_out, wstore_out, bstore_out, same_out, table_out, group_out,
    cats_ref,
    field, values, base_ref, base_cat_ref, weight_cat_ref, base_reg_ref, weight_reg_ref, map_ref, sems,
):
    copies = [
        pltpu.make_async_copy(source, target, sems.at[i])
        for i, (source, target) in enumerate(
            (
                (cats_hbm, cats_ref),
                (base_hbm, base_ref),
                (weight_cat_hbm, weight_cat_ref),
                (base_cat_hbm, base_cat_ref),
                (map_hbm, map_ref),
                (weight_reg_hbm, weight_reg_ref),
                (base_reg_hbm, base_reg_ref),
            )
        )
    ]
    for copy in copies:
        copy.start()
    for copy in copies:
        copy.wait()
    horizon, n, _ = base_ref.shape
    n_regions = weight_reg_ref.shape[1]
    square = jnp.concatenate([cats_ref[...].astype(jnp.float32)] * (LANES // min(n, LANES)), axis=0)
    labels = lax.broadcasted_iota(jnp.int32, (LANES, WIDE), 1)
    columns = [
        jnp.transpose(square[i : i + LANES]).astype(jnp.int32) % WIDE
        for i in range(0, square.shape[0], LANES)
    ]
    for j in range(n):
        column = jnp.broadcast_to(columns[j // LANES][:, j % LANES : j % LANES + 1], (LANES, WIDE))
        table_out[j * LANES : (j + 1) * LANES, :] = jnp.where(
            column == labels, 1.0, 0.0
        ).astype(jnp.bfloat16)
        group = jnp.broadcast_to(cats_ref[j : j + 1, :] // WIDE, (PAD, LANES))
        group_out[:, j * LANES : (j + 1) * LANES] = group.astype(jnp.float32).astype(jnp.bfloat16)

    field[...] = jnp.zeros_like(field)
    for h in range(horizon):
        field[h * n : (h + 1) * n, :] = base_ref[h]
    sums = category_sums(field, table_out, group_out, n, wcat_out.shape[0])
    wcat_out[...] = jnp.zeros_like(wcat_out)
    values[...] = jnp.zeros_like(values)
    for g in range(0, wcat_out.shape[0], PAD):
        for lane in range(0, WIDE, LANES):
            tile = (g // PAD * WIDE + lane) // LANES
            lanes = slice(lane, lane + LANES)
            weight = weight_cat_ref[:, tile, :]
            wcat_out[g : g + horizon, lanes] = weight
            values[g : g + horizon, lanes] = weight * (
                base_cat_ref[:, tile, :] - sums[g : g + horizon, lanes]
            )
    for tile in tiles_of(n):

        def put(h, value):
            spread_out[h, tile, :] = value

        category_spread(values, cats_ref[tile, :], horizon, put)

    labels = lax.broadcasted_iota(jnp.int32, (n_regions, n), 0)
    table = jnp.where(labels == map_ref[...], 1.0, 0.0).astype(jnp.bfloat16)
    same_out[...] = product(table, table, ((0,), (0,))).astype(jnp.bfloat16)
    for source, target in ((weight_reg_ref, wstore_out), (base_reg_ref, bstore_out)):
        for h in range(horizon):
            high, low = split(source[h])
            rest = source[h] - high.astype(jnp.float32) - low.astype(jnp.float32)
            target[h] = (
                product(table, high, ((0,), (0,)))
                + product(table, low, ((0,), (0,)))
                + product(table, rest.astype(jnp.bfloat16), ((0,), (0,)))
            )


def region_start_body(got_ref, spread_ref, wstore_ref, bstore_ref, same_ref, reg_out, send_ref):
    horizon, n, _ = spread_ref.shape
    sums = region_sums(lambda h: rows_of(got_ref, n, h), same_ref[...], n, horizon)
    for h in range(horizon):
        put_rows(send_ref, n, h, spread_ref[h])
        part = wstore_ref[h] * (bstore_ref[h] - sums[h])
        reg_out[h] = part
        put_rows(send_ref, n, horizon + h, part)


def region_part(rs, wstore_ref, same_ref, put):
    horizon, n, _ = wstore_ref.shape
    sums = region_sums(lambda h: rs[h], same_ref[...], n, horizon)
    share = jnp.zeros((n, LANES), jnp.float32)
    for h in range(horizon):
        part = wstore_ref[h] * sums[h]
        share = share + part * rs[h]
        put(h, part)
    return share


def store_part(r_ref, sums, gamma, delta, eps, diag_ref, wcat_ref, cats_ref, put, put_line, values):
    horizon, n, _ = diag_ref.shape
    scaled = wcat_ref[...] * sums
    values[...] = scaled
    square = scaled * sums
    delta = jnp.sum(delta, axis=0, keepdims=True)
    for lane in range(0, WIDE, LANES):
        delta = delta + jnp.sum(square[:, lane : lane + LANES], axis=0, keepdims=True)
    lane = lax.broadcasted_iota(jnp.int32, (1, LANES), 1)
    line = jnp.zeros((1, LANES), jnp.float32)
    for i, part in enumerate((gamma, delta, eps)):
        if part is not None:
            whole = jnp.sum(jnp.sum(part, axis=0, keepdims=True), axis=1, keepdims=True)
            line = jnp.where(lane == i, whole, line)
    put_line(jnp.broadcast_to(line, (n, LANES)))
    for tile in tiles_of(n):

        def finish(h, value):
            put(h, tile, value + diag_ref[h, tile, :] * r_ref[h, tile, :])

        category_spread(values, cats_ref[tile, :], horizon, finish)


def totals(got_ref, n, row):
    total = jnp.sum(rows_of(got_ref, n, row), axis=0, keepdims=True)
    total = jnp.broadcast_to(total, (8, LANES))
    return [
        jnp.take_along_axis(total, jnp.full((8, LANES), i, jnp.int32), axis=1)[0:1] for i in range(3)
    ]


def wide(line):
    return jnp.concatenate([line] * (WIDE // LANES), axis=1)


def region_sender(ref, n, first, keep):
    def put(h, value):
        if keep is not None:
            keep[h] = value
        put_rows(ref, n, first + h, value)

    return put


def store_sender(ref, n, keep):
    def put(h, tile, value):
        keep[h, tile, :] = value
        if ref is not None:
            put_tile(ref, n, h, tile, value)

    return put


def clear_tail(field, horizon, n):
    field[horizon * n :, :] = jnp.zeros((field.shape[0] - horizon * n, LANES), jnp.float32)


def first_body(
    a_ref, reg_ref, got_ref, diag_ref, wcat_ref, wstore_ref, table_ref, group_ref, cats_ref, same_ref,
    r_out, rs_out, cr_out, a_out, reg_out, send_ref, values, field,
):
    horizon, n, _ = diag_ref.shape
    clear_tail(field, horizon, n)
    gamma = jnp.zeros((n, LANES), jnp.float32)
    delta = jnp.zeros((n, LANES), jnp.float32)
    for h in range(horizon):
        r = a_ref[h] + rows_of(got_ref, n, horizon + h)
        r_out[h] = r
        field[h * n : (h + 1) * n, :] = r
        gamma = gamma + r * r
        delta = delta + diag_ref[h] * r * r
    sums = category_sums(field, table_ref, group_ref, n, wcat_ref.shape[0])
    cr_out[...] = sums
    for h in range(horizon):
        rs_out[h] = rows_of(got_ref, n, h) + reg_ref[h]
    delta = delta + region_part(
        rs_out, wstore_ref, same_ref, region_sender(send_ref, n, horizon, reg_out)
    )
    store_part(
        r_out, sums, gamma, delta, None, diag_ref, wcat_ref, cats_ref,
        store_sender(send_ref, n, a_out),
        lambda line: put_rows(send_ref, n, 2 * horizon, line), values,
    )


def second_body(
    a_ref, reg_ref, got_ref, x_ref, r_ref, rs_ref, cr_ref,
    diag_ref, wcat_ref, wstore_ref, table_ref, group_ref, cats_ref, same_ref,
    x_out, r_out, rs_out, s_out, ss_out, cr_out, cs_out, scal_ref, a_out, reg_out, send_ref,
    values, field,
):
    horizon, n, _ = diag_ref.shape
    clear_tail(field, horizon, n)
    for h in range(horizon):
        field[h * n : (h + 1) * n, :] = a_ref[h] + rows_of(got_ref, n, horizon + h)
    sums = category_sums(field, table_ref, group_ref, n, wcat_ref.shape[0])
    cs_out[...] = sums
    gamma, delta, _ = totals(got_ref, n, 2 * horizon)
    alpha = gamma / delta
    scal_ref[0:1, :] = gamma
    scal_ref[1:2, :] = delta
    for h in range(horizon):
        ws = rows_of(got_ref, n, h) + reg_ref[h]
        ss_out[h] = ws
        rs_out[h] = rs_ref[h] - alpha * ws
    delta = region_part(
        rs_out, wstore_ref, same_ref, region_sender(send_ref, n, horizon, reg_out)
    )
    gamma = jnp.zeros((n, LANES), jnp.float32)
    eps = jnp.zeros((n, LANES), jnp.float32)
    for h in range(horizon):
        s = field[h * n : (h + 1) * n, :]
        s_out[h] = s
        r = r_ref[h]
        x_out[h] = x_ref[h] + alpha * r
        r = r - alpha * s
        r_out[h] = r
        gamma = gamma + r * r
        delta = delta + diag_ref[h] * r * r
        eps = eps + r * s
    sums = cr_ref[...] - wide(alpha) * sums
    cr_out[...] = sums
    store_part(
        r_out, sums, gamma, delta, eps, diag_ref, wcat_ref, cats_ref,
        store_sender(send_ref, n, a_out),
        lambda line: put_rows(send_ref, n, 2 * horizon, line), values,
    )


def third_body(
    a_ref, reg_ref, got_ref, x_ref, r_ref, rs_ref, p_ref, s_ref, ss_ref, cr_ref, cs_ref, scal_ref,
    diag_ref, wcat_ref, wstore_ref, table_ref, group_ref, cats_ref, same_ref,
    x_out, r_out, p_out, s_out, scal_out, a_out, send_ref, values, field, rs_out,
):
    horizon, n, _ = diag_ref.shape
    clear_tail(field, horizon, n)
    for h in range(horizon):
        field[h * n : (h + 1) * n, :] = a_ref[h] + rows_of(got_ref, n, horizon + h)
    sums = category_sums(field, table_ref, group_ref, n, wcat_ref.shape[0])
    gamma, delta, eps = totals(got_ref, n, 2 * horizon)
    beta = gamma / scal_ref[0:1, :]
    curve = delta + 2.0 * beta * eps + beta * beta * scal_ref[1:2, :]
    alpha = gamma / curve
    scal_out[0:1, :] = gamma
    scal_out[1:2, :] = curve
    for h in range(horizon):
        ws = rows_of(got_ref, n, h) + reg_ref[h]
        rs_out[h] = rs_ref[h] - alpha * (ws + beta * ss_ref[h])
    delta = region_part(rs_out, wstore_ref, same_ref, region_sender(send_ref, n, 0, None))
    gamma = jnp.zeros((n, LANES), jnp.float32)
    eps = jnp.zeros((n, LANES), jnp.float32)
    for h in range(horizon):
        s = field[h * n : (h + 1) * n, :] + beta * s_ref[h]
        s_out[h] = s
        r = r_ref[h]
        p = r + beta * p_ref[h]
        p_out[h] = p
        x_out[h] = x_ref[h] + alpha * p
        r = r - alpha * s
        r_out[h] = r
        gamma = gamma + r * r
        delta = delta + diag_ref[h] * r * r
        eps = eps + r * s
    sums = cr_ref[...] - wide(alpha) * (sums + wide(beta) * cs_ref[...])
    store_part(
        r_out, sums, gamma, delta, eps, diag_ref, wcat_ref, cats_ref,
        store_sender(None, n, a_out), lambda line: put_rows(send_ref, n, horizon, line), values,
    )


def last_body(a_ref, got_ref, x_ref, r_ref, p_ref, s_ref, scal_ref, x_out, r_out):
    horizon, n, _ = a_ref.shape
    gamma, delta, eps = totals(got_ref, n, horizon)
    beta = gamma / scal_ref[0:1, :]
    alpha = gamma / (delta + 2.0 * beta * eps + beta * beta * scal_ref[1:2, :])
    for h in range(horizon):
        r = r_ref[h]
        s = a_ref[h] + rows_of(got_ref, n, h) + beta * s_ref[h]
        x_out[h] = x_ref[h] + alpha * (r + beta * p_ref[h])
        r_out[h] = r - alpha * s


def on_device(
    base_bottom,
    weight_bottom,
    base_category,
    weight_category,
    base_region,
    weight_region,
    category_map,
    region_map,
):
    stores, horizon, skus = base_bottom.shape
    n = region_map.shape[0]
    groups = weight_category.shape[2] // WIDE
    tiles = weight_category.shape[2] // LANES
    field = (horizon, n, LANES)
    padded = (PAD * n, LANES)
    by_category = (horizon, tiles, LANES)
    scal = (2, LANES)
    values = pltpu.VMEM((groups * PAD, WIDE), jnp.float32)

    x = base_bottom.reshape(field)
    diag = weight_bottom.reshape(field)
    (sent,) = call(
        pack_body,
        [(n * horizon, LANES)],
        [pltpu.VMEM(field, jnp.float32), pltpu.SemaphoreType.DMA],
        (x,),
        [HBM],
        True,
    )
    got = exchange(sent, n)
    arguments = (
        x,
        base_category.reshape(by_category),
        weight_category.reshape(by_category),
        jnp.transpose(base_region, (1, 0, 2)),
        jnp.transpose(weight_region, (1, 0, 2)),
        category_map.reshape(n, LANES),
        region_map.reshape(1, n),
    )
    held = [pltpu.VMEM(arguments[i].shape, arguments[i].dtype) for i in (0, 1, 2, 3, 4, 6)]
    spread, wcat, wstore, bstore, same, table, group, cats = call(
        prepare_body,
        [
            field,
            (groups * PAD, WIDE),
            field,
            field,
            jax.ShapeDtypeStruct((n, n), jnp.bfloat16),
            jax.ShapeDtypeStruct((skus, WIDE), jnp.bfloat16),
            jax.ShapeDtypeStruct((PAD, skus), jnp.bfloat16),
            jax.ShapeDtypeStruct((n, LANES), jnp.int32),
        ],
        [
            pltpu.VMEM(padded, jnp.float32),
            values,
            *held,
            pltpu.SemaphoreType.DMA((len(arguments),)),
        ],
        arguments,
        [HBM] * len(arguments),
    )
    reg, sent = call(
        region_start_body,
        [field, (n * 2 * horizon, LANES)],
        [],
        (got, spread, wstore, bstore, same),
    )
    got = exchange(sent, n)
    fixed = (diag, wcat, wstore, table, group, cats, same)
    both = (n * (2 * horizon + 1), LANES)
    work = [values, pltpu.VMEM(padded, jnp.float32)]
    sums = (groups * PAD, WIDE)
    r, rs, cr, a, reg, sent = call(
        first_body, [field, field, sums, field, field, both], work, (spread, reg, got) + fixed
    )
    got = exchange(sent, n)
    p = r
    x, r, rs, s, ss, cr, cs, scalars, a, reg, sent = call(
        second_body,
        [field, field, field, field, field, sums, sums, scal, field, field, both],
        work,
        (a, reg, got, x, r, rs, cr) + fixed,
    )
    got = exchange(sent, n)
    x, r, p, s, scalars, a, sent = call(
        third_body,
        [field, field, field, field, scal, field, (n * (horizon + 1), LANES)],
        work + [pltpu.VMEM(field, jnp.float32)],
        (a, reg, got, x, r, rs, p, s, ss, cr, cs, scalars) + fixed,
    )
    got = exchange(sent, n)
    x, r = call(last_body, [field, field], [], (a, got, x, r, p, s, scalars))
    return x.reshape(base_bottom.shape), r.reshape(base_bottom.shape)


def week_rows(tiles, n, regions):
    sizes = (n, n, tiles, tiles, regions, regions)
    return [sum(sizes[:i]) for i in range(len(sizes) + 1)]


def week_pack_body(*refs):
    sources, out, sems = refs[:-2], refs[-2], refs[-1]
    horizon = sources[0].shape[0]
    copies, start = [], 0
    for i, source in enumerate(sources):
        rows = source.shape[1]
        target = out.at[pl.ds(0, horizon), pl.ds(start, rows)]
        copies.append(pltpu.make_async_copy(source, target, sems.at[i]))
        start += rows
    for copy in copies:
        copy.start()
    for copy in copies:
        copy.wait()


def week_table_body(
    map_ref, cats_ref, table_out, flipped_out, group_out, same_out, region_out, regions
):
    n = cats_ref.shape[0]
    lane = lax.broadcasted_iota(jnp.int32, (n, LANES), 1)
    line = lax.broadcasted_iota(jnp.int32, (n, LANES), 0)
    across = jnp.zeros((n, LANES), jnp.int32)
    down = jnp.zeros((n, LANES), jnp.int32)
    for s in range(n):
        across = jnp.where(lane % n == s, map_ref[s], across)
        down = jnp.where(line == s, map_ref[s], down)
    same_out[...] = jnp.where(across == down, 1.0, 0.0).astype(jnp.bfloat16)
    region_out[...] = jnp.where(lane % regions == down, 1.0, 0.0).astype(jnp.bfloat16)
    square = jnp.concatenate([cats_ref[...].astype(jnp.float32)] * (LANES // min(n, LANES)), axis=0)
    labels = lax.broadcasted_iota(jnp.int32, (LANES, WIDE), 1)
    downward = lax.broadcasted_iota(jnp.int32, (WIDE, LANES), 0)
    columns = [
        jnp.transpose(square[i : i + LANES]).astype(jnp.int32) & (WIDE - 1)
        for i in range(0, square.shape[0], LANES)
    ]
    for j in range(n):
        column = jnp.broadcast_to(columns[j // LANES][:, j % LANES : j % LANES + 1], (LANES, WIDE))
        table_out[j * LANES : (j + 1) * LANES, :] = jnp.where(
            column == labels, 1.0, 0.0
        ).astype(jnp.bfloat16)
        flipped_out[:, j * LANES : (j + 1) * LANES] = jnp.where(
            (cats_ref[j : j + 1, :] & (WIDE - 1)) == downward, 1.0, 0.0
        ).astype(jnp.bfloat16)
        group = cats_ref[j : j + 1, :] >> (WIDE.bit_length() - 1)
        group = jnp.broadcast_to(group, (group_out.shape[0], LANES))
        group_out[:, j * LANES : (j + 1) * LANES] = group.astype(jnp.float32).astype(jnp.bfloat16)


def ratio(top, bottom):
    return jnp.where(bottom > 0.0, top / bottom, 0.0)


def whole_sum(part):
    total = jnp.sum(jnp.sum(part, axis=0, keepdims=True), axis=1, keepdims=True)
    return jnp.broadcast_to(total, (1, LANES))


def week_body(
    core_ref, place_ref, own_ref, other_ref, table_ref, flipped_ref, group_ref, same_ref, region_ref,
    cats_ref, kept_out, line_out,
    base, basis, diag, wstore, bstore, wcat, bcat, raw_weight, raw_base, held,
    side,
):
    core = core_ref[0]
    n, skus = base.shape
    per = own_ref.shape[0] // line_out.shape[0]
    regions = raw_weight.shape[0]
    tiles = wcat.shape[0] // n * (WIDE // LANES)
    starts = week_rows(tiles, n, regions)
    chunk = skus
    chunks = [slice(c, c + chunk) for c in range(0, skus, chunk)]
    for ref, c in ((own_ref, core), (other_ref, 1 - core)):
        for x in range(n // (CORES * side)):
            for t in range(0, side, 8):
                first = (x * side + t) * per
                top = pl.multiple_of(x * CORES * side + c * side + t, 8)

                def rows(row):
                    return ref[pl.ds(first + row, 8, stride=per), :]

                for j in range(n):
                    lanes = slice(j * LANES, (j + 1) * LANES)
                    base[pl.ds(top, 8), lanes] = rows(starts[0] + j)
                    diag[pl.ds(top, 8), lanes] = rows(starts[1] + j)
                for g in range(tiles):
                    lane = g * LANES % WIDE
                    down = pl.multiple_of(g * LANES // WIDE * n + top, 8)
                    wcat[pl.ds(down, 8), lane : lane + LANES] = rows(starts[2] + g)
                    bcat[pl.ds(down, 8), lane : lane + LANES] = rows(starts[3] + g)
            for k in range(side):
                first = (x * side + k) * per
                j = x * CORES * side + c * side + k
                lanes = pl.ds(pl.multiple_of(j * LANES, LANES), LANES)
                raw_base[:, lanes] = ref[first + starts[4] : first + starts[5], :]
                raw_weight[:, lanes] = ref[first + starts[5] : first + starts[6], :]

    region_table = region_ref[:, : 3 * regions]
    same = same_ref[:, : 2 * n]
    for source, target in ((raw_weight, wstore), (raw_base, bstore)):
        for lanes in chunks:
            parts = jnp.concatenate(split_all(source[:, lanes]), axis=0)
            target[:, lanes] = product(region_table, parts, ((1,), (0,)))

    def by_category(field):
        rows = wcat.shape[0]
        group = group_ref[...]
        masks = [group == g for g in range(rows // n)]
        none = jnp.zeros(group.shape, jnp.bfloat16)
        spread = jnp.concatenate(
            [jnp.where(mask, part, none) for part in split(field[...]) for mask in masks], axis=0
        )
        total = product(spread, table_ref[...], ((1,), (0,)))
        return total[:rows] + total[rows:]

    def spread(values, m, put):
        parts = jnp.concatenate(split(values), axis=0)
        groups = values.shape[0] // m
        for lanes in chunks:
            found = product(parts, flipped_ref[:, lanes], ((1,), (0,)))
            for t in range(0, chunk, LANES):
                tile = slice(lanes.start + t, lanes.start + t + LANES)
                members = cats_ref[tile.start // LANES : tile.start // LANES + 1, :]
                group = jnp.broadcast_to(members >> (WIDE.bit_length() - 1), (m, LANES))
                high, low = found[: groups * m, t : t + LANES], found[groups * m :, t : t + LANES]
                one = [
                    high[g * m : (g + 1) * m] + low[g * m : (g + 1) * m] for g in range(groups)
                ]
                bit = 1
                while len(one) > 1:
                    odd = group & bit != 0
                    pairs = [one[i : i + 2] for i in range(0, len(one), 2)]
                    one = [jnp.where(odd, *pair[::-1]) if len(pair) == 2 else pair[0] for pair in pairs]
                    bit *= 2
                put(tile, one[0])

    def by_region(part):
        return product(same, jnp.concatenate(split(part), axis=0), ((1,), (0,)))

    def tiles_in(lanes):
        for t in range(0, chunk, LANES):
            yield slice(lanes.start + t, lanes.start + t + LANES), slice(t, t + LANES)

    zero = jnp.zeros((n, LANES), jnp.float32)
    for lanes in chunks:
        sums = by_region(base[:, lanes])
        for tile, inner in tiles_in(lanes):
            basis[0, :, tile] = wstore[:, tile] * (bstore[:, tile] - sums[:, inner])
    norm = [zero]

    def start(tile, value):
        result = basis[0, :, tile] + value
        basis[0, :, tile] = result
        norm[0] = norm[0] + result * result

    spread(wcat[...] * (bcat[...] - by_category(base)), n, start)
    norms, quotients = [whole_sum(norm[0])], []
    for k in range(3):
        field, image = basis.at[k], basis.at[k + 1]
        sums = by_category(field)
        values = wcat[...] * sums
        square = values * sums
        dot = zero
        for lane in range(0, WIDE, LANES):
            for g in range(0, square.shape[0], n):
                dot = dot + square[g : g + n, lane : lane + LANES]
        for lanes in chunks:
            sums = by_region(field[:, lanes])
            for tile, inner in tiles_in(lanes):
                part = field[:, tile]
                result = diag[:, tile] * part + wstore[:, tile] * sums[:, inner]
                image[:, tile] = result
                dot = dot + part * result
        quotients.append(ratio(whole_sum(dot), norms[k]))
        back = ratio(norms[k], norms[k - 1]) if k else None
        if k == 2:
            break
        norm = [zero]

        def step(tile, value):
            result = image[:, tile] + value - quotients[k] * field[:, tile]
            if k:
                result = result - back * basis[k - 1, :, tile]
            image[:, tile] = result
            norm[0] = norm[0] + result * result

        spread(values, n, step)
        norms.append(whole_sum(norm[0]))

    lane = lax.broadcasted_iota(jnp.int32, line_out.shape, 1)
    place = lax.broadcasted_iota(jnp.int32, line_out.shape, 0)
    line = jnp.where((lane == 6) & (place == place_ref[0]), 1.0, 0.0)
    for i, value in enumerate(norms + quotients):
        line = jnp.where(lane == i, jnp.broadcast_to(value, line.shape), line)
    line_out[...] = line

    held[...] = values
    weeks = line_out.shape[0]
    tops = [
        pl.multiple_of(x * CORES * side + core * side + t, 8)
        for x in range(n // (CORES * side))
        for t in range(0, side, 8)
    ]
    for i, top in enumerate(tops):
        kept_out[4, i * 8 : i * 8 + 8, :] = base[pl.ds(top, 8), :]
        for k in range(4):
            kept_out[k, i * 8 : i * 8 + 8, :] = basis[k, pl.ds(top, 8), :]
    mine = jnp.concatenate(
        [held[pl.ds(g + top, 8), :] for g in range(0, held.shape[0], n) for top in tops], axis=0
    )

    def finish(tile, value):
        result = kept_out[3, :, tile] + value - quotients[2] * kept_out[2, :, tile]
        kept_out[3, :, tile] = result - back * kept_out[1, :, tile]

    spread(mine, weeks, finish)


def week_combine_body(lines_ref, kept_ref, send_ref, horizon):
    weeks = lines_ref.shape[0]
    n = kept_ref.shape[2] // LANES
    week = lax.broadcasted_iota(jnp.int32, (weeks, LANES), 0)
    lines = jnp.where(week < horizon, lines_ref[...], 0.0)
    n1, n2, n3, a1, a2, a3, mark = [
        jnp.take_along_axis(lines, jnp.full((weeks, LANES), i, jnp.int32), axis=1) for i in range(7)
    ]
    e2, e3 = ratio(n2, n1), ratio(n3, n2)

    def dot(left, right):
        terms = n1 * left[0] * right[0] + n2 * left[1] * right[1] + n3 * left[2] * right[2]
        return jnp.sum(terms, axis=0, keepdims=True)

    zero = jnp.zeros((weeks, LANES), jnp.float32)
    x = [zero, zero, zero]
    r = [zero + 1.0, zero, zero, zero]
    p = r[:3]
    rr = dot(r, r)
    for k in range(3):
        image = [
            a1 * p[0] + e2 * p[1],
            p[0] + a2 * p[1] + e3 * p[2],
            p[1] + a3 * p[2],
            p[2],
        ]
        alpha = rr / dot(p, image)
        x = [left + alpha * right for left, right in zip(x, p)]
        r = [left - alpha * right for left, right in zip(r, image)]
        if k < 2:
            new = dot(r, r)
            p = [left + new / rr * right for left, right in zip(r[:3], p)]
            rr = new
    mine = mark > 0.0
    x = [jnp.sum(jnp.where(mine, value, 0.0), axis=0, keepdims=True) for value in x]
    r = [jnp.sum(jnp.where(mine, value, 0.0), axis=0, keepdims=True) for value in r]
    rows = send_ref.shape[0] // weeks
    for t in range(0, weeks, 8):
        for j in range(n):
            lanes = slice(j * LANES, (j + 1) * LANES)
            parts = [kept_ref[k, t : t + 8, lanes] for k in range(4)]
            left = kept_ref[4, t : t + 8, lanes]
            right = r[3] * parts[3]
            for k in range(3):
                left = left + x[k] * parts[k]
                right = right + r[k] * parts[k]
            first = t * rows + j
            send_ref[pl.ds(first, 8, stride=rows), :] = left
            send_ref[pl.ds(first + n, 8, stride=rows), :] = right


def week_last_body(got_ref, x_out, r_out, sems):
    horizon, n, _ = x_out.shape
    copies = [
        pltpu.make_async_copy(
            got_ref.at[pl.ds(0, horizon), pl.ds(i * n, n)], target, sems.at[i]
        )
        for i, target in enumerate((x_out, r_out))
    ]
    for copy in copies:
        copy.start()
    for copy in copies:
        copy.wait()


def exchange_weeks(blocks):
    return lax.all_to_all(blocks, ("x", "sku"), split_axis=0, concat_axis=0, tiled=True)


def by_weeks(
    base_bottom,
    weight_bottom,
    base_category,
    weight_category,
    base_region,
    weight_region,
    category_map,
    region_map,
):
    stores, horizon, skus = base_bottom.shape
    n = region_map.shape[0]
    regions = weight_region.shape[0]
    tiles = weight_category.shape[2] // LANES
    groups = weight_category.shape[2] // WIDE
    side = lax.axis_size("sku")
    weeks = lax.axis_size("x") * side
    place = lax.axis_index("x") * side + lax.axis_index("sku")
    place = place.astype(jnp.int32).reshape(1)
    core = lax.axis_index("core").astype(jnp.int32).reshape(1)
    cats = category_map.reshape(n, LANES)
    sources = (
        base_bottom.reshape(horizon, n, LANES),
        weight_bottom.reshape(horizon, n, LANES),
        weight_category.reshape(horizon, tiles, LANES),
        base_category.reshape(horizon, tiles, LANES),
        jnp.transpose(base_region, (1, 0, 2)),
        jnp.transpose(weight_region, (1, 0, 2)),
    )
    per = week_rows(tiles, n, regions)[-1]
    (sent,) = call(
        week_pack_body,
        [(weeks, per, LANES)],
        [pltpu.SemaphoreType.DMA((len(sources),))],
        sources,
        [HBM] * len(sources),
        out_specs=(HBM,),
    )
    own = exchange_weeks(sent)
    other = lax.ppermute(own, "core", [(0, 1), (1, 0)])
    table, flipped, group, same, region = call(
        lambda *refs: week_table_body(*refs, regions),
        [
            jax.ShapeDtypeStruct((skus, WIDE), jnp.bfloat16),
            jax.ShapeDtypeStruct((WIDE, skus), jnp.bfloat16),
            jax.ShapeDtypeStruct((n, skus), jnp.bfloat16),
            jax.ShapeDtypeStruct((n, LANES), jnp.bfloat16),
            jax.ShapeDtypeStruct((n, LANES), jnp.bfloat16),
        ],
        [],
        (region_map, cats),
        [SMEM, VMEM],
    )
    full = pltpu.VMEM((n, skus), jnp.float32)
    raw = pltpu.VMEM((regions, skus), jnp.float32)
    cat = pltpu.VMEM((groups * n, WIDE), jnp.float32)
    kept, line = call(
        lambda *refs: week_body(*refs, side),
        [(5, weeks, skus), (weeks, LANES)],
        [
            full, pltpu.VMEM((4, n, skus), jnp.float32),
            full, full, full, cat, cat, raw, raw, cat,
        ],
        (
            core, place, own.reshape(-1, LANES), other.reshape(-1, LANES),
            table, flipped, group, same, region, cats,
        ),
        [SMEM, SMEM, VMEM, FREE] + [VMEM] * 6,
    )
    lines = exchange_weeks(line.reshape(weeks, 1, LANES)).reshape(weeks, LANES)
    (sent,) = call(
        lambda *refs: week_combine_body(*refs, horizon),
        [(weeks * 2 * n, LANES)],
        [],
        (lines, kept),
        [VMEM] * 2,
    )
    got = exchange_weeks(sent.reshape(weeks, 2 * n, LANES))
    x, r = call(
        week_last_body,
        [(horizon, n, LANES)] * 2,
        [pltpu.SemaphoreType.DMA((2,))],
        (got,),
        [VMEM],
        out_specs=(HBM, HBM),
    )
    return x.reshape(base_bottom.shape), r.reshape(base_bottom.shape)


def solution(mesh):
    def mapped(device_mesh, body, stores):
        split_stores = P(stores, None, None)
        split_skus = P(None, None, stores)
        return jax.shard_map(
            body,
            mesh=device_mesh,
            in_specs=(split_stores,) * 4 + (split_skus,) * 2 + (P(), P()),
            out_specs=(split_stores,) * 2,
            check_vma=False,
        )

    side = mesh.shape["sku"]
    chips = mesh.devices.reshape(-1, CORES, side)

    def program(base_bottom, *others):
        stores, horizon, skus = base_bottom.shape
        fits = 16 * stores * skus * 4 <= 16 << 20
        fits = fits and 3 * others[3].shape[0] <= LANES and LANES % stores == 0
        if fits and horizon <= chips.shape[0] * side and side % 8 == 0:
            device_mesh = Mesh(chips, ("x", "core", "sku"))
            return mapped(device_mesh, by_weeks, ("x", "core", "sku"))(base_bottom, *others)
        return mapped(mesh, on_device, ("store", "sku"))(base_bottom, *others)

    return program
```

```python
import jax
import jax.numpy as jnp
from jax import lax
from jax.experimental import pallas as pl
from jax.experimental.pallas import tpu as pltpu
from jax.sharding import Mesh
from jax.sharding import PartitionSpec as P

LANES = 128
PAD = 16
WIDE = 256
VMEM = pl.BlockSpec(memory_space=pltpu.VMEM)
HBM = pl.BlockSpec(memory_space=pltpu.HBM)
SMEM = pl.BlockSpec(memory_space=pltpu.SMEM)
FREE = pl.BlockSpec(memory_space=pltpu.VMEM)
CORES = 2
CUTS = 4


def exchange(blocks, n):
    moved = lax.all_to_all(
        blocks.reshape(n, 1, -1), ("store", "sku"), split_axis=0, concat_axis=0, tiled=True
    )
    return moved.reshape(blocks.shape)


def call(body, outs, scratch, args, specs=None, held=False, out_specs=None):
    outs = [
        out if isinstance(out, jax.ShapeDtypeStruct) else jax.ShapeDtypeStruct(out, jnp.float32)
        for out in outs
    ]
    specs = specs or [VMEM] * len(args)
    args = [
        arg if spec is SMEM or spec is FREE else pltpu.with_memory_space_constraint(arg, spec.memory_space)
        for arg, spec in zip(args, specs)
    ]
    return pl.pallas_call(
        body,
        out_shape=tuple(pltpu.VMEM(out.shape, out.dtype) if held else out for out in outs),
        in_specs=specs,
        out_specs=out_specs or tuple(VMEM for _ in outs),
        scratch_shapes=scratch,
        compiler_params=pltpu.CompilerParams(vmem_limit_bytes=24 << 20),
    )(*args)


def split(value):
    high = value.astype(jnp.bfloat16)
    return high, (value - high.astype(jnp.float32)).astype(jnp.bfloat16)


def split_all(value):
    high, low = split(value)
    rest = value - high.astype(jnp.float32) - low.astype(jnp.float32)
    return high, low, rest.astype(jnp.bfloat16)


def product(left, right, contract):
    return lax.dot_general(left, right, (contract, ((), ())), preferred_element_type=jnp.float32)


def rows_of(ref, n, h):
    return ref[pl.ds(h, n, stride=ref.shape[0] // n), :]


def put_rows(ref, n, h, value):
    ref[pl.ds(h, n, stride=ref.shape[0] // n), :] = value


def category_sums(field, table_ref, group_ref, n, rows):
    width = 4 if n % 4 == 0 else 1
    lanes = width * LANES

    def step(c, total):
        pieces = [field[pl.ds(c * width + i, PAD, stride=n), :] for i in range(width)]
        parts = split_all(jnp.concatenate(pieces, axis=1))
        start = pl.multiple_of(c * lanes, lanes)
        group = group_ref[:, pl.ds(start, lanes)]
        masks = [group == g for g in range(rows // PAD)]
        none = jnp.zeros((PAD, lanes), jnp.bfloat16)
        spread = jnp.concatenate(
            [jnp.where(mask, part, none) for part in parts for mask in masks], axis=0
        )
        return total + product(spread, table_ref[pl.ds(start, lanes), :], ((1,), (0,)))

    steps = n // width
    total = lax.fori_loop(
        0, steps, step, jnp.zeros((3 * rows, WIDE), jnp.float32), unroll=min(steps, 8)
    )
    return total[:rows] + (total[rows : 2 * rows] + total[2 * rows :])


def category_spread(values, cats, horizon, put):
    place = cats & (LANES - 1)
    group = cats >> (LANES.bit_length() - 1)
    for h in range(horizon):
        found = []
        for g in range(0, values.shape[0], PAD):
            for lane in range(0, WIDE, LANES):
                row = jnp.broadcast_to(values[g + h : g + h + 1, lane : lane + LANES], cats.shape)
                found.append(jnp.take_along_axis(row, place, axis=1))
        for bit in range((len(found) - 1).bit_length()):
            mask = group & (1 << bit) != 0
            pairs = [found[i : i + 2] for i in range(0, len(found), 2)]
            found = [jnp.where(mask, pair[1], pair[0]) if len(pair) == 2 else pair[0] for pair in pairs]
        put(h, found[0])


def tiles_of(n):
    return [slice(t, t + 8) for t in range(0, n, 8)]


def put_tile(ref, n, h, tile, value):
    rows = ref.shape[0] // n
    ref[pl.ds(tile.start * rows + h, 8, stride=rows), :] = value


def region_sums(load, same, n, horizon):
    high, low = split(jnp.concatenate([load(h) for h in range(horizon)], axis=1))
    total = product(same, high, ((1,), (0,))) + product(same, low, ((1,), (0,)))
    return [total[:, h * LANES : (h + 1) * LANES] for h in range(horizon)]


def pack_body(base_hbm, out_ref, base_ref, sem):
    copy = pltpu.make_async_copy(base_hbm, base_ref, sem)
    copy.start()
    copy.wait()
    n = base_ref.shape[1]
    for h in range(base_ref.shape[0]):
        put_rows(out_ref, n, h, base_ref[h])


def prepare_body(
    base_hbm, base_cat_hbm, weight_cat_hbm, base_reg_hbm, weight_reg_hbm, cats_hbm, map_hbm,
    spread_out, wcat_out, wstore_out, bstore_out, same_out, table_out, group_out,
    cats_ref,
    field, values, base_ref, base_cat_ref, weight_cat_ref, base_reg_ref, weight_reg_ref, map_ref, sems,
):
    copies = [
        pltpu.make_async_copy(source, target, sems.at[i])
        for i, (source, target) in enumerate(
            (
                (cats_hbm, cats_ref),
                (base_hbm, base_ref),
                (weight_cat_hbm, weight_cat_ref),
                (base_cat_hbm, base_cat_ref),
                (map_hbm, map_ref),
                (weight_reg_hbm, weight_reg_ref),
                (base_reg_hbm, base_reg_ref),
            )
        )
    ]
    for copy in copies:
        copy.start()
    for copy in copies:
        copy.wait()
    horizon, n, _ = base_ref.shape
    n_regions = weight_reg_ref.shape[1]
    square = jnp.concatenate([cats_ref[...].astype(jnp.float32)] * (LANES // min(n, LANES)), axis=0)
    labels = lax.broadcasted_iota(jnp.int32, (LANES, WIDE), 1)
    columns = [
        jnp.transpose(square[i : i + LANES]).astype(jnp.int32) % WIDE
        for i in range(0, square.shape[0], LANES)
    ]
    for j in range(n):
        column = jnp.broadcast_to(columns[j // LANES][:, j % LANES : j % LANES + 1], (LANES, WIDE))
        table_out[j * LANES : (j + 1) * LANES, :] = jnp.where(
            column == labels, 1.0, 0.0
        ).astype(jnp.bfloat16)
        group = jnp.broadcast_to(cats_ref[j : j + 1, :] // WIDE, (PAD, LANES))
        group_out[:, j * LANES : (j + 1) * LANES] = group.astype(jnp.float32).astype(jnp.bfloat16)

    field[...] = jnp.zeros_like(field)
    for h in range(horizon):
        field[h * n : (h + 1) * n, :] = base_ref[h]
    sums = category_sums(field, table_out, group_out, n, wcat_out.shape[0])
    wcat_out[...] = jnp.zeros_like(wcat_out)
    values[...] = jnp.zeros_like(values)
    for g in range(0, wcat_out.shape[0], PAD):
        for lane in range(0, WIDE, LANES):
            tile = (g // PAD * WIDE + lane) // LANES
            lanes = slice(lane, lane + LANES)
            weight = weight_cat_ref[:, tile, :]
            wcat_out[g : g + horizon, lanes] = weight
            values[g : g + horizon, lanes] = weight * (
                base_cat_ref[:, tile, :] - sums[g : g + horizon, lanes]
            )
    for tile in tiles_of(n):

        def put(h, value):
            spread_out[h, tile, :] = value

        category_spread(values, cats_ref[tile, :], horizon, put)

    labels = lax.broadcasted_iota(jnp.int32, (n_regions, n), 0)
    table = jnp.where(labels == map_ref[...], 1.0, 0.0).astype(jnp.bfloat16)
    same_out[...] = product(table, table, ((0,), (0,))).astype(jnp.bfloat16)
    for source, target in ((weight_reg_ref, wstore_out), (base_reg_ref, bstore_out)):
        for h in range(horizon):
            high, low = split(source[h])
            rest = source[h] - high.astype(jnp.float32) - low.astype(jnp.float32)
            target[h] = (
                product(table, high, ((0,), (0,)))
                + product(table, low, ((0,), (0,)))
                + product(table, rest.astype(jnp.bfloat16), ((0,), (0,)))
            )


def region_start_body(got_ref, spread_ref, wstore_ref, bstore_ref, same_ref, reg_out, send_ref):
    horizon, n, _ = spread_ref.shape
    sums = region_sums(lambda h: rows_of(got_ref, n, h), same_ref[...], n, horizon)
    for h in range(horizon):
        put_rows(send_ref, n, h, spread_ref[h])
        part = wstore_ref[h] * (bstore_ref[h] - sums[h])
        reg_out[h] = part
        put_rows(send_ref, n, horizon + h, part)


def region_part(rs, wstore_ref, same_ref, put):
    horizon, n, _ = wstore_ref.shape
    sums = region_sums(lambda h: rs[h], same_ref[...], n, horizon)
    share = jnp.zeros((n, LANES), jnp.float32)
    for h in range(horizon):
        part = wstore_ref[h] * sums[h]
        share = share + part * rs[h]
        put(h, part)
    return share


def store_part(r_ref, sums, gamma, delta, eps, diag_ref, wcat_ref, cats_ref, put, put_line, values):
    horizon, n, _ = diag_ref.shape
    scaled = wcat_ref[...] * sums
    values[...] = scaled
    square = scaled * sums
    delta = jnp.sum(delta, axis=0, keepdims=True)
    for lane in range(0, WIDE, LANES):
        delta = delta + jnp.sum(square[:, lane : lane + LANES], axis=0, keepdims=True)
    lane = lax.broadcasted_iota(jnp.int32, (1, LANES), 1)
    line = jnp.zeros((1, LANES), jnp.float32)
    for i, part in enumerate((gamma, delta, eps)):
        if part is not None:
            whole = jnp.sum(jnp.sum(part, axis=0, keepdims=True), axis=1, keepdims=True)
            line = jnp.where(lane == i, whole, line)
    put_line(jnp.broadcast_to(line, (n, LANES)))
    for tile in tiles_of(n):

        def finish(h, value):
            put(h, tile, value + diag_ref[h, tile, :] * r_ref[h, tile, :])

        category_spread(values, cats_ref[tile, :], horizon, finish)


def totals(got_ref, n, row):
    total = jnp.sum(rows_of(got_ref, n, row), axis=0, keepdims=True)
    total = jnp.broadcast_to(total, (8, LANES))
    return [
        jnp.take_along_axis(total, jnp.full((8, LANES), i, jnp.int32), axis=1)[0:1] for i in range(3)
    ]


def wide(line):
    return jnp.concatenate([line] * (WIDE // LANES), axis=1)


def region_sender(ref, n, first, keep):
    def put(h, value):
        if keep is not None:
            keep[h] = value
        put_rows(ref, n, first + h, value)

    return put


def store_sender(ref, n, keep):
    def put(h, tile, value):
        keep[h, tile, :] = value
        if ref is not None:
            put_tile(ref, n, h, tile, value)

    return put


def clear_tail(field, horizon, n):
    field[horizon * n :, :] = jnp.zeros((field.shape[0] - horizon * n, LANES), jnp.float32)


def first_body(
    a_ref, reg_ref, got_ref, diag_ref, wcat_ref, wstore_ref, table_ref, group_ref, cats_ref, same_ref,
    r_out, rs_out, cr_out, a_out, reg_out, send_ref, values, field,
):
    horizon, n, _ = diag_ref.shape
    clear_tail(field, horizon, n)
    gamma = jnp.zeros((n, LANES), jnp.float32)
    delta = jnp.zeros((n, LANES), jnp.float32)
    for h in range(horizon):
        r = a_ref[h] + rows_of(got_ref, n, horizon + h)
        r_out[h] = r
        field[h * n : (h + 1) * n, :] = r
        gamma = gamma + r * r
        delta = delta + diag_ref[h] * r * r
    sums = category_sums(field, table_ref, group_ref, n, wcat_ref.shape[0])
    cr_out[...] = sums
    for h in range(horizon):
        rs_out[h] = rows_of(got_ref, n, h) + reg_ref[h]
    delta = delta + region_part(
        rs_out, wstore_ref, same_ref, region_sender(send_ref, n, horizon, reg_out)
    )
    store_part(
        r_out, sums, gamma, delta, None, diag_ref, wcat_ref, cats_ref,
        store_sender(send_ref, n, a_out),
        lambda line: put_rows(send_ref, n, 2 * horizon, line), values,
    )


def second_body(
    a_ref, reg_ref, got_ref, x_ref, r_ref, rs_ref, cr_ref,
    diag_ref, wcat_ref, wstore_ref, table_ref, group_ref, cats_ref, same_ref,
    x_out, r_out, rs_out, s_out, ss_out, cr_out, cs_out, scal_ref, a_out, reg_out, send_ref,
    values, field,
):
    horizon, n, _ = diag_ref.shape
    clear_tail(field, horizon, n)
    for h in range(horizon):
        field[h * n : (h + 1) * n, :] = a_ref[h] + rows_of(got_ref, n, horizon + h)
    sums = category_sums(field, table_ref, group_ref, n, wcat_ref.shape[0])
    cs_out[...] = sums
    gamma, delta, _ = totals(got_ref, n, 2 * horizon)
    alpha = gamma / delta
    scal_ref[0:1, :] = gamma
    scal_ref[1:2, :] = delta
    for h in range(horizon):
        ws = rows_of(got_ref, n, h) + reg_ref[h]
        ss_out[h] = ws
        rs_out[h] = rs_ref[h] - alpha * ws
    delta = region_part(
        rs_out, wstore_ref, same_ref, region_sender(send_ref, n, horizon, reg_out)
    )
    gamma = jnp.zeros((n, LANES), jnp.float32)
    eps = jnp.zeros((n, LANES), jnp.float32)
    for h in range(horizon):
        s = field[h * n : (h + 1) * n, :]
        s_out[h] = s
        r = r_ref[h]
        x_out[h] = x_ref[h] + alpha * r
        r = r - alpha * s
        r_out[h] = r
        gamma = gamma + r * r
        delta = delta + diag_ref[h] * r * r
        eps = eps + r * s
    sums = cr_ref[...] - wide(alpha) * sums
    cr_out[...] = sums
    store_part(
        r_out, sums, gamma, delta, eps, diag_ref, wcat_ref, cats_ref,
        store_sender(send_ref, n, a_out),
        lambda line: put_rows(send_ref, n, 2 * horizon, line), values,
    )


def third_body(
    a_ref, reg_ref, got_ref, x_ref, r_ref, rs_ref, p_ref, s_ref, ss_ref, cr_ref, cs_ref, scal_ref,
    diag_ref, wcat_ref, wstore_ref, table_ref, group_ref, cats_ref, same_ref,
    x_out, r_out, p_out, s_out, scal_out, a_out, send_ref, values, field, rs_out,
):
    horizon, n, _ = diag_ref.shape
    clear_tail(field, horizon, n)
    for h in range(horizon):
        field[h * n : (h + 1) * n, :] = a_ref[h] + rows_of(got_ref, n, horizon + h)
    sums = category_sums(field, table_ref, group_ref, n, wcat_ref.shape[0])
    gamma, delta, eps = totals(got_ref, n, 2 * horizon)
    beta = gamma / scal_ref[0:1, :]
    curve = delta + 2.0 * beta * eps + beta * beta * scal_ref[1:2, :]
    alpha = gamma / curve
    scal_out[0:1, :] = gamma
    scal_out[1:2, :] = curve
    for h in range(horizon):
        ws = rows_of(got_ref, n, h) + reg_ref[h]
        rs_out[h] = rs_ref[h] - alpha * (ws + beta * ss_ref[h])
    delta = region_part(rs_out, wstore_ref, same_ref, region_sender(send_ref, n, 0, None))
    gamma = jnp.zeros((n, LANES), jnp.float32)
    eps = jnp.zeros((n, LANES), jnp.float32)
    for h in range(horizon):
        s = field[h * n : (h + 1) * n, :] + beta * s_ref[h]
        s_out[h] = s
        r = r_ref[h]
        p = r + beta * p_ref[h]
        p_out[h] = p
        x_out[h] = x_ref[h] + alpha * p
        r = r - alpha * s
        r_out[h] = r
        gamma = gamma + r * r
        delta = delta + diag_ref[h] * r * r
        eps = eps + r * s
    sums = cr_ref[...] - wide(alpha) * (sums + wide(beta) * cs_ref[...])
    store_part(
        r_out, sums, gamma, delta, eps, diag_ref, wcat_ref, cats_ref,
        store_sender(None, n, a_out), lambda line: put_rows(send_ref, n, horizon, line), values,
    )


def last_body(a_ref, got_ref, x_ref, r_ref, p_ref, s_ref, scal_ref, x_out, r_out):
    horizon, n, _ = a_ref.shape
    gamma, delta, eps = totals(got_ref, n, horizon)
    beta = gamma / scal_ref[0:1, :]
    alpha = gamma / (delta + 2.0 * beta * eps + beta * beta * scal_ref[1:2, :])
    for h in range(horizon):
        r = r_ref[h]
        s = a_ref[h] + rows_of(got_ref, n, h) + beta * s_ref[h]
        x_out[h] = x_ref[h] + alpha * (r + beta * p_ref[h])
        r_out[h] = r - alpha * s


def on_device(
    base_bottom,
    weight_bottom,
    base_category,
    weight_category,
    base_region,
    weight_region,
    category_map,
    region_map,
):
    stores, horizon, skus = base_bottom.shape
    n = region_map.shape[0]
    groups = weight_category.shape[2] // WIDE
    tiles = weight_category.shape[2] // LANES
    field = (horizon, n, LANES)
    padded = (PAD * n, LANES)
    by_category = (horizon, tiles, LANES)
    scal = (2, LANES)
    values = pltpu.VMEM((groups * PAD, WIDE), jnp.float32)

    x = base_bottom.reshape(field)
    diag = weight_bottom.reshape(field)
    (sent,) = call(
        pack_body,
        [(n * horizon, LANES)],
        [pltpu.VMEM(field, jnp.float32), pltpu.SemaphoreType.DMA],
        (x,),
        [HBM],
        True,
    )
    got = exchange(sent, n)
    arguments = (
        x,
        base_category.reshape(by_category),
        weight_category.reshape(by_category),
        jnp.transpose(base_region, (1, 0, 2)),
        jnp.transpose(weight_region, (1, 0, 2)),
        category_map.reshape(n, LANES),
        region_map.reshape(1, n),
    )
    held = [pltpu.VMEM(arguments[i].shape, arguments[i].dtype) for i in (0, 1, 2, 3, 4, 6)]
    spread, wcat, wstore, bstore, same, table, group, cats = call(
        prepare_body,
        [
            field,
            (groups * PAD, WIDE),
            field,
            field,
            jax.ShapeDtypeStruct((n, n), jnp.bfloat16),
            jax.ShapeDtypeStruct((skus, WIDE), jnp.bfloat16),
            jax.ShapeDtypeStruct((PAD, skus), jnp.bfloat16),
            jax.ShapeDtypeStruct((n, LANES), jnp.int32),
        ],
        [
            pltpu.VMEM(padded, jnp.float32),
            values,
            *held,
            pltpu.SemaphoreType.DMA((len(arguments),)),
        ],
        arguments,
        [HBM] * len(arguments),
    )
    reg, sent = call(
        region_start_body,
        [field, (n * 2 * horizon, LANES)],
        [],
        (got, spread, wstore, bstore, same),
    )
    got = exchange(sent, n)
    fixed = (diag, wcat, wstore, table, group, cats, same)
    both = (n * (2 * horizon + 1), LANES)
    work = [values, pltpu.VMEM(padded, jnp.float32)]
    sums = (groups * PAD, WIDE)
    r, rs, cr, a, reg, sent = call(
        first_body, [field, field, sums, field, field, both], work, (spread, reg, got) + fixed
    )
    got = exchange(sent, n)
    p = r
    x, r, rs, s, ss, cr, cs, scalars, a, reg, sent = call(
        second_body,
        [field, field, field, field, field, sums, sums, scal, field, field, both],
        work,
        (a, reg, got, x, r, rs, cr) + fixed,
    )
    got = exchange(sent, n)
    x, r, p, s, scalars, a, sent = call(
        third_body,
        [field, field, field, field, scal, field, (n * (horizon + 1), LANES)],
        work + [pltpu.VMEM(field, jnp.float32)],
        (a, reg, got, x, r, rs, p, s, ss, cr, cs, scalars) + fixed,
    )
    got = exchange(sent, n)
    x, r = call(last_body, [field, field], [], (a, got, x, r, p, s, scalars))
    return x.reshape(base_bottom.shape), r.reshape(base_bottom.shape)


def week_rows(tiles, n, regions):
    sizes = (n, n, tiles, tiles, regions, regions)
    return [sum(sizes[:i]) for i in range(len(sizes) + 1)]


def week_cuts(horizon):
    ends = [horizon * i // CUTS for i in range(CUTS + 1)]
    return [(a, b - a) for a, b in zip(ends, ends[1:]) if b > a]


def week_pack_body(*refs):
    sources, out, sems = refs[:-2], refs[-2], refs[-1]
    horizon = sources[0].shape[0]
    copies, start = [], 0
    for source in sources:
        rows = source.shape[1]
        for first, number in week_cuts(horizon):
            weeks = pl.ds(first, number)
            target = out.at[weeks, pl.ds(start, rows)]
            copies.append(pltpu.make_async_copy(source.at[weeks], target, sems.at[len(copies)]))
        start += rows
    for copy in copies:
        copy.start()
    for copy in copies:
        copy.wait()


def week_table_body(
    map_ref, cats_ref, table_out, flipped_out, group_out, same_out, region_out, regions
):
    n = cats_ref.shape[0]
    lane = lax.broadcasted_iota(jnp.int32, (n, LANES), 1)
    line = lax.broadcasted_iota(jnp.int32, (n, LANES), 0)
    across = jnp.zeros((n, LANES), jnp.int32)
    down = jnp.zeros((n, LANES), jnp.int32)
    for s in range(n):
        across = jnp.where(lane % n == s, map_ref[s], across)
        down = jnp.where(line == s, map_ref[s], down)
    same_out[...] = jnp.where(across == down, 1.0, 0.0).astype(jnp.bfloat16)
    region_out[...] = jnp.where(lane % regions == down, 1.0, 0.0).astype(jnp.bfloat16)
    square = jnp.concatenate([cats_ref[...].astype(jnp.float32)] * (LANES // min(n, LANES)), axis=0)
    labels = lax.broadcasted_iota(jnp.int32, (LANES, WIDE), 1)
    downward = lax.broadcasted_iota(jnp.int32, (WIDE, LANES), 0)
    columns = [
        jnp.transpose(square[i : i + LANES]).astype(jnp.int32) & (WIDE - 1)
        for i in range(0, square.shape[0], LANES)
    ]
    for j in range(n):
        column = jnp.broadcast_to(columns[j // LANES][:, j % LANES : j % LANES + 1], (LANES, WIDE))
        table_out[j * LANES : (j + 1) * LANES, :] = jnp.where(
            column == labels, 1.0, 0.0
        ).astype(jnp.bfloat16)
        flipped_out[:, j * LANES : (j + 1) * LANES] = jnp.where(
            (cats_ref[j : j + 1, :] & (WIDE - 1)) == downward, 1.0, 0.0
        ).astype(jnp.bfloat16)
        group = cats_ref[j : j + 1, :] >> (WIDE.bit_length() - 1)
        group = jnp.broadcast_to(group, (group_out.shape[0], LANES))
        group_out[:, j * LANES : (j + 1) * LANES] = group.astype(jnp.float32).astype(jnp.bfloat16)


def ratio(top, bottom):
    return jnp.where(bottom > 0.0, top / bottom, 0.0)


def whole_sum(part):
    total = jnp.sum(jnp.sum(part, axis=0, keepdims=True), axis=1, keepdims=True)
    return jnp.broadcast_to(total, (1, LANES))


def week_body(
    core_ref, place_ref, own_ref, other_ref, table_ref, flipped_ref, group_ref, same_ref, region_ref,
    cats_ref, kept_out, line_out,
    base, basis, diag, wstore, bstore, wcat, bcat, raw_weight, raw_base, held,
    side,
):
    core = core_ref[0]
    n, skus = base.shape
    per = own_ref.shape[0] // line_out.shape[0]
    regions = raw_weight.shape[0]
    tiles = wcat.shape[0] // n * (WIDE // LANES)
    starts = week_rows(tiles, n, regions)
    chunk = skus
    chunks = [slice(c, c + chunk) for c in range(0, skus, chunk)]
    for ref, c in ((own_ref, core), (other_ref, 1 - core)):
        for x in range(n // (CORES * side)):
            for t in range(0, side, 8):
                first = (x * side + t) * per
                top = pl.multiple_of(x * CORES * side + c * side + t, 8)

                def rows(row):
                    return ref[pl.ds(first + row, 8, stride=per), :]

                for j in range(n):
                    lanes = slice(j * LANES, (j + 1) * LANES)
                    base[pl.ds(top, 8), lanes] = rows(starts[0] + j)
                    diag[pl.ds(top, 8), lanes] = rows(starts[1] + j)
                for g in range(tiles):
                    lane = g * LANES % WIDE
                    down = pl.multiple_of(g * LANES // WIDE * n + top, 8)
                    wcat[pl.ds(down, 8), lane : lane + LANES] = rows(starts[2] + g)
                    bcat[pl.ds(down, 8), lane : lane + LANES] = rows(starts[3] + g)
            for k in range(side):
                first = (x * side + k) * per
                j = x * CORES * side + c * side + k
                lanes = pl.ds(pl.multiple_of(j * LANES, LANES), LANES)
                raw_base[:, lanes] = ref[first + starts[4] : first + starts[5], :]
                raw_weight[:, lanes] = ref[first + starts[5] : first + starts[6], :]

    region_table = region_ref[:, : 3 * regions]
    same = same_ref[:, : 2 * n]
    for source, target in ((raw_weight, wstore), (raw_base, bstore)):
        for lanes in chunks:
            parts = jnp.concatenate(split_all(source[:, lanes]), axis=0)
            target[:, lanes] = product(region_table, parts, ((1,), (0,)))

    def by_category(field):
        rows = wcat.shape[0]
        group = group_ref[...]
        masks = [group == g for g in range(rows // n)]
        none = jnp.zeros(group.shape, jnp.bfloat16)
        spread = jnp.concatenate(
            [jnp.where(mask, part, none) for part in split(field[...]) for mask in masks], axis=0
        )
        total = product(spread, table_ref[...], ((1,), (0,)))
        return total[:rows] + total[rows:]

    def spread(values, m, put):
        parts = jnp.concatenate(split(values), axis=0)
        groups = values.shape[0] // m
        for lanes in chunks:
            found = product(parts, flipped_ref[:, lanes], ((1,), (0,)))
            for t in range(0, chunk, LANES):
                tile = slice(lanes.start + t, lanes.start + t + LANES)
                members = cats_ref[tile.start // LANES : tile.start // LANES + 1, :]
                group = jnp.broadcast_to(members >> (WIDE.bit_length() - 1), (m, LANES))
                high, low = found[: groups * m, t : t + LANES], found[groups * m :, t : t + LANES]
                one = [
                    high[g * m : (g + 1) * m] + low[g * m : (g + 1) * m] for g in range(groups)
                ]
                bit = 1
                while len(one) > 1:
                    odd = group & bit != 0
                    pairs = [one[i : i + 2] for i in range(0, len(one), 2)]
                    one = [jnp.where(odd, *pair[::-1]) if len(pair) == 2 else pair[0] for pair in pairs]
                    bit *= 2
                put(tile, one[0])

    def by_region(part):
        return product(same, jnp.concatenate(split(part), axis=0), ((1,), (0,)))

    def tiles_in(lanes):
        for t in range(0, chunk, LANES):
            yield slice(lanes.start + t, lanes.start + t + LANES), slice(t, t + LANES)

    zero = jnp.zeros((n, LANES), jnp.float32)
    for lanes in chunks:
        sums = by_region(base[:, lanes])
        for tile, inner in tiles_in(lanes):
            basis[0, :, tile] = wstore[:, tile] * (bstore[:, tile] - sums[:, inner])
    norm = [zero]

    def start(tile, value):
        result = basis[0, :, tile] + value
        basis[0, :, tile] = result
        norm[0] = norm[0] + result * result

    spread(wcat[...] * (bcat[...] - by_category(base)), n, start)
    norms, quotients = [whole_sum(norm[0])], []
    for k in range(3):
        field, image = basis.at[k], basis.at[k + 1]
        sums = by_category(field)
        values = wcat[...] * sums
        square = values * sums
        dot = zero
        for lane in range(0, WIDE, LANES):
            for g in range(0, square.shape[0], n):
                dot = dot + square[g : g + n, lane : lane + LANES]
        for lanes in chunks:
            sums = by_region(field[:, lanes])
            for tile, inner in tiles_in(lanes):
                part = field[:, tile]
                result = diag[:, tile] * part + wstore[:, tile] * sums[:, inner]
                image[:, tile] = result
                dot = dot + part * result
        quotients.append(ratio(whole_sum(dot), norms[k]))
        back = ratio(norms[k], norms[k - 1]) if k else None
        if k == 2:
            break
        norm = [zero]

        def step(tile, value):
            result = image[:, tile] + value - quotients[k] * field[:, tile]
            if k:
                result = result - back * basis[k - 1, :, tile]
            image[:, tile] = result
            norm[0] = norm[0] + result * result

        spread(values, n, step)
        norms.append(whole_sum(norm[0]))

    lane = lax.broadcasted_iota(jnp.int32, line_out.shape, 1)
    place = lax.broadcasted_iota(jnp.int32, line_out.shape, 0)
    line = jnp.where((lane == 6) & (place == place_ref[0]), 1.0, 0.0)
    for i, value in enumerate(norms + quotients):
        line = jnp.where(lane == i, jnp.broadcast_to(value, line.shape), line)
    line_out[...] = line

    held[...] = values
    weeks = line_out.shape[0]
    tops = [
        pl.multiple_of(x * CORES * side + core * side + t, 8)
        for x in range(n // (CORES * side))
        for t in range(0, side, 8)
    ]
    for i, top in enumerate(tops):
        kept_out[4, i * 8 : i * 8 + 8, :] = base[pl.ds(top, 8), :]
        for k in range(4):
            kept_out[k, i * 8 : i * 8 + 8, :] = basis[k, pl.ds(top, 8), :]
    mine = jnp.concatenate(
        [held[pl.ds(g + top, 8), :] for g in range(0, held.shape[0], n) for top in tops], axis=0
    )

    def finish(tile, value):
        result = kept_out[3, :, tile] + value - quotients[2] * kept_out[2, :, tile]
        kept_out[3, :, tile] = result - back * kept_out[1, :, tile]

    spread(mine, weeks, finish)


def week_combine_body(lines_ref, kept_ref, send_ref, horizon):
    weeks = lines_ref.shape[0]
    n = kept_ref.shape[2] // LANES
    week = lax.broadcasted_iota(jnp.int32, (weeks, LANES), 0)
    lines = jnp.where(week < horizon, lines_ref[...], 0.0)
    n1, n2, n3, a1, a2, a3, mark = [
        jnp.take_along_axis(lines, jnp.full((weeks, LANES), i, jnp.int32), axis=1) for i in range(7)
    ]
    e2, e3 = ratio(n2, n1), ratio(n3, n2)

    def dot(left, right):
        terms = n1 * left[0] * right[0] + n2 * left[1] * right[1] + n3 * left[2] * right[2]
        return jnp.sum(terms, axis=0, keepdims=True)

    zero = jnp.zeros((weeks, LANES), jnp.float32)
    x = [zero, zero, zero]
    r = [zero + 1.0, zero, zero, zero]
    p = r[:3]
    rr = dot(r, r)
    for k in range(3):
        image = [
            a1 * p[0] + e2 * p[1],
            p[0] + a2 * p[1] + e3 * p[2],
            p[1] + a3 * p[2],
            p[2],
        ]
        alpha = rr / dot(p, image)
        x = [left + alpha * right for left, right in zip(x, p)]
        r = [left - alpha * right for left, right in zip(r, image)]
        if k < 2:
            new = dot(r, r)
            p = [left + new / rr * right for left, right in zip(r[:3], p)]
            rr = new
    mine = mark > 0.0
    x = [jnp.sum(jnp.where(mine, value, 0.0), axis=0, keepdims=True) for value in x]
    r = [jnp.sum(jnp.where(mine, value, 0.0), axis=0, keepdims=True) for value in r]
    rows = send_ref.shape[0] // weeks
    for t in range(0, weeks, 8):
        for j in range(n):
            lanes = slice(j * LANES, (j + 1) * LANES)
            parts = [kept_ref[k, t : t + 8, lanes] for k in range(4)]
            left = kept_ref[4, t : t + 8, lanes]
            right = r[3] * parts[3]
            for k in range(3):
                left = left + x[k] * parts[k]
                right = right + r[k] * parts[k]
            first = t * rows + j
            send_ref[pl.ds(first, 8, stride=rows), :] = left
            send_ref[pl.ds(first + n, 8, stride=rows), :] = right


def week_last_body(got_ref, x_out, r_out, sems):
    horizon, n, _ = x_out.shape
    copies = []
    for i, target in enumerate((x_out, r_out)):
        for first, number in week_cuts(horizon):
            weeks = pl.ds(first, number)
            source = got_ref.at[weeks, pl.ds(i * n, n)]
            copies.append(pltpu.make_async_copy(source, target.at[weeks], sems.at[len(copies)]))
    for copy in copies:
        copy.start()
    for copy in copies:
        copy.wait()


def exchange_weeks(blocks):
    return lax.all_to_all(blocks, ("x", "sku"), split_axis=0, concat_axis=0, tiled=True)


def by_weeks(
    base_bottom,
    weight_bottom,
    base_category,
    weight_category,
    base_region,
    weight_region,
    category_map,
    region_map,
):
    stores, horizon, skus = base_bottom.shape
    n = region_map.shape[0]
    regions = weight_region.shape[0]
    tiles = weight_category.shape[2] // LANES
    groups = weight_category.shape[2] // WIDE
    side = lax.axis_size("sku")
    weeks = lax.axis_size("x") * side
    place = lax.axis_index("x") * side + lax.axis_index("sku")
    place = place.astype(jnp.int32).reshape(1)
    core = lax.axis_index("core").astype(jnp.int32).reshape(1)
    cats = category_map.reshape(n, LANES)
    sources = (
        base_bottom.reshape(horizon, n, LANES),
        weight_bottom.reshape(horizon, n, LANES),
        weight_category.reshape(horizon, tiles, LANES),
        base_category.reshape(horizon, tiles, LANES),
        jnp.transpose(base_region, (1, 0, 2)),
        jnp.transpose(weight_region, (1, 0, 2)),
    )
    per = week_rows(tiles, n, regions)[-1]
    (sent,) = call(
        week_pack_body,
        [(weeks, per, LANES)],
        [pltpu.SemaphoreType.DMA((CUTS * len(sources),))],
        sources,
        [HBM] * len(sources),
        out_specs=(HBM,),
    )
    own = exchange_weeks(sent)
    other = lax.ppermute(own, "core", [(0, 1), (1, 0)])
    table, flipped, group, same, region = call(
        lambda *refs: week_table_body(*refs, regions),
        [
            jax.ShapeDtypeStruct((skus, WIDE), jnp.bfloat16),
            jax.ShapeDtypeStruct((WIDE, skus), jnp.bfloat16),
            jax.ShapeDtypeStruct((n, skus), jnp.bfloat16),
            jax.ShapeDtypeStruct((n, LANES), jnp.bfloat16),
            jax.ShapeDtypeStruct((n, LANES), jnp.bfloat16),
        ],
        [],
        (region_map, cats),
        [SMEM, VMEM],
    )
    full = pltpu.VMEM((n, skus), jnp.float32)
    raw = pltpu.VMEM((regions, skus), jnp.float32)
    cat = pltpu.VMEM((groups * n, WIDE), jnp.float32)
    kept, line = call(
        lambda *refs: week_body(*refs, side),
        [(5, weeks, skus), (weeks, LANES)],
        [
            full, pltpu.VMEM((4, n, skus), jnp.float32),
            full, full, full, cat, cat, raw, raw, cat,
        ],
        (
            core, place, own.reshape(-1, LANES), other.reshape(-1, LANES),
            table, flipped, group, same, region, cats,
        ),
        [SMEM, SMEM, VMEM, FREE] + [VMEM] * 6,
    )
    lines = exchange_weeks(line.reshape(weeks, 1, LANES)).reshape(weeks, LANES)
    (sent,) = call(
        lambda *refs: week_combine_body(*refs, horizon),
        [(weeks * 2 * n, LANES)],
        [],
        (lines, kept),
        [VMEM] * 2,
    )
    got = exchange_weeks(sent.reshape(weeks, 2 * n, LANES))
    x, r = call(
        week_last_body,
        [(horizon, n, LANES)] * 2,
        [pltpu.SemaphoreType.DMA((2 * CUTS,))],
        (got,),
        [VMEM],
        out_specs=(HBM, HBM),
    )
    return x.reshape(base_bottom.shape), r.reshape(base_bottom.shape)


def solution(mesh):
    def mapped(device_mesh, body, stores):
        split_stores = P(stores, None, None)
        split_skus = P(None, None, stores)
        return jax.shard_map(
            body,
            mesh=device_mesh,
            in_specs=(split_stores,) * 4 + (split_skus,) * 2 + (P(), P()),
            out_specs=(split_stores,) * 2,
            check_vma=False,
        )

    side = mesh.shape["sku"]
    chips = mesh.devices.reshape(-1, CORES, side)

    def program(base_bottom, *others):
        stores, horizon, skus = base_bottom.shape
        fits = 16 * stores * skus * 4 <= 16 << 20
        fits = fits and 3 * others[3].shape[0] <= LANES and LANES % stores == 0
        if fits and horizon <= chips.shape[0] * side and side % 8 == 0:
            device_mesh = Mesh(chips, ("x", "core", "sku"))
            return mapped(device_mesh, by_weeks, ("x", "core", "sku"))(base_bottom, *others)
        return mapped(mesh, on_device, ("store", "sku"))(base_bottom, *others)

    return program
```
